32 devices in a mesh: batch: 2 (over x), blk: 16 (over z, y, core).
Axes of the slice: x: 2, y: 2, z: 4, core: 2. Of those that a mesh axis runs over, the one named last changes fastest.
Arguments:
- tokens: bfloat16 [5120, 1024], P(('batch', 'blk')), may hold values from -6 to 6
- grad_out: bfloat16 [5120, 1024], P(('batch', 'blk')), may hold values from -6 to 6
- first_rows: int32 [2], P('batch'), may hold values from 64 to 160, as said below
- span_of: int32 [16], replicated, may hold values from 0 to 15, each once
- w_qkv: bfloat16 [2, 1024, 3072], P(None, 'blk'), may hold values from -0.1875 to 0.1875
- w_out: bfloat16 [2, 1024, 1024], P(None, 'blk'), may hold values from -0.1875 to 0.1875
- w_up: bfloat16 [2, 1024, 4096], P(None, 'blk'), may hold values from -0.1875 to 0.1875
- w_down: bfloat16 [2, 4096, 1024], P(None, 'blk'), may hold values from -0.09375 to 0.09375
- vec_gain: float32 [2, 3, 1024], replicated, may hold values from 0.5 to 1.5
- vec_bias: float32 [2, 7, 1024], replicated, may hold values from -2 to 2
- mid_gain: float32 [2, 4096], replicated, may hold values from 0.5 to 1.5
- mid_bias: float32 [2, 2, 4096], replicated, may hold values from -2 to 2
- head_scale: float32 [2, 16], replicated, may hold values from 0.25 to 1.75
Outputs:
- outputs: bfloat16 [5120, 1024], P(('batch', 'blk'))
- grad_tokens: float32 [5120, 1024], P(('batch', 'blk'))
- grad_w_qkv: float32 [2, 1024, 3072], P(None, 'blk')
- grad_w_out: float32 [2, 1024, 1024], P(None, 'blk')
- grad_w_up: float32 [2, 1024, 4096], P(None, 'blk')
- grad_w_down: float32 [2, 4096, 1024], P(None, 'blk')
- grad_vec_gain: float32 [2, 3, 1024], replicated
- grad_vec_bias: float32 [2, 7, 1024], replicated
- grad_mid_gain: float32 [2, 4096], replicated
- grad_mid_bias: float32 [2, 2, 4096], replicated
- grad_head_scale: float32 [2, 16], replicated
The draws below stay inside these ranges and needn't reach their ends.
Inputs may be any that keep to these rules, and one draw needn't show every extreme that they name: Every one of the 16 devices of group b holds first_rows[b] rows of the group's first sequence, then the rest of its 160 rows, if any, of a second sequence; first_rows[b] is 2, 3 or 5 times 32, and some group holds 160. Index j of blk holds span span_of[j], counted from a sequence's start, of every sequence of its group.
All inputs are finite; a program needn't handle non-finite values.
Results may differ from the reference program's by a relative error of at most 0.034.
Values may be sent and summed in bfloat16 or wider, within the bound.
A program may use at most 320 MiB of HBM per device.

```python
import math
from functools import partial
import jax
import jax.numpy as jnp
from jax import lax

D = 1024
HEADS = 16
HEAD_DIM = 64
FF = 4096
UNIT = 32
TOK_DEV = 160
GROUP_TOK = 2560
TOKENS = 5120
N_BATCH = 2
N_BLK = 16


def draw_first_rows(key, part):
    key = jax.random.fold_in(key, 7)
    pick_key = jax.random.fold_in(key, 11)
    place_key = jax.random.fold_in(key, 23)
    group_index = jnp.arange(N_BATCH, dtype=jnp.int32)
    chosen = jax.vmap(lambda index: jax.random.randint(jax.random.fold_in(pick_key, index), (), 0, 3))(group_index)
    unit_count = jnp.where(chosen == 0, 2, jnp.where(chosen == 1, 3, 5))
    longest = jax.random.randint(place_key, (), 0, N_BATCH)
    unit_count = jnp.where(group_index == longest, 5, unit_count)
    return (unit_count * UNIT).astype(jnp.int32)


def block_levels(key, dims, cuts, smallest, largest):
    gain = 1.0
    for axis_at, shards_of in cuts:
        draws = jax.random.uniform(jax.random.fold_in(jax.random.fold_in(key, 6), axis_at), (shards_of,), jnp.float32, smallest / len(cuts), largest / len(cuts))
        gain = gain * jnp.repeat(jnp.exp(draws), dims[axis_at] // shards_of).reshape((-1,) + (1,) * (len(dims) - 1 - axis_at))
    return gain


def centred(own_key, shape, width, most, cuts=(), kind=jnp.bfloat16):
    entries = jax.random.normal(own_key, shape, jnp.float32) * width
    if len(cuts) > 0:
        entries = block_levels(own_key, shape, cuts, -0.22, 0.18) * entries
    return jnp.clip(entries, min=-most, max=most).astype(kind)


def setup_inputs(seed: int = 0) -> dict:
    arg_keys = jax.random.split(jax.random.key(seed), 14)
    tokens = centred(arg_keys[0], (TOKENS, D), 1.0, 6.0, ((0, 32),))
    grad_out = centred(arg_keys[1], (TOKENS, D), 1.0, 6.0, ((0, 32),))
    first_rows = draw_first_rows(jax.random.fold_in(arg_keys[13], 71), 0)
    span_of = jax.random.permutation(arg_keys[3], N_BLK).astype(jnp.int32)
    w_qkv = centred(arg_keys[4], (2, D, 3 * D), D ** -0.5, 0.1875, ((1, 16),))
    w_out = centred(arg_keys[5], (2, D, D), D ** -0.5, 0.1875, ((1, 16),))
    w_up = centred(arg_keys[6], (2, D, FF), D ** -0.5, 0.1875, ((1, 16),))
    w_down = centred(arg_keys[7], (2, FF, D), FF ** -0.5, 0.09375, ((1, 16),))
    vec_gain = jnp.clip(1.0 + 0.1 * jax.random.normal(arg_keys[8], (2, 3, D), jnp.float32), 0.5, 1.5)
    vec_bias = centred(arg_keys[9], (2, 7, D), 0.3, 2.0, (), jnp.float32)
    mid_gain = jnp.clip(1.0 + 0.1 * jax.random.normal(arg_keys[10], (2, FF), jnp.float32), 0.5, 1.5)
    mid_bias = centred(arg_keys[11], (2, 2, FF), 0.3, 2.0, (), jnp.float32)
    head_scale = jnp.clip(1.0 + 0.15 * jax.random.normal(arg_keys[12], (2, HEADS), jnp.float32), 0.25, 1.75)
    return dict(tokens=tokens, grad_out=grad_out, first_rows=first_rows, span_of=span_of, w_qkv=w_qkv, w_out=w_out, w_up=w_up, w_down=w_down, vec_gain=vec_gain, vec_bias=vec_bias, mid_gain=mid_gain, mid_bias=mid_bias, head_scale=head_scale)


@jax.custom_vjp
def low(v):
    return lax.optimization_barrier(v.astype(jnp.bfloat16)).astype(jnp.float32)

@jax.custom_vjp
def low_back(v):
    return v

def low_keep(v):
    return (low(v), None)

def low_pass(kept, grad):
    return (grad,)

def back_keep(v):
    return (v, None)

def back_low(kept, grad):
    return (low(grad),)
low.defvjp(low_keep, low_pass)
low_back.defvjp(back_keep, back_low)
EPSILON = 1e-05
NEGATIVE = -1e+30
HIGHEST = lax.Precision.HIGHEST

def norm_rows(values, gains, shifts):
    average = lax.optimization_barrier(jnp.mean(values, axis=-1, keepdims=True))
    centered = values - average
    spread = lax.optimization_barrier(jnp.mean(centered * centered, axis=-1, keepdims=True))
    return centered * lax.rsqrt(spread + EPSILON) * gains + shifts

def product(left, right):
    return jnp.dot(left, right, precision=HIGHEST)

def attend_group(query, keys, values, seq_ids, places):
    group_rows = query.shape[0]
    query_rows = math.gcd(group_rows, 512)
    key_heads = keys.reshape(group_rows, HEADS, HEAD_DIM)
    value_heads = values.reshape(group_rows, HEADS, HEAD_DIM)
    scale_factor = HEAD_DIM ** (-0.5)

    def one_block(inputs):
        query_block, seq_block, place_block = inputs
        query_heads = query_block.reshape(query_rows, HEADS, HEAD_DIM)
        scores = low_back(jnp.einsum('qhd,khd->hqk', query_heads, key_heads, precision=HIGHEST) * scale_factor)
        visible = (seq_block[:, None] == seq_ids[None, :]) & (places[None, :] <= place_block[:, None])
        masked = jnp.where(visible[None], scores, NEGATIVE)
        peak_value = lax.optimization_barrier(jnp.max(masked, axis=-1, keepdims=True))
        summed = lax.optimization_barrier(jnp.sum(jnp.where(visible[None], jnp.exp(masked - peak_value), 0.0), axis=-1, keepdims=True))
        log_total = peak_value + jnp.log(summed)
        probs = low(jnp.where(visible[None], jnp.exp(masked - log_total), 0.0))
        mixed_heads = jnp.einsum('hqk,khd->qhd', probs, value_heads, precision=HIGHEST)
        return mixed_heads.reshape(query_rows, HEADS * HEAD_DIM)
    blocks_count = group_rows // query_rows
    pieces = lax.map(jax.checkpoint(one_block), (query.reshape(blocks_count, query_rows, -1), seq_ids.reshape(blocks_count, query_rows), places.reshape(blocks_count, query_rows)))
    return pieces.reshape(group_rows, -1)

def layer_pass(inputs, weight_qkv, weight_out, weight_up, weight_down, gains, biases, middle_gain, middle_bias, heads_scale, seq_ids, places):
    row_width = inputs.shape[1]
    normed = low(norm_rows(inputs, gains[0], biases[0]))
    projected = product(normed, weight_qkv)
    query = low_back(low(projected[:, :row_width] + biases[3]))
    keys = low_back(low(projected[:, row_width:2 * row_width]))
    values = low_back(low(projected[:, 2 * row_width:] + biases[4]))
    mixed = low_back(attend_group(query, keys, values, seq_ids, places))
    scaled = low(mixed * jnp.repeat(heads_scale, HEAD_DIM))
    branch = low_back(product(scaled, weight_out) + biases[5])
    middle_res = inputs + norm_rows(branch, gains[1], biases[1])
    ffn_in = low(norm_rows(middle_res, gains[2], biases[2]))
    upper = low_back(product(ffn_in, weight_up) + middle_bias[1])
    middle = low(norm_rows(jax.nn.gelu(upper, approximate=False), middle_gain, middle_bias[0]))
    return middle_res + low_back(product(middle, weight_down) + biases[6])

def group_forward(params, inputs):
    w_qkv, w_out, w_up, w_down, vec_gain, vec_bias, mid_gain, mid_bias, head_scale = params
    group_tokens, seq_ids, places = inputs
    current = group_tokens
    for layer_index in range(2):
        current = layer_pass(current, w_qkv[layer_index], w_out[layer_index], w_up[layer_index], w_down[layer_index], vec_gain[layer_index], vec_bias[layer_index], mid_gain[layer_index], mid_bias[layer_index], head_scale[layer_index], seq_ids, places)
    return current

def forward(tokens, w_qkv, w_out, w_up, w_down, vec_gain, vec_bias, mid_gain, mid_bias, head_scale, seq_ids, places):
    params = (w_qkv, w_out, w_up, w_down, vec_gain, vec_bias, mid_gain, mid_bias, head_scale)
    grouped = tokens.reshape(N_BATCH, GROUP_TOK, D)
    results = lax.map(jax.checkpoint(partial(group_forward, params)), (grouped, seq_ids, places))
    return results.reshape(TOKENS, D)

def layout(first_rows, span_of):
    rows_all = jnp.arange(GROUP_TOK, dtype=jnp.int32)
    device_of = rows_all // TOK_DEV
    within = rows_all % TOK_DEV
    first_len = first_rows.astype(jnp.int32)[:, None]
    second = (within[None, :] >= first_len).astype(jnp.int32)
    seq_rows = jnp.where(second == 1, TOK_DEV - first_len, first_len)
    places = span_of.astype(jnp.int32)[device_of][None, :] * seq_rows + within[None, :] - second * first_len
    return (second, places.astype(jnp.int32))

def reference(tokens, grad_out, first_rows, span_of, w_qkv, w_out, w_up, w_down, vec_gain, vec_bias, mid_gain, mid_bias, head_scale):
    seq_ids, places = layout(first_rows, span_of)
    run = partial(forward, seq_ids=seq_ids, places=places)
    primal, pullback = jax.vjp(run, tokens.astype(jnp.float32), w_qkv.astype(jnp.float32), w_out.astype(jnp.float32), w_up.astype(jnp.float32), w_down.astype(jnp.float32), vec_gain.astype(jnp.float32), vec_bias.astype(jnp.float32), mid_gain.astype(jnp.float32), mid_bias.astype(jnp.float32), head_scale.astype(jnp.float32))
    grads = pullback(grad_out.astype(jnp.float32))
    return (primal.astype(jnp.bfloat16), grads[0], grads[1], grads[2], grads[3], grads[4], grads[5], grads[6], grads[7], grads[8], grads[9])
```

```python
import functools

import jax
import jax.numpy as jnp
from jax import lax
from jax.experimental import pallas as pl
from jax.experimental.pallas import tpu as pltpu
from jax.sharding import PartitionSpec as P

HEAD_DIM = 64


EPSILON = 1e-05
NEGATIVE = -1e30


def shifted(x, axis, by):
    devices = lax.axis_size(axis)
    return lax.ppermute(x, axis, [(i, (i + by) % devices) for i in range(devices)])


def norm_rows(values, gains, shifts):
    average = jnp.mean(values, axis=-1, keepdims=True)
    centered = values - average
    spread = jnp.mean(centered * centered, axis=-1, keepdims=True)
    return centered * lax.rsqrt(spread + EPSILON) * gains + shifts


def mid_piece(upper, gains, shifts):
    return norm_rows(jax.nn.gelu(upper, approximate=False), gains, shifts)


def split_heads(matrix):
    return matrix.reshape(matrix.shape[0], -1, HEAD_DIM)


def block_rows(total_rows):
    chosen = total_rows
    while chosen > 1024 and chosen % 2 == 0:
        chosen = chosen // 2
    return chosen


def row_layout(first_rows, rows_here):
    within = jnp.arange(rows_here, dtype=jnp.int32)
    first_len = first_rows[0]
    second = (within >= first_len).astype(jnp.int32)
    return (second, within - second * first_len)


def visible_pairs(query_seq, query_off, query_span, key_seq, key_off, key_span):
    earlier = key_span[None, :] < query_span[:, None]
    same_span = (key_span[None, :] == query_span[:, None]) & (
        key_off[None, :] <= query_off[:, None]
    )
    return (query_seq[:, None] == key_seq[None, :]) & (earlier | same_span)


def merge_block(state_in, query_heads, keys_block, values_block, visible):
    run_peak, run_total, accumulated = state_in
    query_rows = query_heads.shape[0]
    scores = jnp.einsum(
        "qhd,khd->hqk", query_heads, split_heads(keys_block), preferred_element_type=jnp.float32
    ) * HEAD_DIM ** (-0.5)
    masked = jnp.where(visible[None], scores, NEGATIVE)
    new_peak = jnp.maximum(run_peak, jnp.max(masked, axis=-1))
    weights = jnp.where(visible[None], jnp.exp(masked - new_peak[:, :, None]), 0.0)
    factor = jnp.exp(run_peak - new_peak)
    new_total = run_total * factor + jnp.sum(weights, axis=-1)
    update = jnp.einsum(
        "hqk,khd->qhd",
        weights.astype(jnp.bfloat16),
        split_heads(values_block),
        preferred_element_type=jnp.float32,
    )
    rescaled = split_heads(accumulated) * jnp.transpose(factor)[:, :, None]
    return (new_peak, new_total, (rescaled + update).reshape(query_rows, -1))


def grad_block(query_heads, log_total, delta, dout_heads, keys_block, values_block, visible):
    key_heads = split_heads(keys_block)
    value_heads = split_heads(values_block)
    scores = jnp.einsum(
        "qhd,khd->hqk", query_heads, key_heads, preferred_element_type=jnp.float32
    ) * HEAD_DIM ** (-0.5)
    probs = jnp.where(visible[None], jnp.exp(scores - log_total[:, :, None]), 0.0)
    dprobs = jnp.einsum("qhd,khd->hqk", dout_heads, value_heads, preferred_element_type=jnp.float32)
    dscores = (probs * (dprobs - delta[:, :, None])).astype(jnp.bfloat16)
    add_query = jnp.einsum("hqk,khd->qhd", dscores, key_heads, preferred_element_type=jnp.float32)
    add_keys = jnp.einsum("hqk,qhd->khd", dscores, query_heads, preferred_element_type=jnp.float32)
    add_values = jnp.einsum(
        "hqk,qhd->khd", probs.astype(jnp.bfloat16), dout_heads, preferred_element_type=jnp.float32
    )
    return (
        add_query.reshape(query_heads.shape[0], -1),
        add_keys.reshape(key_heads.shape[0], -1),
        add_values.reshape(key_heads.shape[0], -1),
    )


def unchanged(state_in):
    return state_in


def attention_forward(query_low, keys_low, values_low, layout):
    seq_ids, offsets, span_of, my_span, my_index = layout
    rows_here, row_width = query_low.shape
    heads_here = row_width // HEAD_DIM
    query_heads = split_heads(query_low)
    query_span = jnp.full((rows_here,), my_span, jnp.int32)
    initial = (
        jnp.full((heads_here, rows_here), NEGATIVE, jnp.float32),
        jnp.zeros((heads_here, rows_here), jnp.float32),
        jnp.zeros((rows_here, row_width), jnp.float32),
    )
    running = initial
    key_part = lax.all_gather(keys_low, "blk", axis=0, tiled=True)
    value_part = lax.all_gather(values_low, "blk", axis=0, tiled=True)
    part_rows = key_part.shape[0]
    step_rows = block_rows(part_rows)

    def one_step(state_in, step_index):
        block_start = step_index * step_rows
        global_rows = block_start + jnp.arange(step_rows, dtype=jnp.int32)
        key_span = span_of[global_rows // rows_here]
        local_rows = global_rows % rows_here
        visible = visible_pairs(
            seq_ids, offsets, query_span, seq_ids[local_rows], offsets[local_rows], key_span
        )
        keys_block = lax.dynamic_slice_in_dim(key_part, block_start, step_rows, 0)
        values_block = lax.dynamic_slice_in_dim(value_part, block_start, step_rows, 0)

        def one_compute(inner_state):
            return merge_block(inner_state, query_heads, keys_block, values_block, visible)

        return (lax.cond(jnp.any(key_span <= my_span), one_compute, unchanged, state_in), None)

    running, _ = lax.scan(one_step, running, jnp.arange(part_rows // step_rows, dtype=jnp.int32))
    run_peak, run_total, accumulated = running
    mixed_heads = (split_heads(accumulated) / jnp.transpose(run_total)[:, :, None]).reshape(
        rows_here, row_width
    )
    return (mixed_heads, run_peak + jnp.log(run_total))


def cycle_backward(query_low, keys_low, values_low, log_total, delta, dout_low, layout):
    seq_ids, offsets, span_of, my_span, my_index = layout
    rows_here, row_width = query_low.shape
    blocks_total = lax.axis_size("blk")
    query_heads = split_heads(query_low)
    dout_heads = split_heads(dout_low)
    query_span = jnp.full((rows_here,), my_span, jnp.int32)

    def turn(turn_index, carried):
        keys_now, values_now, dkeys, dvalues, dquery = carried
        source = (my_index - turn_index) % blocks_total
        source_span = span_of[source]
        key_span = jnp.full((rows_here,), source_span, jnp.int32)
        visible = visible_pairs(seq_ids, offsets, query_span, seq_ids, offsets, key_span)

        def turn_compute(inner_state):
            add_query, add_keys, add_values = grad_block(
                query_heads, log_total, delta, dout_heads, keys_now, values_now, visible
            )
            return (
                inner_state[0] + add_query,
                inner_state[1] + add_keys,
                inner_state[2] + add_values,
            )

        dquery, dkeys, dvalues = lax.cond(
            source_span <= my_span, turn_compute, unchanged, (dquery, dkeys, dvalues)
        )
        keys_now, values_now = shifted((keys_now, values_now), "blk", 1)
        dkeys, dvalues = (
            shifted(dkeys.astype(jnp.bfloat16), "blk", 1).astype(dkeys.dtype),
            shifted(dvalues.astype(jnp.bfloat16), "blk", 1).astype(dvalues.dtype),
        )
        return (keys_now, values_now, dkeys, dvalues, dquery)

    zeros_rows = jnp.zeros((rows_here, row_width), jnp.float32)
    result = lax.fori_loop(
        0, blocks_total, turn, (keys_low, values_low, zeros_rows, zeros_rows, zeros_rows)
    )
    return (result[4], result[2], result[3])


def layer_forward(inputs, weights, gains, biases, middle_gain, middle_bias, heads_scale, layout):
    weight_qkv, weight_out, weight_up, weight_down = weights
    row_width = inputs.shape[1]
    normed, pre_pull = jax.vjp(norm_rows, inputs, gains[0], biases[0])
    normed_low = normed.astype(jnp.bfloat16)
    projected = jnp.dot(normed_low, weight_qkv, preferred_element_type=jnp.float32)
    query_low = (projected[:, :row_width] + biases[3]).astype(jnp.bfloat16)
    keys_low = projected[:, row_width : 2 * row_width].astype(jnp.bfloat16)
    values_low = (projected[:, 2 * row_width :] + biases[4]).astype(jnp.bfloat16)
    mixed_heads, log_total = attention_forward(query_low, keys_low, values_low, layout)
    scaled_low = (mixed_heads * jnp.repeat(heads_scale, HEAD_DIM)).astype(jnp.bfloat16)
    branch = jnp.dot(scaled_low, weight_out, preferred_element_type=jnp.float32) + biases[5]
    post_normed, post_pull = jax.vjp(norm_rows, branch, gains[1], biases[1])
    middle_res = inputs + post_normed
    ffn_normed, ffn_pull = jax.vjp(norm_rows, middle_res, gains[2], biases[2])
    ffn_low = ffn_normed.astype(jnp.bfloat16)
    upper = jnp.dot(ffn_low, weight_up, preferred_element_type=jnp.float32) + middle_bias[1]
    middle, mid_pull = jax.vjp(mid_piece, upper, middle_gain, middle_bias[0])
    middle_low = middle.astype(jnp.bfloat16)
    results = middle_res + (
        jnp.dot(middle_low, weight_down, preferred_element_type=jnp.float32) + biases[6]
    )
    record = {
        "pre_pull": pre_pull,
        "normed_low": normed_low,
        "query_low": query_low,
        "keys_low": keys_low,
        "values_low": values_low,
        "log_total": log_total,
        "mixed_heads": mixed_heads,
        "scaled_low": scaled_low,
        "post_pull": post_pull,
        "ffn_pull": ffn_pull,
        "ffn_low": ffn_low,
        "mid_pull": mid_pull,
        "middle_low": middle_low,
        "weights": weights,
    }
    return (results, record)


def layer_backward(d_results, record, weights, heads_scale, layout):
    weight_qkv, weight_out, weight_up, weight_down = weights
    rows_here, row_width = d_results.shape
    d_results_low = d_results.astype(jnp.bfloat16)
    grad_down = jnp.einsum(
        "tf,td->fd", record["middle_low"], d_results_low, preferred_element_type=jnp.float32
    )
    grad_down_bias = jnp.sum(d_results_low, axis=0, dtype=jnp.float32)
    d_middle = jnp.einsum(
        "td,fd->tf", d_results_low, weight_down, preferred_element_type=jnp.float32
    )
    d_upper, grad_mid_gain, grad_mid_shift = record["mid_pull"](d_middle)
    d_upper_low = d_upper.astype(jnp.bfloat16)
    grad_up = jnp.einsum(
        "td,tf->df", record["ffn_low"], d_upper_low, preferred_element_type=jnp.float32
    )
    grad_up_bias = jnp.sum(d_upper_low, axis=0, dtype=jnp.float32)
    d_ffn = jnp.einsum("tf,df->td", d_upper_low, weight_up, preferred_element_type=jnp.float32)
    d_res_part, grad_gain_ffn, grad_shift_ffn = record["ffn_pull"](d_ffn)
    d_middle_res = d_results + d_res_part
    d_branch, grad_gain_post, grad_shift_post = record["post_pull"](d_middle_res)
    d_branch_low = d_branch.astype(jnp.bfloat16)
    grad_out_w = jnp.einsum(
        "tc,td->cd", record["scaled_low"], d_branch_low, preferred_element_type=jnp.float32
    )
    grad_out_bias = jnp.sum(d_branch_low, axis=0, dtype=jnp.float32)
    d_scaled = jnp.einsum("td,cd->tc", d_branch_low, weight_out, preferred_element_type=jnp.float32)
    mixed_heads = record["mixed_heads"]
    grad_heads = jnp.sum((d_scaled * mixed_heads).reshape(rows_here, -1, HEAD_DIM), axis=(0, 2))
    d_mixed_low = (d_scaled * jnp.repeat(heads_scale, HEAD_DIM)).astype(jnp.bfloat16)
    delta = jnp.transpose(
        jnp.sum(
            (d_mixed_low.astype(jnp.float32) * mixed_heads).reshape(rows_here, -1, HEAD_DIM), axis=2
        )
    )
    dquery, dkeys, dvalues = cycle_backward(
        record["query_low"],
        record["keys_low"],
        record["values_low"],
        record["log_total"],
        delta,
        d_mixed_low,
        layout,
    )
    scale_factor = HEAD_DIM ** (-0.5)
    d_proj_low = jnp.concatenate(
        [dquery * scale_factor, dkeys * scale_factor, dvalues], axis=1
    ).astype(jnp.bfloat16)
    grad_qkv = jnp.einsum(
        "tc,te->ce", record["normed_low"], d_proj_low, preferred_element_type=jnp.float32
    )
    grad_q_bias = jnp.sum(d_proj_low[:, :row_width], axis=0, dtype=jnp.float32)
    grad_v_bias = jnp.sum(d_proj_low[:, 2 * row_width :], axis=0, dtype=jnp.float32)
    d_normed = jnp.einsum("te,ce->tc", d_proj_low, weight_qkv, preferred_element_type=jnp.float32)
    d_in_part, grad_gain_pre, grad_shift_pre = record["pre_pull"](d_normed)
    d_inputs = d_middle_res + d_in_part
    big_grads = (grad_qkv, grad_out_w, grad_up, grad_down)
    gain_grads = jnp.stack([grad_gain_pre, grad_gain_post, grad_gain_ffn])
    bias_grads = jnp.stack(
        [
            grad_shift_pre,
            grad_shift_post,
            grad_shift_ffn,
            grad_q_bias,
            grad_v_bias,
            grad_out_bias,
            grad_down_bias,
        ]
    )
    small_grads = (
        gain_grads,
        bias_grads,
        grad_mid_gain,
        jnp.stack([grad_mid_shift, grad_up_bias]),
        grad_heads,
    )
    return (d_inputs, big_grads, small_grads)


def general(
    tokens,
    grad_out,
    first_rows,
    span_of,
    w_qkv,
    w_out,
    w_up,
    w_down,
    vec_gain,
    vec_bias,
    mid_gain,
    mid_bias,
    head_scale,
):
    rows_here = tokens.shape[0]
    my_index = lax.axis_index("blk")
    my_span = span_of[my_index]
    seq_ids, offsets = row_layout(first_rows, rows_here)
    layout = (seq_ids, offsets, span_of, my_span, my_index)
    current = tokens.astype(jnp.float32)
    records = []
    for layer_index in range(2):
        weights = (
            lax.all_gather(w_qkv[layer_index], "blk", axis=0, tiled=True),
            lax.all_gather(w_out[layer_index], "blk", axis=0, tiled=True),
            lax.all_gather(w_up[layer_index], "blk", axis=0, tiled=True),
            lax.all_gather(w_down[layer_index], "blk", axis=0, tiled=True),
        )
        current, record = layer_forward(
            current,
            weights,
            vec_gain[layer_index],
            vec_bias[layer_index],
            mid_gain[layer_index],
            mid_bias[layer_index],
            head_scale[layer_index],
            layout,
        )
        records.append(record)
    results_low = current.astype(jnp.bfloat16)
    d_current = grad_out.astype(jnp.float32)
    shard_grads = [None, None]
    small_grads = [None, None]
    for layer_index in (1, 0):
        weights = (
            lax.all_gather(w_qkv[layer_index], "blk", axis=0, tiled=True),
            lax.all_gather(w_out[layer_index], "blk", axis=0, tiled=True),
            lax.all_gather(w_up[layer_index], "blk", axis=0, tiled=True),
            lax.all_gather(w_down[layer_index], "blk", axis=0, tiled=True),
        )
        d_current, big_grads, small_part = layer_backward(
            d_current, records[layer_index], weights, head_scale[layer_index], layout
        )
        shard_grads[layer_index] = (
            lax.psum_scatter(
                big_grads[0].astype(jnp.bfloat16), "blk", scatter_dimension=0, tiled=True
            ).astype(jnp.float32),
            lax.psum_scatter(
                big_grads[1].astype(jnp.bfloat16), "blk", scatter_dimension=0, tiled=True
            ).astype(jnp.float32),
            lax.psum_scatter(
                big_grads[2].astype(jnp.bfloat16), "blk", scatter_dimension=0, tiled=True
            ).astype(jnp.float32),
            lax.psum_scatter(
                big_grads[3].astype(jnp.bfloat16), "blk", scatter_dimension=0, tiled=True
            ).astype(jnp.float32),
        )
        small_grads[layer_index] = small_part
    stacked_small = [
        jnp.stack([small_grads[0][item_index], small_grads[1][item_index]])
        for item_index in range(5)
    ]
    summed_small = (
        lax.psum(stacked_small[0].astype(jnp.bfloat16), "blk").astype(jnp.float32),
        lax.psum(stacked_small[1].astype(jnp.bfloat16), "blk").astype(jnp.float32),
        lax.psum(stacked_small[2].astype(jnp.bfloat16), "blk").astype(jnp.float32),
        lax.psum(stacked_small[3].astype(jnp.bfloat16), "blk").astype(jnp.float32),
        lax.psum(stacked_small[4].astype(jnp.bfloat16), "blk").astype(jnp.float32),
    )
    stacked_big = [
        jnp.stack([shard_grads[0][item_index], shard_grads[1][item_index]])
        for item_index in range(4)
    ]
    totals = (
        lax.psum(stacked_big[0].astype(jnp.bfloat16), "batch").astype(jnp.float32),
        lax.psum(stacked_big[1].astype(jnp.bfloat16), "batch").astype(jnp.float32),
        lax.psum(stacked_big[2].astype(jnp.bfloat16), "batch").astype(jnp.float32),
        lax.psum(stacked_big[3].astype(jnp.bfloat16), "batch").astype(jnp.float32),
        lax.psum(summed_small[0].astype(jnp.bfloat16), "batch").astype(jnp.float32),
        lax.psum(summed_small[1].astype(jnp.bfloat16), "batch").astype(jnp.float32),
        lax.psum(summed_small[2].astype(jnp.bfloat16), "batch").astype(jnp.float32),
        lax.psum(summed_small[3].astype(jnp.bfloat16), "batch").astype(jnp.float32),
        lax.psum(summed_small[4].astype(jnp.bfloat16), "batch").astype(jnp.float32),
    )
    return (
        results_low,
        d_current,
        totals[0],
        totals[1],
        totals[2],
        totals[3],
        totals[4],
        totals[5],
        totals[6],
        totals[7],
        totals[8],
    )


MESH = pl.DeviceIdType.MESH
LINE = 4
HALVES = 2
CHUNK = 32
TILE = 512


def place():
    k = lax.axis_index("blk")
    return k // 4, lax.rem(k // 2, 2), lax.rem(k, 2)


def index_of(z, y, c):
    return (z * 2 + y) * 2 + c


def device(z, y, c):
    return {"blk": index_of(z, y, c)}


def hail(where):
    pl.semaphore_signal(pltpu.get_barrier_semaphore(), inc=1, device_id=where, device_id_type=MESH)


def greet_neighbours(z, y, c):
    hail(device(z, y, 1 - c))
    hail(device(z, 1 - y, c))

    @pl.when(z > 0)
    def _():
        hail(device(z - 1, y, c))

    @pl.when(z < LINE - 1)
    def _():
        hail(device(z + 1, y, c))

    pl.semaphore_wait(pltpu.get_barrier_semaphore(), 3 + jnp.where((z > 0) & (z < LINE - 1), 1, 0))


def remote(src, dst, send, recv, where):
    return pltpu.make_async_remote_copy(
        src_ref=src, dst_ref=dst, send_sem=send, recv_sem=recv, device_id=where, device_id_type=MESH
    )


def gather_kernel(x_ref, o_ref, sr, rr, sl, rl, sy, ry, sc, rc, own_sem):
    z, y, c = place()
    rows = x_ref.shape[0]
    half = rows // HALVES
    greet_neighbours(z, y, c)

    def block(zz, yy, h):
        return o_ref.at[pl.ds(index_of(zz, yy, c) * rows + h * half, half)]

    def source(zz, yy, h, own):
        return x_ref.at[pl.ds(h * half, half)] if own else block(zz, yy, h)

    def right(s, h):
        zz = z - s + 1
        return remote(source(zz, y, h, s == 1), block(zz, y, h), sr.at[s, h], rr.at[s, h], device(z + 1, y, c))

    def left(s, h):
        zz = z + s - 1
        return remote(source(zz, y, h, s == 1), block(zz, y, h), sl.at[s, h], rl.at[s, h], device(z - 1, y, c))

    def across(zz, h, own=False):
        return remote(source(zz, y, h, own), block(zz, y, h), sy.at[zz, h], ry.at[zz, h], device(z, 1 - y, c))

    def twin(zz, yy, h, own=False):
        slot = zz * 2 + yy
        return remote(source(zz, yy, h, own), block(zz, yy, h), sc.at[slot, h], rc.at[slot, h], device(z, y, 1 - c))

    def arrival(ref, send, recv):
        remote(ref, ref, send, recv, device(z, y, 1 - c)).wait_recv()

    own = pltpu.make_async_copy(x_ref, o_ref.at[pl.ds(index_of(z, y, c) * rows, rows)], own_sem)
    own.start()
    for h in range(HALVES):

        @pl.when(z < LINE - 1)
        def _():
            right(1, h).start()

        @pl.when(z > 0)
        def _():
            left(1, h).start()

        across(z, h, True).start()
    for h in range(HALVES):
        twin(z, y, h, True).start()

    def from_line(zz, h, send, recv):
        arrival(block(zz, y, h), send, recv)

    def pass_on(zz, h):
        across(zz, h).start()
        twin(zz, y, h).start()

    def from_across(zz, h):
        arrival(block(zz, 1 - y, h), sy.at[zz, h], ry.at[zz, h])
        twin(zz, 1 - y, h).start()

    for s in range(1, LINE):
        for h in range(HALVES):

            @pl.when(z >= s)
            def _():
                from_line(z - s, h, sr.at[s, h], rr.at[s, h])
                if s < LINE - 1:

                    @pl.when(z < LINE - 1)
                    def _():
                        right(s + 1, h).start()

                pass_on(z - s, h)

            @pl.when(z + s <= LINE - 1)
            def _():
                from_line(z + s, h, sl.at[s, h], rl.at[s, h])
                if s < LINE - 1:

                    @pl.when(z > 0)
                    def _():
                        left(s + 1, h).start()

                pass_on(z + s, h)

            if s == 1:
                from_across(z, h)
            else:

                @pl.when(z >= s - 1)
                def _():
                    from_across(z - s + 1, h)

                @pl.when(z + s - 1 <= LINE - 1)
                def _():
                    from_across(z + s - 1, h)

    for h in range(HALVES):

        @pl.when(z >= LINE - 1)
        def _():
            from_across(z - LINE + 1, h)

        @pl.when(z <= 0)
        def _():
            from_across(z + LINE - 1, h)

    own.wait()
    for h in range(HALVES):
        for zz in range(LINE):
            for yy in range(2):
                slot = zz * 2 + yy
                rows_there = o_ref.at[pl.ds(index_of(zz, yy, 1 - c) * rows + h * half, half)]
                arrival(rows_there, sc.at[slot, h], rc.at[slot, h])
                twin(zz, yy, h).wait_send()
            across(zz, h).wait_send()
        for s in range(1, LINE):

            @pl.when((z < LINE - 1) & (z >= s - 1))
            def _():
                right(s, h).wait_send()

            @pl.when((z > 0) & (z + s - 1 <= LINE - 1))
            def _():
                left(s, h).wait_send()


def gather_rows(x, collective_id):
    rows, columns = x.shape
    dma = pltpu.SemaphoreType.DMA
    return pl.pallas_call(
        gather_kernel,
        out_shape=jax.ShapeDtypeStruct((4 * LINE * rows, columns), x.dtype),
        in_specs=[pl.BlockSpec(memory_space=pl.ANY)],
        out_specs=pl.BlockSpec(memory_space=pl.ANY),
        scratch_shapes=[dma((LINE, HALVES))] * 6 + [dma((2 * LINE, HALVES))] * 2 + [dma],
        compiler_params=pltpu.CompilerParams(collective_id=collective_id, has_side_effects=True),
        name="gather_rows",
    )(x)


def order_at(z, t):
    table = ((3, 2, 1, 0), (3, 0, 2, 1), (0, 3, 1, 2), (0, 1, 2, 3))
    low = jnp.where(z == 0, table[0][t], table[1][t])
    high = jnp.where(z == 2, table[2][t], table[3][t])
    return jnp.where(z < 2, low, high)


def scatter_kernel(p_ref, o_ref, mine, twins, ysend, yrecv, zsend, zright, zleft, sm, sc, rc, sy, ry, sz, rzr, rzl):
    z, y, c = place()
    rows = mine.shape[1]
    half = rows // HALVES
    greet_neighbours(z, y, c)

    def part(h):
        return pl.ds(h * half, half)

    def source(t, own_y, cc, h):
        yy = y if own_y else 1 - y
        return p_ref.at[pl.ds(index_of(order_at(z, t), yy, cc) * rows + h * half, half)]

    def twin(t, own_y, h):
        slot = t * 2 + own_y
        return remote(source(t, own_y, 1 - c, h), twins.at[slot, part(h)], sc.at[slot, h], rc.at[slot, h], device(z, y, 1 - c))

    def local_copy(t, own_y, h):
        slot = t * 2 + own_y
        return pltpu.make_async_copy(source(t, own_y, c, h), mine.at[slot, part(h)], sm.at[slot, h])

    def across(t, h):
        return remote(ysend.at[t, part(h)], yrecv.at[t, part(h)], sy.at[t, h], ry.at[t, h], device(z, 1 - y, c))

    def wide(ref, slot, h):
        return ref[slot, part(h)].astype(jnp.float32)

    for own_y in (0, 1):
        for t in range(LINE):
            for h in range(HALVES):
                twin(t, own_y, h).start()
                local_copy(t, own_y, h).start()
    for t in range(LINE):
        for h in range(HALVES):
            twin(t, 0, h).wait_recv()
            local_copy(t, 0, h).wait()
            ysend[t, part(h)] = (wide(mine, 2 * t, h) + wide(twins, 2 * t, h)).astype(jnp.bfloat16)
            across(t, h).start()

    def along(d, t, h, to_right):
        buf, sem = (zright, rzr) if to_right else (zleft, rzl)
        where = device(z + 1, y, c) if to_right else device(z - 1, y, c)
        return remote(zsend.at[t, part(h)], buf.at[d, part(h)], sz.at[t, h], sem.at[d, h], where)

    def arrived(d, h, to_right):
        buf, sem = (zright, rzr) if to_right else (zleft, rzl)
        remote(buf.at[d, part(h)], buf.at[d, part(h)], sz.at[0, h], sem.at[d, h], device(z, y, 1 - c)).wait_recv()

    for t in range(LINE):
        d = order_at(z, t)
        for h in range(HALVES):
            twin(t, 1, h).wait_recv()
            local_copy(t, 1, h).wait()
            across(t, h).wait_recv()

            def summed(t=t, h=h):
                return wide(mine, 2 * t + 1, h) + wide(twins, 2 * t + 1, h) + wide(yrecv, t, h)

            if t < LINE - 1:
                for to_right in (True, False):

                    @pl.when((d > z) if to_right else (d < z))
                    def _():
                        first = (z == 0) if to_right else (z == LINE - 1)
                        buf = zright if to_right else zleft

                        @pl.when(first)
                        def _():
                            zsend[t, part(h)] = summed().astype(jnp.bfloat16)

                        @pl.when(jnp.logical_not(first))
                        def _():
                            arrived(d, h, to_right)
                            zsend[t, part(h)] = (summed() + wide(buf, d, h)).astype(jnp.bfloat16)

                        along(d, t, h, to_right).start()
            else:

                @pl.when(z > 0)
                def _():
                    arrived(z, h, True)

                @pl.when(z < LINE - 1)
                def _():
                    arrived(z, h, False)

                @pl.when(z == 0)
                def _():
                    o_ref[part(h)] = summed() + wide(zleft, z, h)

                @pl.when(z == LINE - 1)
                def _():
                    o_ref[part(h)] = summed() + wide(zright, z, h)

                @pl.when((z > 0) & (z < LINE - 1))
                def _():
                    o_ref[part(h)] = summed() + wide(zright, z, h) + wide(zleft, z, h)

    for h in range(HALVES):
        for t in range(LINE):
            across(t, h).wait_send()
            twin(t, 0, h).wait_send()
            twin(t, 1, h).wait_send()
        for t in range(LINE - 1):
            along(0, t, h, True).wait_send()


def scatter_rows(parts, collective_id):
    rows, columns = parts.shape[0] // (4 * LINE), parts.shape[1]
    dma = pltpu.SemaphoreType.DMA

    def blocks(n):
        return pltpu.VMEM((n, rows, columns), parts.dtype)

    return pl.pallas_call(
        scatter_kernel,
        out_shape=jax.ShapeDtypeStruct((rows, columns), jnp.float32),
        in_specs=[pl.BlockSpec(memory_space=pl.ANY)],
        out_specs=pl.BlockSpec(memory_space=pltpu.VMEM),
        scratch_shapes=[blocks(2 * LINE), blocks(2 * LINE), blocks(LINE), blocks(LINE), blocks(LINE - 1), blocks(LINE), blocks(LINE)]
        + [dma((2 * LINE, HALVES))] * 3
        + [dma((LINE, HALVES))] * 5,
        compiler_params=pltpu.CompilerParams(
            collective_id=collective_id, has_side_effects=True, vmem_limit_bytes=40 << 20
        ),
        name="scatter_rows",
    )(parts)


def swap_kernel(x_ref, o_ref, ss, rs, own_sem):
    k = lax.axis_index("blk")
    n = x_ref.shape[0]

    def greet(i, carry):
        hail({"blk": lax.rem(k + i, n)})
        return carry

    lax.fori_loop(1, n, greet, 0)
    pl.semaphore_wait(pltpu.get_barrier_semaphore(), n - 1)

    def send(i):
        to = lax.rem(k + i, n)
        return remote(x_ref.at[to], o_ref.at[k], ss.at[i], rs.at[i], {"blk": to})

    def receive(i):
        at = lax.rem(k - i + n, n)
        return remote(x_ref.at[at], o_ref.at[at], ss.at[i], rs.at[i], {"blk": at})

    def begin(i, carry):
        send(i).start()
        return carry

    lax.fori_loop(1, n, begin, 0)
    own = pltpu.make_async_copy(x_ref.at[k], o_ref.at[k], own_sem)
    own.start()
    own.wait()

    def finish(i, carry):
        receive(i).wait_recv()
        send(i).wait_send()
        return carry

    lax.fori_loop(1, n, finish, 0)


def swap_blocks(x, collective_id):
    n = x.shape[0]
    dma = pltpu.SemaphoreType.DMA
    return pl.pallas_call(
        swap_kernel,
        out_shape=jax.ShapeDtypeStruct(x.shape, x.dtype),
        in_specs=[pl.BlockSpec(memory_space=pl.ANY)],
        out_specs=pl.BlockSpec(memory_space=pl.ANY),
        scratch_shapes=[dma((n,)), dma((n,)), dma],
        compiler_params=pltpu.CompilerParams(collective_id=collective_id, has_side_effects=True),
        name="swap_blocks",
    )(x)


def pool_kernel(count, x_ref, o_ref, sent, got, ss, rs):
    z, y, c = place()
    hail(device(z, y, 1 - c))
    hail(device(z, 1 - y, c))
    for s in range(1, LINE):
        hail(device(lax.rem(z + s, LINE), y, c))
    pl.semaphore_wait(pltpu.get_barrier_semaphore(), LINE + 1)

    def pooled(values, share):
        if count is None:
            return functools.reduce(jnp.add, values)
        means = [v[0:1] for v in values]
        mean = functools.reduce(jnp.add, means) * (1.0 / len(values))
        squares = functools.reduce(jnp.add, [v[1:2] for v in values])
        apart = functools.reduce(jnp.add, [(m - mean) * (m - mean) for m in means])
        return jnp.concatenate([mean, squares + apart * share], axis=0)

    def exchange(slot, where):
        return remote(sent.at[slot], got.at[slot], ss.at[slot], rs.at[slot], where)

    value = x_ref[...]
    share = count
    for stage, where in enumerate((device(z, y, 1 - c), device(z, 1 - y, c))):
        sent[stage] = value
        copy = exchange(stage, where)
        copy.start()
        copy.wait()
        value = pooled([value, got[stage]], share)
        share = None if count is None else 2 * share
    sent[2] = value
    copies = []
    for s in range(1, LINE):
        where = device(lax.rem(z + s, LINE), y, c)
        copies.append(remote(sent.at[2], got.at[1 + s], ss.at[1 + s], rs.at[1 + s], where))
    for copy in copies:
        copy.start()
    for copy in copies:
        copy.wait()
    o_ref[...] = pooled([value] + [got[1 + s] for s in range(1, LINE)], share)


def pool_rows(x, count, collective_id):
    dma = pltpu.SemaphoreType.DMA
    return pl.pallas_call(
        functools.partial(pool_kernel, count),
        out_shape=jax.ShapeDtypeStruct(x.shape, x.dtype),
        in_specs=[pl.BlockSpec(memory_space=pltpu.VMEM)],
        out_specs=pl.BlockSpec(memory_space=pltpu.VMEM),
        scratch_shapes=[
            pltpu.VMEM((3,) + x.shape, x.dtype),
            pltpu.VMEM((LINE + 1,) + x.shape, x.dtype),
            dma((LINE + 1,)),
            dma((LINE + 1,)),
        ],
        compiler_params=pltpu.CompilerParams(collective_id=collective_id, has_side_effects=True),
        name="pool_rows",
    )(x)


NN = (((1,), (0,)), ((), ()))
NT = (((1,), (1,)), ((), ()))
TN = (((0,), (0,)), ((), ()))


def mul(a, b, dims=NN):
    return lax.dot_general(a, b, dims, preferred_element_type=jnp.float32)


def tile_at(t):
    return pl.ds(pl.multiple_of(t * TILE, TILE), TILE)


def chunk_at(index, rows=CHUNK):
    return pl.ds(pl.multiple_of(index * rows, rows), rows)


def diagonal(p):
    key = lax.broadcasted_iota(jnp.int32, p.shape, 0)
    query = lax.broadcasted_iota(jnp.int32, p.shape, 1)
    return key <= query


def attend_kernel(table, x_ref, w_ref, b_ref, scale_ref, qvk_ref, lse_ref, out_ref, packed_ref, flat, keys, values_t):
    total = x_ref.shape[0]
    tiles = total // TILE
    chunks = total // CHUNK

    def project(t, carry):
        flat[tile_at(t)] = (mul(x_ref[tile_at(t)], w_ref[...]) + b_ref[...]).astype(jnp.bfloat16)
        return carry

    lax.fori_loop(0, tiles, project, 0)

    def arrange(p, carry):
        qvk_ref[chunk_at(p)] = flat[chunk_at(table[p])]
        return carry

    lax.fori_loop(0, chunks, arrange, 0)

    def prepare(t, carry):
        keys[tile_at(t)] = qvk_ref[tile_at(t), 128:192]
        values_t[:, tile_at(t)] = jnp.transpose(qvk_ref[tile_at(t), 0:128].astype(jnp.float32))[64:128].astype(jnp.bfloat16)
        return carry

    lax.fori_loop(0, tiles, prepare, 0)
    cut = table[chunks]
    for i in range(tiles):
        at = slice(i * TILE, (i + 1) * TILE)
        query = qvk_ref[at, 0:64] * 0.125

        def block(j, state, masked):
            peak, part, mixed = state
            scores = mul(keys[tile_at(j)], query, NT)
            if masked:
                keep = diagonal(scores)
                scores = jnp.where(keep, scores, -1e30)
            new_peak = jnp.maximum(peak, jnp.max(scores, axis=0, keepdims=True))
            weights = jnp.exp(scores - new_peak)
            if masked:
                weights = jnp.where(keep, weights, 0.0)
            factor = jnp.exp(peak - new_peak)
            part = part * factor + jnp.sum(weights, axis=0, keepdims=True)
            mixed = mixed * factor + mul(values_t[:, tile_at(j)], weights.astype(jnp.bfloat16))
            return (new_peak, part, mixed)

        state = (
            jnp.full((1, TILE), -1e30, jnp.float32),
            jnp.zeros((1, TILE), jnp.float32),
            jnp.zeros((64, TILE), jnp.float32),
        )
        state = block(i, state, True)
        state = lax.fori_loop(jnp.where(i >= cut, cut, 0), i, functools.partial(block, masked=False), state)
        peak, part, mixed = state
        mixed = mixed / part
        lse_ref[:, at] = peak + jnp.log(part)
        out_ref[:, at] = mixed
        heads_out = jnp.transpose(mixed) * scale_ref[0, 0]
        pairs = heads_out.reshape(TILE // CHUNK, 2, CHUNK // 2, 64)
        pairs = jnp.concatenate([pairs[:, 0], pairs[:, 1]], axis=-1).astype(jnp.bfloat16)
        for q in range(TILE // CHUNK):
            packed_ref[chunk_at(table[i * (TILE // CHUNK) + q], CHUNK // 2)] = pairs[q]


def attend(table, x, w, b, scale):
    total = x.shape[0]
    vmem = pl.BlockSpec(memory_space=pltpu.VMEM)
    smem = pl.BlockSpec(memory_space=pltpu.SMEM)
    return pl.pallas_call(
        attend_kernel,
        out_shape=(
            jax.ShapeDtypeStruct((total, 192), jnp.bfloat16),
            jax.ShapeDtypeStruct((1, total), jnp.float32),
            jax.ShapeDtypeStruct((64, total), jnp.float32),
            jax.ShapeDtypeStruct((total // 2, 128), jnp.bfloat16),
        ),
        in_specs=[smem, vmem, vmem, vmem, smem],
        out_specs=(vmem, vmem, vmem, vmem),
        scratch_shapes=[
            pltpu.VMEM((total, 192), jnp.bfloat16),
            pltpu.VMEM((total, 64), jnp.bfloat16),
            pltpu.VMEM((64, total), jnp.bfloat16),
        ],
        compiler_params=pltpu.CompilerParams(vmem_limit_bytes=50 << 20),
        name="attend",
    )(table, x, w, b, scale)


def attend_back_kernel(
    table, da_ref, x_ref, w_ref, scale_ref, qvk_ref, lse_ref, out_ref,
    part_ref, gw_ref, gb_ref, gs_ref,
    packed, dout, delta, query, keys, values, keys_t, dkeys, dvalues, dquery_t, flat,
):
    total = x_ref.shape[0]
    tiles = total // TILE
    chunks = total // CHUNK
    per_tile = TILE // CHUNK

    def arrange(p, carry):
        packed[chunk_at(p, CHUNK // 2)] = da_ref[chunk_at(table[p], CHUNK // 2)]
        return carry

    lax.fori_loop(0, chunks, arrange, 0)
    scale = scale_ref[0, 0]

    def prepare(t, carry):
        at = tile_at(t)
        pairs = packed[chunk_at(t, TILE // 2)].astype(jnp.float32).reshape(per_tile, CHUNK // 2, 128)
        pairs = jnp.concatenate([pairs[:, :, 0:64], pairs[:, :, 64:128]], axis=1).reshape(TILE, 64)
        low = (pairs * scale).astype(jnp.bfloat16)
        dout[at] = low
        delta[:, at] = jnp.sum(jnp.transpose(low.astype(jnp.float32)) * out_ref[:, at], axis=0, keepdims=True)
        query[at] = qvk_ref[at, 0:64] * 0.125
        values[at] = qvk_ref[at, 64:128]
        key = qvk_ref[at, 128:192]
        keys[at] = key
        keys_t[:, at] = jnp.transpose(key.astype(jnp.float32)).astype(jnp.bfloat16)
        dkeys[at] = jnp.zeros((TILE, 64), jnp.float32)
        dvalues[at] = jnp.zeros((TILE, 64), jnp.float32)
        return carry

    lax.fori_loop(0, tiles, prepare, 0)
    gs_ref[...] = jnp.sum(delta[...], axis=1, keepdims=True) / scale
    cut = table[chunks]
    for i in range(tiles):
        at = slice(i * TILE, (i + 1) * TILE)
        query_i, dout_i, lse_i, delta_i = query[at], dout[at], lse_ref[:, at], delta[:, at]

        def block(j, total_dq, masked):
            there = tile_at(j)
            scores = mul(keys[there], query_i, NT)
            weights = jnp.exp(scores - lse_i)
            if masked:
                weights = jnp.where(diagonal(scores), weights, 0.0)
            dweights = mul(values[there], dout_i, NT)
            dscores = (weights * (dweights - delta_i)).astype(jnp.bfloat16)
            dvalues[there] += mul(weights.astype(jnp.bfloat16), dout_i)
            dkeys[there] += mul(dscores, query_i)
            return total_dq + mul(keys_t[:, there], dscores)

        total_dq = block(i, jnp.zeros((64, TILE), jnp.float32), True)
        total_dq = lax.fori_loop(jnp.where(i >= cut, cut, 0), i, functools.partial(block, masked=False), total_dq)
        dquery_t[:, at] = total_dq * 0.125

    gb_ref[...] = jnp.zeros_like(gb_ref)
    for i in range(tiles):
        at = slice(i * TILE, (i + 1) * TILE)
        joined = jnp.concatenate([jnp.transpose(dquery_t[:, at]), dvalues[at], dkeys[at]], axis=1).astype(jnp.bfloat16)
        gb_ref[...] += jnp.sum(joined.astype(jnp.float32), axis=0, keepdims=True)
        for q in range(per_tile):
            flat[chunk_at(table[i * per_tile + q])] = joined[q * CHUNK : (q + 1) * CHUNK]
    gw_ref[...] = jnp.zeros_like(gw_ref)

    def finish(t, carry):
        rows = flat[tile_at(t)]
        part_ref[tile_at(t)] = mul(rows, w_ref[...], NT).astype(jnp.bfloat16)
        gw_ref[...] += mul(rows, x_ref[tile_at(t)], TN)
        return carry

    lax.fori_loop(0, tiles, finish, 0)


def attend_back(table, da, x, w, scale, qvk, lse, out):
    total, width = x.shape
    vmem = pl.BlockSpec(memory_space=pltpu.VMEM)
    smem = pl.BlockSpec(memory_space=pltpu.SMEM)
    low = lambda *shape: pltpu.VMEM(shape, jnp.bfloat16)
    full = lambda *shape: pltpu.VMEM(shape, jnp.float32)
    return pl.pallas_call(
        attend_back_kernel,
        out_shape=(
            jax.ShapeDtypeStruct((total, width), jnp.bfloat16),
            jax.ShapeDtypeStruct((192, width), jnp.float32),
            jax.ShapeDtypeStruct((1, 192), jnp.float32),
            jax.ShapeDtypeStruct((1, 1), jnp.float32),
        ),
        in_specs=[smem, vmem, vmem, vmem, smem, vmem, vmem, vmem],
        out_specs=(vmem, vmem, vmem, vmem),
        scratch_shapes=[
            low(total // 2, 128), low(total, 64), full(1, total), low(total, 64), low(total, 64), low(total, 64),
            low(64, total), full(total, 64), full(total, 64), full(64, total), low(total, 192),
        ],
        compiler_params=pltpu.CompilerParams(vmem_limit_bytes=56 << 20),
        name="attend_back",
    )(table, da, x, w, scale, qvk, lse, out)


def up_kernel(x_ref, w_ref, b_ref, act_ref, slope_ref, stat_ref):
    def step(t, carry):
        at = tile_at(t)
        upper = mul(w_ref[...], x_ref[at], NT) + b_ref[...]
        chance = 0.5 * (1.0 + lax.erf(upper * (0.5**0.5)))
        act = upper * chance
        act_ref[:, at] = act
        slope_ref[:, at] = chance + upper * (jnp.exp(-0.5 * upper * upper) * 0.3989422804014327)
        mean = jnp.mean(act, axis=0, keepdims=True)
        apart = act - mean
        stat_ref[0:1, at] = mean
        stat_ref[1:2, at] = jnp.sum(apart * apart, axis=0, keepdims=True)
        return carry

    lax.fori_loop(0, x_ref.shape[0] // TILE, step, 0)


def up(x, w, b):
    total, hidden = x.shape[0], w.shape[0]
    vmem = pl.BlockSpec(memory_space=pltpu.VMEM)
    return pl.pallas_call(
        up_kernel,
        out_shape=(
            jax.ShapeDtypeStruct((hidden, total), jnp.float32),
            jax.ShapeDtypeStruct((hidden, total), jnp.float32),
            jax.ShapeDtypeStruct((2, total), jnp.float32),
        ),
        in_specs=[vmem] * 3,
        out_specs=(vmem,) * 3,
        compiler_params=pltpu.CompilerParams(vmem_limit_bytes=50 << 20),
        name="up",
    )(x, w, b)


def centred(act, stat, hidden_all):
    return (act - stat[0:1]) * lax.rsqrt(stat[1:2] * (1.0 / hidden_all) + EPSILON)


def down_kernel(hidden_all, act_ref, stat_ref, gain_ref, shift_ref, w_ref, part_ref, mid_ref):
    def step(t, carry):
        at = tile_at(t)
        vh = centred(act_ref[:, at], stat_ref[:, at], hidden_all)
        low = (vh * gain_ref[...] + shift_ref[...]).astype(jnp.bfloat16)
        mid_ref[:, at] = low
        part_ref[at] = mul(low, w_ref[...], TN).astype(jnp.bfloat16)
        return carry

    lax.fori_loop(0, act_ref.shape[1] // TILE, step, 0)


def down(hidden_all, act, stat, gain, shift, w):
    hidden, total = act.shape
    vmem = pl.BlockSpec(memory_space=pltpu.VMEM)
    return pl.pallas_call(
        functools.partial(down_kernel, hidden_all),
        out_shape=(
            jax.ShapeDtypeStruct((total, w.shape[1]), jnp.bfloat16),
            jax.ShapeDtypeStruct((hidden, total), jnp.bfloat16),
        ),
        in_specs=[vmem] * 5,
        out_specs=(vmem,) * 2,
        compiler_params=pltpu.CompilerParams(vmem_limit_bytes=50 << 20),
        name="down",
    )(act, stat, gain, shift, w)


def down_back_kernel(hidden_all, dy_ref, w_ref, act_ref, stat_ref, gain_ref, mid_ref, dmid_ref, sums_ref, gw_ref, gg_ref, gs_ref):
    gw_ref[...] = jnp.zeros_like(gw_ref)
    gg_ref[...] = jnp.zeros_like(gg_ref)
    gs_ref[...] = jnp.zeros_like(gs_ref)

    def step(t, carry):
        at = tile_at(t)
        dmid = mul(w_ref[...], dy_ref[at], NT)
        dmid_ref[:, at] = dmid
        vh = centred(act_ref[:, at], stat_ref[:, at], hidden_all)
        gg_ref[...] += jnp.sum(dmid * vh, axis=1, keepdims=True)
        gs_ref[...] += jnp.sum(dmid, axis=1, keepdims=True)
        scaled = dmid * gain_ref[...]
        sums_ref[0:1, at] = jnp.sum(scaled, axis=0, keepdims=True)
        sums_ref[1:2, at] = jnp.sum(scaled * vh, axis=0, keepdims=True)
        gw_ref[...] += mul(mid_ref[:, at], dy_ref[at])
        return carry

    lax.fori_loop(0, act_ref.shape[1] // TILE, step, 0)


def down_back(hidden_all, dy, w, act, stat, gain, mid):
    hidden, total = act.shape
    vmem = pl.BlockSpec(memory_space=pltpu.VMEM)
    return pl.pallas_call(
        functools.partial(down_back_kernel, hidden_all),
        out_shape=(
            jax.ShapeDtypeStruct((hidden, total), jnp.float32),
            jax.ShapeDtypeStruct((2, total), jnp.float32),
            jax.ShapeDtypeStruct(w.shape, jnp.float32),
            jax.ShapeDtypeStruct((hidden, 1), jnp.float32),
            jax.ShapeDtypeStruct((hidden, 1), jnp.float32),
        ),
        in_specs=[vmem] * 6,
        out_specs=(vmem,) * 5,
        compiler_params=pltpu.CompilerParams(vmem_limit_bytes=50 << 20),
        name="down_back",
    )(dy, w, act, stat, gain, mid)


def up_back_kernel(hidden_all, dmid_ref, act_ref, slope_ref, stat_ref, sums_ref, gain_ref, x_ref, w_ref, part_ref, gw_ref, gb_ref):
    gw_ref[...] = jnp.zeros_like(gw_ref)
    gb_ref[...] = jnp.zeros_like(gb_ref)

    def step(t, carry):
        at = tile_at(t)
        stat = stat_ref[:, at]
        vh = centred(act_ref[:, at], stat, hidden_all)
        rate = lax.rsqrt(stat[1:2] * (1.0 / hidden_all) + EPSILON)
        sums = sums_ref[:, at] * (1.0 / hidden_all)
        dact = rate * (dmid_ref[:, at] * gain_ref[...] - sums[0:1] - vh * sums[1:2])
        low = (dact * slope_ref[:, at]).astype(jnp.bfloat16)
        gb_ref[...] += jnp.sum(low.astype(jnp.float32), axis=1, keepdims=True)
        gw_ref[...] += mul(low, x_ref[at])
        part_ref[at] = mul(low, w_ref[...], TN).astype(jnp.bfloat16)
        return carry

    lax.fori_loop(0, act_ref.shape[1] // TILE, step, 0)


def up_back(hidden_all, dmid, act, slope, stat, sums, gain, x, w):
    hidden, total = act.shape
    vmem = pl.BlockSpec(memory_space=pltpu.VMEM)
    return pl.pallas_call(
        functools.partial(up_back_kernel, hidden_all),
        out_shape=(
            jax.ShapeDtypeStruct((total, w.shape[1]), jnp.bfloat16),
            jax.ShapeDtypeStruct(w.shape, jnp.float32),
            jax.ShapeDtypeStruct((hidden, 1), jnp.float32),
        ),
        in_specs=[vmem] * 8,
        out_specs=(vmem,) * 3,
        compiler_params=pltpu.CompilerParams(vmem_limit_bytes=56 << 20),
        name="up_back",
    )(dmid, act, slope, stat, sums, gain, x, w)


def chunk_table(first_rows, span_of, rows_here):
    blocks = span_of.shape[0]
    device_of = jnp.zeros((blocks,), jnp.int32).at[span_of].set(jnp.arange(blocks, dtype=jnp.int32))
    first = first_rows[0]
    second = rows_here - first
    row = jnp.arange(blocks * rows_here // CHUNK, dtype=jnp.int32) * CHUNK
    later = row >= first * blocks
    inside = jnp.where(later, row - first * blocks, row)
    length = jnp.where(later, jnp.maximum(second, 1), first)
    span = jnp.minimum(inside // length, blocks - 1)
    source = device_of[span] * rows_here + jnp.where(later, first, 0) + inside - span * length
    return jnp.concatenate([source // CHUNK, (first * blocks // TILE)[None]]).astype(jnp.int32)


def pack_rows(matrix):
    rows = matrix.shape[0]
    split = matrix.reshape(rows // CHUNK, 2, CHUNK // 2, -1, HEAD_DIM)
    return split.transpose(3, 0, 2, 1, 4).reshape(-1, rows // 2, 2 * HEAD_DIM)


def unpack_rows(blocks):
    heads, half_rows, _ = blocks.shape
    split = blocks.reshape(heads, half_rows // (CHUNK // 2), CHUNK // 2, 2, HEAD_DIM)
    return split.transpose(1, 3, 2, 0, 4).reshape(2 * half_rows, heads * HEAD_DIM)


def own_share(vector, index, size):
    return lax.dynamic_slice_in_dim(vector, index * size, size, 0)


def spread(vector, index, whole):
    return lax.dynamic_update_slice_in_dim(jnp.zeros((whole,), jnp.float32), vector, index * vector.shape[0], 0)


def exchange_weights(w_qkv, w_up, blocks):
    layers, rows, _ = w_qkv.shape
    width = rows * blocks
    by_head = w_qkv.reshape(layers, rows, 3, blocks, HEAD_DIM).transpose(3, 1, 0, 2, 4)
    by_head = by_head[:, :, :, jnp.array([0, 2, 1])].reshape(blocks, rows, -1)
    by_unit = w_up.reshape(layers, rows, blocks, -1).transpose(2, 1, 0, 3).reshape(blocks, rows, -1)
    by_head = swap_blocks(by_head, 2).reshape(width, layers, -1)
    by_unit = lax.all_to_all(by_unit, "blk", 0, 0, tiled=True).reshape(width, layers, -1)
    return by_head.transpose(1, 0, 2), by_unit.transpose(1, 2, 0)


def travel(
    tokens, grad_out, first_rows, span_of, w_qkv, w_out, w_up, w_down, vec_gain, vec_bias, mid_gain, mid_bias, head_scale
):
    blocks = lax.axis_size("blk")
    rows_here, row_width = tokens.shape
    index = lax.axis_index("blk")
    hidden_all = mid_gain.shape[1]
    hidden = hidden_all // blocks
    table = chunk_table(first_rows, span_of, rows_here)
    head_w, unit_w = exchange_weights(w_qkv, w_up, blocks)
    out_w = [lax.all_gather(w_out[layer], "blk", axis=0, tiled=True) for layer in range(2)]
    scales = [own_share(head_scale[layer], index, 1).reshape(1, 1) for layer in range(2)]
    middle_gain = [own_share(mid_gain[layer], index, hidden)[:, None] for layer in range(2)]
    middle_shift = [own_share(mid_bias[layer, 0], index, hidden)[:, None] for layer in range(2)]
    middle_bias = [own_share(mid_bias[layer, 1], index, hidden)[:, None] for layer in range(2)]
    current = tokens.astype(jnp.float32)
    records = []
    for layer in range(2):
        gains, biases = vec_gain[layer], vec_bias[layer]
        normed, pre_pull = jax.vjp(norm_rows, current, gains[0], biases[0])
        normed_all = gather_rows(normed.astype(jnp.bfloat16), 0)
        head_bias = jnp.concatenate(
            [
                own_share(biases[3], index, HEAD_DIM),
                own_share(biases[4], index, HEAD_DIM),
                jnp.zeros((HEAD_DIM,), jnp.float32),
            ]
        )[None]
        qvk, lse, head_out, packed = attend(table, normed_all, head_w[layer], head_bias, scales[layer])
        scaled_low = unpack_rows(swap_blocks(packed.reshape(blocks, rows_here // 2, 128), 3))
        branch = jnp.dot(scaled_low, out_w[layer], preferred_element_type=jnp.float32) + biases[5]
        post_normed, post_pull = jax.vjp(norm_rows, branch, gains[1], biases[1])
        middle_res = current + post_normed
        ffn_normed, ffn_pull = jax.vjp(norm_rows, middle_res, gains[2], biases[2])
        ffn_all = gather_rows(ffn_normed.astype(jnp.bfloat16), 0)
        act, slope, stat = up(ffn_all, unit_w[layer], middle_bias[layer])
        stat = pool_rows(stat, hidden, 4)
        parts, mid_low = down(hidden_all, act, stat, middle_gain[layer], middle_shift[layer], w_down[layer])
        current = middle_res + (scatter_rows(parts, 1) + biases[6])
        records.append(
            (pre_pull, post_pull, ffn_pull, normed_all, ffn_all, qvk, lse, head_out, scaled_low, act, slope, stat, mid_low)
        )
    results_low = current.astype(jnp.bfloat16)
    d_current = grad_out.astype(jnp.float32)
    head_grads, unit_grads, out_grads, down_grads = [None] * 2, [None] * 2, [None] * 2, [None] * 2
    small = [None] * 2
    for layer in (1, 0):
        pre_pull, post_pull, ffn_pull, normed_all, ffn_all, qvk, lse, head_out, scaled_low, act, slope, stat, mid_low = records[layer]
        d_low = d_current.astype(jnp.bfloat16)
        d_all = gather_rows(d_low, 0)
        dmid, sums, down_grads[layer], grad_mid_gain, grad_mid_shift = down_back(
            hidden_all, d_all, w_down[layer], act, stat, middle_gain[layer], mid_low
        )
        sums = pool_rows(sums, None, 5)
        parts, unit_grads[layer], grad_up_bias = up_back(
            hidden_all, dmid, act, slope, stat, sums, middle_gain[layer], ffn_all, unit_w[layer]
        )
        d_res_part, grad_gain_ffn, grad_shift_ffn = ffn_pull(scatter_rows(parts, 1))
        d_middle_res = d_current + d_res_part
        d_branch, grad_gain_post, grad_shift_post = post_pull(d_middle_res)
        d_branch_low = d_branch.astype(jnp.bfloat16)
        d_scaled = jnp.einsum("td,cd->tc", d_branch_low, out_w[layer], preferred_element_type=jnp.float32)
        out_grad = jnp.einsum("tc,td->cd", scaled_low, d_branch_low, preferred_element_type=jnp.float32)
        out_grads[layer] = lax.psum_scatter(out_grad.astype(jnp.bfloat16), "blk", scatter_dimension=0, tiled=True)
        d_heads = swap_blocks(pack_rows(d_scaled.astype(jnp.bfloat16)), 3).reshape(-1, 128)
        parts, head_grads[layer], head_bias, grad_scale = attend_back(
            table, d_heads, normed_all, head_w[layer], scales[layer], qvk, lse, head_out
        )
        d_in_part, grad_gain_pre, grad_shift_pre = pre_pull(scatter_rows(parts, 1))
        d_current = d_middle_res + d_in_part
        small[layer] = jnp.concatenate(
            [
                grad_gain_pre,
                grad_gain_post,
                grad_gain_ffn,
                grad_shift_pre,
                grad_shift_post,
                grad_shift_ffn,
                spread(head_bias[0, :HEAD_DIM], index, row_width),
                spread(head_bias[0, HEAD_DIM : 2 * HEAD_DIM], index, row_width),
                jnp.sum(d_branch_low, axis=0, dtype=jnp.float32),
                jnp.sum(d_low, axis=0, dtype=jnp.float32),
                spread(grad_mid_gain[:, 0], index, hidden_all),
                spread(grad_mid_shift[:, 0], index, hidden_all),
                spread(grad_up_bias[:, 0], index, hidden_all),
                spread(grad_scale[0], index, blocks),
            ]
        )
    small = lax.psum(jnp.stack(small), ("batch", "blk"))
    turned = [jnp.concatenate([head_grads[layer], unit_grads[layer]], axis=0).astype(jnp.bfloat16) for layer in range(2)]
    turned = lax.psum(jnp.stack(turned), "batch")
    turned = turned.reshape(2, -1, blocks, row_width // blocks).transpose(2, 0, 3, 1)
    turned = lax.all_to_all(turned, "blk", 0, 0, tiled=True).astype(jnp.float32)
    heads_back = turned[..., : 3 * HEAD_DIM].reshape(blocks, 2, -1, 3, HEAD_DIM)[:, :, :, jnp.array([0, 2, 1])]
    grad_qkv = heads_back.transpose(1, 2, 3, 0, 4).reshape(w_qkv.shape)
    grad_up = turned[..., 3 * HEAD_DIM :].transpose(1, 2, 0, 3).reshape(w_up.shape)
    grad_out_w = lax.psum(jnp.stack(out_grads), "batch").astype(jnp.float32)
    grad_down = lax.psum(jnp.stack(down_grads).astype(jnp.bfloat16), "batch").astype(jnp.float32)
    vec_end = 10 * row_width
    vectors = small[:, :vec_end].reshape(2, 10, row_width)
    middles = small[:, vec_end : vec_end + 3 * hidden_all].reshape(2, 3, hidden_all)
    return (
        results_low,
        d_current,
        grad_qkv,
        grad_out_w,
        grad_up,
        grad_down,
        vectors[:, :3],
        vectors[:, 3:],
        middles[:, 0],
        middles[:, 1:],
        small[:, vec_end + 3 * hidden_all :],
    )


def local(*args):
    tokens, w_qkv = args[0], args[4]
    blocks = lax.axis_size("blk")
    heads = w_qkv.shape[2] // (3 * HEAD_DIM)
    if blocks == heads and blocks == 4 * LINE and tokens.shape[0] * blocks % TILE == 0:
        return travel(*args)
    return general(*args)


def solution(mesh):
    placed = (
        P(("batch", "blk"), None),
        P(("batch", "blk"), None),
        P("batch"),
        P(),
        P(None, "blk", None),
        P(None, "blk", None),
        P(None, "blk", None),
        P(None, "blk", None),
        P(),
        P(),
        P(),
        P(),
        P(),
    )
    return jax.shard_map(
        local,
        mesh=mesh,
        in_specs=placed,
        out_specs=(
            P(("batch", "blk"), None),
            P(("batch", "blk"), None),
            P(None, "blk", None),
            P(None, "blk", None),
            P(None, "blk", None),
            P(None, "blk", None),
            P(),
            P(),
            P(),
            P(),
            P(),
        ),
        check_vma=False,
    )
```

```python
import functools

import jax
import jax.numpy as jnp
from jax import lax
from jax.experimental import pallas as pl
from jax.experimental.pallas import tpu as pltpu
from jax.sharding import PartitionSpec as P

HEAD_DIM = 64


EPSILON = 1e-05
NEGATIVE = -1e30


def shifted(x, axis, by):
    devices = lax.axis_size(axis)
    return lax.ppermute(x, axis, [(i, (i + by) % devices) for i in range(devices)])


def norm_rows(values, gains, shifts):
    average = jnp.mean(values, axis=-1, keepdims=True)
    centered = values - average
    spread = jnp.mean(centered * centered, axis=-1, keepdims=True)
    return centered * lax.rsqrt(spread + EPSILON) * gains + shifts


def mid_piece(upper, gains, shifts):
    return norm_rows(jax.nn.gelu(upper, approximate=False), gains, shifts)


def split_heads(matrix):
    return matrix.reshape(matrix.shape[0], -1, HEAD_DIM)


def block_rows(total_rows):
    chosen = total_rows
    while chosen > 1024 and chosen % 2 == 0:
        chosen = chosen // 2
    return chosen


def row_layout(first_rows, rows_here):
    within = jnp.arange(rows_here, dtype=jnp.int32)
    first_len = first_rows[0]
    second = (within >= first_len).astype(jnp.int32)
    return (second, within - second * first_len)


def visible_pairs(query_seq, query_off, query_span, key_seq, key_off, key_span):
    earlier = key_span[None, :] < query_span[:, None]
    same_span = (key_span[None, :] == query_span[:, None]) & (
        key_off[None, :] <= query_off[:, None]
    )
    return (query_seq[:, None] == key_seq[None, :]) & (earlier | same_span)


def merge_block(state_in, query_heads, keys_block, values_block, visible):
    run_peak, run_total, accumulated = state_in
    query_rows = query_heads.shape[0]
    scores = jnp.einsum(
        "qhd,khd->hqk", query_heads, split_heads(keys_block), preferred_element_type=jnp.float32
    ) * HEAD_DIM ** (-0.5)
    masked = jnp.where(visible[None], scores, NEGATIVE)
    new_peak = jnp.maximum(run_peak, jnp.max(masked, axis=-1))
    weights = jnp.where(visible[None], jnp.exp(masked - new_peak[:, :, None]), 0.0)
    factor = jnp.exp(run_peak - new_peak)
    new_total = run_total * factor + jnp.sum(weights, axis=-1)
    update = jnp.einsum(
        "hqk,khd->qhd",
        weights.astype(jnp.bfloat16),
        split_heads(values_block),
        preferred_element_type=jnp.float32,
    )
    rescaled = split_heads(accumulated) * jnp.transpose(factor)[:, :, None]
    return (new_peak, new_total, (rescaled + update).reshape(query_rows, -1))


def grad_block(query_heads, log_total, delta, dout_heads, keys_block, values_block, visible):
    key_heads = split_heads(keys_block)
    value_heads = split_heads(values_block)
    scores = jnp.einsum(
        "qhd,khd->hqk", query_heads, key_heads, preferred_element_type=jnp.float32
    ) * HEAD_DIM ** (-0.5)
    probs = jnp.where(visible[None], jnp.exp(scores - log_total[:, :, None]), 0.0)
    dprobs = jnp.einsum("qhd,khd->hqk", dout_heads, value_heads, preferred_element_type=jnp.float32)
    dscores = (probs * (dprobs - delta[:, :, None])).astype(jnp.bfloat16)
    add_query = jnp.einsum("hqk,khd->qhd", dscores, key_heads, preferred_element_type=jnp.float32)
    add_keys = jnp.einsum("hqk,qhd->khd", dscores, query_heads, preferred_element_type=jnp.float32)
    add_values = jnp.einsum(
        "hqk,qhd->khd", probs.astype(jnp.bfloat16), dout_heads, preferred_element_type=jnp.float32
    )
    return (
        add_query.reshape(query_heads.shape[0], -1),
        add_keys.reshape(key_heads.shape[0], -1),
        add_values.reshape(key_heads.shape[0], -1),
    )


def unchanged(state_in):
    return state_in


def attention_forward(query_low, keys_low, values_low, layout):
    seq_ids, offsets, span_of, my_span, my_index = layout
    rows_here, row_width = query_low.shape
    heads_here = row_width // HEAD_DIM
    query_heads = split_heads(query_low)
    query_span = jnp.full((rows_here,), my_span, jnp.int32)
    initial = (
        jnp.full((heads_here, rows_here), NEGATIVE, jnp.float32),
        jnp.zeros((heads_here, rows_here), jnp.float32),
        jnp.zeros((rows_here, row_width), jnp.float32),
    )
    running = initial
    key_part = lax.all_gather(keys_low, "blk", axis=0, tiled=True)
    value_part = lax.all_gather(values_low, "blk", axis=0, tiled=True)
    part_rows = key_part.shape[0]
    step_rows = block_rows(part_rows)

    def one_step(state_in, step_index):
        block_start = step_index * step_rows
        global_rows = block_start + jnp.arange(step_rows, dtype=jnp.int32)
        key_span = span_of[global_rows // rows_here]
        local_rows = global_rows % rows_here
        visible = visible_pairs(
            seq_ids, offsets, query_span, seq_ids[local_rows], offsets[local_rows], key_span
        )
        keys_block = lax.dynamic_slice_in_dim(key_part, block_start, step_rows, 0)
        values_block = lax.dynamic_slice_in_dim(value_part, block_start, step_rows, 0)

        def one_compute(inner_state):
            return merge_block(inner_state, query_heads, keys_block, values_block, visible)

        return (lax.cond(jnp.any(key_span <= my_span), one_compute, unchanged, state_in), None)

    running, _ = lax.scan(one_step, running, jnp.arange(part_rows // step_rows, dtype=jnp.int32))
    run_peak, run_total, accumulated = running
    mixed_heads = (split_heads(accumulated) / jnp.transpose(run_total)[:, :, None]).reshape(
        rows_here, row_width
    )
    return (mixed_heads, run_peak + jnp.log(run_total))


def cycle_backward(query_low, keys_low, values_low, log_total, delta, dout_low, layout):
    seq_ids, offsets, span_of, my_span, my_index = layout
    rows_here, row_width = query_low.shape
    blocks_total = lax.axis_size("blk")
    query_heads = split_heads(query_low)
    dout_heads = split_heads(dout_low)
    query_span = jnp.full((rows_here,), my_span, jnp.int32)

    def turn(turn_index, carried):
        keys_now, values_now, dkeys, dvalues, dquery = carried
        source = (my_index - turn_index) % blocks_total
        source_span = span_of[source]
        key_span = jnp.full((rows_here,), source_span, jnp.int32)
        visible = visible_pairs(seq_ids, offsets, query_span, seq_ids, offsets, key_span)

        def turn_compute(inner_state):
            add_query, add_keys, add_values = grad_block(
                query_heads, log_total, delta, dout_heads, keys_now, values_now, visible
            )
            return (
                inner_state[0] + add_query,
                inner_state[1] + add_keys,
                inner_state[2] + add_values,
            )

        dquery, dkeys, dvalues = lax.cond(
            source_span <= my_span, turn_compute, unchanged, (dquery, dkeys, dvalues)
        )
        keys_now, values_now = shifted((keys_now, values_now), "blk", 1)
        dkeys, dvalues = (
            shifted(dkeys.astype(jnp.bfloat16), "blk", 1).astype(dkeys.dtype),
            shifted(dvalues.astype(jnp.bfloat16), "blk", 1).astype(dvalues.dtype),
        )
        return (keys_now, values_now, dkeys, dvalues, dquery)

    zeros_rows = jnp.zeros((rows_here, row_width), jnp.float32)
    result = lax.fori_loop(
        0, blocks_total, turn, (keys_low, values_low, zeros_rows, zeros_rows, zeros_rows)
    )
    return (result[4], result[2], result[3])


def layer_forward(inputs, weights, gains, biases, middle_gain, middle_bias, heads_scale, layout):
    weight_qkv, weight_out, weight_up, weight_down = weights
    row_width = inputs.shape[1]
    normed, pre_pull = jax.vjp(norm_rows, inputs, gains[0], biases[0])
    normed_low = normed.astype(jnp.bfloat16)
    projected = jnp.dot(normed_low, weight_qkv, preferred_element_type=jnp.float32)
    query_low = (projected[:, :row_width] + biases[3]).astype(jnp.bfloat16)
    keys_low = projected[:, row_width : 2 * row_width].astype(jnp.bfloat16)
    values_low = (projected[:, 2 * row_width :] + biases[4]).astype(jnp.bfloat16)
    mixed_heads, log_total = attention_forward(query_low, keys_low, values_low, layout)
    scaled_low = (mixed_heads * jnp.repeat(heads_scale, HEAD_DIM)).astype(jnp.bfloat16)
    branch = jnp.dot(scaled_low, weight_out, preferred_element_type=jnp.float32) + biases[5]
    post_normed, post_pull = jax.vjp(norm_rows, branch, gains[1], biases[1])
    middle_res = inputs + post_normed
    ffn_normed, ffn_pull = jax.vjp(norm_rows, middle_res, gains[2], biases[2])
    ffn_low = ffn_normed.astype(jnp.bfloat16)
    upper = jnp.dot(ffn_low, weight_up, preferred_element_type=jnp.float32) + middle_bias[1]
    middle, mid_pull = jax.vjp(mid_piece, upper, middle_gain, middle_bias[0])
    middle_low = middle.astype(jnp.bfloat16)
    results = middle_res + (
        jnp.dot(middle_low, weight_down, preferred_element_type=jnp.float32) + biases[6]
    )
    record = {
        "pre_pull": pre_pull,
        "normed_low": normed_low,
        "query_low": query_low,
        "keys_low": keys_low,
        "values_low": values_low,
        "log_total": log_total,
        "mixed_heads": mixed_heads,
        "scaled_low": scaled_low,
        "post_pull": post_pull,
        "ffn_pull": ffn_pull,
        "ffn_low": ffn_low,
        "mid_pull": mid_pull,
        "middle_low": middle_low,
        "weights": weights,
    }
    return (results, record)


def layer_backward(d_results, record, weights, heads_scale, layout):
    weight_qkv, weight_out, weight_up, weight_down = weights
    rows_here, row_width = d_results.shape
    d_results_low = d_results.astype(jnp.bfloat16)
    grad_down = jnp.einsum(
        "tf,td->fd", record["middle_low"], d_results_low, preferred_element_type=jnp.float32
    )
    grad_down_bias = jnp.sum(d_results_low, axis=0, dtype=jnp.float32)
    d_middle = jnp.einsum(
        "td,fd->tf", d_results_low, weight_down, preferred_element_type=jnp.float32
    )
    d_upper, grad_mid_gain, grad_mid_shift = record["mid_pull"](d_middle)
    d_upper_low = d_upper.astype(jnp.bfloat16)
    grad_up = jnp.einsum(
        "td,tf->df", record["ffn_low"], d_upper_low, preferred_element_type=jnp.float32
    )
    grad_up_bias = jnp.sum(d_upper_low, axis=0, dtype=jnp.float32)
    d_ffn = jnp.einsum("tf,df->td", d_upper_low, weight_up, preferred_element_type=jnp.float32)
    d_res_part, grad_gain_ffn, grad_shift_ffn = record["ffn_pull"](d_ffn)
    d_middle_res = d_results + d_res_part
    d_branch, grad_gain_post, grad_shift_post = record["post_pull"](d_middle_res)
    d_branch_low = d_branch.astype(jnp.bfloat16)
    grad_out_w = jnp.einsum(
        "tc,td->cd", record["scaled_low"], d_branch_low, preferred_element_type=jnp.float32
    )
    grad_out_bias = jnp.sum(d_branch_low, axis=0, dtype=jnp.float32)
    d_scaled = jnp.einsum("td,cd->tc", d_branch_low, weight_out, preferred_element_type=jnp.float32)
    mixed_heads = record["mixed_heads"]
    grad_heads = jnp.sum((d_scaled * mixed_heads).reshape(rows_here, -1, HEAD_DIM), axis=(0, 2))
    d_mixed_low = (d_scaled * jnp.repeat(heads_scale, HEAD_DIM)).astype(jnp.bfloat16)
    delta = jnp.transpose(
        jnp.sum(
            (d_mixed_low.astype(jnp.float32) * mixed_heads).reshape(rows_here, -1, HEAD_DIM), axis=2
        )
    )
    dquery, dkeys, dvalues = cycle_backward(
        record["query_low"],
        record["keys_low"],
        record["values_low"],
        record["log_total"],
        delta,
        d_mixed_low,
        layout,
    )
    scale_factor = HEAD_DIM ** (-0.5)
    d_proj_low = jnp.concatenate(
        [dquery * scale_factor, dkeys * scale_factor, dvalues], axis=1
    ).astype(jnp.bfloat16)
    grad_qkv = jnp.einsum(
        "tc,te->ce", record["normed_low"], d_proj_low, preferred_element_type=jnp.float32
    )
    grad_q_bias = jnp.sum(d_proj_low[:, :row_width], axis=0, dtype=jnp.float32)
    grad_v_bias = jnp.sum(d_proj_low[:, 2 * row_width :], axis=0, dtype=jnp.float32)
    d_normed = jnp.einsum("te,ce->tc", d_proj_low, weight_qkv, preferred_element_type=jnp.float32)
    d_in_part, grad_gain_pre, grad_shift_pre = record["pre_pull"](d_normed)
    d_inputs = d_middle_res + d_in_part
    big_grads = (grad_qkv, grad_out_w, grad_up, grad_down)
    gain_grads = jnp.stack([grad_gain_pre, grad_gain_post, grad_gain_ffn])
    bias_grads = jnp.stack(
        [
            grad_shift_pre,
            grad_shift_post,
            grad_shift_ffn,
            grad_q_bias,
            grad_v_bias,
            grad_out_bias,
            grad_down_bias,
        ]
    )
    small_grads = (
        gain_grads,
        bias_grads,
        grad_mid_gain,
        jnp.stack([grad_mid_shift, grad_up_bias]),
        grad_heads,
    )
    return (d_inputs, big_grads, small_grads)


def general(
    tokens,
    grad_out,
    first_rows,
    span_of,
    w_qkv,
    w_out,
    w_up,
    w_down,
    vec_gain,
    vec_bias,
    mid_gain,
    mid_bias,
    head_scale,
):
    rows_here = tokens.shape[0]
    my_index = lax.axis_index("blk")
    my_span = span_of[my_index]
    seq_ids, offsets = row_layout(first_rows, rows_here)
    layout = (seq_ids, offsets, span_of, my_span, my_index)
    current = tokens.astype(jnp.float32)
    records = []
    for layer_index in range(2):
        weights = (
            lax.all_gather(w_qkv[layer_index], "blk", axis=0, tiled=True),
            lax.all_gather(w_out[layer_index], "blk", axis=0, tiled=True),
            lax.all_gather(w_up[layer_index], "blk", axis=0, tiled=True),
            lax.all_gather(w_down[layer_index], "blk", axis=0, tiled=True),
        )
        current, record = layer_forward(
            current,
            weights,
            vec_gain[layer_index],
            vec_bias[layer_index],
            mid_gain[layer_index],
            mid_bias[layer_index],
            head_scale[layer_index],
            layout,
        )
        records.append(record)
    results_low = current.astype(jnp.bfloat16)
    d_current = grad_out.astype(jnp.float32)
    shard_grads = [None, None]
    small_grads = [None, None]
    for layer_index in (1, 0):
        weights = (
            lax.all_gather(w_qkv[layer_index], "blk", axis=0, tiled=True),
            lax.all_gather(w_out[layer_index], "blk", axis=0, tiled=True),
            lax.all_gather(w_up[layer_index], "blk", axis=0, tiled=True),
            lax.all_gather(w_down[layer_index], "blk", axis=0, tiled=True),
        )
        d_current, big_grads, small_part = layer_backward(
            d_current, records[layer_index], weights, head_scale[layer_index], layout
        )
        shard_grads[layer_index] = (
            lax.psum_scatter(
                big_grads[0].astype(jnp.bfloat16), "blk", scatter_dimension=0, tiled=True
            ).astype(jnp.float32),
            lax.psum_scatter(
                big_grads[1].astype(jnp.bfloat16), "blk", scatter_dimension=0, tiled=True
            ).astype(jnp.float32),
            lax.psum_scatter(
                big_grads[2].astype(jnp.bfloat16), "blk", scatter_dimension=0, tiled=True
            ).astype(jnp.float32),
            lax.psum_scatter(
                big_grads[3].astype(jnp.bfloat16), "blk", scatter_dimension=0, tiled=True
            ).astype(jnp.float32),
        )
        small_grads[layer_index] = small_part
    stacked_small = [
        jnp.stack([small_grads[0][item_index], small_grads[1][item_index]])
        for item_index in range(5)
    ]
    summed_small = (
        lax.psum(stacked_small[0].astype(jnp.bfloat16), "blk").astype(jnp.float32),
        lax.psum(stacked_small[1].astype(jnp.bfloat16), "blk").astype(jnp.float32),
        lax.psum(stacked_small[2].astype(jnp.bfloat16), "blk").astype(jnp.float32),
        lax.psum(stacked_small[3].astype(jnp.bfloat16), "blk").astype(jnp.float32),
        lax.psum(stacked_small[4].astype(jnp.bfloat16), "blk").astype(jnp.float32),
    )
    stacked_big = [
        jnp.stack([shard_grads[0][item_index], shard_grads[1][item_index]])
        for item_index in range(4)
    ]
    totals = (
        lax.psum(stacked_big[0].astype(jnp.bfloat16), "batch").astype(jnp.float32),
        lax.psum(stacked_big[1].astype(jnp.bfloat16), "batch").astype(jnp.float32),
        lax.psum(stacked_big[2].astype(jnp.bfloat16), "batch").astype(jnp.float32),
        lax.psum(stacked_big[3].astype(jnp.bfloat16), "batch").astype(jnp.float32),
        lax.psum(summed_small[0].astype(jnp.bfloat16), "batch").astype(jnp.float32),
        lax.psum(summed_small[1].astype(jnp.bfloat16), "batch").astype(jnp.float32),
        lax.psum(summed_small[2].astype(jnp.bfloat16), "batch").astype(jnp.float32),
        lax.psum(summed_small[3].astype(jnp.bfloat16), "batch").astype(jnp.float32),
        lax.psum(summed_small[4].astype(jnp.bfloat16), "batch").astype(jnp.float32),
    )
    return (
        results_low,
        d_current,
        totals[0],
        totals[1],
        totals[2],
        totals[3],
        totals[4],
        totals[5],
        totals[6],
        totals[7],
        totals[8],
    )


MESH = pl.DeviceIdType.MESH
LINE = 4
HALVES = 2
CHUNK = 32
TILE = 512


def place():
    k = lax.axis_index("blk")
    return k // 4, lax.rem(k // 2, 2), lax.rem(k, 2)


def index_of(z, y, c):
    return (z * 2 + y) * 2 + c


def device(z, y, c):
    return {"blk": index_of(z, y, c)}


def hail(where):
    pl.semaphore_signal(pltpu.get_barrier_semaphore(), inc=1, device_id=where, device_id_type=MESH)


def other_group():
    return {"batch": 1 - lax.axis_index("batch")}


def greet_neighbours(z, y, c, also=None):
    if also is not None:
        hail(also)
    hail(device(z, y, 1 - c))
    hail(device(z, 1 - y, c))

    @pl.when(z > 0)
    def _():
        hail(device(z - 1, y, c))

    @pl.when(z < LINE - 1)
    def _():
        hail(device(z + 1, y, c))

    greeted = 3 if also is None else 4
    pl.semaphore_wait(pltpu.get_barrier_semaphore(), greeted + jnp.where((z > 0) & (z < LINE - 1), 1, 0))


def lasting(microseconds):
    return pl.CostEstimate(flops=0, bytes_accessed=int(microseconds * 3.5e6), transcendentals=0)


def remote(src, dst, send, recv, where):
    return pltpu.make_async_remote_copy(
        src_ref=src, dst_ref=dst, send_sem=send, recv_sem=recv, device_id=where, device_id_type=MESH
    )


class Swap:
    def __init__(self, x_ref, o_ref, ss, rs, own_sem):
        self.x_ref, self.o_ref, self.ss, self.rs, self.own_sem = x_ref, o_ref, ss, rs, own_sem
        self.k, self.n = lax.axis_index("blk"), o_ref.shape[0]

    @staticmethod
    def result(x):
        return jax.ShapeDtypeStruct((4 * LINE,) + x.shape[1:], x.dtype)

    @staticmethod
    def scratch():
        dma = pltpu.SemaphoreType.DMA
        return [dma((4 * LINE,)), dma((4 * LINE,)), dma]

    def source(self, to):
        return self.x_ref.at[lax.rem(to, self.x_ref.shape[0])]

    def send(self, i):
        to = lax.rem(self.k + i, self.n)
        return remote(self.source(to), self.o_ref.at[self.k], self.ss.at[i], self.rs.at[i], {"blk": to})

    def receive(self, i):
        at = lax.rem(self.k - i + self.n, self.n)
        return remote(self.o_ref.at[at], self.o_ref.at[at], self.ss.at[i], self.rs.at[i], {"blk": at})

    def own(self):
        return pltpu.make_async_copy(self.source(self.k), self.o_ref.at[self.k], self.own_sem)

    def start(self):
        def one(i, carry):
            self.send(i).start()
            return carry

        lax.fori_loop(1, self.n, one, 0)
        self.own().start()

    def finish(self):
        def one(i, carry):
            self.receive(i).wait_recv()
            self.send(i).wait_send()
            return carry

        self.own().wait()
        lax.fori_loop(1, self.n, one, 0)


class Trade:
    def __init__(self, x_ref, o_ref, ss, rs, own_sem):
        self.x_ref, self.o_ref, self.ss, self.rs, self.own_sem = x_ref, o_ref, ss, rs, own_sem
        self.z, self.y, self.c = place()

    @staticmethod
    def result(x):
        return jax.ShapeDtypeStruct((LINE,) + x.shape[1:], x.dtype)

    @staticmethod
    def scratch():
        dma = pltpu.SemaphoreType.DMA
        return [dma((LINE,)), dma((LINE,)), dma]

    def source(self, to):
        return self.x_ref.at[lax.rem(to, self.x_ref.shape[0])]

    def send(self, s):
        to = lax.rem(self.z + s, LINE)
        return remote(self.source(to), self.o_ref.at[self.z], self.ss.at[s], self.rs.at[s], device(to, self.y, self.c))

    def own(self):
        return pltpu.make_async_copy(self.source(self.z), self.o_ref.at[self.z], self.own_sem)

    def start(self):
        for s in range(1, LINE):
            self.send(s).start()
        self.own().start()

    def finish(self):
        self.own().wait()
        for s in range(1, LINE):
            at = lax.rem(self.z - s + LINE, LINE)
            slot = self.o_ref.at[at]
            remote(slot, slot, self.ss.at[s], self.rs.at[s], device(at, self.y, self.c)).wait_recv()
            self.send(s).wait_send()


class Cross:
    def __init__(self, x_ref, o_ref, ss, rs):
        self.copy = remote(x_ref, o_ref, ss, rs, other_group())

    @staticmethod
    def result(x):
        return jax.ShapeDtypeStruct(x.shape, x.dtype)

    @staticmethod
    def scratch():
        return [pltpu.SemaphoreType.DMA] * 2

    def start(self):
        self.copy.start()

    def finish(self):
        self.copy.wait()


class Rides:
    def __init__(self, rides):
        self.kinds = [kind for kind, _ in rides]
        self.arrays = [array for _, array in rides]

    def results(self):
        return [kind.result(array) for kind, array in zip(self.kinds, self.arrays)]

    def specs(self):
        return [pl.BlockSpec(memory_space=pl.ANY)] * len(self.kinds)

    def scratch(self):
        return [entry for kind in self.kinds for entry in kind.scratch()]

    def split(self, refs, inputs, outputs):
        n = len(self.kinds)
        ins, refs = refs[:inputs], refs[inputs:]
        sources, refs = refs[:n], refs[n:]
        outs, refs = refs[:outputs], refs[outputs:]
        results, refs = refs[:n], refs[n:]
        count = len(self.scratch())
        own, sems = refs[: len(refs) - count], list(refs[len(refs) - count :])
        objects = []
        for kind, source, result in zip(self.kinds, sources, results):
            k = len(kind.scratch())
            objects.append(kind(source, result, *sems[:k]))
            sems = sems[k:]
        return ins + outs + own, objects

    def far(self):
        return any(kind in (Swap, Trade) for kind in self.kinds)

    def crossing(self):
        return Cross in self.kinds


def start_all(rides):
    for ride in rides:
        ride.start()


def finish_all(rides):
    for ride in rides:
        ride.finish()


def greet_group(crossing=False, plane=False):
    k, n = lax.axis_index("blk"), 4 * LINE

    def one(i, carry):
        hail({"blk": lax.rem(k + i, n)})
        return carry

    lax.fori_loop(1, n, one, 0)
    more = 0
    if plane:
        x, z, y, c = plane_place()
        for d in range(4):
            hail(plane_device(1 - x, z, 1 - y if d & 2 else y, 1 - c if d & 1 else c))
        more = 4
    elif crossing:
        hail(other_group())
        more = 1
    pl.semaphore_wait(pltpu.get_barrier_semaphore(), n - 1 + more)


def gather_kernel(rides, *refs):
    (x_ref, o_ref, sr, rr, sl, rl, sy, ry, sc, rc, own_sem), riders = rides.split(refs, 1, 1)
    z, y, c = place()
    rows = x_ref.shape[0]
    half = rows // HALVES
    if rides.far():
        greet_group(rides.crossing())
    else:
        greet_neighbours(z, y, c, other_group() if rides.crossing() else None)

    def block(zz, yy, h):
        return o_ref.at[pl.ds(index_of(zz, yy, c) * rows + h * half, half)]

    def source(zz, yy, h, own):
        return x_ref.at[pl.ds(h * half, half)] if own else block(zz, yy, h)

    def right(s, h):
        zz = z - s + 1
        return remote(source(zz, y, h, s == 1), block(zz, y, h), sr.at[s, h], rr.at[s, h], device(z + 1, y, c))

    def left(s, h):
        zz = z + s - 1
        return remote(source(zz, y, h, s == 1), block(zz, y, h), sl.at[s, h], rl.at[s, h], device(z - 1, y, c))

    def across(zz, h, own=False):
        return remote(source(zz, y, h, own), block(zz, y, h), sy.at[zz, h], ry.at[zz, h], device(z, 1 - y, c))

    def twin(zz, yy, h, own=False):
        slot = zz * 2 + yy
        return remote(source(zz, yy, h, own), block(zz, yy, h), sc.at[slot, h], rc.at[slot, h], device(z, y, 1 - c))

    def arrival(ref, send, recv):
        remote(ref, ref, send, recv, device(z, y, 1 - c)).wait_recv()

    own = pltpu.make_async_copy(x_ref, o_ref.at[pl.ds(index_of(z, y, c) * rows, rows)], own_sem)
    own.start()
    for h in range(HALVES):

        @pl.when(z < LINE - 1)
        def _():
            right(1, h).start()

        @pl.when(z > 0)
        def _():
            left(1, h).start()

        across(z, h, True).start()
    for h in range(HALVES):
        twin(z, y, h, True).start()
    start_all(riders)

    def from_line(zz, h, send, recv):
        arrival(block(zz, y, h), send, recv)

    def pass_on(zz, h):
        across(zz, h).start()
        twin(zz, y, h).start()

    def from_across(zz, h):
        arrival(block(zz, 1 - y, h), sy.at[zz, h], ry.at[zz, h])
        twin(zz, 1 - y, h).start()

    for s in range(1, LINE):
        for h in range(HALVES):

            @pl.when(z >= s)
            def _():
                from_line(z - s, h, sr.at[s, h], rr.at[s, h])
                if s < LINE - 1:

                    @pl.when(z < LINE - 1)
                    def _():
                        right(s + 1, h).start()

                pass_on(z - s, h)

            @pl.when(z + s <= LINE - 1)
            def _():
                from_line(z + s, h, sl.at[s, h], rl.at[s, h])
                if s < LINE - 1:

                    @pl.when(z > 0)
                    def _():
                        left(s + 1, h).start()

                pass_on(z + s, h)

            if s == 1:
                from_across(z, h)
            else:

                @pl.when(z >= s - 1)
                def _():
                    from_across(z - s + 1, h)

                @pl.when(z + s - 1 <= LINE - 1)
                def _():
                    from_across(z + s - 1, h)

    for h in range(HALVES):

        @pl.when(z >= LINE - 1)
        def _():
            from_across(z - LINE + 1, h)

        @pl.when(z <= 0)
        def _():
            from_across(z + LINE - 1, h)

    own.wait()
    for h in range(HALVES):
        for zz in range(LINE):
            for yy in range(2):
                slot = zz * 2 + yy
                rows_there = o_ref.at[pl.ds(index_of(zz, yy, 1 - c) * rows + h * half, half)]
                arrival(rows_there, sc.at[slot, h], rc.at[slot, h])
                twin(zz, yy, h).wait_send()
            across(zz, h).wait_send()
        for s in range(1, LINE):

            @pl.when((z < LINE - 1) & (z >= s - 1))
            def _():
                right(s, h).wait_send()

            @pl.when((z > 0) & (z + s - 1 <= LINE - 1))
            def _():
                left(s, h).wait_send()

    finish_all(riders)


def gather_rows(x, collective_id, rides=()):
    rows, columns = x.shape
    dma = pltpu.SemaphoreType.DMA
    rides = Rides(rides)
    return pl.pallas_call(
        functools.partial(gather_kernel, rides),
        out_shape=[jax.ShapeDtypeStruct((4 * LINE * rows, columns), x.dtype)] + rides.results(),
        in_specs=[pl.BlockSpec(memory_space=pl.ANY)] + rides.specs(),
        out_specs=[pl.BlockSpec(memory_space=pl.ANY)] + rides.specs(),
        scratch_shapes=[dma((LINE, HALVES))] * 6 + [dma((2 * LINE, HALVES))] * 2 + [dma] + rides.scratch(),
        cost_estimate=lasting(30),
        compiler_params=pltpu.CompilerParams(collective_id=collective_id, has_side_effects=True),
        name="gather_rows",
    )(x, *rides.arrays)


def order_at(z, t):
    table = ((3, 2, 1, 0), (3, 0, 2, 1), (0, 3, 1, 2), (0, 1, 2, 3))
    low = jnp.where(z == 0, table[0][t], table[1][t])
    high = jnp.where(z == 2, table[2][t], table[3][t])
    return jnp.where(z < 2, low, high)


def scatter_kernel(rides, *refs):
    refs, riders = rides.split(refs, 1, 1)
    p_ref, o_ref, mine, twins, ysend, yrecv, zsend, zright, zleft, sm, sc, rc, sy, ry, sz, rzr, rzl = refs
    z, y, c = place()
    rows = mine.shape[1]
    half = rows // HALVES
    if rides.far():
        greet_group(rides.crossing())
    else:
        greet_neighbours(z, y, c, other_group() if rides.crossing() else None)

    def part(h):
        return pl.ds(h * half, half)

    def source(t, own_y, cc, h):
        yy = y if own_y else 1 - y
        return p_ref.at[pl.ds(index_of(order_at(z, t), yy, cc) * rows + h * half, half)]

    def twin(t, own_y, h):
        slot = t * 2 + own_y
        return remote(source(t, own_y, 1 - c, h), twins.at[slot, part(h)], sc.at[slot, h], rc.at[slot, h], device(z, y, 1 - c))

    def local_copy(t, own_y, h):
        slot = t * 2 + own_y
        return pltpu.make_async_copy(source(t, own_y, c, h), mine.at[slot, part(h)], sm.at[slot, h])

    def across(t, h):
        return remote(ysend.at[t, part(h)], yrecv.at[t, part(h)], sy.at[t, h], ry.at[t, h], device(z, 1 - y, c))

    def wide(ref, slot, h):
        return ref[slot, part(h)].astype(jnp.float32)

    for own_y in (0, 1):
        for t in range(LINE):
            for h in range(HALVES):
                twin(t, own_y, h).start()
                local_copy(t, own_y, h).start()
    start_all(riders)
    for t in range(LINE):
        for h in range(HALVES):
            twin(t, 0, h).wait_recv()
            local_copy(t, 0, h).wait()
            ysend[t, part(h)] = (wide(mine, 2 * t, h) + wide(twins, 2 * t, h)).astype(jnp.bfloat16)
            across(t, h).start()

    def along(d, t, h, to_right):
        buf, sem = (zright, rzr) if to_right else (zleft, rzl)
        where = device(z + 1, y, c) if to_right else device(z - 1, y, c)
        return remote(zsend.at[t, part(h)], buf.at[d, part(h)], sz.at[t, h], sem.at[d, h], where)

    def arrived(d, h, to_right):
        buf, sem = (zright, rzr) if to_right else (zleft, rzl)
        remote(buf.at[d, part(h)], buf.at[d, part(h)], sz.at[0, h], sem.at[d, h], device(z, y, 1 - c)).wait_recv()

    for t in range(LINE):
        d = order_at(z, t)
        for h in range(HALVES):
            twin(t, 1, h).wait_recv()
            local_copy(t, 1, h).wait()
            across(t, h).wait_recv()

            def summed(t=t, h=h):
                return wide(mine, 2 * t + 1, h) + wide(twins, 2 * t + 1, h) + wide(yrecv, t, h)

            if t < LINE - 1:
                for to_right in (True, False):

                    @pl.when((d > z) if to_right else (d < z))
                    def _():
                        first = (z == 0) if to_right else (z == LINE - 1)
                        buf = zright if to_right else zleft

                        @pl.when(first)
                        def _():
                            zsend[t, part(h)] = summed().astype(jnp.bfloat16)

                        @pl.when(jnp.logical_not(first))
                        def _():
                            arrived(d, h, to_right)
                            zsend[t, part(h)] = (summed() + wide(buf, d, h)).astype(jnp.bfloat16)

                        along(d, t, h, to_right).start()
            else:

                @pl.when(z > 0)
                def _():
                    arrived(z, h, True)

                @pl.when(z < LINE - 1)
                def _():
                    arrived(z, h, False)

                @pl.when(z == 0)
                def _():
                    o_ref[part(h)] = summed() + wide(zleft, z, h)

                @pl.when(z == LINE - 1)
                def _():
                    o_ref[part(h)] = summed() + wide(zright, z, h)

                @pl.when((z > 0) & (z < LINE - 1))
                def _():
                    o_ref[part(h)] = summed() + wide(zright, z, h) + wide(zleft, z, h)

    for h in range(HALVES):
        for t in range(LINE):
            across(t, h).wait_send()
            twin(t, 0, h).wait_send()
            twin(t, 1, h).wait_send()
        for t in range(LINE - 1):
            along(0, t, h, True).wait_send()
    finish_all(riders)


def scatter_rows(parts, collective_id, rides=()):
    rows, columns = parts.shape[0] // (4 * LINE), parts.shape[1]
    dma = pltpu.SemaphoreType.DMA

    def blocks(n):
        return pltpu.VMEM((n, rows, columns), parts.dtype)

    rides = Rides(rides)
    return pl.pallas_call(
        functools.partial(scatter_kernel, rides),
        out_shape=[jax.ShapeDtypeStruct((rows, columns), jnp.float32)] + rides.results(),
        in_specs=[pl.BlockSpec(memory_space=pl.ANY)] + rides.specs(),
        out_specs=[pl.BlockSpec(memory_space=pltpu.VMEM)] + rides.specs(),
        scratch_shapes=[blocks(2 * LINE), blocks(2 * LINE), blocks(LINE), blocks(LINE), blocks(LINE - 1), blocks(LINE), blocks(LINE)]
        + [dma((2 * LINE, HALVES))] * 3
        + [dma((LINE, HALVES))] * 5
        + rides.scratch(),
        cost_estimate=lasting(32),
        compiler_params=pltpu.CompilerParams(
            collective_id=collective_id, has_side_effects=True, vmem_limit_bytes=40 << 20
        ),
        name="scatter_rows",
    )(parts, *rides.arrays)


def swap_kernel(rides, *refs):
    _, riders = rides.split(refs, 0, 0)
    greet_group(rides.crossing())
    start_all(riders)
    finish_all(riders)


def swap_blocks(x, collective_id, rides=()):
    rides = Rides([(Swap, x), *rides])
    return pl.pallas_call(
        functools.partial(swap_kernel, rides),
        out_shape=rides.results(),
        in_specs=rides.specs(),
        out_specs=rides.specs(),
        scratch_shapes=rides.scratch(),
        cost_estimate=lasting(10),
        compiler_params=pltpu.CompilerParams(collective_id=collective_id, has_side_effects=True),
        name="swap_blocks",
    )(*rides.arrays)


def finale_kernel(rides, *refs):
    (v_ref, vo_ref, sent, got, vs, vr), riders = rides.split(refs, 1, 1)
    z, y, c = place()
    greet_group(True)
    cross = remote(v_ref, got.at[0], vs.at[0], vr.at[0], other_group())
    cross.start()
    start_all(riders)

    def wide(ref):
        return ref.astype(jnp.float32)

    cross.wait_recv()
    value = wide(v_ref[...]) + wide(got[0])
    for stage, where in ((1, device(z, y, 1 - c)), (2, device(z, 1 - y, c))):
        sent[stage - 1] = value.astype(jnp.bfloat16)
        copy = remote(sent.at[stage - 1], got.at[stage], vs.at[stage], vr.at[stage], where)
        copy.start()
        copy.wait_recv()
        value = wide(sent[stage - 1]) + wide(got[stage])
    sent[2] = value.astype(jnp.bfloat16)
    copies = []
    for s in range(1, LINE):
        where = device(lax.rem(z + s, LINE), y, c)
        copies.append(remote(sent.at[2], got.at[2 + s], vs.at[2 + s], vr.at[2 + s], where))
    for copy in copies:
        copy.start()
    for copy in copies:
        copy.wait_recv()
    total = jnp.zeros_like(value)
    for zz in range(LINE):
        term = wide(sent[2])
        for s in range(1, LINE):
            term = jnp.where(lax.rem(z - s + LINE, LINE) == zz, wide(got[2 + s]), term)
        total += term
    vo_ref[...] = total
    cross.wait_send()
    for stage in (1, 2):
        remote(sent.at[stage - 1], got.at[stage], vs.at[stage], vr.at[stage], device(z, y, 1 - c)).wait_send()
    for copy in copies:
        copy.wait_send()
    finish_all(riders)


def finale(v, collective_id, rides):
    rides = Rides(rides)
    dma = pltpu.SemaphoreType.DMA
    vmem = [pl.BlockSpec(memory_space=pltpu.VMEM)]
    return pl.pallas_call(
        functools.partial(finale_kernel, rides),
        out_shape=[jax.ShapeDtypeStruct(v.shape, jnp.float32)] + rides.results(),
        in_specs=vmem + rides.specs(),
        out_specs=vmem + rides.specs(),
        scratch_shapes=[
            pltpu.VMEM((3,) + v.shape, v.dtype),
            pltpu.VMEM((LINE + 2,) + v.shape, v.dtype),
            dma((LINE + 2,)),
            dma((LINE + 2,)),
        ]
        + rides.scratch(),
        cost_estimate=lasting(18),
        compiler_params=pltpu.CompilerParams(collective_id=collective_id, has_side_effects=True),
        name="finale",
    )(v, *rides.arrays)


NN = (((1,), (0,)), ((), ()))
NT = (((1,), (1,)), ((), ()))
TN = (((0,), (0,)), ((), ()))


def mul(a, b, dims=NN):
    return lax.dot_general(a, b, dims, preferred_element_type=jnp.float32)


def tile_at(t):
    return pl.ds(pl.multiple_of(t * TILE, TILE), TILE)


def chunk_at(index, rows=CHUNK):
    return pl.ds(pl.multiple_of(index * rows, rows), rows)


def diagonal(p):
    key = lax.broadcasted_iota(jnp.int32, p.shape, 0)
    query = lax.broadcasted_iota(jnp.int32, p.shape, 1)
    return key <= query


def attend_kernel(table, x_ref, w_ref, b_ref, scale_ref, qvk_ref, lse_ref, out_ref, packed_ref, flat, keys, values_t):
    total = x_ref.shape[0]
    tiles = total // TILE
    chunks = total // CHUNK

    def project(t, carry):
        flat[tile_at(t)] = (mul(x_ref[tile_at(t)], w_ref[...]) + b_ref[...]).astype(jnp.bfloat16)
        return carry

    lax.fori_loop(0, tiles, project, 0)

    def arrange(p, carry):
        qvk_ref[chunk_at(p)] = flat[chunk_at(table[p])]
        return carry

    lax.fori_loop(0, chunks, arrange, 0)

    def prepare(t, carry):
        keys[tile_at(t)] = qvk_ref[tile_at(t), 128:192]
        values_t[:, tile_at(t)] = jnp.transpose(qvk_ref[tile_at(t), 0:128].astype(jnp.float32))[64:128].astype(jnp.bfloat16)
        return carry

    lax.fori_loop(0, tiles, prepare, 0)
    cut = table[chunks]
    for i in range(tiles):
        at = slice(i * TILE, (i + 1) * TILE)
        query = qvk_ref[at, 0:64] * 0.125

        def block(j, state, masked):
            peak, part, mixed = state
            scores = mul(keys[tile_at(j)], query, NT)
            if masked:
                keep = diagonal(scores)
                scores = jnp.where(keep, scores, -1e30)
            new_peak = jnp.maximum(peak, jnp.max(scores, axis=0, keepdims=True))
            weights = jnp.exp(scores - new_peak)
            if masked:
                weights = jnp.where(keep, weights, 0.0)
            factor = jnp.exp(peak - new_peak)
            part = part * factor + jnp.sum(weights, axis=0, keepdims=True)
            mixed = mixed * factor + mul(values_t[:, tile_at(j)], weights.astype(jnp.bfloat16))
            return (new_peak, part, mixed)

        state = (
            jnp.full((1, TILE), -1e30, jnp.float32),
            jnp.zeros((1, TILE), jnp.float32),
            jnp.zeros((64, TILE), jnp.float32),
        )
        state = block(i, state, True)
        state = lax.fori_loop(jnp.where(i >= cut, cut, 0), i, functools.partial(block, masked=False), state)
        peak, part, mixed = state
        mixed = mixed / part
        lse_ref[:, at] = peak + jnp.log(part)
        out_ref[:, at] = mixed
        heads_out = jnp.transpose(mixed) * scale_ref[0, 0]
        pairs = heads_out.reshape(TILE // CHUNK, 2, CHUNK // 2, 64)
        pairs = jnp.concatenate([pairs[:, 0], pairs[:, 1]], axis=-1).astype(jnp.bfloat16)
        for q in range(TILE // CHUNK):
            packed_ref[chunk_at(table[i * (TILE // CHUNK) + q], CHUNK // 2)] = pairs[q]


def attend(table, x, w, b, scale):
    total = x.shape[0]
    vmem = pl.BlockSpec(memory_space=pltpu.VMEM)
    smem = pl.BlockSpec(memory_space=pltpu.SMEM)
    return pl.pallas_call(
        attend_kernel,
        out_shape=(
            jax.ShapeDtypeStruct((total, 192), jnp.bfloat16),
            jax.ShapeDtypeStruct((1, total), jnp.float32),
            jax.ShapeDtypeStruct((64, total), jnp.float32),
            jax.ShapeDtypeStruct((total // 2, 128), jnp.bfloat16),
        ),
        in_specs=[smem, vmem, vmem, vmem, smem],
        out_specs=(vmem, vmem, vmem, vmem),
        scratch_shapes=[
            pltpu.VMEM((total, 192), jnp.bfloat16),
            pltpu.VMEM((total, 64), jnp.bfloat16),
            pltpu.VMEM((64, total), jnp.bfloat16),
        ],
        cost_estimate=lasting(11),
        compiler_params=pltpu.CompilerParams(vmem_limit_bytes=50 << 20),
        name="attend",
    )(table, x, w, b, scale)


def attend_back_kernel(
    table, da_ref, x_ref, w_ref, scale_ref, qvk_ref, lse_ref, out_ref,
    part_ref, gwt_ref, gb_ref, gs_ref,
    gw_ref, packed, dout, delta, query, keys, values, keys_t, dkeys, dvalues, dquery_t, flat,
):
    total = x_ref.shape[0]
    tiles = total // TILE
    chunks = total // CHUNK
    per_tile = TILE // CHUNK

    def arrange(p, carry):
        packed[chunk_at(p, CHUNK // 2)] = da_ref[chunk_at(table[p], CHUNK // 2)]
        return carry

    lax.fori_loop(0, chunks, arrange, 0)
    scale = scale_ref[0, 0]

    def prepare(t, carry):
        at = tile_at(t)
        pairs = packed[chunk_at(t, TILE // 2)].astype(jnp.float32).reshape(per_tile, CHUNK // 2, 128)
        pairs = jnp.concatenate([pairs[:, :, 0:64], pairs[:, :, 64:128]], axis=1).reshape(TILE, 64)
        low = (pairs * scale).astype(jnp.bfloat16)
        dout[at] = low
        delta[:, at] = jnp.sum(jnp.transpose(low.astype(jnp.float32)) * out_ref[:, at], axis=0, keepdims=True)
        query[at] = qvk_ref[at, 0:64] * 0.125
        values[at] = qvk_ref[at, 64:128]
        key = qvk_ref[at, 128:192]
        keys[at] = key
        keys_t[:, at] = jnp.transpose(key.astype(jnp.float32)).astype(jnp.bfloat16)
        dkeys[at] = jnp.zeros((TILE, 64), jnp.float32)
        dvalues[at] = jnp.zeros((TILE, 64), jnp.float32)
        return carry

    lax.fori_loop(0, tiles, prepare, 0)
    gs_ref[...] = jnp.sum(delta[...], axis=1, keepdims=True) / scale
    cut = table[chunks]
    for i in range(tiles):
        at = slice(i * TILE, (i + 1) * TILE)
        query_i, dout_i, lse_i, delta_i = query[at], dout[at], lse_ref[:, at], delta[:, at]

        def block(j, total_dq, masked):
            there = tile_at(j)
            scores = mul(keys[there], query_i, NT)
            weights = jnp.exp(scores - lse_i)
            if masked:
                weights = jnp.where(diagonal(scores), weights, 0.0)
            dweights = mul(values[there], dout_i, NT)
            dscores = (weights * (dweights - delta_i)).astype(jnp.bfloat16)
            dvalues[there] += mul(weights.astype(jnp.bfloat16), dout_i)
            dkeys[there] += mul(dscores, query_i)
            return total_dq + mul(keys_t[:, there], dscores)

        total_dq = block(i, jnp.zeros((64, TILE), jnp.float32), True)
        total_dq = lax.fori_loop(jnp.where(i >= cut, cut, 0), i, functools.partial(block, masked=False), total_dq)
        dquery_t[:, at] = total_dq * 0.125

    gb_ref[...] = jnp.zeros_like(gb_ref)
    for i in range(tiles):
        at = slice(i * TILE, (i + 1) * TILE)
        joined = jnp.concatenate([jnp.transpose(dquery_t[:, at]), dvalues[at], dkeys[at]], axis=1).astype(jnp.bfloat16)
        gb_ref[...] += jnp.sum(joined.astype(jnp.float32), axis=0, keepdims=True)
        for q in range(per_tile):
            flat[chunk_at(table[i * per_tile + q])] = joined[q * CHUNK : (q + 1) * CHUNK]
    gw_ref[...] = jnp.zeros_like(gw_ref)

    def finish(t, carry):
        rows = flat[tile_at(t)]
        part_ref[tile_at(t)] = mul(rows, w_ref[...], NT).astype(jnp.bfloat16)
        gw_ref[...] += mul(rows, x_ref[tile_at(t)], TN)
        return carry

    lax.fori_loop(0, tiles, finish, 0)
    gwt_ref[...] = jnp.transpose(gw_ref[...]).astype(jnp.bfloat16)


def attend_back(table, da, x, w, scale, qvk, lse, out):
    total, width = x.shape
    vmem = pl.BlockSpec(memory_space=pltpu.VMEM)
    smem = pl.BlockSpec(memory_space=pltpu.SMEM)
    low = lambda *shape: pltpu.VMEM(shape, jnp.bfloat16)
    full = lambda *shape: pltpu.VMEM(shape, jnp.float32)
    return pl.pallas_call(
        attend_back_kernel,
        out_shape=(
            jax.ShapeDtypeStruct((total, width), jnp.bfloat16),
            jax.ShapeDtypeStruct((width, 192), jnp.bfloat16),
            jax.ShapeDtypeStruct((1, 192), jnp.float32),
            jax.ShapeDtypeStruct((1, 1), jnp.float32),
        ),
        in_specs=[smem, vmem, vmem, vmem, smem, vmem, vmem, vmem],
        out_specs=(vmem, vmem, vmem, vmem),
        scratch_shapes=[
            full(192, width), low(total // 2, 128), low(total, 64), full(1, total), low(total, 64), low(total, 64), low(total, 64),
            low(64, total), full(total, 64), full(total, 64), full(64, total), low(total, 192),
        ],
        cost_estimate=lasting(19),
        compiler_params=pltpu.CompilerParams(vmem_limit_bytes=56 << 20),
        name="attend_back",
    )(table, da, x, w, scale, qvk, lse, out)


PLANE = 8


def plane_place():
    x = lax.axis_index("batch")
    z, y, c = place()
    return x, z, y, c


def plane_device(x, z, y, c):
    return {"batch": x, "blk": index_of(z, y, c)}


def plane_index(x, y, c):
    return (x * 2 + y) * 2 + c


class PlaneGather:
    def __init__(self, all_ref, sems):
        self.all_ref = all_ref
        self.sx, self.rx, self.sy, self.ry, self.sc, self.rc = sems
        self.x, self.z, self.y, self.c = plane_place()
        self.half = all_ref.shape[0] // (2 * PLANE)

    @staticmethod
    def scratch():
        dma = pltpu.SemaphoreType.DMA
        return [dma((3,))] * 4 + [dma((PLANE,))] * 2

    def piece(self, x, y, c, h):
        return self.all_ref.at[pl.ds(plane_index(x, y, c) * 2 * self.half + h * self.half, self.half)]

    def over_x(self, i):
        x, y, c = self.x, self.y, self.c
        piece = self.piece(x, y if i < 2 else 1 - y, c, (0, 1, 1)[i])
        return remote(piece, piece, self.sx.at[i], self.rx.at[i], plane_device(1 - x, self.z, y, c))

    def over_y(self, i):
        x, y, c = self.x, self.y, self.c
        piece = self.piece(x if i < 2 else 1 - x, y, c, (1, 0, 0)[i])
        return remote(piece, piece, self.sy.at[i], self.ry.at[i], plane_device(x, self.z, 1 - y, c))

    def from_x(self, i):
        x, y, c = self.x, self.y, self.c
        piece = self.piece(1 - x, y if i < 2 else 1 - y, c, (0, 1, 1)[i])
        remote(piece, piece, self.sx.at[i], self.rx.at[i], plane_device(1 - x, self.z, y, c)).wait_recv()

    def from_y(self, i):
        x, y, c = self.x, self.y, self.c
        piece = self.piece(x if i < 2 else 1 - x, 1 - y, c, (1, 0, 0)[i])
        remote(piece, piece, self.sy.at[i], self.ry.at[i], plane_device(x, self.z, 1 - y, c)).wait_recv()

    def twin(self, other_x, other_y, h):
        x = 1 - self.x if other_x else self.x
        y = 1 - self.y if other_y else self.y
        slot = (other_x * 2 + other_y) * 2 + h
        piece = self.piece(x, y, self.c, h)
        return remote(piece, piece, self.sc.at[slot], self.rc.at[slot], plane_device(self.x, self.z, self.y, 1 - self.c))

    def from_twin(self, other_x, other_y, h):
        x = 1 - self.x if other_x else self.x
        y = 1 - self.y if other_y else self.y
        slot = (other_x * 2 + other_y) * 2 + h
        piece = self.piece(x, y, 1 - self.c, h)
        where = plane_device(self.x, self.z, self.y, 1 - self.c)
        remote(piece, piece, self.sc.at[slot], self.rc.at[slot], where).wait_recv()

    def start(self):
        self.over_x(0).start()
        self.over_y(0).start()
        self.over_x(1).start()
        self.over_y(1).start()
        self.twin(0, 0, 0).start()
        self.twin(0, 0, 1).start()

    def near(self):
        self.from_x(0)
        self.over_y(2).start()
        self.twin(1, 0, 0).start()
        self.from_y(0)
        self.over_x(2).start()
        self.twin(0, 1, 1).start()
        self.from_y(1)
        self.twin(0, 1, 0).start()
        for other_y in range(2):
            for h in range(2):
                self.from_twin(0, other_y, h)

    def far(self):
        self.from_x(1)
        self.twin(1, 0, 1).start()
        self.from_x(2)
        self.twin(1, 1, 1).start()
        self.from_y(2)
        self.twin(1, 1, 0).start()
        for other_y in range(2):
            for h in range(2):
                self.from_twin(1, other_y, h)

    def finish(self):
        for i in range(3):
            self.over_x(i).wait_send()
            self.over_y(i).wait_send()
        for other_x in range(2):
            for other_y in range(2):
                for h in range(2):
                    self.twin(other_x, other_y, h).wait_send()


class PlaneScatter:
    def __init__(self, part_ref, bufs, sems):
        self.part_ref = part_ref
        self.twins, self.xs, self.xr, self.ys, self.yr = bufs
        self.sx, self.rx, self.sy, self.ry, self.sc, self.rc = sems
        self.x, self.z, self.y, self.c = plane_place()
        self.half = part_ref.shape[0] // (2 * PLANE)

    @staticmethod
    def scratch(rows, columns):
        dma = pltpu.SemaphoreType.DMA
        half = pltpu.VMEM((3, rows // 2, columns), jnp.bfloat16)
        return [pltpu.VMEM((4, rows, columns), jnp.bfloat16)] + [half] * 4, [dma((3,))] * 4 + [dma((4,))] * 2

    def rows(self, which, c, h=None):
        x = self.x if which >= 2 else 1 - self.x
        y = self.y if which % 2 else 1 - self.y
        at = plane_index(x, y, c) * 2 * self.half
        return pl.ds(at, 2 * self.half) if h is None else pl.ds(at + h * self.half, self.half)

    def twin(self, which):
        where = plane_device(self.x, self.z, self.y, 1 - self.c)
        source = self.part_ref.at[self.rows(which, 1 - self.c)]
        return remote(source, self.twins.at[which], self.sc.at[which], self.rc.at[which], where)

    def over_x(self, i):
        return remote(
            self.xs.at[i], self.xr.at[i], self.sx.at[i], self.rx.at[i], plane_device(1 - self.x, self.z, self.y, self.c)
        )

    def over_y(self, i):
        return remote(
            self.ys.at[i], self.yr.at[i], self.sy.at[i], self.ry.at[i], plane_device(self.x, self.z, 1 - self.y, self.c)
        )

    def chip(self, which, h):
        own = self.part_ref[self.rows(which, self.c, h)].astype(jnp.float32)
        return own + self.twins[which, h * self.half : (h + 1) * self.half].astype(jnp.float32)

    def first(self):
        self.twin(0).wait_recv()
        self.xs[0] = self.chip(0, 0).astype(jnp.bfloat16)
        self.over_x(0).start()
        self.ys[0] = self.chip(0, 1).astype(jnp.bfloat16)
        self.over_y(0).start()
        self.twin(1).wait_recv()
        self.xs[1] = self.chip(1, 0).astype(jnp.bfloat16)
        self.over_x(1).start()
        self.twin(2).wait_recv()
        self.ys[1] = self.chip(2, 1).astype(jnp.bfloat16)
        self.over_y(1).start()

    def second(self):
        self.over_x(0).wait_recv()
        self.ys[2] = (self.chip(2, 0) + self.xr[0].astype(jnp.float32)).astype(jnp.bfloat16)
        self.over_y(2).start()
        self.over_y(0).wait_recv()
        self.xs[2] = (self.chip(1, 1) + self.yr[0].astype(jnp.float32)).astype(jnp.bfloat16)
        self.over_x(2).start()

    def finish(self, o_ref):
        half = self.half
        self.twin(3).wait_recv()
        self.over_x(1).wait_recv()
        self.over_y(1).wait_recv()
        self.over_y(2).wait_recv()
        o_ref[0:half] = self.chip(3, 0) + self.xr[1].astype(jnp.float32) + self.yr[2].astype(jnp.float32)
        self.over_x(2).wait_recv()
        o_ref[half : 2 * half] = self.chip(3, 1) + self.yr[1].astype(jnp.float32) + self.xr[2].astype(jnp.float32)
        for which in range(4):
            self.twin(which).wait_send()
        for i in range(3):
            self.over_x(i).wait_send()
            self.over_y(i).wait_send()


class PlanePool:
    def __init__(self, own_ref, got_ref, send, recv):
        self.own_ref, self.got_ref, self.send, self.recv = own_ref, got_ref, send, recv
        self.x, self.z, self.y, self.c = plane_place()

    def others(self):
        for d in range(1, PLANE):
            x = 1 - self.x if d & 4 else self.x
            y = 1 - self.y if d & 2 else self.y
            c = 1 - self.c if d & 1 else self.c
            yield d, x, y, c

    def run(self):
        me = plane_index(self.x, self.y, self.c)
        copies = [
            remote(self.own_ref, self.got_ref.at[me], self.send.at[d], self.recv.at[d], plane_device(x, self.z, y, c))
            for d, x, y, c in self.others()
        ]
        for copy in copies:
            copy.start()
        self.got_ref[me] = self.own_ref[...]
        for d, x, y, c in self.others():
            slot = self.got_ref.at[plane_index(x, y, c)]
            remote(slot, slot, self.send.at[d], self.recv.at[d], plane_device(x, self.z, y, c)).wait_recv()
        for copy in copies:
            copy.wait_send()


def greet_plane():
    x, z, y, c = plane_place()
    for d in range(1, PLANE):
        hail(plane_device(1 - x if d & 4 else x, z, 1 - y if d & 2 else y, 1 - c if d & 1 else c))
    pl.semaphore_wait(pltpu.get_barrier_semaphore(), PLANE - 1)


def greet_for(rides):
    if rides.far():
        greet_group(plane=True)
    else:
        greet_plane()


def span_at(th, width):
    return pl.ds(pl.multiple_of(th * width, 128), width)


def units_at(ut):
    return pl.ds(pl.multiple_of(ut * 256, 256), 256)


def mean_and_rate(stat, hidden_all):
    return stat[0:1], lax.rsqrt(stat[1:2] * (1.0 / hidden_all) + EPSILON)


def ffn_kernel(hidden_all, rides, *refs):
    refs, riders = rides.split(refs, 6, 6)
    x_ref, wu_ref, b_ref, gain_ref, shift_ref, wd_ref = refs[:6]
    y_ref, xo_ref, acto_ref, slopeo_ref, stat_ref, mido_ref = refs[6:12]
    rows_all, act, slope, mid, part, own_stat, got_stat, ps, pr, out_sem = refs[12:22]
    refs = refs[22:]
    gather = PlaneGather(rows_all, refs[:6])
    scatter = PlaneScatter(part, refs[6:11], refs[11:17])
    pool = PlanePool(own_stat, got_stat, ps, pr)
    x, z, y, c = plane_place()
    rows = x_ref.shape[0]
    hidden, total = act.shape
    width = total // 2
    rows_all[pl.ds(plane_index(x, y, c) * rows, rows)] = x_ref[...]
    greet_for(rides)
    gather.start()
    start_all(riders)

    def climb(th):
        at = span_at(th, width)

        def units(ut, carry):
            here = units_at(ut)
            upper = mul(wu_ref[here], rows_all[pl.ds(th * width, width)], NT) + b_ref[here]
            chance = 0.5 * (1.0 + lax.erf(upper * (0.5**0.5)))
            act[here, at] = upper * chance
            slope[here, at] = chance + upper * (jnp.exp(-0.5 * upper * upper) * 0.3989422804014327)
            return carry

        lax.fori_loop(0, hidden // 256, units, 0)
        values = act[:, at]
        mean = jnp.mean(values, axis=0, keepdims=True)
        apart = values - mean
        own_stat[0:1, at] = mean
        own_stat[1:2, at] = jnp.sum(apart * apart, axis=0, keepdims=True)

    gather.near()
    climb(x)
    gather.far()
    climb(1 - x)
    pool.run()
    means = [got_stat[i, 0:1] for i in range(PLANE)]
    mean = functools.reduce(jnp.add, means) * (1.0 / PLANE)
    apart = functools.reduce(jnp.add, [(m - mean) * (m - mean) for m in means])
    stat_ref[0:1] = mean
    stat_ref[1:2] = functools.reduce(jnp.add, [got_stat[i, 1:2] for i in range(PLANE)]) + apart * float(hidden)
    outs = [
        pltpu.make_async_copy(source, dest, out_sem.at[i])
        for i, (source, dest) in enumerate(((rows_all, xo_ref), (act, acto_ref), (slope, slopeo_ref), (mid, mido_ref)))
    ]
    for copy in outs[:3]:
        copy.start()

    def descend(th):
        at = span_at(th, width)
        mean, rate = mean_and_rate(stat_ref[:, at], hidden_all)

        def units(ut, carry):
            here = units_at(ut)
            mid[here, at] = ((act[here, at] - mean) * rate * gain_ref[here] + shift_ref[here]).astype(jnp.bfloat16)
            return carry

        lax.fori_loop(0, hidden // 256, units, 0)
        part[pl.ds(th * width, width)] = mul(mid[:, at], wd_ref[...], TN).astype(jnp.bfloat16)

    descend(1 - x)
    scatter.twin(0).start()
    scatter.twin(1).start()
    descend(x)
    scatter.twin(2).start()
    scatter.twin(3).start()
    outs[3].start()
    scatter.first()
    scatter.second()
    scatter.finish(y_ref)
    gather.finish()
    for copy in outs:
        copy.wait()
    finish_all(riders)


def ffn(hidden_all, x, w_up, bias, gain, shift, w_down, collective_id, rides=()):
    rides = Rides(rides)
    rows, columns = x.shape
    hidden, total = w_up.shape[0], rows * PLANE
    vmem, anywhere = pl.BlockSpec(memory_space=pltpu.VMEM), pl.BlockSpec(memory_space=pl.ANY)
    dma = pltpu.SemaphoreType.DMA
    full = lambda *shape: pltpu.VMEM(shape, jnp.float32)
    low = lambda *shape: pltpu.VMEM(shape, jnp.bfloat16)
    bufs, sems = PlaneScatter.scratch(rows, columns)
    return pl.pallas_call(
        functools.partial(ffn_kernel, hidden_all, rides),
        out_shape=[
            jax.ShapeDtypeStruct((rows, columns), jnp.float32),
            jax.ShapeDtypeStruct((total, columns), jnp.bfloat16),
            jax.ShapeDtypeStruct((hidden, total), jnp.float32),
            jax.ShapeDtypeStruct((hidden, total), jnp.float32),
            jax.ShapeDtypeStruct((2, total), jnp.float32),
            jax.ShapeDtypeStruct((hidden, total), jnp.bfloat16),
        ]
        + rides.results(),
        in_specs=[vmem] * 6 + rides.specs(),
        out_specs=[vmem, anywhere, anywhere, anywhere, vmem, anywhere] + rides.specs(),
        scratch_shapes=[
            low(total, columns), full(hidden, total), full(hidden, total), low(hidden, total), low(total, columns),
            full(2, total), full(PLANE, 2, total), dma((PLANE,)), dma((PLANE,)), dma((4,)),
        ]
        + PlaneGather.scratch()
        + bufs
        + sems
        + rides.scratch(),
        cost_estimate=lasting(40),
        compiler_params=pltpu.CompilerParams(
            collective_id=collective_id, has_side_effects=True, vmem_limit_bytes=50 << 20
        ),
        name="ffn",
    )(x, w_up, bias, gain, shift, w_down, *rides.arrays)


def ffn_back_kernel(hidden_all, rides, *refs):
    refs, riders = rides.split(refs, 9, 6)
    dy_ref, wu_ref, gain_ref, wd_ref, stat_ref, xi_ref, acti_ref, slopei_ref, midi_ref = refs[:9]
    dx_ref, gdown_ref, gup_ref, gg_ref, gs_ref, gb_ref = refs[9:15]
    rows_all, dy_all, act, slope, mid, dmid, part, own_sums, got_sums, sums, ps, pr, in_sem = refs[15:28]
    refs = refs[28:]
    gather = PlaneGather(dy_all, refs[:6])
    scatter = PlaneScatter(part, refs[6:11], refs[11:17])
    pool = PlanePool(own_sums, got_sums, ps, pr)
    x, z, y, c = plane_place()
    rows = dy_ref.shape[0]
    hidden, total = act.shape
    width = total // 2
    dy_all[pl.ds(plane_index(x, y, c) * rows, rows)] = dy_ref[...]
    greet_for(rides)
    gather.start()
    start_all(riders)
    ins = [
        pltpu.make_async_copy(source, dest, in_sem.at[i])
        for i, (source, dest) in enumerate(((acti_ref, act), (slopei_ref, slope), (midi_ref, mid), (xi_ref, rows_all)))
    ]
    for copy in ins:
        copy.start()
    gg_ref[...] = jnp.zeros_like(gg_ref)
    gs_ref[...] = jnp.zeros_like(gs_ref)
    gb_ref[...] = jnp.zeros_like(gb_ref)
    own_sums[...] = jnp.zeros_like(own_sums)

    def climb(th):
        at = span_at(th, width)
        mean, rate = mean_and_rate(stat_ref[:, at], hidden_all)

        def units(ut, carry):
            here = units_at(ut)
            dm = mul(wd_ref[here], dy_all[pl.ds(th * width, width)], NT)
            dmid[here, at] = dm
            vh = (act[here, at] - mean) * rate
            act[here, at] = vh
            gg_ref[here] += jnp.sum(dm * vh, axis=1, keepdims=True)
            gs_ref[here] += jnp.sum(dm, axis=1, keepdims=True)
            scaled = dm * gain_ref[here]
            own_sums[0:1, at] += jnp.sum(scaled, axis=0, keepdims=True)
            own_sums[1:2, at] += jnp.sum(scaled * vh, axis=0, keepdims=True)
            return carry

        lax.fori_loop(0, hidden // 256, units, 0)

    gather.near()
    ins[0].wait()
    climb(x)
    gather.far()
    climb(1 - x)
    pool.run()
    sums[...] = functools.reduce(jnp.add, [got_sums[i] for i in range(PLANE)]) * (1.0 / hidden_all)
    ins[1].wait()

    def descend(th):
        at = span_at(th, width)
        mean, rate = mean_and_rate(stat_ref[:, at], hidden_all)
        sum0, sum1 = sums[0:1, at], sums[1:2, at]

        def units(ut, carry):
            here = units_at(ut)
            dact = rate * (dmid[here, at] * gain_ref[here] - sum0 - act[here, at] * sum1)
            du = (dact * slope[here, at]).astype(jnp.bfloat16)
            du_ref[here, at] = du
            gb_ref[here] += jnp.sum(du.astype(jnp.float32), axis=1, keepdims=True)
            return carry

        lax.fori_loop(0, hidden // 256, units, 0)
        part[pl.ds(th * width, width)] = mul(du_ref[:, at], wu_ref[...], TN).astype(jnp.bfloat16)

    du_ref = refs[17]
    descend(1 - x)
    scatter.twin(0).start()
    scatter.twin(1).start()
    descend(x)
    scatter.twin(2).start()
    scatter.twin(3).start()
    scatter.first()
    ins[2].wait()

    def down_grad(ut, carry):
        here = units_at(ut)
        gdown_ref[here] = mul(mid[here], dy_all[...]).astype(jnp.bfloat16)
        return carry

    lax.fori_loop(0, hidden // 256, down_grad, 0)
    scatter.second()
    ins[3].wait()

    def up_grad(ut, carry):
        here = units_at(ut)
        gup_ref[:, here] = jnp.transpose(mul(du_ref[here], rows_all[...])).astype(jnp.bfloat16)
        return carry

    lax.fori_loop(0, hidden // 256, up_grad, 0)
    scatter.finish(dx_ref)
    gather.finish()
    finish_all(riders)


def ffn_back(hidden_all, dy, w_up, gain, w_down, stat, x_all, act, slope, mid, collective_id, rides=()):
    rides = Rides(rides)
    rows, columns = dy.shape
    hidden, total = act.shape
    vmem, anywhere = pl.BlockSpec(memory_space=pltpu.VMEM), pl.BlockSpec(memory_space=pl.ANY)
    dma = pltpu.SemaphoreType.DMA
    full = lambda *shape: pltpu.VMEM(shape, jnp.float32)
    low = lambda *shape: pltpu.VMEM(shape, jnp.bfloat16)
    bufs, sems = PlaneScatter.scratch(rows, columns)
    column = jax.ShapeDtypeStruct((hidden, 1), jnp.float32)
    return pl.pallas_call(
        functools.partial(ffn_back_kernel, hidden_all, rides),
        out_shape=[
            jax.ShapeDtypeStruct((rows, columns), jnp.float32),
            jax.ShapeDtypeStruct((hidden, columns), jnp.bfloat16),
            jax.ShapeDtypeStruct((columns, hidden), jnp.bfloat16),
            column,
            column,
            column,
        ]
        + rides.results(),
        in_specs=[vmem] * 5 + [anywhere] * 4 + rides.specs(),
        out_specs=[vmem] * 6 + rides.specs(),
        scratch_shapes=[
            low(total, columns), low(total, columns), full(hidden, total), full(hidden, total), low(hidden, total),
            full(hidden, total), low(total, columns), full(2, total), full(PLANE, 2, total), full(2, total),
            dma((PLANE,)), dma((PLANE,)), dma((4,)),
        ]
        + PlaneGather.scratch()
        + bufs
        + sems
        + [low(hidden, total)]
        + rides.scratch(),
        cost_estimate=lasting(45),
        compiler_params=pltpu.CompilerParams(
            collective_id=collective_id, has_side_effects=True, vmem_limit_bytes=58 << 20
        ),
        name="ffn_back",
    )(dy, w_up, gain, w_down, stat, x_all, act, slope, mid, *rides.arrays)


def assemble_kernel(head0, head1, near0, near1, far0, far1, qkv_ref, up_ref):
    x = lax.axis_index("batch")
    for layer, head_ref, halves in ((0, head0, (near0, far0)), (1, head1, (near1, far1))):
        width = 64 * head_ref.shape[0]
        for j in range(0, head_ref.shape[0], 2):
            left, right = head_ref[j].astype(jnp.float32), head_ref[j + 1].astype(jnp.float32)
            for part, source in ((0, 0), (1, 128), (2, 64)):
                pair = jnp.concatenate([left[:, source : source + 64], right[:, source : source + 64]], axis=1)
                qkv_ref[layer, :, part * width + j * 64 : part * width + (j + 2) * 64] = pair
        for half, half_ref in zip((x, 1 - x), halves):
            for q in range(half_ref.shape[0]):
                for z in range(LINE):
                    at = pl.ds(pl.multiple_of((z * 4 + q) * 256 + half * 128, 128), 128)
                    up_ref[layer, :, at] = half_ref[q, :, z * 128 : (z + 1) * 128].astype(jnp.float32)


def assemble(heads, near, far, qkv_shape, up_shape):
    vmem = pl.BlockSpec(memory_space=pltpu.VMEM)
    return pl.pallas_call(
        assemble_kernel,
        out_shape=(jax.ShapeDtypeStruct(qkv_shape, jnp.float32), jax.ShapeDtypeStruct(up_shape, jnp.float32)),
        in_specs=[vmem] * 6,
        out_specs=(vmem,) * 2,
        cost_estimate=lasting(5),
        compiler_params=pltpu.CompilerParams(vmem_limit_bytes=40 << 20),
        name="assemble",
    )(*heads, *near, *far)


def chunk_table(first_rows, span_of, rows_here):
    blocks = span_of.shape[0]
    first = first_rows[0]
    second = rows_here - first
    row = jnp.arange(blocks * rows_here // CHUNK, dtype=jnp.int32) * CHUNK
    later = row >= first * blocks
    inside = jnp.where(later, row - first * blocks, row)
    length = jnp.where(later, jnp.maximum(second, 1), first)
    span = inside // length
    of_span = (span_of[None, :] == span[:, None]).astype(jnp.int32)
    device_of = jnp.sum(of_span * jnp.arange(blocks, dtype=jnp.int32)[None, :], axis=1)
    source = device_of * rows_here + jnp.where(later, first, 0) + inside - span * length
    return jnp.concatenate([source // CHUNK, (first * blocks // TILE)[None]]).astype(jnp.int32)


def pack_rows(matrix):
    rows = matrix.shape[0]
    split = matrix.reshape(rows // CHUNK, 2, CHUNK // 2, -1, HEAD_DIM)
    return split.transpose(3, 0, 2, 1, 4).reshape(-1, rows // 2, 2 * HEAD_DIM)


def unpack_rows(blocks):
    heads, half_rows, _ = blocks.shape
    split = blocks.reshape(heads, half_rows // (CHUNK // 2), CHUNK // 2, 2, HEAD_DIM)
    return split.transpose(1, 3, 2, 0, 4).reshape(2 * half_rows, heads * HEAD_DIM)


def fold_halves(blocks):
    n, rows, columns = blocks.shape
    return blocks.reshape(n, 2, rows // 2, columns).transpose(0, 2, 1, 3).reshape(n, rows // 2, 2 * columns)


def unfold_halves(blocks):
    n, rows, columns = blocks.shape
    return blocks.reshape(n, rows, 2, columns // 2).transpose(0, 2, 1, 3).reshape(n, 2 * rows, columns // 2)


def own_share(vector, index, size):
    return lax.dynamic_slice_in_dim(vector, index * size, size, 0)


def spread(vector, index, whole):
    return lax.dynamic_update_slice_in_dim(jnp.zeros((whole,), jnp.float32), vector, index * vector.shape[0], 0)


def own_units(vector, slot):
    return lax.dynamic_slice_in_dim(vector.reshape(LINE, PLANE, -1), slot, 1, 1).reshape(-1, 1)


def spread_units(column, slot):
    parts = column.reshape(LINE, 1, -1)
    whole = jnp.zeros((LINE, PLANE, parts.shape[2]), jnp.float32)
    return lax.dynamic_update_slice_in_dim(whole, parts, slot, 1).reshape(-1)


def add_low(own, other):
    return (own.astype(jnp.float32) + other.astype(jnp.float32)).astype(jnp.bfloat16)


def sum_low(parts):
    return jnp.sum(parts.astype(jnp.float32), axis=0).astype(jnp.bfloat16)


def travel(
    tokens, grad_out, first_rows, span_of, w_qkv, w_out, w_up, w_down, vec_gain, vec_bias, mid_gain, mid_bias, head_scale
):
    blocks = lax.axis_size("blk")
    rows_here, row_width = tokens.shape
    group, index = lax.axis_index("batch"), lax.axis_index("blk")
    hidden_all = mid_gain.shape[1]
    unit_rows = hidden_all // (LINE * PLANE)
    weight_rows = row_width // blocks
    slot = lax.rem(index, 4) * 2 + group
    table = chunk_table(first_rows, span_of, rows_here)
    scales = [own_share(head_scale[layer], index, 1).reshape(1, 1) for layer in range(2)]
    middle_gain = [own_units(mid_gain[layer], slot) for layer in range(2)]
    middle_shift = [own_units(mid_bias[layer, 0], slot) for layer in range(2)]
    middle_bias = [own_units(mid_bias[layer, 1], slot) for layer in range(2)]
    by_head, by_unit, own_down = [], [], []
    for layer in range(2):
        split = w_qkv[layer].reshape(weight_rows, 3, blocks, HEAD_DIM)
        split = jnp.stack([split[:, 0], split[:, 2], split[:, 1]], axis=1).transpose(2, 0, 1, 3)
        by_head.append(fold_halves(split.reshape(blocks, weight_rows, 3 * HEAD_DIM)))
        split = w_up[layer].reshape(weight_rows, LINE, 4, 2, unit_rows)
        split = lax.dynamic_slice_in_dim(split, group, 1, 3).reshape(weight_rows, LINE, 4, unit_rows)
        by_unit.append(split.transpose(2, 0, 1, 3).reshape(4, weight_rows, LINE * unit_rows))
        own_down.append(lax.dynamic_slice_in_dim(w_down[layer].reshape(2, unit_rows, row_width), group, 1, 0))
    head_w, up_w, down_w = [None] * 2, [None] * 2, [None] * 2

    def set_weights(layer, head_blocks, unit_blocks, down_blocks):
        head_w[layer] = unfold_halves(head_blocks).reshape(row_width, -1)
        up_w[layer] = unit_blocks.reshape(row_width, -1).T
        down_w[layer] = down_blocks.reshape(-1, row_width)

    out_w = [lax.all_gather(w_out[layer], "blk", axis=0, tiled=True) for layer in range(2)]
    current = tokens.astype(jnp.float32)
    records = []
    for layer in range(2):
        gains, biases = vec_gain[layer], vec_bias[layer]
        normed, pre_pull = jax.vjp(norm_rows, current, gains[0], biases[0])
        normed_low = normed.astype(jnp.bfloat16)
        if layer == 0:
            normed_all, *got = gather_rows(normed_low, 0, [(Swap, by_head[0]), (Swap, by_unit[0]), (Trade, own_down[0])])
            set_weights(0, *got)
        else:
            (normed_all,) = gather_rows(normed_low, 1)
        head_bias = jnp.concatenate(
            [
                own_share(biases[3], index, HEAD_DIM),
                own_share(biases[4], index, HEAD_DIM),
                jnp.zeros((HEAD_DIM,), jnp.float32),
            ]
        )[None]
        qvk, lse, head_out, packed = attend(table, normed_all, head_w[layer], head_bias, scales[layer])
        (mixed,) = swap_blocks(packed.reshape(blocks, rows_here // 2, 128), 2)
        scaled_low = unpack_rows(mixed)
        branch = jnp.dot(scaled_low, out_w[layer], preferred_element_type=jnp.float32) + biases[5]
        post_normed, post_pull = jax.vjp(norm_rows, branch, gains[1], biases[1])
        middle_res = current + post_normed
        ffn_normed, ffn_pull = jax.vjp(norm_rows, middle_res, gains[2], biases[2])
        rides = [(Swap, by_head[1]), (Swap, by_unit[1]), (Trade, own_down[1])] if layer == 0 else []
        results, ffn_all, act, slope, stat, mid_low, *got = ffn(
            hidden_all, ffn_normed.astype(jnp.bfloat16), up_w[layer], middle_bias[layer], middle_gain[layer],
            middle_shift[layer], down_w[layer], 3 + layer, rides,
        )
        if layer == 0:
            set_weights(1, *got)
        current = middle_res + (results + biases[6])
        records.append(
            (pre_pull, post_pull, ffn_pull, normed_all, ffn_all, qvk, lse, head_out, scaled_low, act, slope, stat, mid_low)
        )
    results_low = current.astype(jnp.bfloat16)
    d_current = grad_out.astype(jnp.float32)
    head_grads, out_grads = [None] * 2, [None] * 2
    near_units, far_units, near_downs, far_downs = [None] * 2, [None] * 2, [None] * 2, [None] * 2
    vectors, middles, scale_grads = [None] * 2, [None] * 2, [None] * 2
    for layer in (1, 0):
        pre_pull, post_pull, ffn_pull, normed_all, ffn_all, qvk, lse, head_out, scaled_low, act, slope, stat, mid_low = records[layer]
        d_low = d_current.astype(jnp.bfloat16)
        rides = [] if layer == 1 else [(Swap, head_blocks), (Swap, unit_grad), (Trade, down_grad)]
        d_ffn, down_grad, unit_grad, grad_mid_gain, grad_mid_shift, grad_up_bias, *got = ffn_back(
            hidden_all, d_low, up_w[layer], middle_gain[layer], down_w[layer], stat, ffn_all, act, slope, mid_low,
            5 + layer, rides,
        )
        down_grad = down_grad.reshape(LINE, unit_rows, row_width)
        unit_grad = unit_grad.reshape(blocks, weight_rows, LINE * unit_rows)
        if layer == 0:
            head_grads[1] = unfold_halves(got[0])
            near_units[1] = sum_low(got[1].reshape(LINE, 4, weight_rows, LINE * unit_rows))
            near_downs[1] = sum_low(got[2])
        d_res_part, grad_gain_ffn, grad_shift_ffn = ffn_pull(d_ffn)
        d_middle_res = d_current + d_res_part
        d_branch, grad_gain_post, grad_shift_post = post_pull(d_middle_res)
        d_branch_low = d_branch.astype(jnp.bfloat16)
        d_scaled = jnp.einsum("td,cd->tc", d_branch_low, out_w[layer], preferred_element_type=jnp.float32)
        out_grad = jnp.einsum("tc,td->cd", scaled_low, d_branch_low, preferred_element_type=jnp.float32)
        out_grads[layer] = lax.psum_scatter(out_grad.astype(jnp.bfloat16), "blk", scatter_dimension=0, tiled=True)
        (d_heads,) = swap_blocks(pack_rows(d_scaled.astype(jnp.bfloat16)), 2)
        parts, head_grad, head_bias, grad_scale = attend_back(
            table, d_heads.reshape(-1, 128), normed_all, head_w[layer], scales[layer], qvk, lse, head_out
        )
        if layer == 1:
            d_in, other_head = scatter_rows(parts, 7, [(Cross, head_grad)])
        else:
            d_in, other_head, far_units[1], far_downs[1], unit_blocks, down_blocks = scatter_rows(
                parts, 8,
                [(Cross, head_grad), (Cross, near_units[1]), (Cross, near_downs[1]), (Swap, unit_grad), (Trade, down_grad)],
            )
            near_units[0] = sum_low(unit_blocks.reshape(LINE, 4, weight_rows, LINE * unit_rows))
            near_downs[0] = sum_low(down_blocks)
        head_blocks = fold_halves(add_low(head_grad, other_head).reshape(blocks, weight_rows, 3 * HEAD_DIM))
        d_in_part, grad_gain_pre, grad_shift_pre = pre_pull(d_in)
        d_current = d_middle_res + d_in_part
        vectors[layer] = jnp.stack(
            [
                grad_gain_pre,
                grad_gain_post,
                grad_gain_ffn,
                grad_shift_pre,
                grad_shift_post,
                grad_shift_ffn,
                spread(head_bias[0, :HEAD_DIM], index, row_width),
                spread(head_bias[0, HEAD_DIM : 2 * HEAD_DIM], index, row_width),
                jnp.sum(d_branch_low, axis=0, dtype=jnp.float32),
                jnp.sum(d_low, axis=0, dtype=jnp.float32),
            ]
        )
        middles[layer] = jnp.stack([spread_units(g, slot) for g in (grad_mid_gain, grad_mid_shift, grad_up_bias)])
        scale_grads[layer] = spread(grad_scale[0], index, blocks)
    scale_row = jnp.zeros((row_width,), jnp.float32).at[: 2 * blocks].set(jnp.concatenate(scale_grads))
    summed = jnp.concatenate([jnp.stack(vectors).reshape(-1), jnp.stack(middles).reshape(-1), scale_row])
    summed = jnp.pad(summed, (0, -summed.shape[0] % (16 * row_width))).reshape(-1, row_width)
    out_near = jnp.concatenate(out_grads)
    summed, head_got, out_far, far_units[0], far_downs[0] = finale(
        summed.astype(jnp.bfloat16), 9,
        [(Swap, head_blocks), (Cross, out_near), (Cross, near_units[0]), (Cross, near_downs[0])],
    )
    head_grads[0] = unfold_halves(head_got)
    grad_out_w = (out_near.astype(jnp.float32) + out_far.astype(jnp.float32)).reshape(w_out.shape)
    grad_qkv, grad_up = assemble(head_grads, near_units, far_units, w_qkv.shape, w_up.shape)
    near_down, far_down = jnp.stack(near_downs).astype(jnp.float32), jnp.stack(far_downs).astype(jnp.float32)
    grad_down = jnp.where(
        group == 0,
        jnp.concatenate([near_down, far_down], axis=1),
        jnp.concatenate([far_down, near_down], axis=1),
    )
    summed = summed.reshape(-1)
    vec_end, mid_end = 20 * row_width, 20 * row_width + 6 * hidden_all
    vectors = summed[:vec_end].reshape(2, 10, row_width)
    middles = summed[vec_end:mid_end].reshape(2, 3, hidden_all)
    return (
        results_low,
        d_current,
        grad_qkv,
        grad_out_w,
        grad_up,
        grad_down,
        vectors[:, :3],
        vectors[:, 3:],
        middles[:, 0],
        middles[:, 1:],
        summed[mid_end : mid_end + 2 * blocks].reshape(2, blocks),
    )


def local(*args):
    tokens, w_qkv = args[0], args[4]
    blocks = lax.axis_size("blk")
    heads = w_qkv.shape[2] // (3 * HEAD_DIM)
    if blocks == heads == 4 * LINE and lax.axis_size("batch") == 2 and tokens.shape[0] * blocks % TILE == 0:
        return travel(*args)
    return general(*args)


def solution(mesh):
    placed = (
        P(("batch", "blk"), None),
        P(("batch", "blk"), None),
        P("batch"),
        P(),
        P(None, "blk", None),
        P(None, "blk", None),
        P(None, "blk", None),
        P(None, "blk", None),
        P(),
        P(),
        P(),
        P(),
        P(),
    )
    return jax.shard_map(
        local,
        mesh=mesh,
        in_specs=placed,
        out_specs=(
            P(("batch", "blk"), None),
            P(("batch", "blk"), None),
            P(None, "blk", None),
            P(None, "blk", None),
            P(None, "blk", None),
            P(None, "blk", None),
            P(),
            P(),
            P(),
            P(),
            P(),
        ),
        check_vma=False,
    )
```

```python
import functools

import jax
import jax.numpy as jnp
from jax import lax
from jax.experimental import pallas as pl
from jax.experimental.pallas import tpu as pltpu
from jax.sharding import PartitionSpec as P

HEAD_DIM = 64


EPSILON = 1e-05
NEGATIVE = -1e30


def shifted(x, axis, by):
    devices = lax.axis_size(axis)
    return lax.ppermute(x, axis, [(i, (i + by) % devices) for i in range(devices)])


def norm_rows(values, gains, shifts):
    average = jnp.mean(values, axis=-1, keepdims=True)
    centered = values - average
    spread = jnp.mean(centered * centered, axis=-1, keepdims=True)
    return centered * lax.rsqrt(spread + EPSILON) * gains + shifts


def mid_piece(upper, gains, shifts):
    return norm_rows(jax.nn.gelu(upper, approximate=False), gains, shifts)


def split_heads(matrix):
    return matrix.reshape(matrix.shape[0], -1, HEAD_DIM)


def block_rows(total_rows):
    chosen = total_rows
    while chosen > 1024 and chosen % 2 == 0:
        chosen = chosen // 2
    return chosen


def row_layout(first_rows, rows_here):
    within = jnp.arange(rows_here, dtype=jnp.int32)
    first_len = first_rows[0]
    second = (within >= first_len).astype(jnp.int32)
    return (second, within - second * first_len)


def visible_pairs(query_seq, query_off, query_span, key_seq, key_off, key_span):
    earlier = key_span[None, :] < query_span[:, None]
    same_span = (key_span[None, :] == query_span[:, None]) & (
        key_off[None, :] <= query_off[:, None]
    )
    return (query_seq[:, None] == key_seq[None, :]) & (earlier | same_span)


def merge_block(state_in, query_heads, keys_block, values_block, visible):
    run_peak, run_total, accumulated = state_in
    query_rows = query_heads.shape[0]
    scores = jnp.einsum(
        "qhd,khd->hqk", query_heads, split_heads(keys_block), preferred_element_type=jnp.float32
    ) * HEAD_DIM ** (-0.5)
    masked = jnp.where(visible[None], scores, NEGATIVE)
    new_peak = jnp.maximum(run_peak, jnp.max(masked, axis=-1))
    weights = jnp.where(visible[None], jnp.exp(masked - new_peak[:, :, None]), 0.0)
    factor = jnp.exp(run_peak - new_peak)
    new_total = run_total * factor + jnp.sum(weights, axis=-1)
    update = jnp.einsum(
        "hqk,khd->qhd",
        weights.astype(jnp.bfloat16),
        split_heads(values_block),
        preferred_element_type=jnp.float32,
    )
    rescaled = split_heads(accumulated) * jnp.transpose(factor)[:, :, None]
    return (new_peak, new_total, (rescaled + update).reshape(query_rows, -1))


def grad_block(query_heads, log_total, delta, dout_heads, keys_block, values_block, visible):
    key_heads = split_heads(keys_block)
    value_heads = split_heads(values_block)
    scores = jnp.einsum(
        "qhd,khd->hqk", query_heads, key_heads, preferred_element_type=jnp.float32
    ) * HEAD_DIM ** (-0.5)
    probs = jnp.where(visible[None], jnp.exp(scores - log_total[:, :, None]), 0.0)
    dprobs = jnp.einsum("qhd,khd->hqk", dout_heads, value_heads, preferred_element_type=jnp.float32)
    dscores = (probs * (dprobs - delta[:, :, None])).astype(jnp.bfloat16)
    add_query = jnp.einsum("hqk,khd->qhd", dscores, key_heads, preferred_element_type=jnp.float32)
    add_keys = jnp.einsum("hqk,qhd->khd", dscores, query_heads, preferred_element_type=jnp.float32)
    add_values = jnp.einsum(
        "hqk,qhd->khd", probs.astype(jnp.bfloat16), dout_heads, preferred_element_type=jnp.float32
    )
    return (
        add_query.reshape(query_heads.shape[0], -1),
        add_keys.reshape(key_heads.shape[0], -1),
        add_values.reshape(key_heads.shape[0], -1),
    )


def unchanged(state_in):
    return state_in


def attention_forward(query_low, keys_low, values_low, layout):
    seq_ids, offsets, span_of, my_span, my_index = layout
    rows_here, row_width = query_low.shape
    heads_here = row_width // HEAD_DIM
    query_heads = split_heads(query_low)
    query_span = jnp.full((rows_here,), my_span, jnp.int32)
    initial = (
        jnp.full((heads_here, rows_here), NEGATIVE, jnp.float32),
        jnp.zeros((heads_here, rows_here), jnp.float32),
        jnp.zeros((rows_here, row_width), jnp.float32),
    )
    running = initial
    key_part = lax.all_gather(keys_low, "blk", axis=0, tiled=True)
    value_part = lax.all_gather(values_low, "blk", axis=0, tiled=True)
    part_rows = key_part.shape[0]
    step_rows = block_rows(part_rows)

    def one_step(state_in, step_index):
        block_start = step_index * step_rows
        global_rows = block_start + jnp.arange(step_rows, dtype=jnp.int32)
        key_span = span_of[global_rows // rows_here]
        local_rows = global_rows % rows_here
        visible = visible_pairs(
            seq_ids, offsets, query_span, seq_ids[local_rows], offsets[local_rows], key_span
        )
        keys_block = lax.dynamic_slice_in_dim(key_part, block_start, step_rows, 0)
        values_block = lax.dynamic_slice_in_dim(value_part, block_start, step_rows, 0)

        def one_compute(inner_state):
            return merge_block(inner_state, query_heads, keys_block, values_block, visible)

        return (lax.cond(jnp.any(key_span <= my_span), one_compute, unchanged, state_in), None)

    running, _ = lax.scan(one_step, running, jnp.arange(part_rows // step_rows, dtype=jnp.int32))
    run_peak, run_total, accumulated = running
    mixed_heads = (split_heads(accumulated) / jnp.transpose(run_total)[:, :, None]).reshape(
        rows_here, row_width
    )
    return (mixed_heads, run_peak + jnp.log(run_total))


def cycle_backward(query_low, keys_low, values_low, log_total, delta, dout_low, layout):
    seq_ids, offsets, span_of, my_span, my_index = layout
    rows_here, row_width = query_low.shape
    blocks_total = lax.axis_size("blk")
    query_heads = split_heads(query_low)
    dout_heads = split_heads(dout_low)
    query_span = jnp.full((rows_here,), my_span, jnp.int32)

    def turn(turn_index, carried):
        keys_now, values_now, dkeys, dvalues, dquery = carried
        source = (my_index - turn_index) % blocks_total
        source_span = span_of[source]
        key_span = jnp.full((rows_here,), source_span, jnp.int32)
        visible = visible_pairs(seq_ids, offsets, query_span, seq_ids, offsets, key_span)

        def turn_compute(inner_state):
            add_query, add_keys, add_values = grad_block(
                query_heads, log_total, delta, dout_heads, keys_now, values_now, visible
            )
            return (
                inner_state[0] + add_query,
                inner_state[1] + add_keys,
                inner_state[2] + add_values,
            )

        dquery, dkeys, dvalues = lax.cond(
            source_span <= my_span, turn_compute, unchanged, (dquery, dkeys, dvalues)
        )
        keys_now, values_now = shifted((keys_now, values_now), "blk", 1)
        dkeys, dvalues = (
            shifted(dkeys.astype(jnp.bfloat16), "blk", 1).astype(dkeys.dtype),
            shifted(dvalues.astype(jnp.bfloat16), "blk", 1).astype(dvalues.dtype),
        )
        return (keys_now, values_now, dkeys, dvalues, dquery)

    zeros_rows = jnp.zeros((rows_here, row_width), jnp.float32)
    result = lax.fori_loop(
        0, blocks_total, turn, (keys_low, values_low, zeros_rows, zeros_rows, zeros_rows)
    )
    return (result[4], result[2], result[3])


def layer_forward(inputs, weights, gains, biases, middle_gain, middle_bias, heads_scale, layout):
    weight_qkv, weight_out, weight_up, weight_down = weights
    row_width = inputs.shape[1]
    normed, pre_pull = jax.vjp(norm_rows, inputs, gains[0], biases[0])
    normed_low = normed.astype(jnp.bfloat16)
    projected = jnp.dot(normed_low, weight_qkv, preferred_element_type=jnp.float32)
    query_low = (projected[:, :row_width] + biases[3]).astype(jnp.bfloat16)
    keys_low = projected[:, row_width : 2 * row_width].astype(jnp.bfloat16)
    values_low = (projected[:, 2 * row_width :] + biases[4]).astype(jnp.bfloat16)
    mixed_heads, log_total = attention_forward(query_low, keys_low, values_low, layout)
    scaled_low = (mixed_heads * jnp.repeat(heads_scale, HEAD_DIM)).astype(jnp.bfloat16)
    branch = jnp.dot(scaled_low, weight_out, preferred_element_type=jnp.float32) + biases[5]
    post_normed, post_pull = jax.vjp(norm_rows, branch, gains[1], biases[1])
    middle_res = inputs + post_normed
    ffn_normed, ffn_pull = jax.vjp(norm_rows, middle_res, gains[2], biases[2])
    ffn_low = ffn_normed.astype(jnp.bfloat16)
    upper = jnp.dot(ffn_low, weight_up, preferred_element_type=jnp.float32) + middle_bias[1]
    middle, mid_pull = jax.vjp(mid_piece, upper, middle_gain, middle_bias[0])
    middle_low = middle.astype(jnp.bfloat16)
    results = middle_res + (
        jnp.dot(middle_low, weight_down, preferred_element_type=jnp.float32) + biases[6]
    )
    record = {
        "pre_pull": pre_pull,
        "normed_low": normed_low,
        "query_low": query_low,
        "keys_low": keys_low,
        "values_low": values_low,
        "log_total": log_total,
        "mixed_heads": mixed_heads,
        "scaled_low": scaled_low,
        "post_pull": post_pull,
        "ffn_pull": ffn_pull,
        "ffn_low": ffn_low,
        "mid_pull": mid_pull,
        "middle_low": middle_low,
        "weights": weights,
    }
    return (results, record)


def layer_backward(d_results, record, weights, heads_scale, layout):
    weight_qkv, weight_out, weight_up, weight_down = weights
    rows_here, row_width = d_results.shape
    d_results_low = d_results.astype(jnp.bfloat16)
    grad_down = jnp.einsum(
        "tf,td->fd", record["middle_low"], d_results_low, preferred_element_type=jnp.float32
    )
    grad_down_bias = jnp.sum(d_results_low, axis=0, dtype=jnp.float32)
    d_middle = jnp.einsum(
        "td,fd->tf", d_results_low, weight_down, preferred_element_type=jnp.float32
    )
    d_upper, grad_mid_gain, grad_mid_shift = record["mid_pull"](d_middle)
    d_upper_low = d_upper.astype(jnp.bfloat16)
    grad_up = jnp.einsum(
        "td,tf->df", record["ffn_low"], d_upper_low, preferred_element_type=jnp.float32
    )
    grad_up_bias = jnp.sum(d_upper_low, axis=0, dtype=jnp.float32)
    d_ffn = jnp.einsum("tf,df->td", d_upper_low, weight_up, preferred_element_type=jnp.float32)
    d_res_part, grad_gain_ffn, grad_shift_ffn = record["ffn_pull"](d_ffn)
    d_middle_res = d_results + d_res_part
    d_branch, grad_gain_post, grad_shift_post = record["post_pull"](d_middle_res)
    d_branch_low = d_branch.astype(jnp.bfloat16)
    grad_out_w = jnp.einsum(
        "tc,td->cd", record["scaled_low"], d_branch_low, preferred_element_type=jnp.float32
    )
    grad_out_bias = jnp.sum(d_branch_low, axis=0, dtype=jnp.float32)
    d_scaled = jnp.einsum("td,cd->tc", d_branch_low, weight_out, preferred_element_type=jnp.float32)
    mixed_heads = record["mixed_heads"]
    grad_heads = jnp.sum((d_scaled * mixed_heads).reshape(rows_here, -1, HEAD_DIM), axis=(0, 2))
    d_mixed_low = (d_scaled * jnp.repeat(heads_scale, HEAD_DIM)).astype(jnp.bfloat16)
    delta = jnp.transpose(
        jnp.sum(
            (d_mixed_low.astype(jnp.float32) * mixed_heads).reshape(rows_here, -1, HEAD_DIM), axis=2
        )
    )
    dquery, dkeys, dvalues = cycle_backward(
        record["query_low"],
        record["keys_low"],
        record["values_low"],
        record["log_total"],
        delta,
        d_mixed_low,
        layout,
    )
    scale_factor = HEAD_DIM ** (-0.5)
    d_proj_low = jnp.concatenate(
        [dquery * scale_factor, dkeys * scale_factor, dvalues], axis=1
    ).astype(jnp.bfloat16)
    grad_qkv = jnp.einsum(
        "tc,te->ce", record["normed_low"], d_proj_low, preferred_element_type=jnp.float32
    )
    grad_q_bias = jnp.sum(d_proj_low[:, :row_width], axis=0, dtype=jnp.float32)
    grad_v_bias = jnp.sum(d_proj_low[:, 2 * row_width :], axis=0, dtype=jnp.float32)
    d_normed = jnp.einsum("te,ce->tc", d_proj_low, weight_qkv, preferred_element_type=jnp.float32)
    d_in_part, grad_gain_pre, grad_shift_pre = record["pre_pull"](d_normed)
    d_inputs = d_middle_res + d_in_part
    big_grads = (grad_qkv, grad_out_w, grad_up, grad_down)
    gain_grads = jnp.stack([grad_gain_pre, grad_gain_post, grad_gain_ffn])
    bias_grads = jnp.stack(
        [
            grad_shift_pre,
            grad_shift_post,
            grad_shift_ffn,
            grad_q_bias,
            grad_v_bias,
            grad_out_bias,
            grad_down_bias,
        ]
    )
    small_grads = (
        gain_grads,
        bias_grads,
        grad_mid_gain,
        jnp.stack([grad_mid_shift, grad_up_bias]),
        grad_heads,
    )
    return (d_inputs, big_grads, small_grads)


def general(
    tokens,
    grad_out,
    first_rows,
    span_of,
    w_qkv,
    w_out,
    w_up,
    w_down,
    vec_gain,
    vec_bias,
    mid_gain,
    mid_bias,
    head_scale,
):
    rows_here = tokens.shape[0]
    my_index = lax.axis_index("blk")
    my_span = span_of[my_index]
    seq_ids, offsets = row_layout(first_rows, rows_here)
    layout = (seq_ids, offsets, span_of, my_span, my_index)
    current = tokens.astype(jnp.float32)
    records = []
    for layer_index in range(2):
        weights = (
            lax.all_gather(w_qkv[layer_index], "blk", axis=0, tiled=True),
            lax.all_gather(w_out[layer_index], "blk", axis=0, tiled=True),
            lax.all_gather(w_up[layer_index], "blk", axis=0, tiled=True),
            lax.all_gather(w_down[layer_index], "blk", axis=0, tiled=True),
        )
        current, record = layer_forward(
            current,
            weights,
            vec_gain[layer_index],
            vec_bias[layer_index],
            mid_gain[layer_index],
            mid_bias[layer_index],
            head_scale[layer_index],
            layout,
        )
        records.append(record)
    results_low = current.astype(jnp.bfloat16)
    d_current = grad_out.astype(jnp.float32)
    shard_grads = [None, None]
    small_grads = [None, None]
    for layer_index in (1, 0):
        weights = (
            lax.all_gather(w_qkv[layer_index], "blk", axis=0, tiled=True),
            lax.all_gather(w_out[layer_index], "blk", axis=0, tiled=True),
            lax.all_gather(w_up[layer_index], "blk", axis=0, tiled=True),
            lax.all_gather(w_down[layer_index], "blk", axis=0, tiled=True),
        )
        d_current, big_grads, small_part = layer_backward(
            d_current, records[layer_index], weights, head_scale[layer_index], layout
        )
        shard_grads[layer_index] = (
            lax.psum_scatter(
                big_grads[0].astype(jnp.bfloat16), "blk", scatter_dimension=0, tiled=True
            ).astype(jnp.float32),
            lax.psum_scatter(
                big_grads[1].astype(jnp.bfloat16), "blk", scatter_dimension=0, tiled=True
            ).astype(jnp.float32),
            lax.psum_scatter(
                big_grads[2].astype(jnp.bfloat16), "blk", scatter_dimension=0, tiled=True
            ).astype(jnp.float32),
            lax.psum_scatter(
                big_grads[3].astype(jnp.bfloat16), "blk", scatter_dimension=0, tiled=True
            ).astype(jnp.float32),
        )
        small_grads[layer_index] = small_part
    stacked_small = [
        jnp.stack([small_grads[0][item_index], small_grads[1][item_index]])
        for item_index in range(5)
    ]
    summed_small = (
        lax.psum(stacked_small[0].astype(jnp.bfloat16), "blk").astype(jnp.float32),
        lax.psum(stacked_small[1].astype(jnp.bfloat16), "blk").astype(jnp.float32),
        lax.psum(stacked_small[2].astype(jnp.bfloat16), "blk").astype(jnp.float32),
        lax.psum(stacked_small[3].astype(jnp.bfloat16), "blk").astype(jnp.float32),
        lax.psum(stacked_small[4].astype(jnp.bfloat16), "blk").astype(jnp.float32),
    )
    stacked_big = [
        jnp.stack([shard_grads[0][item_index], shard_grads[1][item_index]])
        for item_index in range(4)
    ]
    totals = (
        lax.psum(stacked_big[0].astype(jnp.bfloat16), "batch").astype(jnp.float32),
        lax.psum(stacked_big[1].astype(jnp.bfloat16), "batch").astype(jnp.float32),
        lax.psum(stacked_big[2].astype(jnp.bfloat16), "batch").astype(jnp.float32),
        lax.psum(stacked_big[3].astype(jnp.bfloat16), "batch").astype(jnp.float32),
        lax.psum(summed_small[0].astype(jnp.bfloat16), "batch").astype(jnp.float32),
        lax.psum(summed_small[1].astype(jnp.bfloat16), "batch").astype(jnp.float32),
        lax.psum(summed_small[2].astype(jnp.bfloat16), "batch").astype(jnp.float32),
        lax.psum(summed_small[3].astype(jnp.bfloat16), "batch").astype(jnp.float32),
        lax.psum(summed_small[4].astype(jnp.bfloat16), "batch").astype(jnp.float32),
    )
    return (
        results_low,
        d_current,
        totals[0],
        totals[1],
        totals[2],
        totals[3],
        totals[4],
        totals[5],
        totals[6],
        totals[7],
        totals[8],
    )


MESH = pl.DeviceIdType.MESH
LINE = 4
HALVES = 2
CHUNK = 32
TILE = 512


def place():
    k = lax.axis_index("blk")
    return k // 4, lax.rem(k // 2, 2), lax.rem(k, 2)


def index_of(z, y, c):
    return (z * 2 + y) * 2 + c


def device(z, y, c):
    return {"blk": index_of(z, y, c)}


def hail(where):
    pl.semaphore_signal(pltpu.get_barrier_semaphore(), inc=1, device_id=where, device_id_type=MESH)


def other_group():
    return {"batch": 1 - lax.axis_index("batch")}


def lasting(microseconds):
    return pl.CostEstimate(flops=0, bytes_accessed=int(microseconds * 3.5e6), transcendentals=0)


def remote(src, dst, send, recv, where):
    return pltpu.make_async_remote_copy(
        src_ref=src, dst_ref=dst, send_sem=send, recv_sem=recv, device_id=where, device_id_type=MESH
    )


class Swap:
    def __init__(self, x_ref, o_ref, ss, rs, own_sem, per=1):
        self.x_ref, self.o_ref, self.ss, self.rs, self.own_sem = x_ref, o_ref, ss, rs, own_sem
        self.k, self.n, self.per = lax.axis_index("blk"), 4 * LINE, per

    @staticmethod
    def scratch():
        dma = pltpu.SemaphoreType.DMA
        return [dma((4 * LINE,)), dma((4 * LINE,)), dma]

    def source(self, to):
        return self.x_ref.at[pl.ds(lax.rem(to, self.x_ref.shape[0] // self.per) * self.per, self.per)]

    def place(self, at):
        return self.o_ref.at[pl.ds(at * self.per, self.per)]

    def send(self, i):
        to = lax.rem(self.k + i, self.n)
        return remote(self.source(to), self.place(self.k), self.ss.at[i], self.rs.at[i], {"blk": to})

    def receive(self, i):
        at = lax.rem(self.k - i + self.n, self.n)
        return remote(self.place(at), self.place(at), self.ss.at[i], self.rs.at[i], {"blk": at})

    def own(self):
        return pltpu.make_async_copy(self.source(self.k), self.place(self.k), self.own_sem)

    def start(self):
        def one(i, carry):
            self.send(i).start()
            return carry

        lax.fori_loop(1, self.n, one, 0)
        self.own().start()

    def finish(self):
        def one(i, carry):
            self.receive(i).wait_recv()
            self.send(i).wait_send()
            return carry

        self.own().wait()
        lax.fori_loop(1, self.n, one, 0)


class Trade:
    def __init__(self, x_ref, o_ref, ss, rs, own_sem):
        self.x_ref, self.o_ref, self.ss, self.rs, self.own_sem = x_ref, o_ref, ss, rs, own_sem
        self.z, self.y, self.c = place()

    @staticmethod
    def scratch():
        dma = pltpu.SemaphoreType.DMA
        return [dma((LINE,)), dma((LINE,)), dma]

    def source(self, to):
        return self.x_ref.at[lax.rem(to, self.x_ref.shape[0])]

    def send(self, s):
        to = lax.rem(self.z + s, LINE)
        return remote(self.source(to), self.o_ref.at[self.z], self.ss.at[s], self.rs.at[s], device(to, self.y, self.c))

    def own(self):
        return pltpu.make_async_copy(self.source(self.z), self.o_ref.at[self.z], self.own_sem)

    def start(self):
        for s in range(1, LINE):
            self.send(s).start()
        self.own().start()

    def finish(self):
        self.own().wait()
        for s in range(1, LINE):
            at = lax.rem(self.z - s + LINE, LINE)
            slot = self.o_ref.at[at]
            remote(slot, slot, self.ss.at[s], self.rs.at[s], device(at, self.y, self.c)).wait_recv()
            self.send(s).wait_send()


class Cross:
    def __init__(self, x_ref, o_ref, ss, rs):
        self.copy = remote(x_ref, o_ref, ss, rs, other_group())

    @staticmethod
    def scratch():
        return [pltpu.SemaphoreType.DMA] * 2

    def start(self):
        self.copy.start()

    def finish(self):
        self.copy.wait()


def start_all(rides):
    for ride in rides:
        ride.start()


def finish_all(rides):
    for ride in rides:
        ride.finish()


def greet_group(crossing=False, plane=False):
    k, n = lax.axis_index("blk"), 4 * LINE

    def one(i, carry):
        hail({"blk": lax.rem(k + i, n)})
        return carry

    lax.fori_loop(1, n, one, 0)
    more = 0
    if plane:
        x, z, y, c = plane_place()
        for d in range(4):
            hail(plane_device(1 - x, z, 1 - y if d & 2 else y, 1 - c if d & 1 else c))
        more = 4
    elif crossing:
        hail(other_group())
        more = 1
    pl.semaphore_wait(pltpu.get_barrier_semaphore(), n - 1 + more)


class GroupGather:
    def __init__(self, all_ref, sems):
        self.all_ref = all_ref
        self.sr, self.rr, self.sl, self.rl, self.sy, self.ry, self.sc, self.rc = sems
        self.z, self.y, self.c = place()
        self.half = all_ref.shape[0] // (4 * LINE * HALVES)

    @staticmethod
    def scratch():
        dma = pltpu.SemaphoreType.DMA
        return [dma((LINE, HALVES))] * 6 + [dma((2 * LINE, HALVES))] * 2

    def block(self, z, y, h, c=None):
        c = self.c if c is None else c
        return self.all_ref.at[pl.ds((index_of(z, y, c) * HALVES + h) * self.half, self.half)]

    def right(self, s, h):
        block = self.block(self.z - s + 1, self.y, h)
        return remote(block, block, self.sr.at[s, h], self.rr.at[s, h], device(self.z + 1, self.y, self.c))

    def left(self, s, h):
        block = self.block(self.z + s - 1, self.y, h)
        return remote(block, block, self.sl.at[s, h], self.rl.at[s, h], device(self.z - 1, self.y, self.c))

    def across(self, zz, h):
        block = self.block(zz, self.y, h)
        return remote(block, block, self.sy.at[zz, h], self.ry.at[zz, h], device(self.z, 1 - self.y, self.c))

    def twin(self, zz, yy, h):
        block = self.block(zz, yy, h)
        slot = zz * 2 + yy
        return remote(block, block, self.sc.at[slot, h], self.rc.at[slot, h], device(self.z, self.y, 1 - self.c))

    def arrival(self, block, send, recv):
        remote(block, block, send, recv, device(self.z, self.y, 1 - self.c)).wait_recv()

    def start(self):
        z, y = self.z, self.y
        for h in range(HALVES):

            @pl.when(z < LINE - 1)
            def _():
                self.right(1, h).start()

            @pl.when(z > 0)
            def _():
                self.left(1, h).start()

            self.across(z, h).start()
        for h in range(HALVES):
            self.twin(z, y, h).start()

    def from_across(self, zz, h):
        self.arrival(self.block(zz, 1 - self.y, h), self.sy.at[zz, h], self.ry.at[zz, h])
        self.twin(zz, 1 - self.y, h).start()

    def pass_on(self, zz, h):
        self.across(zz, h).start()
        self.twin(zz, self.y, h).start()

    def run(self):
        z, y = self.z, self.y
        for s in range(1, LINE):
            for h in range(HALVES):

                @pl.when(z >= s)
                def _():
                    self.arrival(self.block(z - s, y, h), self.sr.at[s, h], self.rr.at[s, h])
                    if s < LINE - 1:

                        @pl.when(z < LINE - 1)
                        def _():
                            self.right(s + 1, h).start()

                    self.pass_on(z - s, h)

                @pl.when(z + s <= LINE - 1)
                def _():
                    self.arrival(self.block(z + s, y, h), self.sl.at[s, h], self.rl.at[s, h])
                    if s < LINE - 1:

                        @pl.when(z > 0)
                        def _():
                            self.left(s + 1, h).start()

                    self.pass_on(z + s, h)

                if s == 1:
                    self.from_across(z, h)
                else:

                    @pl.when(z >= s - 1)
                    def _():
                        self.from_across(z - s + 1, h)

                    @pl.when(z + s - 1 <= LINE - 1)
                    def _():
                        self.from_across(z + s - 1, h)

        for h in range(HALVES):

            @pl.when(z >= LINE - 1)
            def _():
                self.from_across(z - LINE + 1, h)

            @pl.when(z <= 0)
            def _():
                self.from_across(z + LINE - 1, h)

        for h in range(HALVES):
            for zz in range(LINE):
                for yy in range(2):
                    slot = zz * 2 + yy
                    self.arrival(self.block(zz, yy, h, 1 - self.c), self.sc.at[slot, h], self.rc.at[slot, h])

    def finish(self):
        z = self.z
        for h in range(HALVES):
            for zz in range(LINE):
                self.across(zz, h).wait_send()
                for yy in range(2):
                    self.twin(zz, yy, h).wait_send()
            for s in range(1, LINE):

                @pl.when((z < LINE - 1) & (z >= s - 1))
                def _():
                    self.right(s, h).wait_send()

                @pl.when((z > 0) & (z + s - 1 <= LINE - 1))
                def _():
                    self.left(s, h).wait_send()


def order_at(z, t):
    table = ((3, 2, 1, 0), (3, 0, 2, 1), (0, 3, 1, 2), (0, 1, 2, 3))
    low = jnp.where(z == 0, table[0][t], table[1][t])
    high = jnp.where(z == 2, table[2][t], table[3][t])
    return jnp.where(z < 2, low, high)


class GroupScatter:
    def __init__(self, part_ref, bufs, sems):
        self.part_ref = part_ref
        self.twins, self.ysend, self.yrecv, self.zsend, self.zright, self.zleft = bufs
        self.sc, self.rc, self.sy, self.ry, self.sz, self.rzr, self.rzl = sems
        self.z, self.y, self.c = place()
        self.half = part_ref.shape[0] // (4 * LINE * HALVES)

    @staticmethod
    def scratch(rows, columns):
        dma = pltpu.SemaphoreType.DMA
        bufs = [pltpu.VMEM((n, rows, columns), jnp.bfloat16) for n in (2 * LINE, LINE, LINE, LINE - 1, LINE, LINE)]
        return bufs, [dma((2 * LINE, HALVES))] * 2 + [dma((LINE, HALVES))] * 5

    def part(self, h):
        return pl.ds(h * self.half, self.half)

    def rows(self, t, own_y, c, h):
        y = self.y if own_y else 1 - self.y
        return pl.ds((index_of(order_at(self.z, t), y, c) * HALVES + h) * self.half, self.half)

    def twin(self, t, own_y, h):
        slot = t * 2 + own_y
        source = self.part_ref.at[self.rows(t, own_y, 1 - self.c, h)]
        dest = self.twins.at[slot, self.part(h)]
        return remote(source, dest, self.sc.at[slot, h], self.rc.at[slot, h], device(self.z, self.y, 1 - self.c))

    def across(self, t, h):
        source, dest = self.ysend.at[t, self.part(h)], self.yrecv.at[t, self.part(h)]
        return remote(source, dest, self.sy.at[t, h], self.ry.at[t, h], device(self.z, 1 - self.y, self.c))

    def along(self, d, t, h, to_right):
        buf, sem = (self.zright, self.rzr) if to_right else (self.zleft, self.rzl)
        where = device(self.z + 1, self.y, self.c) if to_right else device(self.z - 1, self.y, self.c)
        return remote(self.zsend.at[t, self.part(h)], buf.at[d, self.part(h)], self.sz.at[t, h], sem.at[d, h], where)

    def arrived(self, d, h, to_right):
        buf, sem = (self.zright, self.rzr) if to_right else (self.zleft, self.rzl)
        slot = buf.at[d, self.part(h)]
        remote(slot, slot, self.sz.at[0, h], sem.at[d, h], device(self.z, self.y, 1 - self.c)).wait_recv()

    def wide(self, ref, slot, h):
        return ref[slot, self.part(h)].astype(jnp.float32)

    def chip(self, t, own_y, h):
        return self.part_ref[self.rows(t, own_y, self.c, h)].astype(jnp.float32) + self.wide(self.twins, t * 2 + own_y, h)

    def start(self):
        for own_y in (0, 1):
            for t in range(LINE):
                for h in range(HALVES):
                    self.twin(t, own_y, h).start()

    def first(self):
        for t in range(LINE):
            for h in range(HALVES):
                self.twin(t, 0, h).wait_recv()
                self.ysend[t, self.part(h)] = self.chip(t, 0, h).astype(jnp.bfloat16)
                self.across(t, h).start()

    def second(self, o_ref):
        z = self.z
        for t in range(LINE):
            d = order_at(z, t)
            for h in range(HALVES):
                self.twin(t, 1, h).wait_recv()
                self.across(t, h).wait_recv()

                def summed(t=t, h=h):
                    return self.chip(t, 1, h) + self.wide(self.yrecv, t, h)

                if t < LINE - 1:
                    for to_right in (True, False):

                        @pl.when((d > z) if to_right else (d < z))
                        def _():
                            first = (z == 0) if to_right else (z == LINE - 1)
                            buf = self.zright if to_right else self.zleft

                            @pl.when(first)
                            def _():
                                self.zsend[t, self.part(h)] = summed().astype(jnp.bfloat16)

                            @pl.when(jnp.logical_not(first))
                            def _():
                                self.arrived(d, h, to_right)
                                self.zsend[t, self.part(h)] = (summed() + self.wide(buf, d, h)).astype(jnp.bfloat16)

                            self.along(d, t, h, to_right).start()
                else:

                    @pl.when(z > 0)
                    def _():
                        self.arrived(z, h, True)

                    @pl.when(z < LINE - 1)
                    def _():
                        self.arrived(z, h, False)

                    @pl.when(z == 0)
                    def _():
                        o_ref[self.part(h)] = summed() + self.wide(self.zleft, z, h)

                    @pl.when(z == LINE - 1)
                    def _():
                        o_ref[self.part(h)] = summed() + self.wide(self.zright, z, h)

                    @pl.when((z > 0) & (z < LINE - 1))
                    def _():
                        o_ref[self.part(h)] = summed() + self.wide(self.zright, z, h) + self.wide(self.zleft, z, h)

    def finish(self):
        for h in range(HALVES):
            for t in range(LINE):
                self.across(t, h).wait_send()
                self.twin(t, 0, h).wait_send()
                self.twin(t, 1, h).wait_send()
            for t in range(LINE - 1):
                self.along(0, t, h, True).wait_send()


NN = (((1,), (0,)), ((), ()))
NT = (((1,), (1,)), ((), ()))
TN = (((0,), (0,)), ((), ()))


def mul(a, b, dims=NN):
    return lax.dot_general(a, b, dims, preferred_element_type=jnp.float32)


def tile_at(t):
    return pl.ds(pl.multiple_of(t * TILE, TILE), TILE)


def chunk_at(index, rows=CHUNK):
    return pl.ds(pl.multiple_of(index * rows, rows), rows)


def diagonal(p):
    key = lax.broadcasted_iota(jnp.int32, p.shape, 0)
    query = lax.broadcasted_iota(jnp.int32, p.shape, 1)
    return key <= query


PLANE = 8


def plane_place():
    x = lax.axis_index("batch")
    z, y, c = place()
    return x, z, y, c


def plane_device(x, z, y, c):
    return {"batch": x, "blk": index_of(z, y, c)}


def plane_index(x, y, c):
    return (x * 2 + y) * 2 + c


class PlaneGather:
    def __init__(self, all_ref, sems):
        self.all_ref = all_ref
        self.sx, self.rx, self.sy, self.ry, self.sc, self.rc = sems
        self.x, self.z, self.y, self.c = plane_place()
        self.half = all_ref.shape[0] // (2 * PLANE)

    @staticmethod
    def scratch():
        dma = pltpu.SemaphoreType.DMA
        return [dma((3,))] * 4 + [dma((PLANE,))] * 2

    def piece(self, x, y, c, h):
        return self.all_ref.at[pl.ds(plane_index(x, y, c) * 2 * self.half + h * self.half, self.half)]

    def over_x(self, i):
        x, y, c = self.x, self.y, self.c
        piece = self.piece(x, y if i < 2 else 1 - y, c, (0, 1, 1)[i])
        return remote(piece, piece, self.sx.at[i], self.rx.at[i], plane_device(1 - x, self.z, y, c))

    def over_y(self, i):
        x, y, c = self.x, self.y, self.c
        piece = self.piece(x if i < 2 else 1 - x, y, c, (1, 0, 0)[i])
        return remote(piece, piece, self.sy.at[i], self.ry.at[i], plane_device(x, self.z, 1 - y, c))

    def from_x(self, i):
        x, y, c = self.x, self.y, self.c
        piece = self.piece(1 - x, y if i < 2 else 1 - y, c, (0, 1, 1)[i])
        remote(piece, piece, self.sx.at[i], self.rx.at[i], plane_device(1 - x, self.z, y, c)).wait_recv()

    def from_y(self, i):
        x, y, c = self.x, self.y, self.c
        piece = self.piece(x if i < 2 else 1 - x, 1 - y, c, (1, 0, 0)[i])
        remote(piece, piece, self.sy.at[i], self.ry.at[i], plane_device(x, self.z, 1 - y, c)).wait_recv()

    def twin(self, other_x, other_y, h):
        x = 1 - self.x if other_x else self.x
        y = 1 - self.y if other_y else self.y
        slot = (other_x * 2 + other_y) * 2 + h
        piece = self.piece(x, y, self.c, h)
        return remote(piece, piece, self.sc.at[slot], self.rc.at[slot], plane_device(self.x, self.z, self.y, 1 - self.c))

    def from_twin(self, other_x, other_y, h):
        x = 1 - self.x if other_x else self.x
        y = 1 - self.y if other_y else self.y
        slot = (other_x * 2 + other_y) * 2 + h
        piece = self.piece(x, y, 1 - self.c, h)
        where = plane_device(self.x, self.z, self.y, 1 - self.c)
        remote(piece, piece, self.sc.at[slot], self.rc.at[slot], where).wait_recv()

    def start(self):
        self.over_x(0).start()
        self.over_y(0).start()
        self.over_x(1).start()
        self.over_y(1).start()
        self.twin(0, 0, 0).start()
        self.twin(0, 0, 1).start()

    def near(self):
        self.from_x(0)
        self.over_y(2).start()
        self.twin(1, 0, 0).start()
        self.from_y(0)
        self.over_x(2).start()
        self.twin(0, 1, 1).start()
        self.from_y(1)
        self.twin(0, 1, 0).start()
        for other_y in range(2):
            for h in range(2):
                self.from_twin(0, other_y, h)

    def far(self):
        self.from_x(1)
        self.twin(1, 0, 1).start()
        self.from_x(2)
        self.twin(1, 1, 1).start()
        self.from_y(2)
        self.twin(1, 1, 0).start()
        for other_y in range(2):
            for h in range(2):
                self.from_twin(1, other_y, h)

    def finish(self):
        for i in range(3):
            self.over_x(i).wait_send()
            self.over_y(i).wait_send()
        for other_x in range(2):
            for other_y in range(2):
                for h in range(2):
                    self.twin(other_x, other_y, h).wait_send()


class PlaneScatter:
    def __init__(self, part_ref, bufs, sems):
        self.part_ref = part_ref
        self.twins, self.xs, self.xr, self.ys, self.yr = bufs
        self.sx, self.rx, self.sy, self.ry, self.sc, self.rc = sems
        self.x, self.z, self.y, self.c = plane_place()
        self.half = part_ref.shape[0] // (2 * PLANE)

    @staticmethod
    def scratch(rows, columns):
        dma = pltpu.SemaphoreType.DMA
        half = pltpu.VMEM((3, rows // 2, columns), jnp.bfloat16)
        return [pltpu.VMEM((4, rows, columns), jnp.bfloat16)] + [half] * 4, [dma((3,))] * 4 + [dma((4,))] * 2

    def rows(self, which, c, h=None):
        x = self.x if which >= 2 else 1 - self.x
        y = self.y if which % 2 else 1 - self.y
        at = plane_index(x, y, c) * 2 * self.half
        return pl.ds(at, 2 * self.half) if h is None else pl.ds(at + h * self.half, self.half)

    def twin(self, which):
        where = plane_device(self.x, self.z, self.y, 1 - self.c)
        source = self.part_ref.at[self.rows(which, 1 - self.c)]
        return remote(source, self.twins.at[which], self.sc.at[which], self.rc.at[which], where)

    def over_x(self, i):
        return remote(
            self.xs.at[i], self.xr.at[i], self.sx.at[i], self.rx.at[i], plane_device(1 - self.x, self.z, self.y, self.c)
        )

    def over_y(self, i):
        return remote(
            self.ys.at[i], self.yr.at[i], self.sy.at[i], self.ry.at[i], plane_device(self.x, self.z, 1 - self.y, self.c)
        )

    def chip(self, which, h):
        own = self.part_ref[self.rows(which, self.c, h)].astype(jnp.float32)
        return own + self.twins[which, h * self.half : (h + 1) * self.half].astype(jnp.float32)

    def first(self):
        self.twin(0).wait_recv()
        self.xs[0] = self.chip(0, 0).astype(jnp.bfloat16)
        self.over_x(0).start()
        self.ys[0] = self.chip(0, 1).astype(jnp.bfloat16)
        self.over_y(0).start()
        self.twin(1).wait_recv()
        self.xs[1] = self.chip(1, 0).astype(jnp.bfloat16)
        self.over_x(1).start()
        self.twin(2).wait_recv()
        self.ys[1] = self.chip(2, 1).astype(jnp.bfloat16)
        self.over_y(1).start()

    def second(self):
        self.over_x(0).wait_recv()
        self.ys[2] = (self.chip(2, 0) + self.xr[0].astype(jnp.float32)).astype(jnp.bfloat16)
        self.over_y(2).start()
        self.over_y(0).wait_recv()
        self.xs[2] = (self.chip(1, 1) + self.yr[0].astype(jnp.float32)).astype(jnp.bfloat16)
        self.over_x(2).start()

    def finish(self, o_ref):
        half = self.half
        self.twin(3).wait_recv()
        self.over_x(1).wait_recv()
        self.over_y(1).wait_recv()
        self.over_y(2).wait_recv()
        o_ref[0:half] = self.chip(3, 0) + self.xr[1].astype(jnp.float32) + self.yr[2].astype(jnp.float32)
        self.over_x(2).wait_recv()
        o_ref[half : 2 * half] = self.chip(3, 1) + self.yr[1].astype(jnp.float32) + self.xr[2].astype(jnp.float32)
        for which in range(4):
            self.twin(which).wait_send()
        for i in range(3):
            self.over_x(i).wait_send()
            self.over_y(i).wait_send()


class PlanePool:
    def __init__(self, own_ref, got_ref, send, recv):
        self.own_ref, self.got_ref, self.send, self.recv = own_ref, got_ref, send, recv
        self.x, self.z, self.y, self.c = plane_place()

    def others(self):
        for d in range(1, PLANE):
            x = 1 - self.x if d & 4 else self.x
            y = 1 - self.y if d & 2 else self.y
            c = 1 - self.c if d & 1 else self.c
            yield d, x, y, c

    def copies(self):
        slot = self.got_ref.at[plane_index(self.x, self.y, self.c)]
        for d, x, y, c in self.others():
            yield remote(self.own_ref, slot, self.send.at[d], self.recv.at[d], plane_device(x, self.z, y, c))

    def start(self):
        for copy in self.copies():
            copy.start()
        self.got_ref[plane_index(self.x, self.y, self.c)] = self.own_ref[...]

    def finish(self):
        for d, x, y, c in self.others():
            slot = self.got_ref.at[plane_index(x, y, c)]
            remote(slot, slot, self.send.at[d], self.recv.at[d], plane_device(x, self.z, y, c)).wait_recv()
        for copy in self.copies():
            copy.wait_send()


def span_at(th, width):
    return pl.ds(pl.multiple_of(th * width, 128), width)


def units_at(ut):
    return pl.ds(pl.multiple_of(ut * 256, 256), 256)


def mean_and_rate(stat, hidden_all):
    return stat[0:1], lax.rsqrt(stat[1:2] * (1.0 / hidden_all) + EPSILON)


class Refs:
    def __init__(self, **named):
        self.__dict__.update(named)


def launch(call, kernel, inputs, outputs, scratch, collective_id, microseconds, vmem_mib):
    def body(*refs):
        refs = list(refs)
        named = Refs()
        for key in [*inputs, *outputs]:
            setattr(named, key, refs.pop(0))
        for key, what in scratch.items():
            if isinstance(what, list):
                setattr(named, key, [refs.pop(0) for _ in what])
            else:
                setattr(named, key, refs.pop(0))
        kernel(named)

    results = call(
        body,
        out_shape=[shape for shape, _ in outputs.values()],
        in_specs=[pl.BlockSpec(memory_space=space) for _, space in inputs.values()],
        out_specs=[pl.BlockSpec(memory_space=space) for _, space in outputs.values()],
        scratch_shapes=[entry for what in scratch.values() for entry in (what if isinstance(what, list) else [what])],
        cost_estimate=lasting(microseconds),
        compiler_params=pltpu.CompilerParams(
            collective_id=collective_id, has_side_effects=True, vmem_limit_bytes=vmem_mib << 20
        ),
    )(*[array for array, _ in inputs.values()])
    return Refs(**dict(zip(outputs, results)))


def normed(values, gain, shift):
    centred = values - jnp.mean(values, axis=-1, keepdims=True)
    spread = jnp.mean(centred * centred, axis=-1, keepdims=True)
    return centred * lax.rsqrt(spread + EPSILON) * gain + shift


def normed_back(values, gain, grads):
    centred = values - jnp.mean(values, axis=-1, keepdims=True)
    rate = lax.rsqrt(jnp.mean(centred * centred, axis=-1, keepdims=True) + EPSILON)
    unit = centred * rate
    scaled = grads * gain
    back = rate * (
        scaled - jnp.mean(scaled, axis=-1, keepdims=True) - unit * jnp.mean(scaled * unit, axis=-1, keepdims=True)
    )
    return back, jnp.sum(grads * unit, axis=0, keepdims=True), jnp.sum(grads, axis=0, keepdims=True)


def unfold_head(blocks_ref, w_ref):
    for j in range(blocks_ref.shape[0]):
        for part in range(2):
            at = slice(64 * j + 32 * part, 64 * j + 32 * part + 32)
            w_ref[at, 0:128] = blocks_ref[j, :, 128 * part : 128 * part + 128]
            w_ref[at, 128:192] = blocks_ref[j, :, 256 + 64 * part : 320 + 64 * part]


def fold_head(w, head):
    width = w.shape[1] // 3
    at = [slice(part * width + 64 * head, part * width + 64 * head + 64) for part in range(3)]
    halves = [w[0:32], w[32:64]]
    pieces = [half[:, at[part]] for half in halves for part in (0, 2)] + [half[:, at[1]] for half in halves]
    return jnp.concatenate(pieces, axis=1)


def unit_lanes(z, slot):
    return pl.ds(pl.multiple_of(z * PLANE * 128 + slot * 128, 128), 128)


def unit_columns(vectors, slot, column_refs):
    pieces = [vector[:, unit_lanes(z, slot)] for vector in vectors for z in range(LINE)]
    pieces.append(jnp.zeros((16 - len(pieces), 128), jnp.float32))
    turned = jnp.transpose(jnp.concatenate(pieces, axis=0))
    for i, ref in enumerate(column_refs):
        for z in range(LINE):
            ref[128 * z : 128 * z + 128] = turned[:, i * LINE + z : i * LINE + z + 1]


def of_layer(ref, layer):
    return [ref.at[kind, pl.ds(layer, 1)] for kind in range(ref.shape[0])]


def own_head(row, index):
    pair = row[:, pl.ds(pl.multiple_of(index // 2 * 128, 128), 128)]
    return jnp.where(lax.rem(index, 2) == 0, pair[:, 0:64], pair[:, 64:128])


def chunks_of(ref, t):
    per_tile = TILE // CHUNK
    part = ref[pl.ds(t * per_tile, per_tile)]
    return part.reshape(per_tile * part.shape[1], part.shape[2])


def alive(cut, i, j):
    return jnp.where((i >= cut) & (j < cut), NEGATIVE, 0.0)


def natural_rows(slot, zz):
    x, y, c = slot // 4, slot // 2 % 2, slot % 2
    return 64 * index_of(zz, y, c) + 32 * x


def forward_kernel(layer, hidden_all, r):
    first = layer == 0
    x, z, y, c = plane_place()
    index, slot = index_of(z, y, c), plane_index(x, y, c)
    unit_slot = (y * 2 + c) * 2 + x
    rows, columns = r.x_in.shape
    total = r.hb_all.shape[0]
    tiles, chunks, per_tile = total // TILE, total // CHUNK, TILE // CHUNK
    gather = GroupGather(r.hb_all, r.gather_sems)
    gains, biases = of_layer(r.gains, layer), of_layer(r.biases, layer)
    if first:
        load_qkv = pltpu.make_async_copy(r.w_qkv, r.qkv_in, r.prep_sem.at[0])
        load_qkv.start()
        for l in range(2):
            for q in range(4):
                for zz in range(LINE):
                    source = r.w_up.at[l, :, unit_lanes(zz, q * 2 + x)]
                    dest = r.unit_src.at[l, q, :, pl.ds(zz * 128, 128)]
                    pltpu.make_async_copy(source, dest, r.prep_sem.at[1 + l]).start()
    value = r.x_in[...].astype(jnp.float32)
    r.hb_all[pl.ds(index * rows, rows)] = normed(value, gains[0][...], biases[0][...]).astype(jnp.bfloat16)
    head_ride = Swap(r.head_src.at[0], r.head_blocks, *r.head_sems) if first else None
    unit_ride = Swap(r.unit_src.at[0], r.unit_blocks, *r.unit_sems) if first else None
    down_ride = Trade(r.w_down.at[layer, pl.ds(x, 1)], r.down_blocks, *r.down_sems)
    out_ride = Trade(r.w_out.at[layer, pl.ds(x, 1)], r.out_got, *r.out_sems)
    next_rides = [Swap(r.head_src.at[1], r.next_head, *r.next_head_sems)] if first else []
    next_rides += [Swap(r.unit_src.at[1], r.next_unit, *r.next_unit_sems)] if first else []
    if first:
        load_qkv.wait()
        for head in range(4 * LINE):
            r.head_src[0, head] = fold_head(r.qkv_in[0], head)
    load_head = pltpu.make_async_copy(r.head_blocks, r.head_in, r.load_sem.at[0])
    load_unit = pltpu.make_async_copy(r.unit_blocks, r.unit_in, r.load_sem.at[1])
    load_down = pltpu.make_async_copy(r.down_blocks, r.down_w, r.load_sem.at[2])
    greet_group(plane=True)
    if first:
        head_ride.start()
    gather.start()
    out_ride.start()
    mids = [r.mid_gain_all.at[pl.ds(layer, 1)], r.mid_bias_all.at[layer, pl.ds(0, 1)], r.mid_bias_all.at[layer, pl.ds(1, 1)]]
    unit_columns(mids, unit_slot, (r.mid_gain, r.mid_shift, r.mid_bias))
    head_bias = [own_head(biases[row], index) for row in (3, 4)] + [jnp.zeros((1, 64), jnp.float32)]
    head_bias = jnp.concatenate(head_bias, axis=1)
    if first:
        for head in range(4 * LINE):
            r.head_src[1, head] = fold_head(r.qkv_in[1], head)
        for l in range(2):
            pltpu.make_async_copy(r.unit_src.at[l], r.unit_src.at[l], r.prep_sem.at[1 + l]).wait()
    if not first:
        load_head.start()
        load_unit.start()
    gather.run()
    if first:
        unit_ride.start()
        head_ride.finish()
        load_head.start()
    else:
        down_ride.start()
    load_head.wait()
    unfold_head(r.head_in, r.head_w)

    def project(t, carry):
        rows_t = (mul(r.hb_all[tile_at(t)], r.head_w[...]) + head_bias).astype(jnp.bfloat16)
        r.flat[pl.ds(t * per_tile, per_tile)] = rows_t.reshape(per_tile, CHUNK, 192)
        return carry

    lax.fori_loop(0, tiles, project, 0)
    out_ride.finish()
    out_rows = r.out_all.shape[0] // PLANE
    for zz in range(LINE):
        r.out_all[pl.ds(slot * out_rows + zz * 32, 32)] = r.out_got[zz]
    out_gather = PlaneGather(r.out_all, r.out_gather_sems)
    out_gather.start()

    def arrange(p, carry):
        r.qvk[p] = r.flat[r.table[p]]
        return carry

    lax.fori_loop(0, chunks, arrange, 0)

    def prepare(t, carry):
        rows_t = chunks_of(r.qvk, t)
        r.queries[tile_at(t)] = rows_t[:, 0:64] * 0.125
        r.keys[tile_at(t)] = rows_t[:, 128:192]
        turned = jnp.transpose(rows_t[:, 0:128].astype(jnp.float32))
        r.values_t[:, tile_at(t)] = turned[64:128].astype(jnp.bfloat16)
        return carry

    lax.fori_loop(0, tiles, prepare, 0)
    cut = r.table[2 * chunks]
    for i in range(tiles):
        at = slice(i * TILE, (i + 1) * TILE)
        query = r.queries[at]

        def block(j, state, masked):
            peak, part, mixed = state
            scores = mul(r.keys[tile_at(j)], query, NT)
            bias = 0.0 if masked else alive(cut, i, j)
            if masked:
                keep = diagonal(scores)
                scores = jnp.where(keep, scores, NEGATIVE)
            new_peak = jnp.maximum(peak, jnp.max(scores, axis=0, keepdims=True) + bias)
            weights = jnp.exp(scores - (new_peak - bias))
            if masked:
                weights = jnp.where(keep, weights, 0.0)
            factor = jnp.exp(peak - new_peak)
            part = part * factor + jnp.sum(weights, axis=0, keepdims=True)
            mixed = mixed * factor + mul(r.values_t[:, tile_at(j)], weights.astype(jnp.bfloat16))
            return (new_peak, part, mixed)

        state = (
            jnp.full((1, TILE), NEGATIVE, jnp.float32),
            jnp.zeros((1, TILE), jnp.float32),
            jnp.zeros((64, TILE), jnp.float32),
        )
        state = block(i, state, True)
        if i > 0:
            state = lax.fori_loop(0, i, functools.partial(block, masked=False), state)
        peak, part, mixed = state
        mixed = mixed / part
        r.lse[:, at] = peak + jnp.log(part)
        r.head_out[:, at] = mixed
        pairs = (jnp.transpose(mixed) * r.scales[layer, index]).reshape(per_tile, 2, CHUNK // 2, 64)
        pairs = jnp.concatenate([pairs[:, 0], pairs[:, 1]], axis=-1).astype(jnp.bfloat16)
        r.pairs[i * per_tile : (i + 1) * per_tile] = pairs
        if i == 2:
            out_gather.near()
    per_block = rows // CHUNK

    def pack(p, carry):
        r.packed[p] = r.pairs[r.table[chunks + p]]
        return carry

    lax.fori_loop(0, chunks, pack, 0)
    mix = Swap(r.packed, r.mixed, *r.mix_sems, per=per_block)
    mix.start()
    out_gather.far()
    for s in range(PLANE):
        for zz in range(LINE):
            at = natural_rows(s, zz)
            r.out_w[at : at + 32] = r.out_all[s * out_rows + zz * 32 : s * out_rows + zz * 32 + 32]
    out_gather.finish()
    mix.finish()
    if first:
        down_ride.start()
    for g in range(columns // 128):
        left, right = (
            r.mixed[h * per_block : (h + 1) * per_block].reshape(rows // 2, 128) for h in (2 * g, 2 * g + 1)
        )
        low = jnp.concatenate([left[:, 0:64], right[:, 0:64]], axis=1)
        high = jnp.concatenate([left[:, 64:128], right[:, 64:128]], axis=1)
        for p in range(per_block):
            at = slice(p * (CHUNK // 2), (p + 1) * (CHUNK // 2))
            r.ab[p * CHUNK : p * CHUNK + CHUNK // 2, 128 * g : 128 * g + 128] = low[at]
            r.ab[p * CHUNK + CHUNK // 2 : (p + 1) * CHUNK, 128 * g : 128 * g + 128] = high[at]
    branch = mul(r.ab[...], r.out_w[...]) + biases[5][...]
    r.branch[...] = branch
    middle = value + normed(branch, gains[1][...], biases[1][...])
    r.middle[...] = middle

    own = pl.ds(slot * rows, rows)
    r.rows_all[own] = normed(middle, gains[2][...], biases[2][...]).astype(jnp.bfloat16)
    plane_gather = PlaneGather(r.rows_all, r.plane_gather_sems)
    plane_scatter = PlaneScatter(r.part, r.plane_bufs, r.plane_sems)
    pool = PlanePool(r.own_stat, r.got_stat, *r.pool_sems)
    plane_gather.start()
    hidden = r.act.shape[0]
    width = r.act.shape[1] // 2
    if first:
        plane_gather.near()
        plane_gather.far()
        unit_ride.finish()
        load_unit.start()
    load_unit.wait()
    for j in range(r.unit_in.shape[0] // 2):
        pair = r.unit_in[2 * j : 2 * j + 2].reshape(128, hidden)
        r.unit_t[:, 128 * j : 128 * j + 128] = jnp.transpose(pair)

    def climb(th):
        at = span_at(th, width)

        def units(ut, carry):
            here = units_at(ut)
            upper = mul(r.unit_t[here], r.rows_all[pl.ds(th * width, width)], NT) + r.mid_bias[here]
            chance = 0.5 * (1.0 + lax.erf(upper * (0.5**0.5)))
            r.act[here, at] = upper * chance
            slope = chance + upper * (jnp.exp(-0.5 * upper * upper) * 0.3989422804014327)
            r.slope[here, at] = slope.astype(jnp.bfloat16)
            return carry

        lax.fori_loop(0, hidden // 256, units, 0)
        values = r.act[:, at]
        mean = jnp.mean(values, axis=0, keepdims=True)
        apart = values - mean
        r.own_stat[0:1, at] = mean
        r.own_stat[1:2, at] = jnp.sum(apart * apart, axis=0, keepdims=True)

    if not first:
        plane_gather.near()
    climb(x)
    if not first:
        plane_gather.far()
    climb(1 - x)
    pool.start()
    down_ride.finish()
    load_down.start()
    start_all(next_rides)
    pool.finish()
    load_down.wait()
    means = [r.got_stat[i, 0:1] for i in range(PLANE)]
    mean = functools.reduce(jnp.add, means) * (1.0 / PLANE)
    apart = functools.reduce(jnp.add, [(m - mean) * (m - mean) for m in means])
    r.stat[0:1] = mean
    r.stat[1:2] = functools.reduce(jnp.add, [r.got_stat[i, 1:2] for i in range(PLANE)]) + apart * float(hidden)

    def descend(th):
        at = span_at(th, width)
        mean, rate = mean_and_rate(r.stat[:, at], hidden_all)

        def units(ut, carry):
            here = units_at(ut)
            low = (r.act[here, at] - mean) * rate * r.mid_gain[here] + r.mid_shift[here]
            r.mid[here, at] = low.astype(jnp.bfloat16)
            return carry

        lax.fori_loop(0, hidden // 256, units, 0)
        down_w = r.down_w[...].reshape(hidden, columns)
        r.part[pl.ds(th * width, width)] = mul(r.mid[:, at], down_w, TN).astype(jnp.bfloat16)

    descend(1 - x)
    plane_scatter.twin(0).start()
    plane_scatter.twin(1).start()
    descend(x)
    plane_scatter.twin(2).start()
    plane_scatter.twin(3).start()
    saved = (
        (r.hb_all, r.hb_all_out), (r.qvk, r.qvk_out), (r.out_w, r.out_w_out), (r.rows_all, r.rows_all_out),
        (r.unit_t, r.unit_t_out), (r.act, r.act_out), (r.slope, r.slope_out), (r.mid, r.mid_out),
    )
    saves = [pltpu.make_async_copy(source, dest, r.save_sem.at[i]) for i, (source, dest) in enumerate(saved)]
    for save in saves:
        save.start()
    plane_scatter.first()
    plane_scatter.second()
    plane_scatter.finish(r.result)
    r.y_out[...] = (r.middle[...] + (r.result[...] + biases[6][...])).astype(r.y_out.dtype)
    gather.finish()
    plane_gather.finish()
    for save in saves:
        save.wait()
    finish_all(next_rides)


def layer_forward_kernel(layer, table, x_in, params, blocks, y_type, collective_id):
    rows, columns = x_in.shape
    hidden_all = params.mid_gain.shape[1]
    total, plane_rows, hidden = rows * 4 * LINE, rows * PLANE, hidden_all // PLANE
    vmem, anywhere, smem = pltpu.VMEM, pl.ANY, pltpu.SMEM
    dma = pltpu.SemaphoreType.DMA
    low = lambda *shape: pltpu.VMEM(shape, jnp.bfloat16)
    full = lambda *shape: pltpu.VMEM(shape, jnp.float32)
    low_out = lambda *shape: jax.ShapeDtypeStruct(shape, jnp.bfloat16)
    full_out = lambda *shape: jax.ShapeDtypeStruct(shape, jnp.float32)
    swap_sems, trade_sems = Swap.scratch(), Trade.scratch()
    inputs = dict(
        table=(table, smem), scales=(params.head_scale, smem), x_in=(x_in, vmem), gains=(params.vec_gain, vmem),
        biases=(params.vec_bias, vmem), mid_gain_all=(params.mid_gain, vmem), mid_bias_all=(params.mid_bias, vmem),
        w_down=(params.w_down, anywhere), w_out=(params.w_out, anywhere),
    )
    head_shape, unit_shape = (4 * LINE, 32, 384), (4 * LINE, columns // (4 * LINE), hidden)
    outputs = dict(
        y_out=(jax.ShapeDtypeStruct((rows, columns), y_type), vmem), branch=(full_out(rows, columns), vmem),
        middle=(full_out(rows, columns), vmem), ab=(low_out(rows, columns), vmem),
        lse=(full_out(1, total), vmem), head_out=(full_out(64, total), vmem),
        stat=(full_out(2, plane_rows), vmem), hb_all_out=(low_out(total, columns), anywhere),
        qvk_out=(low_out(total // CHUNK, CHUNK, 192), anywhere), out_w_out=(low_out(columns, columns), anywhere),
        rows_all_out=(low_out(plane_rows, columns), anywhere), unit_t_out=(low_out(hidden, columns), anywhere),
        act_out=(full_out(hidden, plane_rows), anywhere), slope_out=(low_out(hidden, plane_rows), anywhere),
        mid_out=(low_out(hidden, plane_rows), anywhere), down_blocks=(low_out(LINE, hidden // LINE, columns), anywhere),
    )
    first = layer == 0
    if first:
        inputs.update(w_qkv=(params.w_qkv, anywhere), w_up=(params.w_up, anywhere))
        head_got, unit_got = (low_out(*head_shape), anywhere), (low_out(*unit_shape), anywhere)
        outputs.update(head_blocks=head_got, unit_blocks=unit_got, next_head=head_got, next_unit=unit_got)
    else:
        inputs.update(head_blocks=(blocks.head, anywhere), unit_blocks=(blocks.unit, anywhere))
    plane_bufs, plane_sems = PlaneScatter.scratch(rows, columns)
    scratch = dict(
        hb_all=low(total, columns), flat=low(total // CHUNK, CHUNK, 192),
        qvk=low(total // CHUNK, CHUNK, 192), queries=low(total, 64), keys=low(total, 64),
        values_t=low(64, total), pairs=low(total // CHUNK, CHUNK // 2, 128),
        packed=low(total // CHUNK, CHUNK // 2, 128), mixed=low(total // CHUNK, CHUNK // 2, 128), head_in=low(4 * LINE, 32, 384), head_w=low(columns, 192),
        unit_in=low(4 * LINE, columns // (4 * LINE), hidden), unit_t=low(hidden, columns),
        down_w=low(LINE, hidden // LINE, columns), out_got=low(LINE, 32, columns),
        out_all=low(columns, columns), out_w=low(columns, columns), rows_all=low(plane_rows, columns),
        act=full(hidden, plane_rows), slope=low(hidden, plane_rows), mid=low(hidden, plane_rows),
        part=low(plane_rows, columns), own_stat=full(2, plane_rows), got_stat=full(PLANE, 2, plane_rows),
        result=full(rows, columns), plane_bufs=plane_bufs, plane_sems=plane_sems,
        gather_sems=GroupGather.scratch(), plane_gather_sems=PlaneGather.scratch(),
        out_gather_sems=PlaneGather.scratch(), pool_sems=([dma((PLANE,)), dma((PLANE,))]),
        head_sems=swap_sems, unit_sems=swap_sems, next_head_sems=swap_sems, next_unit_sems=swap_sems,
        mix_sems=swap_sems, down_sems=trade_sems, out_sems=trade_sems, load_sem=dma((3,)),
        save_sem=dma((8,)),
    )
    scratch.update(mid_gain=full(hidden, 1), mid_shift=full(hidden, 1), mid_bias=full(hidden, 1))
    if first:
        scratch.update(qkv_in=low(*params.w_qkv.shape), head_src=low(2, *head_shape), prep_sem=dma((3,)))
        scratch.update(unit_src=low(2, 4, columns // (4 * LINE), hidden))
    kernel = functools.partial(forward_kernel, layer, hidden_all)
    call = lambda body, **how: pl.pallas_call(body, name="layer_forward", **how)
    return launch(call, kernel, inputs, outputs, scratch, collective_id, 95, 56)


class AllSum:
    def __init__(self, own_ref, sent, got, send, recv):
        self.own_ref, self.sent, self.got, self.send, self.recv = own_ref, sent, got, send, recv
        self.z, self.y, self.c = place()

    @staticmethod
    def scratch(shape, kind):
        dma = pltpu.SemaphoreType.DMA
        return [pltpu.VMEM((3, *shape), kind), pltpu.VMEM((LINE + 2, *shape), kind), dma((LINE + 2,)), dma((LINE + 2,))]

    def copy(self, i):
        z, y, c = self.z, self.y, self.c
        where = (other_group(), device(z, y, 1 - c), device(z, 1 - y, c))[i] if i < 3 else None
        if i >= 3:
            where = device(lax.rem(z + i - 2, LINE), y, c)
        source = self.own_ref if i == 0 else self.sent.at[min(i, 3) - 1]
        return remote(source, self.got.at[i], self.send.at[i], self.recv.at[i], where)

    def start(self):
        self.copy(0).start()

    def step(self, i):
        self.copy(i - 1).wait_recv()
        own = self.own_ref[...] if i == 1 else self.sent[i - 2]
        self.sent[i - 1] = (own.astype(jnp.float32) + self.got[i - 1].astype(jnp.float32)).astype(self.sent.dtype)
        for k in range(i, i + 1 if i < 3 else LINE + 2):
            self.copy(k).start()

    def finish(self, o_ref):
        for i in range(3, LINE + 2):
            self.copy(i).wait_recv()
        total = None
        for zz in range(LINE):
            term = self.sent[2].astype(jnp.float32)
            for s in range(1, LINE):
                term = jnp.where(lax.rem(self.z - s + LINE, LINE) == zz, self.got[2 + s].astype(jnp.float32), term)
            total = term if total is None else total + term
        o_ref[...] = total
        for i in range(LINE + 2):
            self.copy(i).wait_send()


OUT_BIAS, DOWN_BIAS, QUERY_BIAS, VALUE_BIAS, SCALES, MID, SMALL = 6, 7, 8, 9, 10, 12, 24


def spread_head(piece, index, width):
    nothing = jnp.zeros_like(piece)
    even = lax.rem(index, 2) == 0
    pair = jnp.concatenate([jnp.where(even, piece, nothing), jnp.where(even, nothing, piece)], axis=1)
    lanes = lax.broadcasted_iota(jnp.int32, (1, width), 1) // 128
    return jnp.where(lanes == index // 2, jnp.concatenate([pair] * (width // 128), axis=1), 0.0)


def backward_kernel(layer, hidden_all, r):
    first = layer == 1
    x, z, y, c = plane_place()
    index, unit_slot = index_of(z, y, c), (y * 2 + c) * 2 + x
    rows, columns = r.dy.shape
    total = r.hb_all_in.shape[0]
    tiles, chunks, per_tile = total // TILE, total // CHUNK, TILE // CHUNK
    hidden, plane_rows = r.act.shape
    width = plane_rows // 2
    dy_all, x_all = r.wide.at[pl.ds(0, plane_rows)], r.wide.at[pl.ds(plane_rows, plane_rows)]
    plane_gather = PlaneGather(dy_all, r.plane_gather_sems)
    plane_scatter = PlaneScatter(r.part, r.plane_bufs, r.plane_sems)
    out_part = r.part.at[pl.ds(0, LINE * PLANE * 32)]
    out_scatter = PlaneScatter(out_part, r.out_bufs, r.out_sems)
    scatter = GroupScatter(r.wide, r.group_bufs, r.group_sems)
    pool = PlanePool(r.own_sums, r.got_sums, *r.pool_sems)
    unit_ride = Swap(r.gup, r.unit_got, *r.unit_sems)
    out_ride = Trade(r.out_own, r.out_got, *r.out_ride_sems)
    head_ride = Swap(r.head_fold, r.head_got, *r.head_sems)
    head_cross = Cross(r.head_own, r.head_other, *r.head_cross_sems)
    down_ride = Trade(r.gdown, r.gdown_got, *r.gdown_sems)
    near_rides = [
        Cross(r.unit_near, r.unit_far, *r.unit_cross_sems), Cross(r.down_near, r.down_far, *r.down_cross_sems),
        Cross(r.out_near, r.out_far, *r.out_cross_sems),
    ]
    if not first:
        bulk = AllSum(r.bulk, *r.bulk_sum)
        rest = AllSum(r.rest, *r.rest_sum)
    gains = of_layer(r.gains, layer)
    r.small[...] = jnp.zeros_like(r.small)
    dy = r.dy[...].astype(jnp.float32)
    dy_low = dy.astype(jnp.bfloat16)
    r.small[DOWN_BIAS : DOWN_BIAS + 1] = jnp.sum(dy_low.astype(jnp.float32), axis=0, keepdims=True)
    dy_all[pl.ds(plane_index(x, y, c) * rows, rows)] = dy_low
    loads = [
        pltpu.make_async_copy(source, dest, r.load_sem.at[i])
        for i, (source, dest) in enumerate(
            (
                (r.down_blocks, r.down_w), (r.act_in, r.act), (r.slope_in, r.slope), (r.unit_t_in, r.unit_t),
                (r.mid_in, r.mid), (r.rows_all_in, x_all), (r.out_w_in, r.out_w), (r.qvk_in, r.qvk),
            )
        )
    ]
    for load in loads[:6]:
        load.start()
    greet_group(plane=True)
    plane_gather.start()
    for load in loads[6:]:
        load.start()

    def tile_load(t):
        return pltpu.make_async_copy(r.hb_all_in.at[pl.ds(t * TILE, TILE)], r.hb_tiles.at[t % 2], r.tile_sem.at[t % 2])

    tile_load(0).start()
    tile_load(1).start()
    unit_columns([r.mid_gain_all.at[pl.ds(layer, 1)]], unit_slot, [r.mid_gain])
    r.gg[...] = jnp.zeros_like(r.gg)
    r.gs[...] = jnp.zeros_like(r.gs)
    r.gb[...] = jnp.zeros_like(r.gb)
    r.own_sums[...] = jnp.zeros_like(r.own_sums)

    def climb(th):
        at = span_at(th, width)
        mean, rate = mean_and_rate(r.stat[:, at], hidden_all)

        def units(ut, carry):
            here = units_at(ut)
            down_w = r.down_w[pl.ds(ut * 2, 2)].reshape(256, columns)
            dm = mul(down_w, dy_all[pl.ds(th * width, width)], NT)
            r.dmid[here, at] = dm
            vh = (r.act[here, at] - mean) * rate
            r.act[here, at] = vh
            r.gg[here] += jnp.sum(dm * vh, axis=1, keepdims=True)
            r.gs[here] += jnp.sum(dm, axis=1, keepdims=True)
            scaled = dm * r.mid_gain[here]
            r.own_sums[0:1, at] += jnp.sum(scaled, axis=0, keepdims=True)
            r.own_sums[1:2, at] += jnp.sum(scaled * vh, axis=0, keepdims=True)
            return carry

        lax.fori_loop(0, hidden // 256, units, 0)

    plane_gather.near()
    loads[0].wait()
    loads[1].wait()
    climb(x)
    plane_gather.far()
    climb(1 - x)
    pool.start()
    loads[4].wait()
    for ut in range(hidden // 256):
        grad = mul(r.mid[ut * 256 : (ut + 1) * 256], dy_all[...]).astype(jnp.bfloat16)
        r.gdown[2 * ut : 2 * ut + 2] = grad.reshape(2, 128, columns)
    down_ride.start()
    pool.finish()
    r.sums[...] = functools.reduce(jnp.add, [r.got_sums[i] for i in range(PLANE)]) * (1.0 / hidden_all)
    loads[2].wait()
    loads[3].wait()

    def descend(th):
        at = span_at(th, width)
        _, rate = mean_and_rate(r.stat[:, at], hidden_all)
        sum0, sum1 = r.sums[0:1, at], r.sums[1:2, at]

        def units(ut, carry):
            here = units_at(ut)
            dact = rate * (r.dmid[here, at] * r.mid_gain[here] - sum0 - r.act[here, at] * sum1)
            du = (dact * r.slope[here, at].astype(jnp.float32)).astype(jnp.bfloat16)
            r.du[here, at] = du
            r.gb[here] += jnp.sum(du.astype(jnp.float32), axis=1, keepdims=True)
            return carry

        lax.fori_loop(0, hidden // 256, units, 0)
        r.part[pl.ds(th * width, width)] = mul(r.du[:, at], r.unit_t[...], TN).astype(jnp.bfloat16)

    descend(1 - x)
    plane_scatter.twin(0).start()
    plane_scatter.twin(1).start()
    descend(x)
    plane_scatter.twin(2).start()
    plane_scatter.twin(3).start()
    plane_scatter.first()
    loads[5].wait()
    plane_scatter.second()
    for ut in range(hidden // 256):
        grad = jnp.transpose(mul(r.du[ut * 256 : (ut + 1) * 256], x_all[...])).astype(jnp.bfloat16)
        r.gup[:, :, ut * 256 : (ut + 1) * 256] = grad.reshape(r.gup.shape[0], -1, 256)
    plane_scatter.finish(r.dffn)
    plane_gather.finish()

    back, r.small[2:3], r.small[5:6] = normed_back(r.middle[...], gains[2][...], r.dffn[...])
    r.dmiddle[...] = dy + back
    back, r.small[1:2], r.small[4:5] = normed_back(r.branch[...], gains[1][...], r.dmiddle[...])
    dz = back.astype(jnp.bfloat16)
    r.small[OUT_BIAS : OUT_BIAS + 1] = jnp.sum(dz.astype(jnp.float32), axis=0, keepdims=True)
    loads[6].wait()
    da = mul(dz, r.out_w[...], NT).astype(jnp.bfloat16)
    per_block = rows // CHUNK
    halves = da.reshape(per_block, 2, CHUNK // 2, columns)
    low, high = halves[:, 0].reshape(rows // 2, columns), halves[:, 1].reshape(rows // 2, columns)
    for h in range(columns // 64):
        at = slice(64 * h, 64 * h + 64)
        pairs = jnp.concatenate([low[:, at], high[:, at]], axis=1)
        r.packed[h * per_block : (h + 1) * per_block] = pairs.reshape(per_block, CHUNK // 2, 128)
    mix = Swap(r.packed, r.mixed, *r.mix_sems, per=per_block)
    mix.start()
    out_rows = LINE * 32
    for zz in range(LINE):
        grad = mul(r.ab[:, 256 * zz : 256 * zz + 256], dz, TN).astype(jnp.bfloat16)
        for s in range(PLANE):
            at = natural_rows(s, 0)
            out_part[s * out_rows + zz * 32 : s * out_rows + zz * 32 + 32] = grad[at : at + 32]
    for which in range(4):
        out_scatter.twin(which).start()
    turned = [ref[128 * zz : 128 * zz + 128] for ref in (r.gg, r.gs, r.gb) for zz in range(LINE)]
    turned = jnp.transpose(jnp.concatenate(turned + [jnp.zeros((128, 4), jnp.float32)], axis=1))
    for i in range(3 * LINE):
        r.small[MID + i : MID + i + 1, unit_lanes(0, unit_slot)] = turned[i : i + 1]
    if not first:
        r.bulk[0:SMALL] = r.small_in[...].astype(jnp.bfloat16)
        r.bulk[SMALL : 2 * SMALL] = r.small[...].astype(jnp.bfloat16)
        bulk.start()
    loads[7].wait()
    load_head = pltpu.make_async_copy(r.head_blocks, r.head_fold, r.load_sem.at[6])
    load_head.start()
    scale = r.scales[layer, index]

    def prepare(t, carry):
        at = tile_at(t)
        rows_t = chunks_of(r.qvk, t)
        r.query[at] = rows_t[:, 0:64] * 0.125
        r.values[at] = rows_t[:, 64:128]
        key = rows_t[:, 128:192]
        r.keys[at] = key
        r.keys_t[:, at] = jnp.transpose(key.astype(jnp.float32)).astype(jnp.bfloat16)
        r.dkeys[at] = jnp.zeros((TILE, 64), jnp.float32)
        r.dvalues[at] = jnp.zeros((TILE, 64), jnp.float32)
        return carry

    lax.fori_loop(0, tiles, prepare, 0)
    load_head.wait()
    unfold_head(r.head_fold, r.head_w)
    out_scatter.first()
    mix.finish()
    unit_ride.start()

    def arrange(p, carry):
        r.pairs[p] = r.mixed[r.table[p]]
        return carry

    lax.fori_loop(0, chunks, arrange, 0)

    def unpack(t, carry):
        at = tile_at(t)
        pairs = r.pairs[pl.ds(t * per_tile, per_tile)].astype(jnp.float32)
        pairs = jnp.concatenate([pairs[:, :, 0:64], pairs[:, :, 64:128]], axis=1).reshape(TILE, 64)
        low = (pairs * scale).astype(jnp.bfloat16)
        r.dout[at] = low
        r.delta[:, at] = jnp.sum(jnp.transpose(low.astype(jnp.float32)) * r.head_out[:, at], axis=0, keepdims=True)
        return carry

    lax.fori_loop(0, tiles, unpack, 0)
    lanes = lax.broadcasted_iota(jnp.int32, (1, columns), 1)
    scale_grad = jnp.sum(r.delta[...], axis=1, keepdims=True) / scale
    r.small[SCALES : SCALES + 1] = jnp.where(lanes == layer * 4 * LINE + index, scale_grad, 0.0)
    cut = r.table[2 * chunks]
    for i in range(tiles):
        at = slice(i * TILE, (i + 1) * TILE)
        query, dout, lse, delta = r.query[at], r.dout[at], r.lse[:, at], r.delta[:, at]

        def block(j, total_dq, masked):
            there = tile_at(j)
            scores = mul(r.keys[there], query, NT)
            weights = jnp.exp(scores - (lse if masked else lse - alive(cut, i, j)))
            if masked:
                weights = jnp.where(diagonal(scores), weights, 0.0)
            dweights = mul(r.values[there], dout, NT)
            dscores = (weights * (dweights - delta)).astype(jnp.bfloat16)
            r.dvalues[there] += mul(weights.astype(jnp.bfloat16), dout)
            r.dkeys[there] += mul(dscores, query)
            return total_dq + mul(r.keys_t[:, there], dscores)

        total_dq = block(i, jnp.zeros((64, TILE), jnp.float32), True)
        if i > 0:
            total_dq = lax.fori_loop(0, i, functools.partial(block, masked=False), total_dq)
        r.dquery_t[:, at] = total_dq * 0.125
        if i == 1:
            out_scatter.second()
            if not first:
                bulk.step(1)
        if i == 2:
            out_scatter.finish(r.out_sum)
            r.out_own[...] = r.out_sum[...].reshape(r.out_own.shape).astype(jnp.bfloat16)
            out_ride.start()
            if not first:
                bulk.step(2)

    head_bias = jnp.zeros((1, 192), jnp.float32)
    for i in range(tiles):
        at = slice(i * TILE, (i + 1) * TILE)
        joined = jnp.concatenate([jnp.transpose(r.dquery_t[:, at]), r.dvalues[at], r.dkeys[at]], axis=1).astype(jnp.bfloat16)
        head_bias += jnp.sum(joined.astype(jnp.float32), axis=0, keepdims=True)
        r.qvk[i * per_tile : (i + 1) * per_tile] = joined.reshape(per_tile, CHUNK, 192)

    r.small[QUERY_BIAS : QUERY_BIAS + 1] = spread_head(head_bias[:, 0:64], index, columns)
    r.small[VALUE_BIAS : VALUE_BIAS + 1] = spread_head(head_bias[:, 64:128], index, columns)

    def restore(p, carry):
        r.flat[p] = r.qvk[r.table[chunks + p]]
        return carry

    lax.fori_loop(0, chunks, restore, 0)

    def project(t, carry):
        r.wide[tile_at(t)] = mul(chunks_of(r.flat, t), r.head_w[...], NT).astype(jnp.bfloat16)
        return carry

    lax.fori_loop(0, tiles, project, 0)
    scatter.start()
    for t in range(tiles):
        tile_load(t).wait()
        grad = mul(chunks_of(r.flat, t), r.hb_tiles[t % 2], TN)
        r.gw[...] = grad if t == 0 else r.gw[...] + grad
        if t + 2 < tiles:
            tile_load(t + 2).start()
    r.head_own[...] = jnp.transpose(r.gw[...]).astype(jnp.bfloat16)
    head_cross.start()
    scatter.first()
    if not first:
        bulk.step(3)
    down_ride.finish()
    out_ride.finish()
    unit_ride.finish()
    reloads = [
        pltpu.make_async_copy(source, dest, r.load_sem.at[i])
        for i, (source, dest) in enumerate(((r.unit_got, r.gup), (r.gdown_got, r.gdown), (r.out_got, r.out_own)))
    ]
    for load in reloads:
        load.start()
    head_cross.finish()
    for j in range(r.head_fold.shape[0]):
        for part in range(2):
            at = slice(64 * j + 32 * part, 64 * j + 32 * part + 32)
            both = (r.head_own[at].astype(jnp.float32) + r.head_other[at].astype(jnp.float32)).astype(jnp.bfloat16)
            r.head_fold[j, :, 128 * part : 128 * part + 128] = both[:, 0:128]
            r.head_fold[j, :, 256 + 64 * part : 320 + 64 * part] = both[:, 128:192]
    head_ride.start()
    for load in reloads:
        load.wait()
    for q in range(4):
        parts = [r.gup[zz * 4 + q].astype(jnp.float32) for zz in range(LINE)]
        r.unit_near[q] = functools.reduce(jnp.add, parts).astype(jnp.bfloat16)
    for near, own in ((r.down_near, r.gdown), (r.out_near, r.out_own)):
        near[...] = functools.reduce(jnp.add, [own[zz].astype(jnp.float32) for zz in range(LINE)]).astype(jnp.bfloat16)
    start_all(near_rides)
    scatter.second(r.dffn)
    back, gain_grad, shift_grad = normed_back(r.x_in[...].astype(jnp.float32), gains[0][...], r.dffn[...])
    r.dx[...] = r.dmiddle[...] + back
    r.small[0:1] = gain_grad
    r.small[3:4] = shift_grad
    if not first:
        r.rest[0:1] = gain_grad
        r.rest[1:2] = shift_grad
        r.rest[2:5] = r.small[QUERY_BIAS : SCALES + 1]
        r.rest[5:8] = jnp.zeros((3, columns), jnp.float32)
        rest.start()
        bulk.finish(r.bulk_out)
        rest.step(1)
        rest.step(2)
        rest.step(3)
        rest.finish(r.rest_out)
    scatter.finish()
    head_ride.finish()
    finish_all(near_rides)


def layer_backward_kernel(layer, table, dy, params, record, small, collective_id):
    rows, columns = dy.shape
    hidden_all = params.mid_gain.shape[1]
    total, plane_rows, hidden = rows * 4 * LINE, rows * PLANE, hidden_all // PLANE
    vmem, anywhere, smem = pltpu.VMEM, pl.ANY, pltpu.SMEM
    dma = pltpu.SemaphoreType.DMA
    low = lambda *shape: pltpu.VMEM(shape, jnp.bfloat16)
    full = lambda *shape: pltpu.VMEM(shape, jnp.float32)
    low_out = lambda *shape: jax.ShapeDtypeStruct(shape, jnp.bfloat16)
    full_out = lambda *shape: jax.ShapeDtypeStruct(shape, jnp.float32)
    swap_sems, trade_sems, cross_sems = Swap.scratch(), Trade.scratch(), Cross.scratch()
    unit_shape = (4 * LINE, columns // (4 * LINE), hidden)
    unit_near, down_near, out_near = (4, *unit_shape[1:]), (hidden // LINE, columns), (32, columns)
    down_shape = (LINE, hidden // LINE, columns)
    inputs = dict(
        table=(table, smem), scales=(params.head_scale, smem), dy=(dy, vmem), gains=(params.vec_gain, vmem),
        mid_gain_all=(params.mid_gain, vmem), x_in=(record.x_in, vmem), branch=(record.branch, vmem),
        middle=(record.middle, vmem), ab=(record.ab, vmem), lse=(record.lse, vmem),
        head_out=(record.head_out, vmem), stat=(record.stat, vmem), hb_all_in=(record.hb_all_out, anywhere),
        qvk_in=(record.qvk_out, anywhere), out_w_in=(record.out_w_out, anywhere),
        rows_all_in=(record.rows_all_out, anywhere), unit_t_in=(record.unit_t_out, anywhere),
        act_in=(record.act_out, anywhere), slope_in=(record.slope_out, anywhere),
        mid_in=(record.mid_out, anywhere), down_blocks=(record.down_blocks, anywhere),
        head_blocks=(record.head_blocks, anywhere),
    )
    outputs = dict(
        dx=(full_out(rows, columns), vmem), unit_got=(low_out(*unit_shape), anywhere),
        gdown_got=(low_out(*down_shape), anywhere), out_got=(low_out(LINE, *out_near), anywhere),
        head_got=(low_out(4 * LINE, 32, 384), anywhere), unit_near=(low_out(*unit_near), vmem),
        down_near=(low_out(*down_near), vmem), out_near=(low_out(*out_near), vmem),
        unit_far=(low_out(*unit_near), anywhere), down_far=(low_out(*down_near), anywhere),
        out_far=(low_out(*out_near), anywhere),
    )
    first = layer == 1
    if first:
        outputs.update(small=(full_out(SMALL, columns), vmem))
    else:
        inputs.update(small_in=(small, vmem))
        outputs.update(bulk_out=(full_out(2 * SMALL, columns), vmem), rest_out=(full_out(8, columns), vmem))
    plane_bufs, plane_sems = PlaneScatter.scratch(rows, columns)
    out_bufs, out_sems = PlaneScatter.scratch(LINE * 32, columns)
    group_bufs, group_sems = GroupScatter.scratch(rows, columns)
    scratch = dict(
        wide=low(total, columns), down_w=low(*down_shape), act=full(hidden, plane_rows),
        slope=low(hidden, plane_rows), unit_t=low(hidden, columns), mid=low(hidden, plane_rows),
        out_w=low(columns, columns), qvk=low(total // CHUNK, CHUNK, 192), hb_tiles=low(2, TILE, columns),
        dmid=full(hidden, plane_rows), du=low(hidden, plane_rows), part=low(plane_rows, columns),
        own_sums=full(2, plane_rows), got_sums=full(PLANE, 2, plane_rows), sums=full(2, plane_rows),
        gup=low(*unit_shape), gdown=low(*down_shape), dffn=full(rows, columns),
        dmiddle=full(rows, columns), packed=low(total // CHUNK, CHUNK // 2, 128),
        mixed=low(total // CHUNK, CHUNK // 2, 128),
        out_sum=full(LINE * 32, columns), out_own=low(LINE, 32, columns),
        pairs=low(total // CHUNK, CHUNK // 2, 128), dout=low(total, 64), delta=full(1, total), query=low(total, 64),
        keys=low(total, 64), values=low(total, 64), keys_t=low(64, total), dkeys=full(total, 64),
        dvalues=full(total, 64), dquery_t=full(64, total), flat=low(total // CHUNK, CHUNK, 192),
        head_w=low(columns, 192), gw=full(192, columns), head_own=low(columns, 192),
        head_other=low(columns, 192), head_fold=low(4 * LINE, 32, 384),
        plane_bufs=plane_bufs, plane_sems=plane_sems, out_bufs=out_bufs, out_sems=out_sems,
        group_bufs=group_bufs, group_sems=group_sems, plane_gather_sems=PlaneGather.scratch(),
        pool_sems=([dma((PLANE,)), dma((PLANE,))]), unit_sems=swap_sems, gdown_sems=trade_sems, head_sems=swap_sems,
        mix_sems=swap_sems, out_ride_sems=trade_sems, head_cross_sems=cross_sems, load_sem=dma((10,)),
        tile_sem=dma((2,)),
    )
    scratch.update(unit_cross_sems=cross_sems, down_cross_sems=cross_sems, out_cross_sems=cross_sems)
    scratch.update(mid_gain=full(hidden, 1), gg=full(hidden, 1), gs=full(hidden, 1), gb=full(hidden, 1))
    if not first:
        scratch.update(small=full(SMALL, columns), bulk=low(2 * SMALL, columns), rest=full(8, columns))
        scratch.update(bulk_sum=AllSum.scratch((2 * SMALL, columns), jnp.bfloat16))
        scratch.update(rest_sum=AllSum.scratch((8, columns), jnp.float32))
    kernel = functools.partial(backward_kernel, layer, hidden_all)
    call = lambda body, **how: pl.pallas_call(body, name="layer_backward", **how)
    return launch(call, kernel, inputs, outputs, scratch, collective_id, 105, 63)


def assemble_kernel(r):
    x = lax.axis_index("batch")
    for layer, got in enumerate((r.layer0, r.layer1)):
        head_ref, unit_near, unit_far, down_near, down_far, out_near, out_far = got
        width = 64 * head_ref.shape[0]
        for j in range(0, head_ref.shape[0], 2):
            left, right = head_ref[j].astype(jnp.float32), head_ref[j + 1].astype(jnp.float32)
            for part in range(2):
                for at, source in ((0, 128 * part), (width, 256 + 64 * part), (2 * width, 64 + 128 * part)):
                    pair = jnp.concatenate([left[:, source : source + 64], right[:, source : source + 64]], axis=1)
                    r.qkv[layer, 32 * part : 32 * part + 32, at + j * 64 : at + (j + 2) * 64] = pair
        for half, unit_ref, down_ref, out_ref in ((x, unit_near, down_near, out_near), (1 - x, unit_far, down_far, out_far)):
            for q in range(unit_ref.shape[0]):
                for z in range(LINE):
                    piece = unit_ref[q, :, z * 128 : (z + 1) * 128].astype(jnp.float32)
                    r.up[layer, :, unit_lanes(z, q * 2 + half)] = piece
            for ref, dest in ((down_ref, r.down), (out_ref, r.out)):
                rows = ref.shape[0]
                dest[layer, pl.ds(pl.multiple_of(half * rows, rows), rows)] = ref[...].astype(jnp.float32)
        bulk = r.bulk[SMALL * (1 - layer) : SMALL * (2 - layer)]
        rest = r.rest[...] if layer == 0 else bulk[0:1] * 0.0
        gain, shift = (rest[0:1], rest[1:2]) if layer == 0 else (bulk[0:1], bulk[3:4])
        heads = rest[2:4] if layer == 0 else bulk[QUERY_BIAS : VALUE_BIAS + 1]
        gain_rows = jnp.concatenate([gain, bulk[1:3]], axis=0)
        bias_rows = jnp.concatenate([shift, bulk[4:6], heads, bulk[OUT_BIAS : DOWN_BIAS + 1]], axis=0)
        for ref, rows in ((r.vec_gain, gain_rows), (r.vec_bias, bias_rows)):
            for i in range(ref.shape[0]):
                ref[i, layer : layer + 1] = rows[i : i + 1]
        for z in range(LINE):
            at = slice(z * PLANE * 128, (z + 1) * PLANE * 128)
            r.mid_gain[layer : layer + 1, at] = bulk[MID + z : MID + z + 1]
            for i in range(2):
                row = MID + (i + 1) * LINE + z
                r.mid_bias[layer, i : i + 1, at] = bulk[row : row + 1]
        row = rest[4:5] if layer == 0 else bulk[SCALES : SCALES + 1]
        heads_here = r.head_scale.shape[1]
        r.head_scale[layer : layer + 1] = row[:, layer * heads_here : (layer + 1) * heads_here]


def assemble(results, dx, back, shapes):
    vmem, anywhere = pl.BlockSpec(memory_space=pltpu.VMEM), pl.BlockSpec(memory_space=pl.ANY)
    arrays = [results, dx]
    for got in back:
        arrays += [got.head_got, got.unit_near, got.unit_far, got.down_near, got.down_far, got.out_near, got.out_far]

    arrays += [back[0].bulk_out, back[0].rest_out]
    n = len(arrays)

    def body(*refs):
        ins, outs, held, sem = refs[:n], refs[n : n + 11], refs[n + 11 : -1], refs[-1]
        loads = [pltpu.make_async_copy(ins[i], held[i], sem.at[i]) for i in range(n)]
        passes = [pltpu.make_async_copy(held[i], outs[i], sem.at[i]) for i in range(2)]
        for load in loads:
            load.start()
        for load in loads:
            load.wait()
        for copy in passes:
            copy.start()
        qkv, out, up, down, vec_gain, vec_bias, mid_gain, mid_bias, head_scale = outs[2:]
        refs = held[2:]
        assemble_kernel(
            Refs(
                layer0=refs[0:7], layer1=refs[7:14], bulk=refs[14], rest=refs[15], qkv=qkv, out=out, up=up, down=down,
                vec_gain=vec_gain, vec_bias=vec_bias, mid_gain=mid_gain, mid_bias=mid_bias, head_scale=head_scale,
            )
        )
        for copy in passes:
            copy.wait()

    return pl.pallas_call(
        body,
        out_shape=[jax.ShapeDtypeStruct(array.shape, array.dtype) for array in (results, dx)]
        + [jax.ShapeDtypeStruct(shape, jnp.float32) for shape in shapes],
        in_specs=[anywhere] * n,
        out_specs=[anywhere] * 2 + [vmem] * len(shapes),
        scratch_shapes=[pltpu.VMEM(array.shape, array.dtype) for array in arrays] + [pltpu.SemaphoreType.DMA((n,))],
        cost_estimate=lasting(5),
        compiler_params=pltpu.CompilerParams(vmem_limit_bytes=62 << 20),
        name="assemble",
    )(*arrays)


def chunk_table(first_rows, span_of, rows_here):
    blocks = span_of.shape[0]
    first = first_rows[0]
    second = rows_here - first
    row = jnp.arange(blocks * rows_here // CHUNK, dtype=jnp.int32) * CHUNK
    later = row >= first * blocks
    inside = jnp.where(later, row - first * blocks, row)
    length = jnp.where(later, jnp.maximum(second, 1), first)
    span = inside // length
    of_span = (span_of[None, :] == span[:, None]).astype(jnp.int32)
    device_of = jnp.sum(of_span * jnp.arange(blocks, dtype=jnp.int32)[None, :], axis=1)
    source = device_of * rows_here + jnp.where(later, first, 0) + inside - span * length
    within = row % rows_here
    behind = within >= first
    place = jnp.repeat(span_of, rows_here // CHUNK) * jnp.where(behind, second, first) + within
    place = place + jnp.where(behind, first * (blocks - 1), 0)
    return jnp.concatenate([source // CHUNK, place // CHUNK, (first * blocks // TILE)[None]]).astype(jnp.int32)


def travel(
    tokens, grad_out, first_rows, span_of, w_qkv, w_out, w_up, w_down, vec_gain, vec_bias, mid_gain, mid_bias, head_scale
):
    rows_here, row_width = tokens.shape
    table = chunk_table(first_rows, span_of, rows_here)
    params = Refs(
        w_qkv=w_qkv, w_up=w_up, w_out=w_out.reshape(2, 2, -1, row_width), w_down=w_down.reshape(2, 2, -1, row_width),
        vec_gain=vec_gain.transpose(1, 0, 2), vec_bias=vec_bias.transpose(1, 0, 2), mid_gain=mid_gain, mid_bias=mid_bias,
        head_scale=head_scale,
    )
    first = layer_forward_kernel(0, table, tokens, params, None, jnp.float32, 0)
    first.x_in = tokens
    blocks = Refs(head=first.next_head, unit=first.next_unit)
    second = layer_forward_kernel(1, table, first.y_out, params, blocks, jnp.bfloat16, 1)
    second.x_in, second.head_blocks = first.y_out, blocks.head
    back_second = layer_backward_kernel(1, table, grad_out, params, second, None, 2)
    back_first = layer_backward_kernel(0, table, back_second.dx, params, first, back_second.small, 3)
    kinds = (w_qkv, w_out, w_up, w_down, params.vec_gain, params.vec_bias, mid_gain, mid_bias, head_scale)
    results = assemble(second.y_out, back_first.dx, [back_first, back_second], [array.shape for array in kinds])
    return (*results[:6], results[6].transpose(1, 0, 2), results[7].transpose(1, 0, 2), *results[8:])


def local(*args):
    tokens, w_qkv = args[0], args[4]
    blocks = lax.axis_size("blk")
    heads = w_qkv.shape[2] // (3 * HEAD_DIM)
    if blocks == heads == 4 * LINE and lax.axis_size("batch") == 2 and tokens.shape[0] * blocks % TILE == 0:
        return travel(*args)
    return general(*args)


def solution(mesh):
    placed = (
        P(("batch", "blk"), None),
        P(("batch", "blk"), None),
        P("batch"),
        P(),
        P(None, "blk", None),
        P(None, "blk", None),
        P(None, "blk", None),
        P(None, "blk", None),
        P(),
        P(),
        P(),
        P(),
        P(),
    )
    return jax.shard_map(
        local,
        mesh=mesh,
        in_specs=placed,
        out_specs=(
            P(("batch", "blk"), None),
            P(("batch", "blk"), None),
            P(None, "blk", None),
            P(None, "blk", None),
            P(None, "blk", None),
            P(None, "blk", None),
            P(),
            P(),
            P(),
            P(),
            P(),
        ),
        check_vma=False,
    )
```

```python
import functools

import jax
import jax.numpy as jnp
from jax import lax
from jax.experimental import pallas as pl
from jax.experimental.pallas import tpu as pltpu
from jax.sharding import PartitionSpec as P

HEAD_DIM = 64


EPSILON = 1e-05
NEGATIVE = -1e30


def shifted(x, axis, by):
    devices = lax.axis_size(axis)
    return lax.ppermute(x, axis, [(i, (i + by) % devices) for i in range(devices)])


def norm_rows(values, gains, shifts):
    average = jnp.mean(values, axis=-1, keepdims=True)
    centered = values - average
    spread = jnp.mean(centered * centered, axis=-1, keepdims=True)
    return centered * lax.rsqrt(spread + EPSILON) * gains + shifts


def mid_piece(upper, gains, shifts):
    return norm_rows(jax.nn.gelu(upper, approximate=False), gains, shifts)


def split_heads(matrix):
    return matrix.reshape(matrix.shape[0], -1, HEAD_DIM)


def block_rows(total_rows):
    chosen = total_rows
    while chosen > 1024 and chosen % 2 == 0:
        chosen = chosen // 2
    return chosen


def row_layout(first_rows, rows_here):
    within = jnp.arange(rows_here, dtype=jnp.int32)
    first_len = first_rows[0]
    second = (within >= first_len).astype(jnp.int32)
    return (second, within - second * first_len)


def visible_pairs(query_seq, query_off, query_span, key_seq, key_off, key_span):
    earlier = key_span[None, :] < query_span[:, None]
    same_span = (key_span[None, :] == query_span[:, None]) & (
        key_off[None, :] <= query_off[:, None]
    )
    return (query_seq[:, None] == key_seq[None, :]) & (earlier | same_span)


def merge_block(state_in, query_heads, keys_block, values_block, visible):
    run_peak, run_total, accumulated = state_in
    query_rows = query_heads.shape[0]
    scores = jnp.einsum(
        "qhd,khd->hqk", query_heads, split_heads(keys_block), preferred_element_type=jnp.float32
    ) * HEAD_DIM ** (-0.5)
    masked = jnp.where(visible[None], scores, NEGATIVE)
    new_peak = jnp.maximum(run_peak, jnp.max(masked, axis=-1))
    weights = jnp.where(visible[None], jnp.exp(masked - new_peak[:, :, None]), 0.0)
    factor = jnp.exp(run_peak - new_peak)
    new_total = run_total * factor + jnp.sum(weights, axis=-1)
    update = jnp.einsum(
        "hqk,khd->qhd",
        weights.astype(jnp.bfloat16),
        split_heads(values_block),
        preferred_element_type=jnp.float32,
    )
    rescaled = split_heads(accumulated) * jnp.transpose(factor)[:, :, None]
    return (new_peak, new_total, (rescaled + update).reshape(query_rows, -1))


def grad_block(query_heads, log_total, delta, dout_heads, keys_block, values_block, visible):
    key_heads = split_heads(keys_block)
    value_heads = split_heads(values_block)
    scores = jnp.einsum(
        "qhd,khd->hqk", query_heads, key_heads, preferred_element_type=jnp.float32
    ) * HEAD_DIM ** (-0.5)
    probs = jnp.where(visible[None], jnp.exp(scores - log_total[:, :, None]), 0.0)
    dprobs = jnp.einsum("qhd,khd->hqk", dout_heads, value_heads, preferred_element_type=jnp.float32)
    dscores = (probs * (dprobs - delta[:, :, None])).astype(jnp.bfloat16)
    add_query = jnp.einsum("hqk,khd->qhd", dscores, key_heads, preferred_element_type=jnp.float32)
    add_keys = jnp.einsum("hqk,qhd->khd", dscores, query_heads, preferred_element_type=jnp.float32)
    add_values = jnp.einsum(
        "hqk,qhd->khd", probs.astype(jnp.bfloat16), dout_heads, preferred_element_type=jnp.float32
    )
    return (
        add_query.reshape(query_heads.shape[0], -1),
        add_keys.reshape(key_heads.shape[0], -1),
        add_values.reshape(key_heads.shape[0], -1),
    )


def unchanged(state_in):
    return state_in


def attention_forward(query_low, keys_low, values_low, layout):
    seq_ids, offsets, span_of, my_span, my_index = layout
    rows_here, row_width = query_low.shape
    heads_here = row_width // HEAD_DIM
    query_heads = split_heads(query_low)
    query_span = jnp.full((rows_here,), my_span, jnp.int32)
    initial = (
        jnp.full((heads_here, rows_here), NEGATIVE, jnp.float32),
        jnp.zeros((heads_here, rows_here), jnp.float32),
        jnp.zeros((rows_here, row_width), jnp.float32),
    )
    running = initial
    key_part = lax.all_gather(keys_low, "blk", axis=0, tiled=True)
    value_part = lax.all_gather(values_low, "blk", axis=0, tiled=True)
    part_rows = key_part.shape[0]
    step_rows = block_rows(part_rows)

    def one_step(state_in, step_index):
        block_start = step_index * step_rows
        global_rows = block_start + jnp.arange(step_rows, dtype=jnp.int32)
        key_span = span_of[global_rows // rows_here]
        local_rows = global_rows % rows_here
        visible = visible_pairs(
            seq_ids, offsets, query_span, seq_ids[local_rows], offsets[local_rows], key_span
        )
        keys_block = lax.dynamic_slice_in_dim(key_part, block_start, step_rows, 0)
        values_block = lax.dynamic_slice_in_dim(value_part, block_start, step_rows, 0)

        def one_compute(inner_state):
            return merge_block(inner_state, query_heads, keys_block, values_block, visible)

        return (lax.cond(jnp.any(key_span <= my_span), one_compute, unchanged, state_in), None)

    running, _ = lax.scan(one_step, running, jnp.arange(part_rows // step_rows, dtype=jnp.int32))
    run_peak, run_total, accumulated = running
    mixed_heads = (split_heads(accumulated) / jnp.transpose(run_total)[:, :, None]).reshape(
        rows_here, row_width
    )
    return (mixed_heads, run_peak + jnp.log(run_total))


def cycle_backward(query_low, keys_low, values_low, log_total, delta, dout_low, layout):
    seq_ids, offsets, span_of, my_span, my_index = layout
    rows_here, row_width = query_low.shape
    blocks_total = lax.axis_size("blk")
    query_heads = split_heads(query_low)
    dout_heads = split_heads(dout_low)
    query_span = jnp.full((rows_here,), my_span, jnp.int32)

    def turn(turn_index, carried):
        keys_now, values_now, dkeys, dvalues, dquery = carried
        source = (my_index - turn_index) % blocks_total
        source_span = span_of[source]
        key_span = jnp.full((rows_here,), source_span, jnp.int32)
        visible = visible_pairs(seq_ids, offsets, query_span, seq_ids, offsets, key_span)

        def turn_compute(inner_state):
            add_query, add_keys, add_values = grad_block(
                query_heads, log_total, delta, dout_heads, keys_now, values_now, visible
            )
            return (
                inner_state[0] + add_query,
                inner_state[1] + add_keys,
                inner_state[2] + add_values,
            )

        dquery, dkeys, dvalues = lax.cond(
            source_span <= my_span, turn_compute, unchanged, (dquery, dkeys, dvalues)
        )
        keys_now, values_now = shifted((keys_now, values_now), "blk", 1)
        dkeys, dvalues = (
            shifted(dkeys.astype(jnp.bfloat16), "blk", 1).astype(dkeys.dtype),
            shifted(dvalues.astype(jnp.bfloat16), "blk", 1).astype(dvalues.dtype),
        )
        return (keys_now, values_now, dkeys, dvalues, dquery)

    zeros_rows = jnp.zeros((rows_here, row_width), jnp.float32)
    result = lax.fori_loop(
        0, blocks_total, turn, (keys_low, values_low, zeros_rows, zeros_rows, zeros_rows)
    )
    return (result[4], result[2], result[3])


def layer_forward(inputs, weights, gains, biases, middle_gain, middle_bias, heads_scale, layout):
    weight_qkv, weight_out, weight_up, weight_down = weights
    row_width = inputs.shape[1]
    normed, pre_pull = jax.vjp(norm_rows, inputs, gains[0], biases[0])
    normed_low = normed.astype(jnp.bfloat16)
    projected = jnp.dot(normed_low, weight_qkv, preferred_element_type=jnp.float32)
    query_low = (projected[:, :row_width] + biases[3]).astype(jnp.bfloat16)
    keys_low = projected[:, row_width : 2 * row_width].astype(jnp.bfloat16)
    values_low = (projected[:, 2 * row_width :] + biases[4]).astype(jnp.bfloat16)
    mixed_heads, log_total = attention_forward(query_low, keys_low, values_low, layout)
    scaled_low = (mixed_heads * jnp.repeat(heads_scale, HEAD_DIM)).astype(jnp.bfloat16)
    branch = jnp.dot(scaled_low, weight_out, preferred_element_type=jnp.float32) + biases[5]
    post_normed, post_pull = jax.vjp(norm_rows, branch, gains[1], biases[1])
    middle_res = inputs + post_normed
    ffn_normed, ffn_pull = jax.vjp(norm_rows, middle_res, gains[2], biases[2])
    ffn_low = ffn_normed.astype(jnp.bfloat16)
    upper = jnp.dot(ffn_low, weight_up, preferred_element_type=jnp.float32) + middle_bias[1]
    middle, mid_pull = jax.vjp(mid_piece, upper, middle_gain, middle_bias[0])
    middle_low = middle.astype(jnp.bfloat16)
    results = middle_res + (
        jnp.dot(middle_low, weight_down, preferred_element_type=jnp.float32) + biases[6]
    )
    record = {
        "pre_pull": pre_pull,
        "normed_low": normed_low,
        "query_low": query_low,
        "keys_low": keys_low,
        "values_low": values_low,
        "log_total": log_total,
        "mixed_heads": mixed_heads,
        "scaled_low": scaled_low,
        "post_pull": post_pull,
        "ffn_pull": ffn_pull,
        "ffn_low": ffn_low,
        "mid_pull": mid_pull,
        "middle_low": middle_low,
        "weights": weights,
    }
    return (results, record)


def layer_backward(d_results, record, weights, heads_scale, layout):
    weight_qkv, weight_out, weight_up, weight_down = weights
    rows_here, row_width = d_results.shape
    d_results_low = d_results.astype(jnp.bfloat16)
    grad_down = jnp.einsum(
        "tf,td->fd", record["middle_low"], d_results_low, preferred_element_type=jnp.float32
    )
    grad_down_bias = jnp.sum(d_results_low, axis=0, dtype=jnp.float32)
    d_middle = jnp.einsum(
        "td,fd->tf", d_results_low, weight_down, preferred_element_type=jnp.float32
    )
    d_upper, grad_mid_gain, grad_mid_shift = record["mid_pull"](d_middle)
    d_upper_low = d_upper.astype(jnp.bfloat16)
    grad_up = jnp.einsum(
        "td,tf->df", record["ffn_low"], d_upper_low, preferred_element_type=jnp.float32
    )
    grad_up_bias = jnp.sum(d_upper_low, axis=0, dtype=jnp.float32)
    d_ffn = jnp.einsum("tf,df->td", d_upper_low, weight_up, preferred_element_type=jnp.float32)
    d_res_part, grad_gain_ffn, grad_shift_ffn = record["ffn_pull"](d_ffn)
    d_middle_res = d_results + d_res_part
    d_branch, grad_gain_post, grad_shift_post = record["post_pull"](d_middle_res)
    d_branch_low = d_branch.astype(jnp.bfloat16)
    grad_out_w = jnp.einsum(
        "tc,td->cd", record["scaled_low"], d_branch_low, preferred_element_type=jnp.float32
    )
    grad_out_bias = jnp.sum(d_branch_low, axis=0, dtype=jnp.float32)
    d_scaled = jnp.einsum("td,cd->tc", d_branch_low, weight_out, preferred_element_type=jnp.float32)
    mixed_heads = record["mixed_heads"]
    grad_heads = jnp.sum((d_scaled * mixed_heads).reshape(rows_here, -1, HEAD_DIM), axis=(0, 2))
    d_mixed_low = (d_scaled * jnp.repeat(heads_scale, HEAD_DIM)).astype(jnp.bfloat16)
    delta = jnp.transpose(
        jnp.sum(
            (d_mixed_low.astype(jnp.float32) * mixed_heads).reshape(rows_here, -1, HEAD_DIM), axis=2
        )
    )
    dquery, dkeys, dvalues = cycle_backward(
        record["query_low"],
        record["keys_low"],
        record["values_low"],
        record["log_total"],
        delta,
        d_mixed_low,
        layout,
    )
    scale_factor = HEAD_DIM ** (-0.5)
    d_proj_low = jnp.concatenate(
        [dquery * scale_factor, dkeys * scale_factor, dvalues], axis=1
    ).astype(jnp.bfloat16)
    grad_qkv = jnp.einsum(
        "tc,te->ce", record["normed_low"], d_proj_low, preferred_element_type=jnp.float32
    )
    grad_q_bias = jnp.sum(d_proj_low[:, :row_width], axis=0, dtype=jnp.float32)
    grad_v_bias = jnp.sum(d_proj_low[:, 2 * row_width :], axis=0, dtype=jnp.float32)
    d_normed = jnp.einsum("te,ce->tc", d_proj_low, weight_qkv, preferred_element_type=jnp.float32)
    d_in_part, grad_gain_pre, grad_shift_pre = record["pre_pull"](d_normed)
    d_inputs = d_middle_res + d_in_part
    big_grads = (grad_qkv, grad_out_w, grad_up, grad_down)
    gain_grads = jnp.stack([grad_gain_pre, grad_gain_post, grad_gain_ffn])
    bias_grads = jnp.stack(
        [
            grad_shift_pre,
            grad_shift_post,
            grad_shift_ffn,
            grad_q_bias,
            grad_v_bias,
            grad_out_bias,
            grad_down_bias,
        ]
    )
    small_grads = (
        gain_grads,
        bias_grads,
        grad_mid_gain,
        jnp.stack([grad_mid_shift, grad_up_bias]),
        grad_heads,
    )
    return (d_inputs, big_grads, small_grads)


def general(
    tokens,
    grad_out,
    first_rows,
    span_of,
    w_qkv,
    w_out,
    w_up,
    w_down,
    vec_gain,
    vec_bias,
    mid_gain,
    mid_bias,
    head_scale,
):
    rows_here = tokens.shape[0]
    my_index = lax.axis_index("blk")
    my_span = span_of[my_index]
    seq_ids, offsets = row_layout(first_rows, rows_here)
    layout = (seq_ids, offsets, span_of, my_span, my_index)
    current = tokens.astype(jnp.float32)
    records = []
    for layer_index in range(2):
        weights = (
            lax.all_gather(w_qkv[layer_index], "blk", axis=0, tiled=True),
            lax.all_gather(w_out[layer_index], "blk", axis=0, tiled=True),
            lax.all_gather(w_up[layer_index], "blk", axis=0, tiled=True),
            lax.all_gather(w_down[layer_index], "blk", axis=0, tiled=True),
        )
        current, record = layer_forward(
            current,
            weights,
            vec_gain[layer_index],
            vec_bias[layer_index],
            mid_gain[layer_index],
            mid_bias[layer_index],
            head_scale[layer_index],
            layout,
        )
        records.append(record)
    results_low = current.astype(jnp.bfloat16)
    d_current = grad_out.astype(jnp.float32)
    shard_grads = [None, None]
    small_grads = [None, None]
    for layer_index in (1, 0):
        weights = (
            lax.all_gather(w_qkv[layer_index], "blk", axis=0, tiled=True),
            lax.all_gather(w_out[layer_index], "blk", axis=0, tiled=True),
            lax.all_gather(w_up[layer_index], "blk", axis=0, tiled=True),
            lax.all_gather(w_down[layer_index], "blk", axis=0, tiled=True),
        )
        d_current, big_grads, small_part = layer_backward(
            d_current, records[layer_index], weights, head_scale[layer_index], layout
        )
        shard_grads[layer_index] = (
            lax.psum_scatter(
                big_grads[0].astype(jnp.bfloat16), "blk", scatter_dimension=0, tiled=True
            ).astype(jnp.float32),
            lax.psum_scatter(
                big_grads[1].astype(jnp.bfloat16), "blk", scatter_dimension=0, tiled=True
            ).astype(jnp.float32),
            lax.psum_scatter(
                big_grads[2].astype(jnp.bfloat16), "blk", scatter_dimension=0, tiled=True
            ).astype(jnp.float32),
            lax.psum_scatter(
                big_grads[3].astype(jnp.bfloat16), "blk", scatter_dimension=0, tiled=True
            ).astype(jnp.float32),
        )
        small_grads[layer_index] = small_part
    stacked_small = [
        jnp.stack([small_grads[0][item_index], small_grads[1][item_index]])
        for item_index in range(5)
    ]
    summed_small = (
        lax.psum(stacked_small[0].astype(jnp.bfloat16), "blk").astype(jnp.float32),
        lax.psum(stacked_small[1].astype(jnp.bfloat16), "blk").astype(jnp.float32),
        lax.psum(stacked_small[2].astype(jnp.bfloat16), "blk").astype(jnp.float32),
        lax.psum(stacked_small[3].astype(jnp.bfloat16), "blk").astype(jnp.float32),
        lax.psum(stacked_small[4].astype(jnp.bfloat16), "blk").astype(jnp.float32),
    )
    stacked_big = [
        jnp.stack([shard_grads[0][item_index], shard_grads[1][item_index]])
        for item_index in range(4)
    ]
    totals = (
        lax.psum(stacked_big[0].astype(jnp.bfloat16), "batch").astype(jnp.float32),
        lax.psum(stacked_big[1].astype(jnp.bfloat16), "batch").astype(jnp.float32),
        lax.psum(stacked_big[2].astype(jnp.bfloat16), "batch").astype(jnp.float32),
        lax.psum(stacked_big[3].astype(jnp.bfloat16), "batch").astype(jnp.float32),
        lax.psum(summed_small[0].astype(jnp.bfloat16), "batch").astype(jnp.float32),
        lax.psum(summed_small[1].astype(jnp.bfloat16), "batch").astype(jnp.float32),
        lax.psum(summed_small[2].astype(jnp.bfloat16), "batch").astype(jnp.float32),
        lax.psum(summed_small[3].astype(jnp.bfloat16), "batch").astype(jnp.float32),
        lax.psum(summed_small[4].astype(jnp.bfloat16), "batch").astype(jnp.float32),
    )
    return (
        results_low,
        d_current,
        totals[0],
        totals[1],
        totals[2],
        totals[3],
        totals[4],
        totals[5],
        totals[6],
        totals[7],
        totals[8],
    )


MESH = pl.DeviceIdType.MESH
LINE = 4
HALVES = 2
CHUNK = 32
TILE = 512


def place():
    k = lax.axis_index("blk")
    return k // 4, lax.rem(k // 2, 2), lax.rem(k, 2)


def index_of(z, y, c):
    return (z * 2 + y) * 2 + c


def device(z, y, c):
    return {"blk": index_of(z, y, c)}


def hail(where):
    pl.semaphore_signal(pltpu.get_barrier_semaphore(), inc=1, device_id=where, device_id_type=MESH)


def other_group():
    return {"batch": 1 - lax.axis_index("batch")}


def lasting(microseconds):
    return pl.CostEstimate(flops=0, bytes_accessed=int(microseconds * 3.5e6), transcendentals=0)


def remote(src, dst, send, recv, where):
    return pltpu.make_async_remote_copy(
        src_ref=src, dst_ref=dst, send_sem=send, recv_sem=recv, device_id=where, device_id_type=MESH
    )


class Swap:
    def __init__(self, x_ref, o_ref, ss, rs, own_sem, per=1):
        self.x_ref, self.o_ref, self.ss, self.rs, self.own_sem = x_ref, o_ref, ss, rs, own_sem
        self.k, self.n, self.per = lax.axis_index("blk"), 4 * LINE, per

    @staticmethod
    def scratch():
        dma = pltpu.SemaphoreType.DMA
        return [dma((4 * LINE,)), dma((4 * LINE,)), dma]

    def source(self, to):
        return self.x_ref.at[pl.ds(lax.rem(to, self.x_ref.shape[0] // self.per) * self.per, self.per)]

    def place(self, at):
        return self.o_ref.at[pl.ds(at * self.per, self.per)]

    def send(self, i):
        to = lax.rem(self.k + i, self.n)
        return remote(self.source(to), self.place(self.k), self.ss.at[i], self.rs.at[i], {"blk": to})

    def receive(self, i):
        at = lax.rem(self.k - i + self.n, self.n)
        return remote(self.place(at), self.place(at), self.ss.at[i], self.rs.at[i], {"blk": at})

    def own(self):
        return pltpu.make_async_copy(self.source(self.k), self.place(self.k), self.own_sem)

    def start(self):
        def one(i, carry):
            self.send(i).start()
            return carry

        lax.fori_loop(1, self.n, one, 0)
        self.own().start()

    def finish(self):
        def one(i, carry):
            self.receive(i).wait_recv()
            self.send(i).wait_send()
            return carry

        self.own().wait()
        lax.fori_loop(1, self.n, one, 0)


class Trade:
    def __init__(self, x_ref, o_ref, ss, rs, own_sem):
        self.x_ref, self.o_ref, self.ss, self.rs, self.own_sem = x_ref, o_ref, ss, rs, own_sem
        self.z, self.y, self.c = place()

    @staticmethod
    def scratch():
        dma = pltpu.SemaphoreType.DMA
        return [dma((LINE,)), dma((LINE,)), dma]

    def source(self, to):
        return self.x_ref.at[lax.rem(to, self.x_ref.shape[0])]

    def send(self, s):
        to = lax.rem(self.z + s, LINE)
        return remote(self.source(to), self.o_ref.at[self.z], self.ss.at[s], self.rs.at[s], device(to, self.y, self.c))

    def own(self):
        return pltpu.make_async_copy(self.source(self.z), self.o_ref.at[self.z], self.own_sem)

    def start(self):
        for s in range(1, LINE):
            self.send(s).start()
        self.own().start()

    def finish(self):
        self.own().wait()
        for s in range(1, LINE):
            at = lax.rem(self.z - s + LINE, LINE)
            slot = self.o_ref.at[at]
            remote(slot, slot, self.ss.at[s], self.rs.at[s], device(at, self.y, self.c)).wait_recv()
            self.send(s).wait_send()


class Share:
    def __init__(self, x_ref, o_ref, sr, rr, sl, rl, own_sem):
        self.x_ref, self.o_ref, self.own_sem = x_ref, o_ref, own_sem
        self.sr, self.rr, self.sl, self.rl = sr, rr, sl, rl
        self.z, self.y, self.c = place()

    @staticmethod
    def scratch():
        dma = pltpu.SemaphoreType.DMA
        return [dma((LINE,))] * 4 + [dma]

    def right(self, s):
        slot = self.o_ref.at[self.z - s]
        source = self.x_ref.at[0] if s == 0 else slot
        return remote(source, slot, self.sr.at[s], self.rr.at[s + 1], device(self.z + 1, self.y, self.c))

    def left(self, s):
        slot = self.o_ref.at[self.z + s]
        source = self.x_ref.at[0] if s == 0 else slot
        return remote(source, slot, self.sl.at[s], self.rl.at[s + 1], device(self.z - 1, self.y, self.c))

    def own(self):
        return pltpu.make_async_copy(self.x_ref.at[0], self.o_ref.at[self.z], self.own_sem)

    def start(self):
        self.own().start()

        @pl.when(self.z < LINE - 1)
        def _():
            self.right(0).start()

        @pl.when(self.z > 0)
        def _():
            self.left(0).start()

    def step(self, s):
        @pl.when(self.z >= s)
        def _():
            slot = self.o_ref.at[self.z - s]
            remote(slot, slot, self.sr.at[s], self.rr.at[s], device(self.z, self.y, 1 - self.c)).wait_recv()
            if s < LINE - 1:

                @pl.when(self.z < LINE - 1)
                def _():
                    self.right(s).start()

        @pl.when(self.z + s <= LINE - 1)
        def _():
            slot = self.o_ref.at[self.z + s]
            remote(slot, slot, self.sl.at[s], self.rl.at[s], device(self.z, self.y, 1 - self.c)).wait_recv()
            if s < LINE - 1:

                @pl.when(self.z > 0)
                def _():
                    self.left(s).start()

    def finish(self):
        self.step(LINE - 1)
        self.own().wait()
        for s in range(LINE - 1):

            @pl.when((self.z < LINE - 1) & (self.z >= s))
            def _():
                self.right(s).wait_send()

            @pl.when((self.z > 0) & (self.z + s <= LINE - 1))
            def _():
                self.left(s).wait_send()


class Quad:
    def __init__(self, x_ref, o_ref, send, recv, own_sem):
        self.x_ref, self.o_ref, self.send, self.recv, self.own_sem = x_ref, o_ref, send, recv, own_sem
        self.z, self.y, self.c = place()

    @staticmethod
    def scratch():
        dma = pltpu.SemaphoreType.DMA
        return [dma((4,)), dma((4,)), dma]

    def to(self, d):
        y = 1 - self.y if d & 2 else self.y
        c = 1 - self.c if d & 1 else self.c
        dest = self.o_ref.at[self.y * 2 + self.c]
        return remote(self.x_ref.at[y * 2 + c], dest, self.send.at[d], self.recv.at[d], device(self.z, y, c))

    def own(self):
        q = self.y * 2 + self.c
        return pltpu.make_async_copy(self.x_ref.at[q], self.o_ref.at[q], self.own_sem)

    def start(self):
        for d in range(1, 4):
            self.to(d).start()
        self.own().start()

    def finish(self):
        self.own().wait()
        for d in range(1, 4):
            y = 1 - self.y if d & 2 else self.y
            c = 1 - self.c if d & 1 else self.c
            slot = self.o_ref.at[y * 2 + c]
            remote(slot, slot, self.send.at[d], self.recv.at[d], device(self.z, y, c)).wait_recv()
            self.to(d).wait_send()


class Cross:
    def __init__(self, x_ref, o_ref, ss, rs):
        self.copy = remote(x_ref, o_ref, ss, rs, other_group())

    @staticmethod
    def scratch():
        return [pltpu.SemaphoreType.DMA] * 2

    def start(self):
        self.copy.start()

    def finish(self):
        self.copy.wait()


def start_all(rides):
    for ride in rides:
        ride.start()


def finish_all(rides):
    for ride in rides:
        ride.finish()


def hail_all():
    k, n = lax.axis_index("blk"), 4 * LINE

    def one(i, carry):
        hail({"blk": lax.rem(k + i, n)})
        return carry

    lax.fori_loop(1, n, one, 0)
    x, z, y, c = plane_place()
    for d in range(4):
        hail(plane_device(1 - x, z, 1 - y if d & 2 else y, 1 - c if d & 1 else c))


def hailed_by_all():
    pl.semaphore_wait(pltpu.get_barrier_semaphore(), 4 * LINE - 1 + 4)


class GroupGather:
    def __init__(self, all_ref, sems):
        self.all_ref = all_ref
        self.sr, self.rr, self.sl, self.rl, self.sy, self.ry, self.sc, self.rc, self.se, self.re = sems
        self.z, self.y, self.c = place()
        self.half = all_ref.shape[0] // (4 * LINE * HALVES)

    @staticmethod
    def scratch():
        dma = pltpu.SemaphoreType.DMA
        return [dma((LINE, HALVES))] * 6 + [dma((2 * LINE, HALVES))] * 2 + [dma((2,))] * 2

    def block(self, z, y, h, c=None):
        c = self.c if c is None else c
        return self.all_ref.at[pl.ds((index_of(z, y, c) * HALVES + h) * self.half, self.half)]

    def right(self, s, h):
        block = self.block(self.z - s + 1, self.y, h)
        return remote(block, block, self.sr.at[s, h], self.rr.at[s, h], device(self.z + 1, self.y, self.c))

    def left(self, s, h):
        block = self.block(self.z + s - 1, self.y, h)
        return remote(block, block, self.sl.at[s, h], self.rl.at[s, h], device(self.z - 1, self.y, self.c))

    def across(self, zz, h):
        block = self.block(zz, self.y, h)
        return remote(block, block, self.sy.at[zz, h], self.ry.at[zz, h], device(self.z, 1 - self.y, self.c))

    def detour(self, to_right):
        block = self.block(self.z, 1 - self.y, HALVES - 1)
        where = device(self.z + 1, self.y, self.c) if to_right else device(self.z - 1, self.y, self.c)
        return remote(block, block, self.se.at[to_right], self.re.at[to_right], where)

    def twin(self, zz, yy, h):
        block = self.block(zz, yy, h)
        slot = zz * 2 + yy
        return remote(block, block, self.sc.at[slot, h], self.rc.at[slot, h], device(self.z, self.y, 1 - self.c))

    def arrival(self, block, send, recv):
        remote(block, block, send, recv, device(self.z, self.y, 1 - self.c)).wait_recv()

    def start(self):
        z, y = self.z, self.y
        for h in range(HALVES):

            @pl.when(z < LINE - 1)
            def _():
                self.right(1, h).start()

            @pl.when(z > 0)
            def _():
                self.left(1, h).start()

            self.across(z, h).start()
        for h in range(HALVES):
            self.twin(z, y, h).start()

    def from_across(self, zz, h, distance, to_right=0):
        if distance == 1 and h == HALVES - 1:
            self.arrival(self.block(zz, 1 - self.y, h), self.se.at[to_right], self.re.at[to_right])
        else:
            self.arrival(self.block(zz, 1 - self.y, h), self.sy.at[zz, h], self.ry.at[zz, h])
        if distance == 0 and h == HALVES - 1:

            @pl.when(self.z < LINE - 1)
            def _():
                self.detour(1).start()

            @pl.when(self.z > 0)
            def _():
                self.detour(0).start()

        self.twin(zz, 1 - self.y, h).start()

    def pass_on(self, zz, h, distance):
        if distance > 1 or h < HALVES - 1:
            self.across(zz, h).start()
        self.twin(zz, self.y, h).start()

    def run(self):
        z, y = self.z, self.y
        for s in range(1, LINE):
            for h in range(HALVES):

                @pl.when(z >= s)
                def _():
                    self.arrival(self.block(z - s, y, h), self.sr.at[s, h], self.rr.at[s, h])
                    if s < LINE - 1:

                        @pl.when(z < LINE - 1)
                        def _():
                            self.right(s + 1, h).start()

                    self.pass_on(z - s, h, s)

                @pl.when(z + s <= LINE - 1)
                def _():
                    self.arrival(self.block(z + s, y, h), self.sl.at[s, h], self.rl.at[s, h])
                    if s < LINE - 1:

                        @pl.when(z > 0)
                        def _():
                            self.left(s + 1, h).start()

                    self.pass_on(z + s, h, s)

                if s == 1:
                    self.from_across(z, h, 0)
                else:

                    @pl.when(z >= s - 1)
                    def _():
                        self.from_across(z - s + 1, h, s - 1, 1)

                    @pl.when(z + s - 1 <= LINE - 1)
                    def _():
                        self.from_across(z + s - 1, h, s - 1, 0)

        for h in range(HALVES):

            @pl.when(z >= LINE - 1)
            def _():
                self.from_across(z - LINE + 1, h, LINE - 1)

            @pl.when(z <= 0)
            def _():
                self.from_across(z + LINE - 1, h, LINE - 1)

        for h in range(HALVES):
            for zz in range(LINE):
                for yy in range(2):
                    slot = zz * 2 + yy
                    self.arrival(self.block(zz, yy, h, 1 - self.c), self.sc.at[slot, h], self.rc.at[slot, h])

    def finish(self):
        z = self.z

        @pl.when(z < LINE - 1)
        def _():
            self.detour(1).wait_send()

        @pl.when(z > 0)
        def _():
            self.detour(0).wait_send()

        for h in range(HALVES):
            for zz in range(LINE):
                if h < HALVES - 1:
                    self.across(zz, h).wait_send()
                else:

                    @pl.when((zz != z - 1) & (zz != z + 1))
                    def _():
                        self.across(zz, h).wait_send()

                for yy in range(2):
                    self.twin(zz, yy, h).wait_send()
            for s in range(1, LINE):

                @pl.when((z < LINE - 1) & (z >= s - 1))
                def _():
                    self.right(s, h).wait_send()

                @pl.when((z > 0) & (z + s - 1 <= LINE - 1))
                def _():
                    self.left(s, h).wait_send()


def order_at(z, t):
    table = ((3, 2, 1, 0), (3, 0, 2, 1), (0, 3, 1, 2), (0, 1, 2, 3))
    low = jnp.where(z == 0, table[0][t], table[1][t])
    high = jnp.where(z == 2, table[2][t], table[3][t])
    return jnp.where(z < 2, low, high)


class GroupScatter:
    def __init__(self, part_ref, bufs, sems):
        self.part_ref = part_ref
        self.twins, self.ysend, self.yrecv, self.zsend, self.zrecv, self.esend, self.erecv = bufs
        self.sc, self.rc, self.sy, self.ry, self.sz, self.rzr, self.rzl, self.se, self.re = sems
        self.z, self.y, self.c = place()
        self.half = part_ref.shape[0] // (4 * LINE * HALVES)

    @staticmethod
    def scratch(rows, columns):
        dma = pltpu.SemaphoreType.DMA
        bufs = [pltpu.VMEM((n, rows, columns), jnp.bfloat16) for n in (2 * LINE, LINE, LINE, LINE - 1, LINE + 1)]
        bufs += [pltpu.VMEM((2, rows // HALVES, columns), jnp.bfloat16)] * 2
        return bufs, [dma((2 * LINE, HALVES))] * 2 + [dma((LINE, HALVES))] * 5 + [dma((2,))] * 2

    def part(self, h):
        return pl.ds(h * self.half, self.half)

    def rows(self, t, own_y, c, h):
        y = self.y if own_y else 1 - self.y
        return pl.ds((index_of(order_at(self.z, t), y, c) * HALVES + h) * self.half, self.half)

    def twin(self, t, own_y, h):
        slot = t * 2 + own_y
        source = self.part_ref.at[self.rows(t, own_y, 1 - self.c, h)]
        dest = self.twins.at[slot, self.part(h)]
        return remote(source, dest, self.sc.at[slot, h], self.rc.at[slot, h], device(self.z, self.y, 1 - self.c))

    def across(self, t, h):
        source, dest = self.ysend.at[t, self.part(h)], self.yrecv.at[t, self.part(h)]
        return remote(source, dest, self.sy.at[t, h], self.ry.at[t, h], device(self.z, 1 - self.y, self.c))

    def along(self, d, t, h, to_right):
        sem = self.rzr if to_right else self.rzl
        where = device(self.z + 1, self.y, self.c) if to_right else device(self.z - 1, self.y, self.c)
        slot = d if to_right else self.from_right(d, self.z - 1)
        return remote(self.zsend.at[t, self.part(h)], self.zrecv.at[slot, self.part(h)], self.sz.at[t, h], sem.at[d, h], where)

    @staticmethod
    def from_right(d, z):
        return jnp.where(d == z, LINE, d)

    def arrived(self, d, h, to_right):
        sem = self.rzr if to_right else self.rzl
        slot = self.zrecv.at[d if to_right else self.from_right(d, self.z), self.part(h)]
        remote(slot, slot, self.sz.at[0, h], sem.at[d, h], device(self.z, self.y, 1 - self.c)).wait_recv()

    def wide(self, ref, slot, h):
        return ref[slot, self.part(h)].astype(jnp.float32)

    def chip(self, t, own_y, h):
        return self.part_ref[self.rows(t, own_y, self.c, h)].astype(jnp.float32) + self.wide(self.twins, t * 2 + own_y, h)

    def owner(self, t, own_y, c):
        return index_of(order_at(self.z, t), self.y if own_y else 1 - self.y, c)

    def start(self, t, own_y):
        for h in range(HALVES):
            self.twin(t, own_y, h).start()

    def detour(self, to_right):
        where = device(self.z + 1, self.y, self.c) if to_right else device(self.z - 1, self.y, self.c)
        source, dest = self.esend.at[to_right], self.erecv.at[to_right]
        return remote(source, dest, self.se.at[to_right], self.re.at[to_right], where)

    def detoured(self, t, h):
        d = order_at(self.z, t)
        return (d == self.z + 1, d == self.z - 1) if h == HALVES - 1 and t < LINE - 1 else (False, False)

    def first(self):
        z = self.z
        for t in range(LINE):
            for h in range(HALVES):
                self.twin(t, 0, h).wait_recv()
                if h < HALVES - 1:
                    self.ysend[t, self.part(h)] = self.chip(t, 0, h).astype(jnp.bfloat16)
                    self.across(t, h).start()
                elif t < LINE - 1:
                    right, left = self.detoured(t, h)
                    for to_right, here in ((1, right), (0, left)):

                        @pl.when(here)
                        def _():
                            self.esend[to_right] = self.chip(t, 0, h).astype(jnp.bfloat16)
                            self.detour(to_right).start()

                    @pl.when(jnp.logical_not(right | left))
                    def _():
                        self.ysend[t, self.part(h)] = self.chip(t, 0, h).astype(jnp.bfloat16)
                        self.across(t, h).start()
                else:

                    def added(to_right):
                        slot = self.erecv.at[to_right]
                        where = device(z, self.y, 1 - self.c)
                        remote(slot, slot, self.se.at[to_right], self.re.at[to_right], where).wait_recv()
                        return self.erecv[to_right].astype(jnp.float32)

                    @pl.when(z == 0)
                    def _():
                        self.ysend[t, self.part(h)] = (self.chip(t, 0, h) + added(0)).astype(jnp.bfloat16)

                    @pl.when(z == LINE - 1)
                    def _():
                        self.ysend[t, self.part(h)] = (self.chip(t, 0, h) + added(1)).astype(jnp.bfloat16)

                    @pl.when((z > 0) & (z < LINE - 1))
                    def _():
                        self.ysend[t, self.part(h)] = (self.chip(t, 0, h) + added(0) + added(1)).astype(jnp.bfloat16)

                    self.across(t, h).start()

    def second(self, o_ref):
        z = self.z
        for t in range(LINE):
            d = order_at(z, t)
            for h in range(HALVES):
                self.twin(t, 1, h).wait_recv()
                if h == HALVES - 1 and t < LINE - 1:
                    right, left = self.detoured(t, h)

                    @pl.when(right | left)
                    def _():
                        self.yrecv[t, self.part(h)] = jnp.zeros((self.half, self.yrecv.shape[2]), jnp.bfloat16)

                    @pl.when(jnp.logical_not(right | left))
                    def _():
                        self.across(t, h).wait_recv()
                else:
                    self.across(t, h).wait_recv()

                def summed(t=t, h=h):
                    return self.chip(t, 1, h) + self.wide(self.yrecv, t, h)

                if t < LINE - 1:
                    for to_right in (True, False):

                        @pl.when((d > z) if to_right else (d < z))
                        def _():
                            first = (z == 0) if to_right else (z == LINE - 1)

                            @pl.when(first)
                            def _():
                                self.zsend[t, self.part(h)] = summed().astype(jnp.bfloat16)

                            @pl.when(jnp.logical_not(first))
                            def _():
                                self.arrived(d, h, to_right)
                                self.zsend[t, self.part(h)] = (summed() + self.wide(self.zrecv, d, h)).astype(jnp.bfloat16)

                            self.along(d, t, h, to_right).start()
                else:

                    @pl.when(z > 0)
                    def _():
                        self.arrived(z, h, True)

                    @pl.when(z < LINE - 1)
                    def _():
                        self.arrived(z, h, False)

                    @pl.when(z == 0)
                    def _():
                        o_ref[self.part(h)] = summed() + self.wide(self.zrecv, LINE, h)

                    @pl.when(z == LINE - 1)
                    def _():
                        o_ref[self.part(h)] = summed() + self.wide(self.zrecv, z, h)

                    @pl.when((z > 0) & (z < LINE - 1))
                    def _():
                        o_ref[self.part(h)] = summed() + self.wide(self.zrecv, z, h) + self.wide(self.zrecv, LINE, h)

    def finish(self):
        for to_right, here in ((1, self.z < LINE - 1), (0, self.z > 0)):

            @pl.when(here)
            def _():
                self.detour(to_right).wait_send()

        for h in range(HALVES):
            for t in range(LINE):
                if h == HALVES - 1 and t < LINE - 1:
                    right, left = self.detoured(t, h)

                    @pl.when(jnp.logical_not(right | left))
                    def _():
                        self.across(t, h).wait_send()
                else:
                    self.across(t, h).wait_send()
                self.twin(t, 0, h).wait_send()
                self.twin(t, 1, h).wait_send()
            for t in range(LINE - 1):
                self.along(0, t, h, True).wait_send()


NN = (((1,), (0,)), ((), ()))
NT = (((1,), (1,)), ((), ()))
TN = (((0,), (0,)), ((), ()))


def mul(a, b, dims=NN):
    return lax.dot_general(a, b, dims, preferred_element_type=jnp.float32)


def tile_at(t):
    return pl.ds(pl.multiple_of(t * TILE, TILE), TILE)


def chunk_at(index, rows=CHUNK):
    return pl.ds(pl.multiple_of(index * rows, rows), rows)


def diagonal(p):
    key = lax.broadcasted_iota(jnp.int32, p.shape, 0)
    query = lax.broadcasted_iota(jnp.int32, p.shape, 1)
    return key <= query


PLANE = 8


def plane_place():
    x = lax.axis_index("batch")
    z, y, c = place()
    return x, z, y, c


def plane_device(x, z, y, c):
    return {"batch": x, "blk": index_of(z, y, c)}


def plane_index(x, y, c):
    return (x * 2 + y) * 2 + c


class PlaneGather:
    def __init__(self, all_ref, sems):
        self.all_ref = all_ref
        self.sx, self.rx, self.sy, self.ry, self.sc, self.rc = sems
        self.x, self.z, self.y, self.c = plane_place()
        self.half = all_ref.shape[0] // (2 * PLANE)

    @staticmethod
    def scratch():
        dma = pltpu.SemaphoreType.DMA
        return [dma((3,))] * 4 + [dma((PLANE,))] * 2

    def piece(self, x, y, c, h):
        return self.all_ref.at[pl.ds(plane_index(x, y, c) * 2 * self.half + h * self.half, self.half)]

    def over_x(self, i):
        x, y, c = self.x, self.y, self.c
        piece = self.piece(x, y if i < 2 else 1 - y, c, (0, 1, 1)[i])
        return remote(piece, piece, self.sx.at[i], self.rx.at[i], plane_device(1 - x, self.z, y, c))

    def over_y(self, i):
        x, y, c = self.x, self.y, self.c
        piece = self.piece(x if i < 2 else 1 - x, y, c, (1, 0, 0)[i])
        return remote(piece, piece, self.sy.at[i], self.ry.at[i], plane_device(x, self.z, 1 - y, c))

    def from_x(self, i):
        x, y, c = self.x, self.y, self.c
        piece = self.piece(1 - x, y if i < 2 else 1 - y, c, (0, 1, 1)[i])
        remote(piece, piece, self.sx.at[i], self.rx.at[i], plane_device(1 - x, self.z, y, c)).wait_recv()

    def from_y(self, i):
        x, y, c = self.x, self.y, self.c
        piece = self.piece(x if i < 2 else 1 - x, 1 - y, c, (1, 0, 0)[i])
        remote(piece, piece, self.sy.at[i], self.ry.at[i], plane_device(x, self.z, 1 - y, c)).wait_recv()

    def twin(self, other_x, other_y, h):
        x = 1 - self.x if other_x else self.x
        y = 1 - self.y if other_y else self.y
        slot = (other_x * 2 + other_y) * 2 + h
        piece = self.piece(x, y, self.c, h)
        return remote(piece, piece, self.sc.at[slot], self.rc.at[slot], plane_device(self.x, self.z, self.y, 1 - self.c))

    def from_twin(self, other_x, other_y, h):
        x = 1 - self.x if other_x else self.x
        y = 1 - self.y if other_y else self.y
        slot = (other_x * 2 + other_y) * 2 + h
        piece = self.piece(x, y, 1 - self.c, h)
        where = plane_device(self.x, self.z, self.y, 1 - self.c)
        remote(piece, piece, self.sc.at[slot], self.rc.at[slot], where).wait_recv()

    def start(self):
        self.over_x(0).start()
        self.over_y(0).start()
        self.over_x(1).start()
        self.over_y(1).start()
        self.twin(0, 0, 0).start()
        self.twin(0, 0, 1).start()

    def near(self):
        self.from_x(0)
        self.over_y(2).start()
        self.twin(1, 0, 0).start()
        self.from_y(0)
        self.over_x(2).start()
        self.twin(0, 1, 1).start()
        self.from_y(1)
        self.twin(0, 1, 0).start()
        for other_y in range(2):
            for h in range(2):
                self.from_twin(0, other_y, h)

    def far(self):
        self.from_x(1)
        self.twin(1, 0, 1).start()
        self.from_x(2)
        self.twin(1, 1, 1).start()
        self.from_y(2)
        self.twin(1, 1, 0).start()
        for other_y in range(2):
            for h in range(2):
                self.from_twin(1, other_y, h)

    def finish(self):
        for i in range(3):
            self.over_x(i).wait_send()
            self.over_y(i).wait_send()
        for other_x in range(2):
            for other_y in range(2):
                for h in range(2):
                    self.twin(other_x, other_y, h).wait_send()


class PlaneScatter:
    def __init__(self, part_ref, bufs, sems):
        self.part_ref = part_ref
        self.twins, self.xs, self.xr, self.ys, self.yr = bufs
        self.sx, self.rx, self.sy, self.ry, self.sc, self.rc = sems
        self.x, self.z, self.y, self.c = plane_place()
        self.half = part_ref.shape[0] // (2 * PLANE)

    @staticmethod
    def scratch(rows, columns):
        dma = pltpu.SemaphoreType.DMA
        half = pltpu.VMEM((3, rows // 2, columns), jnp.bfloat16)
        return [pltpu.VMEM((4, rows, columns), jnp.bfloat16)] + [half] * 4, [dma((3,))] * 4 + [dma((4,))] * 2

    def rows(self, which, c, h=None):
        x = self.x if which >= 2 else 1 - self.x
        y = self.y if which % 2 else 1 - self.y
        at = plane_index(x, y, c) * 2 * self.half
        return pl.ds(at, 2 * self.half) if h is None else pl.ds(at + h * self.half, self.half)

    def twin(self, which):
        where = plane_device(self.x, self.z, self.y, 1 - self.c)
        source = self.part_ref.at[self.rows(which, 1 - self.c)]
        return remote(source, self.twins.at[which], self.sc.at[which], self.rc.at[which], where)

    def over_x(self, i):
        return remote(
            self.xs.at[i], self.xr.at[i], self.sx.at[i], self.rx.at[i], plane_device(1 - self.x, self.z, self.y, self.c)
        )

    def over_y(self, i):
        return remote(
            self.ys.at[i], self.yr.at[i], self.sy.at[i], self.ry.at[i], plane_device(self.x, self.z, 1 - self.y, self.c)
        )

    def chip(self, which, h):
        own = self.part_ref[self.rows(which, self.c, h)].astype(jnp.float32)
        return own + self.twins[which, h * self.half : (h + 1) * self.half].astype(jnp.float32)

    def over_first(self):
        self.twin(0).wait_recv()
        self.xs[0] = self.chip(0, 0).astype(jnp.bfloat16)
        self.over_x(0).start()
        self.ys[0] = self.chip(0, 1).astype(jnp.bfloat16)
        self.over_y(0).start()
        self.twin(1).wait_recv()
        self.xs[1] = self.chip(1, 0).astype(jnp.bfloat16)
        self.over_x(1).start()

    def first(self):
        self.twin(2).wait_recv()
        self.ys[1] = self.chip(2, 1).astype(jnp.bfloat16)
        self.over_y(1).start()

    def second(self):
        self.over_x(0).wait_recv()
        self.ys[2] = (self.chip(2, 0) + self.xr[0].astype(jnp.float32)).astype(jnp.bfloat16)
        self.over_y(2).start()
        self.over_y(0).wait_recv()
        self.xs[2] = (self.chip(1, 1) + self.yr[0].astype(jnp.float32)).astype(jnp.bfloat16)
        self.over_x(2).start()

    def finish(self, o_ref):
        half = self.half
        self.twin(3).wait_recv()
        self.over_x(1).wait_recv()
        self.over_y(1).wait_recv()
        self.over_y(2).wait_recv()
        o_ref[0:half] = self.chip(3, 0) + self.xr[1].astype(jnp.float32) + self.yr[2].astype(jnp.float32)
        self.over_x(2).wait_recv()
        o_ref[half : 2 * half] = self.chip(3, 1) + self.yr[1].astype(jnp.float32) + self.xr[2].astype(jnp.float32)
        for which in range(4):
            self.twin(which).wait_send()
        for i in range(3):
            self.over_x(i).wait_send()
            self.over_y(i).wait_send()


class PlanePool:
    def __init__(self, own_ref, got_ref, send, recv):
        self.own_ref, self.got_ref, self.send, self.recv = own_ref, got_ref, send, recv
        self.x, self.z, self.y, self.c = plane_place()

    def others(self):
        for d in range(1, PLANE):
            x = 1 - self.x if d & 4 else self.x
            y = 1 - self.y if d & 2 else self.y
            c = 1 - self.c if d & 1 else self.c
            yield d, x, y, c

    def copies(self):
        slot = self.got_ref.at[plane_index(self.x, self.y, self.c)]
        own = self.own_ref.at[0] if len(self.own_ref.shape) == len(self.got_ref.shape) else self.own_ref
        for d, x, y, c in self.others():
            yield remote(own, slot, self.send.at[d], self.recv.at[d], plane_device(x, self.z, y, c))

    def start(self):
        for copy in self.copies():
            copy.start()
        self.got_ref[plane_index(self.x, self.y, self.c)] = self.own_ref[...].reshape(self.got_ref.shape[1:])

    def finish(self):
        for d, x, y, c in self.others():
            slot = self.got_ref.at[plane_index(x, y, c)]
            remote(slot, slot, self.send.at[d], self.recv.at[d], plane_device(x, self.z, y, c)).wait_recv()
        for copy in self.copies():
            copy.wait_send()


def span_at(th, width):
    return pl.ds(pl.multiple_of(th * width, 128), width)


def units_at(ut):
    return pl.ds(pl.multiple_of(ut * 256, 256), 256)


def mean_and_rate(stat, hidden_all):
    return stat[0:1], lax.rsqrt(stat[1:2] * (1.0 / hidden_all) + EPSILON)


class Refs:
    def __init__(self, **named):
        self.__dict__.update(named)


def launch(call, kernel, inputs, outputs, scratch, collective_id, microseconds, vmem_mib):
    def body(*refs):
        refs = list(refs)
        named = Refs()
        for key in [*inputs, *outputs]:
            setattr(named, key, refs.pop(0))
        for key, what in scratch.items():
            if isinstance(what, list):
                setattr(named, key, [refs.pop(0) for _ in what])
            else:
                setattr(named, key, refs.pop(0))
        kernel(named)

    results = call(
        body,
        out_shape=[shape for shape, _ in outputs.values()],
        in_specs=[pl.BlockSpec(memory_space=space) for _, space in inputs.values()],
        out_specs=[pl.BlockSpec(memory_space=space) for _, space in outputs.values()],
        scratch_shapes=[entry for what in scratch.values() for entry in (what if isinstance(what, list) else [what])],
        cost_estimate=lasting(microseconds),
        compiler_params=pltpu.CompilerParams(
            collective_id=collective_id, has_side_effects=True, vmem_limit_bytes=vmem_mib << 20
        ),
    )(*[array for array, _ in inputs.values()])
    return Refs(**dict(zip(outputs, results)))


def normed(values, gain, shift):
    centred = values - jnp.mean(values, axis=-1, keepdims=True)
    spread = jnp.mean(centred * centred, axis=-1, keepdims=True)
    return centred * lax.rsqrt(spread + EPSILON) * gain + shift


def normed_back(values, gain, grads):
    centred = values - jnp.mean(values, axis=-1, keepdims=True)
    rate = lax.rsqrt(jnp.mean(centred * centred, axis=-1, keepdims=True) + EPSILON)
    unit = centred * rate
    scaled = grads * gain
    back = rate * (
        scaled - jnp.mean(scaled, axis=-1, keepdims=True) - unit * jnp.mean(scaled * unit, axis=-1, keepdims=True)
    )
    return back, jnp.sum(grads * unit, axis=0, keepdims=True), jnp.sum(grads, axis=0, keepdims=True)


def unfold_head(blocks_ref, w_ref):
    for j in range(blocks_ref.shape[0]):
        for part in range(2):
            at = slice(64 * j + 32 * part, 64 * j + 32 * part + 32)
            w_ref[at, 0:128] = blocks_ref[j, :, 128 * part : 128 * part + 128]
            w_ref[at, 128:192] = blocks_ref[j, :, 256 + 64 * part : 320 + 64 * part]


def fold_head(w, head):
    width = w.shape[1] // 3
    at = [slice(part * width + 64 * head, part * width + 64 * head + 64) for part in range(3)]
    halves = [w[0:32], w[32:64]]
    pieces = [half[:, at[part]] for half in halves for part in (0, 2)] + [half[:, at[1]] for half in halves]
    return jnp.concatenate(pieces, axis=1)


def unit_lanes(z, slot):
    return pl.ds(pl.multiple_of(z * PLANE * 128 + slot * 128, 128), 128)


def unit_columns(vectors, slot, column_refs):
    pieces = [vector[:, unit_lanes(z, slot)] for vector in vectors for z in range(LINE)]
    pieces.append(jnp.zeros((16 - len(pieces), 128), jnp.float32))
    turned = jnp.transpose(jnp.concatenate(pieces, axis=0))
    for i, ref in enumerate(column_refs):
        for z in range(LINE):
            ref[128 * z : 128 * z + 128] = turned[:, i * LINE + z : i * LINE + z + 1]


def of_layer(ref, layer):
    return [ref.at[kind, pl.ds(layer, 1)] for kind in range(ref.shape[0])]


def own_head(row, index):
    pair = row[:, pl.ds(pl.multiple_of(index // 2 * 128, 128), 128)]
    return jnp.where(lax.rem(index, 2) == 0, pair[:, 0:64], pair[:, 64:128])


def chunks_of(ref, t):
    per_tile = TILE // CHUNK
    part = ref[pl.ds(t * per_tile, per_tile)]
    return part.reshape(per_tile * part.shape[1], part.shape[2])


def alive(cut, i, j):
    return jnp.where((i >= cut) & (j < cut), NEGATIVE, 0.0)


def natural_rows(slot, zz):
    x, y, c = slot // 4, slot // 2 % 2, slot % 2
    return 64 * index_of(zz, y, c) + 32 * x


def forward_kernel(layer, hidden_all, r):
    first = layer == 0
    x, z, y, c = plane_place()
    index, slot = index_of(z, y, c), plane_index(x, y, c)
    unit_slot = (y * 2 + c) * 2 + x
    rows, columns = r.x_in.shape
    total = r.hb_all.shape[0]
    tiles, chunks, per_tile = total // TILE, total // CHUNK, TILE // CHUNK
    gather = GroupGather(r.hb_all, r.gather_sems)
    hail_all()
    gains, biases = of_layer(r.gains, layer), of_layer(r.biases, layer)
    if first:
        load_qkv = pltpu.make_async_copy(r.w_qkv, r.qkv_in, r.prep_sem.at[0])
        load_qkv.start()
        for l in range(2):
            for q in range(4):
                for zz in range(LINE):
                    source = r.w_up.at[l, :, unit_lanes(zz, q * 2 + x)]
                    dest = r.unit_src.at[l, q, :, pl.ds(zz * 128, 128)]
                    pltpu.make_async_copy(source, dest, r.prep_sem.at[1 + l]).start()
    value = r.x_in[...].astype(jnp.float32)
    r.hb_all[pl.ds(index * rows, rows)] = normed(value, gains[0][...], biases[0][...]).astype(jnp.bfloat16)
    head_ride = Swap(r.head_src.at[0], r.head_blocks, *r.head_sems) if first else None
    down_ride = Share(r.w_down.at[layer, pl.ds(x, 1)], r.down_blocks, *r.down_sems)
    out_ride = Trade(r.w_out.at[layer, pl.ds(x, 1)], r.out_got, *r.out_sems)
    if first:
        quads = [Quad(r.unit_src.at[l], r.unit_quad.at[l], *r.quad_sems[3 * l : 3 * l + 3]) for l in range(2)]
        unit_ride = Share(r.unit_quad.at[pl.ds(0, 1)], r.unit_blocks, *r.unit_sems)
        next_unit_ride = Share(r.unit_quad.at[pl.ds(1, 1)], r.next_unit, *r.next_unit_sems)
        next_head_ride = Swap(r.head_src.at[1], r.next_head, *r.next_head_sems)
    if first:
        load_qkv.wait()
        for head in range(4 * LINE):
            r.head_src[0, head] = fold_head(r.qkv_in[0], head)
    load_head = pltpu.make_async_copy(r.head_blocks, r.head_in, r.load_sem.at[0])
    load_unit = pltpu.make_async_copy(r.unit_blocks, r.unit_in, r.load_sem.at[1])
    load_down = pltpu.make_async_copy(r.down_blocks, r.down_w, r.load_sem.at[2])
    hailed_by_all()
    if first:
        head_ride.start()
    gather.start()
    out_ride.start()
    mids = [r.mid_gain_all.at[pl.ds(layer, 1)], r.mid_bias_all.at[layer, pl.ds(0, 1)], r.mid_bias_all.at[layer, pl.ds(1, 1)]]
    unit_columns(mids, unit_slot, (r.mid_gain, r.mid_shift, r.mid_bias))
    head_bias = [own_head(biases[row], index) for row in (3, 4)] + [jnp.zeros((1, 64), jnp.float32)]
    head_bias = jnp.concatenate(head_bias, axis=1)
    if not first:
        load_head.start()
        r.dy_all[pl.ds(slot * rows, rows)] = r.dy[...]
        load_unit.start()
    if first:
        for l in range(2):
            pltpu.make_async_copy(r.unit_src.at[l], r.unit_src.at[l], r.prep_sem.at[1 + l]).wait()
        quads[0].start()
    gather.run()
    if first:
        quads[0].finish()
        unit_ride.start()
    out_ride.finish()
    out_rows = r.out_all.shape[0] // PLANE
    for zz in range(LINE):
        r.out_all[pl.ds(slot * out_rows + zz * 32, 32)] = r.out_got[zz]
    out_gather = PlaneGather(r.out_all, r.out_gather_sems)
    out_gather.start()
    dy_gather = None if first else PlaneGather(r.dy_all, r.dy_gather_sems)
    if first:
        head_ride.finish()
        load_head.start()
    else:
        dy_gather.start()
    load_head.wait()
    unfold_head(r.head_in, r.head_w)

    def project(t, carry):
        rows_t = (mul(r.hb_all[tile_at(t)], r.head_w[...]) + head_bias).astype(jnp.bfloat16)
        r.flat[pl.ds(t * per_tile, per_tile)] = rows_t.reshape(per_tile, CHUNK, 192)
        return carry

    lax.fori_loop(0, tiles, project, 0)
    def arrange(p, carry):
        r.qvk[p] = r.flat[r.table[p]]
        return carry

    lax.fori_loop(0, chunks, arrange, 0)

    def prepare(t, carry):
        rows_t = chunks_of(r.qvk, t)
        r.queries[tile_at(t)] = rows_t[:, 0:64] * 0.125
        r.keys[tile_at(t)] = rows_t[:, 128:192]
        turned = jnp.transpose(rows_t[:, 0:128].astype(jnp.float32))
        r.values_t[:, tile_at(t)] = turned[64:128].astype(jnp.bfloat16)
        return carry

    lax.fori_loop(0, tiles, prepare, 0)
    cut = r.table[2 * chunks]
    for i in range(tiles):
        at = slice(i * TILE, (i + 1) * TILE)
        query = r.queries[at]

        def block(j, state, masked):
            peak, part, mixed = state
            scores = mul(r.keys[tile_at(j)], query, NT)
            bias = 0.0 if masked else alive(cut, i, j)
            if masked:
                keep = diagonal(scores)
                scores = jnp.where(keep, scores, NEGATIVE)
            new_peak = jnp.maximum(peak, jnp.max(scores, axis=0, keepdims=True) + bias)
            weights = jnp.exp(scores - (new_peak - bias))
            if masked:
                weights = jnp.where(keep, weights, 0.0)
            factor = jnp.exp(peak - new_peak)
            part = part * factor + jnp.sum(weights, axis=0, keepdims=True)
            mixed = mixed * factor + mul(r.values_t[:, tile_at(j)], weights.astype(jnp.bfloat16))
            return (new_peak, part, mixed)

        state = (
            jnp.full((1, TILE), NEGATIVE, jnp.float32),
            jnp.zeros((1, TILE), jnp.float32),
            jnp.zeros((64, TILE), jnp.float32),
        )
        state = block(i, state, True)
        if i > 0:
            state = lax.fori_loop(0, i, functools.partial(block, masked=False), state)
        peak, part, mixed = state
        mixed = mixed / part
        r.lse[:, at] = peak + jnp.log(part)
        r.head_out[:, at] = mixed
        pairs = (jnp.transpose(mixed) * r.scales[layer, index]).reshape(per_tile, 2, CHUNK // 2, 64)
        pairs = jnp.concatenate([pairs[:, 0], pairs[:, 1]], axis=-1).astype(jnp.bfloat16)
        r.pairs[i * per_tile : (i + 1) * per_tile] = pairs
        if i == 2 and first:
            unit_ride.step(1)
        if i == 3:
            out_gather.near()
    if first:
        unit_ride.step(2)
    else:
        dy_gather.near()
    per_block = rows // CHUNK

    def pack(p, carry):
        r.packed[p] = r.pairs[r.table[chunks + p]]
        return carry

    lax.fori_loop(0, chunks, pack, 0)
    mix = Swap(r.packed, r.mixed, *r.mix_sems, per=per_block)
    mix.start()
    out_gather.far()
    if not first:
        dy_gather.far()
    for s in range(PLANE):
        for zz in range(LINE):
            at = natural_rows(s, zz)
            r.out_w[at : at + 32] = r.out_all[s * out_rows + zz * 32 : s * out_rows + zz * 32 + 32]
    out_gather.finish()

    def turn_units():
        for j in range(2 * LINE):
            pair = r.unit_in[j // 2, j % 2 * 2 : j % 2 * 2 + 2].reshape(128, r.unit_in.shape[3])
            r.unit_t[:, 128 * j : 128 * j + 128] = jnp.transpose(pair)

    if first:
        for head in range(4 * LINE):
            r.head_src[1, head] = fold_head(r.qkv_in[1], head)
    else:
        load_unit.wait()
        turn_units()
    saves = [
        pltpu.make_async_copy(source, dest, r.save_sem.at[i])
        for i, (source, dest) in enumerate(
            (
                (r.hb_all, r.hb_all_out), (r.qvk, r.qvk_out), (r.out_w, r.out_w_out), (r.rows_all, r.rows_all_out),
                (r.unit_t, r.unit_t_out), (r.act, r.act_out), (r.slope, r.slope_out), (r.mid, r.mid_out),
            )
        )
    ]
    start_all(saves[:3])
    mix.finish()
    down_ride.start()
    for g in range(columns // 128):
        left, right = (
            r.mixed[h * per_block : (h + 1) * per_block].reshape(rows // 2, 128) for h in (2 * g, 2 * g + 1)
        )
        low = jnp.concatenate([left[:, 0:64], right[:, 0:64]], axis=1)
        high = jnp.concatenate([left[:, 64:128], right[:, 64:128]], axis=1)
        for p in range(per_block):
            at = slice(p * (CHUNK // 2), (p + 1) * (CHUNK // 2))
            r.ab[p * CHUNK : p * CHUNK + CHUNK // 2, 128 * g : 128 * g + 128] = low[at]
            r.ab[p * CHUNK + CHUNK // 2 : (p + 1) * CHUNK, 128 * g : 128 * g + 128] = high[at]
    branch = mul(r.ab[...], r.out_w[...]) + biases[5][...]
    r.branch[...] = branch
    middle = value + normed(branch, gains[1][...], biases[1][...])
    r.middle[...] = middle

    own = pl.ds(slot * rows, rows)
    r.rows_all[own] = normed(middle, gains[2][...], biases[2][...]).astype(jnp.bfloat16)
    plane_gather = PlaneGather(r.rows_all, r.plane_gather_sems)
    plane_scatter = PlaneScatter(r.part, r.plane_bufs, r.plane_sems)
    pool = PlanePool(r.own_stat, r.got_stat, *r.pool_sems)
    plane_gather.start()
    hidden = r.act.shape[0]
    width = r.act.shape[1] // 2
    if first:
        unit_ride.finish()
        load_unit.start()
        quads[1].start()
    down_ride.step(1)
    if first:
        load_unit.wait()
        turn_units()

    def climb(th):
        at = span_at(th, width)

        def units(ut, carry):
            here = units_at(ut)
            upper = mul(r.unit_t[here], r.rows_all[pl.ds(th * width, width)], NT) + r.mid_bias[here]
            chance = 0.5 * (1.0 + lax.erf(upper * (0.5**0.5)))
            r.act[here, at] = upper * chance
            slope = chance + upper * (jnp.exp(-0.5 * upper * upper) * 0.3989422804014327)
            r.slope[here, at] = slope.astype(jnp.bfloat16)
            return carry

        lax.fori_loop(0, hidden // 256, units, 0)
        values = r.act[:, at]
        mean = jnp.mean(values, axis=0, keepdims=True)
        apart = values - mean
        r.own_stat[0:1, at] = mean
        r.own_stat[1:2, at] = jnp.sum(apart * apart, axis=0, keepdims=True)

    plane_gather.near()
    down_ride.step(2)
    climb(x)
    plane_gather.far()
    climb(1 - x)
    pool.start()
    down_ride.finish()
    load_down.start()
    if first:
        quads[1].finish()
        next_unit_ride.start()
        next_head_ride.start()
    start_all(saves[3:7])
    pool.finish()
    load_down.wait()
    means = [r.got_stat[i, 0:1] for i in range(PLANE)]
    mean = functools.reduce(jnp.add, means) * (1.0 / PLANE)
    apart = functools.reduce(jnp.add, [(m - mean) * (m - mean) for m in means])
    r.stat[0:1] = mean
    r.stat[1:2] = functools.reduce(jnp.add, [r.got_stat[i, 1:2] for i in range(PLANE)]) + apart * float(hidden)

    def descend(th):
        at = span_at(th, width)
        mean, rate = mean_and_rate(r.stat[:, at], hidden_all)

        def units(ut, carry):
            here = units_at(ut)
            low = (r.act[here, at] - mean) * rate * r.mid_gain[here] + r.mid_shift[here]
            r.mid[here, at] = low.astype(jnp.bfloat16)
            return carry

        lax.fori_loop(0, hidden // 256, units, 0)
        down_w = r.down_w[...].reshape(hidden, columns)
        r.part[pl.ds(th * width, width)] = mul(r.mid[:, at], down_w, TN).astype(jnp.bfloat16)

    descend(1 - x)
    plane_scatter.twin(0).start()
    plane_scatter.twin(1).start()
    plane_scatter.over_first()
    descend(x)
    plane_scatter.twin(2).start()
    plane_scatter.twin(3).start()
    if not first:
        dy_gather.finish()
        saves.append(pltpu.make_async_copy(r.dy_all, r.dy_all_out, r.save_sem.at[8]))
    start_all(saves[7:])
    plane_scatter.first()
    if first:
        next_unit_ride.step(1)
    plane_scatter.second()
    if first:
        next_unit_ride.step(2)
    plane_scatter.finish(r.result)
    r.y_out[...] = (r.middle[...] + (r.result[...] + biases[6][...])).astype(r.y_out.dtype)
    gather.finish()
    plane_gather.finish()
    for save in saves:
        save.wait()
    if first:
        next_unit_ride.finish()
        next_head_ride.finish()


def layer_forward_kernel(layer, table, x_in, params, blocks, dy, y_type, collective_id):
    rows, columns = x_in.shape
    hidden_all = params.mid_gain.shape[1]
    total, plane_rows, hidden = rows * 4 * LINE, rows * PLANE, hidden_all // PLANE
    vmem, anywhere, smem = pltpu.VMEM, pl.ANY, pltpu.SMEM
    dma = pltpu.SemaphoreType.DMA
    low = lambda *shape: pltpu.VMEM(shape, jnp.bfloat16)
    full = lambda *shape: pltpu.VMEM(shape, jnp.float32)
    low_out = lambda *shape: jax.ShapeDtypeStruct(shape, jnp.bfloat16)
    full_out = lambda *shape: jax.ShapeDtypeStruct(shape, jnp.float32)
    swap_sems, trade_sems, share_sems = Swap.scratch(), Trade.scratch(), Share.scratch()
    inputs = dict(
        table=(table, smem), scales=(params.head_scale, smem), x_in=(x_in, vmem), gains=(params.vec_gain, vmem),
        biases=(params.vec_bias, vmem), mid_gain_all=(params.mid_gain, vmem), mid_bias_all=(params.mid_bias, vmem),
        w_down=(params.w_down, anywhere), w_out=(params.w_out, anywhere),
    )
    head_shape, unit_shape = (4 * LINE, 32, 384), (LINE, 4, columns // (4 * LINE), hidden)
    outputs = dict(
        y_out=(jax.ShapeDtypeStruct((rows, columns), y_type), vmem), branch=(full_out(rows, columns), vmem),
        middle=(full_out(rows, columns), vmem), ab=(low_out(rows, columns), vmem),
        lse=(full_out(1, total), vmem), head_out=(full_out(64, total), vmem),
        stat=(full_out(2, plane_rows), vmem), hb_all_out=(low_out(total, columns), anywhere),
        qvk_out=(low_out(total // CHUNK, CHUNK, 192), anywhere), out_w_out=(low_out(columns, columns), anywhere),
        rows_all_out=(low_out(plane_rows, columns), anywhere), unit_t_out=(low_out(hidden, columns), anywhere),
        act_out=(full_out(hidden, plane_rows), anywhere), slope_out=(low_out(hidden, plane_rows), anywhere),
        mid_out=(low_out(hidden, plane_rows), anywhere), down_blocks=(low_out(LINE, hidden // LINE, columns), anywhere),
    )
    first = layer == 0
    if first:
        inputs.update(w_qkv=(params.w_qkv, anywhere), w_up=(params.w_up, anywhere))
        head_got, unit_got = (low_out(*head_shape), anywhere), (low_out(*unit_shape), anywhere)
        outputs.update(head_blocks=head_got, unit_blocks=unit_got, next_head=head_got, next_unit=unit_got)
    else:
        inputs.update(head_blocks=(blocks.head, anywhere), unit_blocks=(blocks.unit, anywhere), dy=(dy, vmem))
        outputs.update(dy_all_out=(low_out(plane_rows, columns), anywhere))
    plane_bufs, plane_sems = PlaneScatter.scratch(rows, columns)
    scratch = dict(
        hb_all=low(total, columns), flat=low(total // CHUNK, CHUNK, 192),
        qvk=low(total // CHUNK, CHUNK, 192), queries=low(total, 64), keys=low(total, 64),
        values_t=low(64, total), pairs=low(total // CHUNK, CHUNK // 2, 128),
        packed=low(total // CHUNK, CHUNK // 2, 128), mixed=low(total // CHUNK, CHUNK // 2, 128), head_in=low(4 * LINE, 32, 384), head_w=low(columns, 192),
        unit_in=low(*unit_shape), unit_t=low(hidden, columns),
        down_w=low(LINE, hidden // LINE, columns), out_got=low(LINE, 32, columns),
        out_all=low(columns, columns), out_w=low(columns, columns), rows_all=low(plane_rows, columns),
        act=full(hidden, plane_rows), slope=low(hidden, plane_rows), mid=low(hidden, plane_rows),
        part=low(plane_rows, columns), own_stat=full(2, plane_rows), got_stat=full(PLANE, 2, plane_rows),
        result=full(rows, columns), plane_bufs=plane_bufs, plane_sems=plane_sems,
        gather_sems=GroupGather.scratch(), plane_gather_sems=PlaneGather.scratch(),
        out_gather_sems=PlaneGather.scratch(), pool_sems=([dma((PLANE,)), dma((PLANE,))]),
        head_sems=swap_sems, unit_sems=share_sems, next_head_sems=swap_sems, next_unit_sems=share_sems,
        mix_sems=swap_sems, down_sems=share_sems, out_sems=trade_sems, load_sem=dma((3,)),
        save_sem=dma((9,)),
    )
    scratch.update(mid_gain=full(hidden, 1), mid_shift=full(hidden, 1), mid_bias=full(hidden, 1))
    if first:
        scratch.update(qkv_in=low(*params.w_qkv.shape), head_src=low(2, *head_shape), prep_sem=dma((3,)))
        scratch.update(unit_src=low(2, *unit_shape[1:]), unit_quad=low(2, *unit_shape[1:]), quad_sems=Quad.scratch() * 2)
    else:
        scratch.update(dy_all=low(plane_rows, columns), dy_gather_sems=PlaneGather.scratch())
    kernel = functools.partial(forward_kernel, layer, hidden_all)
    call = lambda body, **how: pl.pallas_call(body, name="layer_forward", **how)
    return launch(call, kernel, inputs, outputs, scratch, collective_id, 95, 56)


class AllSum:
    def __init__(self, own_ref, sent, got, send, recv):
        self.own_ref, self.sent, self.got, self.send, self.recv = own_ref, sent, got, send, recv
        self.z, self.y, self.c = place()

    @staticmethod
    def scratch(shape, kind):
        dma = pltpu.SemaphoreType.DMA
        return [pltpu.VMEM((3, *shape), kind), pltpu.VMEM((LINE + 2, *shape), kind), dma((LINE + 2,)), dma((LINE + 2,))]

    def copy(self, i):
        z, y, c = self.z, self.y, self.c
        where = (other_group(), device(z, y, 1 - c), device(z, 1 - y, c))[i] if i < 3 else None
        if i >= 3:
            where = device(lax.rem(z + i - 2, LINE), y, c)
        source = self.own_ref if i == 0 else self.sent.at[min(i, 3) - 1]
        return remote(source, self.got.at[i], self.send.at[i], self.recv.at[i], where)

    def start(self):
        self.copy(0).start()

    def step(self, i):
        self.copy(i - 1).wait_recv()
        own = self.own_ref[...] if i == 1 else self.sent[i - 2]
        self.sent[i - 1] = (own.astype(jnp.float32) + self.got[i - 1].astype(jnp.float32)).astype(self.sent.dtype)
        for k in range(i, i + 1 if i < 3 else LINE + 2):
            self.copy(k).start()

    def finish(self, o_ref):
        for i in range(3, LINE + 2):
            self.copy(i).wait_recv()
        total = None
        for zz in range(LINE):
            term = self.sent[2].astype(jnp.float32)
            for s in range(1, LINE):
                term = jnp.where(lax.rem(self.z - s + LINE, LINE) == zz, self.got[2 + s].astype(jnp.float32), term)
            total = term if total is None else total + term
        o_ref[...] = total
        for i in range(LINE + 2):
            self.copy(i).wait_send()


class QuickSum:
    def __init__(self, own_ref, plane_got, line_got, sems):
        self.own_ref, self.line_got = own_ref, line_got
        self.pool = PlanePool(own_ref, plane_got, *sems[0:2])
        self.trade = Trade(own_ref, line_got, *sems[2:5])
        self.plane_got = plane_got

    @staticmethod
    def scratch(shape):
        dma = pltpu.SemaphoreType.DMA
        got = [pltpu.VMEM((n, *shape), jnp.float32) for n in (PLANE, LINE)]
        return got, [dma((PLANE,))] * 2 + Trade.scratch()

    def run(self, o_ref):
        self.pool.start()
        self.pool.finish()
        self.own_ref[0] = functools.reduce(jnp.add, [self.plane_got[i] for i in range(PLANE)])
        self.trade.start()
        self.trade.finish()
        o_ref[...] = functools.reduce(jnp.add, [self.line_got[zz] for zz in range(LINE)])


OUT_BIAS, DOWN_BIAS, QUERY_BIAS, VALUE_BIAS, SCALES, MID, SMALL = 6, 7, 8, 9, 10, 12, 24


def spread_head(piece, index, width):
    nothing = jnp.zeros_like(piece)
    even = lax.rem(index, 2) == 0
    pair = jnp.concatenate([jnp.where(even, piece, nothing), jnp.where(even, nothing, piece)], axis=1)
    lanes = lax.broadcasted_iota(jnp.int32, (1, width), 1) // 128
    return jnp.where(lanes == index // 2, jnp.concatenate([pair] * (width // 128), axis=1), 0.0)


def backward_kernel(layer, hidden_all, r):
    first = layer == 1
    x, z, y, c = plane_place()
    index, unit_slot = index_of(z, y, c), (y * 2 + c) * 2 + x
    rows, columns = r.dy.shape
    total = r.hb_all_in.shape[0]
    tiles, chunks, per_tile = total // TILE, total // CHUNK, TILE // CHUNK
    hidden, plane_rows = r.act.shape
    width = plane_rows // 2
    dy_all, x_all = r.wide.at[pl.ds(0, plane_rows)], r.wide.at[pl.ds(plane_rows, plane_rows)]
    plane_gather = PlaneGather(dy_all, r.plane_gather_sems)
    plane_scatter = PlaneScatter(r.part, r.plane_bufs, r.plane_sems)
    out_part = r.part.at[pl.ds(0, LINE * PLANE * 32)]
    out_scatter = PlaneScatter(out_part, r.out_bufs, r.out_sems)
    scatter = GroupScatter(r.wide, r.group_bufs, r.group_sems)
    pool = PlanePool(r.own_sums, r.got_sums, *r.pool_sems)
    unit_ride = Swap(r.gup, r.unit_got, *r.unit_sems)
    out_ride = Trade(r.out_own, r.out_got, *r.out_ride_sems)
    head_ride = Swap(r.head_fold, r.head_got, *r.head_sems)
    head_cross = Cross(r.head_own, r.head_other, *r.head_cross_sems)
    down_ride = Trade(r.gdown, r.gdown_got, *r.gdown_sems)
    near_rides = [
        Cross(r.unit_near, r.unit_far, *r.unit_cross_sems), Cross(r.down_near, r.down_far, *r.down_cross_sems),
        Cross(r.out_near, r.out_far, *r.out_cross_sems),
    ]
    if not first:
        bulk = AllSum(r.bulk, *r.bulk_sum)
        rest = QuickSum(r.rest, *r.rest_got, r.rest_sems)
    hail_all()
    gains = of_layer(r.gains, layer)
    r.small[...] = jnp.zeros_like(r.small)
    dy = r.dy[...].astype(jnp.float32)
    dy_low = dy.astype(jnp.bfloat16)
    r.small[DOWN_BIAS : DOWN_BIAS + 1] = jnp.sum(dy_low.astype(jnp.float32), axis=0, keepdims=True)
    if not first:
        dy_all[pl.ds(plane_index(x, y, c) * rows, rows)] = dy_low
    loads = [
        pltpu.make_async_copy(source, dest, r.load_sem.at[i])
        for i, (source, dest) in enumerate(
            (
                (r.down_blocks, r.down_w), (r.act_in, r.act), (r.slope_in, r.slope), (r.unit_t_in, r.unit_t),
                (r.mid_in, r.mid), (r.rows_all_in, x_all), (r.out_w_in, r.out_w), (r.qvk_in, r.qvk),
            )
        )
    ]
    load_dy = pltpu.make_async_copy(r.dy_all_in, dy_all, r.load_sem.at[8]) if first else None
    if first:
        load_dy.start()
    for load in loads[:6]:
        load.start()
    hailed_by_all()
    if not first:
        plane_gather.start()
    for load in loads[6:]:
        load.start()

    def tile_load(t):
        return pltpu.make_async_copy(r.hb_all_in.at[pl.ds(t * TILE, TILE)], r.hb_tiles.at[t % 2], r.tile_sem.at[t % 2])

    tile_load(0).start()
    tile_load(1).start()
    unit_columns([r.mid_gain_all.at[pl.ds(layer, 1)]], unit_slot, [r.mid_gain])
    r.gg[...] = jnp.zeros_like(r.gg)
    r.gs[...] = jnp.zeros_like(r.gs)
    r.gb[...] = jnp.zeros_like(r.gb)
    r.own_sums[...] = jnp.zeros_like(r.own_sums)

    def climb(th):
        at = span_at(th, width)
        mean, rate = mean_and_rate(r.stat[:, at], hidden_all)

        def units(ut, carry):
            here = units_at(ut)
            down_w = r.down_w[pl.ds(ut * 2, 2)].reshape(256, columns)
            dm = mul(down_w, dy_all[pl.ds(th * width, width)], NT)
            r.dmid[here, at] = dm
            vh = (r.act[here, at] - mean) * rate
            r.act[here, at] = vh
            r.gg[here] += jnp.sum(dm * vh, axis=1, keepdims=True)
            r.gs[here] += jnp.sum(dm, axis=1, keepdims=True)
            scaled = dm * r.mid_gain[here]
            r.own_sums[0:1, at] += jnp.sum(scaled, axis=0, keepdims=True)
            r.own_sums[1:2, at] += jnp.sum(scaled * vh, axis=0, keepdims=True)
            return carry

        lax.fori_loop(0, hidden // 256, units, 0)

    if first:
        load_dy.wait()
    else:
        plane_gather.near()
    loads[0].wait()
    loads[1].wait()
    climb(x)
    if not first:
        plane_gather.far()
    climb(1 - x)
    pool.start()
    loads[4].wait()
    for ut in range(hidden // 256):
        grad = mul(r.mid[ut * 256 : (ut + 1) * 256], dy_all[...]).astype(jnp.bfloat16)
        r.gdown[2 * ut : 2 * ut + 2] = grad.reshape(2, 128, columns)
    down_ride.start()
    pool.finish()
    r.sums[...] = functools.reduce(jnp.add, [r.got_sums[i] for i in range(PLANE)]) * (1.0 / hidden_all)
    loads[2].wait()
    loads[3].wait()

    def descend(th):
        at = span_at(th, width)
        _, rate = mean_and_rate(r.stat[:, at], hidden_all)
        sum0, sum1 = r.sums[0:1, at], r.sums[1:2, at]

        def units(ut, carry):
            here = units_at(ut)
            dact = rate * (r.dmid[here, at] * r.mid_gain[here] - sum0 - r.act[here, at] * sum1)
            du = (dact * r.slope[here, at].astype(jnp.float32)).astype(jnp.bfloat16)
            r.du[here, at] = du
            r.gb[here] += jnp.sum(du.astype(jnp.float32), axis=1, keepdims=True)
            return carry

        lax.fori_loop(0, hidden // 256, units, 0)
        r.part[pl.ds(th * width, width)] = mul(r.du[:, at], r.unit_t[...], TN).astype(jnp.bfloat16)

    descend(1 - x)
    plane_scatter.twin(0).start()
    plane_scatter.twin(1).start()
    plane_scatter.over_first()
    descend(x)
    plane_scatter.twin(2).start()
    plane_scatter.twin(3).start()
    plane_scatter.first()
    loads[5].wait()
    plane_scatter.second()
    for ut in range(hidden // 256):
        grad = jnp.transpose(mul(r.du[ut * 256 : (ut + 1) * 256], x_all[...])).astype(jnp.bfloat16)
        r.gup[:, :, ut * 256 : (ut + 1) * 256] = grad.reshape(r.gup.shape[0], -1, 256)
    plane_scatter.finish(r.dffn)
    if not first:
        plane_gather.finish()

    back, r.small[2:3], r.small[5:6] = normed_back(r.middle[...], gains[2][...], r.dffn[...])
    r.dmiddle[...] = dy + back
    back, r.small[1:2], r.small[4:5] = normed_back(r.branch[...], gains[1][...], r.dmiddle[...])
    dz = back.astype(jnp.bfloat16)
    r.small[OUT_BIAS : OUT_BIAS + 1] = jnp.sum(dz.astype(jnp.float32), axis=0, keepdims=True)
    loads[6].wait()
    da = mul(dz, r.out_w[...], NT).astype(jnp.bfloat16)
    per_block = rows // CHUNK
    halves = da.reshape(per_block, 2, CHUNK // 2, columns)
    low, high = halves[:, 0].reshape(rows // 2, columns), halves[:, 1].reshape(rows // 2, columns)
    for h in range(columns // 64):
        at = slice(64 * h, 64 * h + 64)
        pairs = jnp.concatenate([low[:, at], high[:, at]], axis=1)
        r.packed[h * per_block : (h + 1) * per_block] = pairs.reshape(per_block, CHUNK // 2, 128)
    mix = Swap(r.packed, r.mixed, *r.mix_sems, per=per_block)
    mix.start()
    out_rows = LINE * 32
    for zz in range(LINE):
        grad = mul(r.ab[:, 256 * zz : 256 * zz + 256], dz, TN).astype(jnp.bfloat16)
        for s in range(PLANE):
            at = natural_rows(s, 0)
            out_part[s * out_rows + zz * 32 : s * out_rows + zz * 32 + 32] = grad[at : at + 32]
    for which in range(4):
        out_scatter.twin(which).start()
    turned = [ref[128 * zz : 128 * zz + 128] for ref in (r.gg, r.gs, r.gb) for zz in range(LINE)]
    turned = jnp.transpose(jnp.concatenate(turned + [jnp.zeros((128, 4), jnp.float32)], axis=1))
    for i in range(3 * LINE):
        r.small[MID + i : MID + i + 1, unit_lanes(0, unit_slot)] = turned[i : i + 1]
    if not first:
        r.bulk[0:SMALL] = r.small_in[...].astype(jnp.bfloat16)
        r.bulk[SMALL : 2 * SMALL] = r.small[...].astype(jnp.bfloat16)
        bulk.start()
    loads[7].wait()
    load_head = pltpu.make_async_copy(r.head_blocks, r.head_fold, r.load_sem.at[6])
    load_head.start()
    scale = r.scales[layer, index]

    def prepare(t, carry):
        at = tile_at(t)
        rows_t = chunks_of(r.qvk, t)
        r.query[at] = rows_t[:, 0:64] * 0.125
        r.values[at] = rows_t[:, 64:128]
        key = rows_t[:, 128:192]
        r.keys[at] = key
        r.keys_t[:, at] = jnp.transpose(key.astype(jnp.float32)).astype(jnp.bfloat16)
        r.dkeys[at] = jnp.zeros((TILE, 64), jnp.float32)
        r.dvalues[at] = jnp.zeros((TILE, 64), jnp.float32)
        return carry

    lax.fori_loop(0, tiles, prepare, 0)
    load_head.wait()
    unfold_head(r.head_fold, r.head_w)
    out_scatter.over_first()
    out_scatter.first()
    mix.finish()
    unit_ride.start()

    def arrange(p, carry):
        r.packed[p] = r.mixed[r.table[p]]
        return carry

    lax.fori_loop(0, chunks, arrange, 0)

    def unpack(t, carry):
        at = tile_at(t)
        pairs = r.packed[pl.ds(t * per_tile, per_tile)].astype(jnp.float32)
        pairs = jnp.concatenate([pairs[:, :, 0:64], pairs[:, :, 64:128]], axis=1).reshape(TILE, 64)
        low = (pairs * scale).astype(jnp.bfloat16)
        r.dout[at] = low
        r.delta[:, at] = jnp.sum(jnp.transpose(low.astype(jnp.float32)) * r.head_out[:, at], axis=0, keepdims=True)
        return carry

    lax.fori_loop(0, tiles, unpack, 0)
    lanes = lax.broadcasted_iota(jnp.int32, (1, columns), 1)
    scale_grad = jnp.sum(r.delta[...], axis=1, keepdims=True) / scale
    r.small[SCALES : SCALES + 1] = jnp.where(lanes == layer * 4 * LINE + index, scale_grad, 0.0)
    cut = r.table[2 * chunks]
    for i in range(tiles):
        at = slice(i * TILE, (i + 1) * TILE)
        query, dout, lse, delta = r.query[at], r.dout[at], r.lse[:, at], r.delta[:, at]

        def block(j, total_dq, masked):
            there = tile_at(j)
            scores = mul(r.keys[there], query, NT)
            weights = jnp.exp(scores - (lse if masked else lse - alive(cut, i, j)))
            if masked:
                weights = jnp.where(diagonal(scores), weights, 0.0)
            dweights = mul(r.values[there], dout, NT)
            dscores = (weights * (dweights - delta)).astype(jnp.bfloat16)
            r.dvalues[there] += mul(weights.astype(jnp.bfloat16), dout)
            r.dkeys[there] += mul(dscores, query)
            return total_dq + mul(r.keys_t[:, there], dscores)

        total_dq = block(i, jnp.zeros((64, TILE), jnp.float32), True)
        if i > 0:
            total_dq = lax.fori_loop(0, i, functools.partial(block, masked=False), total_dq)
        r.dquery_t[:, at] = total_dq * 0.125
        if i == 2:
            out_scatter.second()
            if not first:
                bulk.step(1)
    out_sum = r.dffn.at[pl.ds(0, out_rows)]
    out_scatter.finish(out_sum)
    r.out_own[...] = out_sum[...].reshape(r.out_own.shape).astype(jnp.bfloat16)
    out_ride.start()
    if not first:
        bulk.step(2)

    head_bias = jnp.zeros((1, 192), jnp.float32)
    for i in range(tiles):
        at = slice(i * TILE, (i + 1) * TILE)
        joined = jnp.concatenate([jnp.transpose(r.dquery_t[:, at]), r.dvalues[at], r.dkeys[at]], axis=1).astype(jnp.bfloat16)
        head_bias += jnp.sum(joined.astype(jnp.float32), axis=0, keepdims=True)
        r.qvk[i * per_tile : (i + 1) * per_tile] = joined.reshape(per_tile, CHUNK, 192)

    r.small[QUERY_BIAS : QUERY_BIAS + 1] = spread_head(head_bias[:, 0:64], index, columns)
    r.small[VALUE_BIAS : VALUE_BIAS + 1] = spread_head(head_bias[:, 64:128], index, columns)

    def restore(p, carry):
        r.flat[p] = r.qvk[r.table[chunks + p]]
        return carry

    lax.fori_loop(0, chunks, restore, 0)

    def project(owner):
        rows_of = r.flat[pl.ds(owner * per_block, per_block)].reshape(rows, 192)
        r.wide[pl.ds(owner * rows, rows)] = mul(rows_of, r.head_w[...], NT).astype(jnp.bfloat16)

    for own_y in (0, 1):
        for t in range(LINE):
            for other_core in (1, 0):
                project(scatter.owner(t, own_y, 1 - c if other_core else c))
                if other_core:
                    scatter.start(t, own_y)
    for t in range(tiles):
        tile_load(t).wait()
        grad = mul(chunks_of(r.flat, t), r.hb_tiles[t % 2], TN)
        r.gw[...] = grad if t == 0 else r.gw[...] + grad
        if t + 2 < tiles:
            tile_load(t + 2).start()
    r.head_own[...] = jnp.transpose(r.gw[...]).astype(jnp.bfloat16)
    head_cross.start()
    scatter.first()
    if not first:
        bulk.step(3)
    down_ride.finish()
    out_ride.finish()
    unit_ride.finish()
    reloads = [
        pltpu.make_async_copy(source, dest, r.load_sem.at[i])
        for i, (source, dest) in enumerate(((r.unit_got, r.gup), (r.gdown_got, r.gdown), (r.out_got, r.out_own)))
    ]
    for load in reloads:
        load.start()
    head_cross.finish()
    for j in range(r.head_fold.shape[0]):
        for part in range(2):
            at = slice(64 * j + 32 * part, 64 * j + 32 * part + 32)
            both = (r.head_own[at].astype(jnp.float32) + r.head_other[at].astype(jnp.float32)).astype(jnp.bfloat16)
            r.head_fold[j, :, 128 * part : 128 * part + 128] = both[:, 0:128]
            r.head_fold[j, :, 256 + 64 * part : 320 + 64 * part] = both[:, 128:192]
    head_ride.start()
    for load in reloads:
        load.wait()
    for q in range(4):
        parts = [r.gup[zz * 4 + q].astype(jnp.float32) for zz in range(LINE)]
        r.unit_near[q] = functools.reduce(jnp.add, parts).astype(jnp.bfloat16)
    for near, own in ((r.down_near, r.gdown), (r.out_near, r.out_own)):
        near[...] = functools.reduce(jnp.add, [own[zz].astype(jnp.float32) for zz in range(LINE)]).astype(jnp.bfloat16)
    start_all(near_rides)
    scatter.second(r.dffn)
    back, gain_grad, shift_grad = normed_back(r.x_in[...].astype(jnp.float32), gains[0][...], r.dffn[...])
    r.dx[...] = r.dmiddle[...] + back
    r.small[0:1] = gain_grad
    r.small[3:4] = shift_grad
    if not first:
        r.rest[0, 0:1] = gain_grad
        r.rest[0, 1:2] = shift_grad
        r.rest[0, 2:5] = r.small[QUERY_BIAS : SCALES + 1]
        r.rest[0, 5:8] = jnp.zeros((3, columns), jnp.float32)
        bulk.finish(r.bulk_out)
        rest.run(r.rest_out)
    scatter.finish()
    head_ride.finish()
    finish_all(near_rides)


def layer_backward_kernel(layer, table, dy, params, record, small, collective_id):
    rows, columns = dy.shape
    hidden_all = params.mid_gain.shape[1]
    total, plane_rows, hidden = rows * 4 * LINE, rows * PLANE, hidden_all // PLANE
    vmem, anywhere, smem = pltpu.VMEM, pl.ANY, pltpu.SMEM
    dma = pltpu.SemaphoreType.DMA
    low = lambda *shape: pltpu.VMEM(shape, jnp.bfloat16)
    full = lambda *shape: pltpu.VMEM(shape, jnp.float32)
    low_out = lambda *shape: jax.ShapeDtypeStruct(shape, jnp.bfloat16)
    full_out = lambda *shape: jax.ShapeDtypeStruct(shape, jnp.float32)
    swap_sems, trade_sems, cross_sems = Swap.scratch(), Trade.scratch(), Cross.scratch()
    unit_shape = (4 * LINE, columns // (4 * LINE), hidden)
    unit_near, down_near, out_near = (4, *unit_shape[1:]), (hidden // LINE, columns), (32, columns)
    down_shape = (LINE, hidden // LINE, columns)
    inputs = dict(
        table=(table, smem), scales=(params.head_scale, smem), dy=(dy, vmem), gains=(params.vec_gain, vmem),
        mid_gain_all=(params.mid_gain, vmem), x_in=(record.x_in, vmem), branch=(record.branch, vmem),
        middle=(record.middle, vmem), ab=(record.ab, vmem), lse=(record.lse, vmem),
        head_out=(record.head_out, vmem), stat=(record.stat, vmem), hb_all_in=(record.hb_all_out, anywhere),
        qvk_in=(record.qvk_out, anywhere), out_w_in=(record.out_w_out, anywhere),
        rows_all_in=(record.rows_all_out, anywhere), unit_t_in=(record.unit_t_out, anywhere),
        act_in=(record.act_out, anywhere), slope_in=(record.slope_out, anywhere),
        mid_in=(record.mid_out, anywhere), down_blocks=(record.down_blocks, anywhere),
        head_blocks=(record.head_blocks, anywhere),
    )
    outputs = dict(
        dx=(full_out(rows, columns), vmem), unit_got=(low_out(*unit_shape), anywhere),
        gdown_got=(low_out(*down_shape), anywhere), out_got=(low_out(LINE, *out_near), anywhere),
        head_got=(low_out(4 * LINE, 32, 384), anywhere), unit_near=(low_out(*unit_near), vmem),
        down_near=(low_out(*down_near), vmem), out_near=(low_out(*out_near), vmem),
        unit_far=(low_out(*unit_near), anywhere), down_far=(low_out(*down_near), anywhere),
        out_far=(low_out(*out_near), anywhere),
    )
    first = layer == 1
    if first:
        inputs.update(dy_all_in=(record.dy_all_out, anywhere))
        outputs.update(small=(full_out(SMALL, columns), vmem))
    else:
        inputs.update(small_in=(small, vmem))
        outputs.update(bulk_out=(full_out(2 * SMALL, columns), vmem), rest_out=(full_out(8, columns), vmem))
    plane_bufs, plane_sems = PlaneScatter.scratch(rows, columns)
    out_bufs, out_sems = PlaneScatter.scratch(LINE * 32, columns)
    group_bufs, group_sems = GroupScatter.scratch(rows, columns)
    scratch = dict(
        wide=low(total, columns), down_w=low(*down_shape), act=full(hidden, plane_rows),
        slope=low(hidden, plane_rows), unit_t=low(hidden, columns), mid=low(hidden, plane_rows),
        out_w=low(columns, columns), qvk=low(total // CHUNK, CHUNK, 192), hb_tiles=low(2, TILE, columns),
        dmid=full(hidden, plane_rows), du=low(hidden, plane_rows), part=low(plane_rows, columns),
        own_sums=full(2, plane_rows), got_sums=full(PLANE, 2, plane_rows), sums=full(2, plane_rows),
        gup=low(*unit_shape), gdown=low(*down_shape), dffn=full(rows, columns),
        dmiddle=full(rows, columns), packed=low(total // CHUNK, CHUNK // 2, 128),
        mixed=low(total // CHUNK, CHUNK // 2, 128),
        out_own=low(LINE, 32, columns),
        dout=low(total, 64), delta=full(1, total), query=low(total, 64),
        keys=low(total, 64), values=low(total, 64), keys_t=low(64, total), dkeys=full(total, 64),
        dvalues=full(total, 64), dquery_t=full(64, total), flat=low(total // CHUNK, CHUNK, 192),
        head_w=low(columns, 192), gw=full(192, columns), head_own=low(columns, 192),
        head_other=low(columns, 192), head_fold=low(4 * LINE, 32, 384),
        plane_bufs=plane_bufs, plane_sems=plane_sems, out_bufs=out_bufs, out_sems=out_sems,
        group_bufs=group_bufs, group_sems=group_sems, plane_gather_sems=PlaneGather.scratch(),
        pool_sems=([dma((PLANE,)), dma((PLANE,))]), unit_sems=swap_sems, gdown_sems=trade_sems, head_sems=swap_sems,
        mix_sems=swap_sems, out_ride_sems=trade_sems, head_cross_sems=cross_sems, load_sem=dma((10,)),
        tile_sem=dma((2,)),
    )
    scratch.update(unit_cross_sems=cross_sems, down_cross_sems=cross_sems, out_cross_sems=cross_sems)
    scratch.update(mid_gain=full(hidden, 1), gg=full(hidden, 1), gs=full(hidden, 1), gb=full(hidden, 1))
    if not first:
        scratch.update(small=full(SMALL, columns), bulk=low(2 * SMALL, columns), rest=full(1, 8, columns))
        scratch.update(bulk_sum=AllSum.scratch((2 * SMALL, columns), jnp.bfloat16))
        rest_got, rest_sems = QuickSum.scratch((8, columns))
        scratch.update(rest_got=rest_got, rest_sems=rest_sems)
    kernel = functools.partial(backward_kernel, layer, hidden_all)
    call = lambda body, **how: pl.pallas_call(body, name="layer_backward", **how)
    return launch(call, kernel, inputs, outputs, scratch, collective_id, 105, 63)


def assemble_kernel(r):
    x = lax.axis_index("batch")
    for layer, got in enumerate((r.layer0, r.layer1)):
        head_ref, unit_near, unit_far, down_near, down_far, out_near, out_far = got
        width = 64 * head_ref.shape[0]
        for j in range(0, head_ref.shape[0], 2):
            left, right = head_ref[j].astype(jnp.float32), head_ref[j + 1].astype(jnp.float32)
            for part in range(2):
                for at, source in ((0, 128 * part), (width, 256 + 64 * part), (2 * width, 64 + 128 * part)):
                    pair = jnp.concatenate([left[:, source : source + 64], right[:, source : source + 64]], axis=1)
                    r.qkv[layer, 32 * part : 32 * part + 32, at + j * 64 : at + (j + 2) * 64] = pair
        for half, unit_ref, down_ref, out_ref in ((x, unit_near, down_near, out_near), (1 - x, unit_far, down_far, out_far)):
            for q in range(unit_ref.shape[0]):
                for z in range(LINE):
                    piece = unit_ref[q, :, z * 128 : (z + 1) * 128].astype(jnp.float32)
                    r.up[layer, :, unit_lanes(z, q * 2 + half)] = piece
            for ref, dest in ((down_ref, r.down), (out_ref, r.out)):
                rows = ref.shape[0]
                dest[layer, pl.ds(pl.multiple_of(half * rows, rows), rows)] = ref[...].astype(jnp.float32)
        bulk = r.bulk[SMALL * (1 - layer) : SMALL * (2 - layer)]
        rest = r.rest[...] if layer == 0 else bulk[0:1] * 0.0
        gain, shift = (rest[0:1], rest[1:2]) if layer == 0 else (bulk[0:1], bulk[3:4])
        heads = rest[2:4] if layer == 0 else bulk[QUERY_BIAS : VALUE_BIAS + 1]
        gain_rows = jnp.concatenate([gain, bulk[1:3]], axis=0)
        bias_rows = jnp.concatenate([shift, bulk[4:6], heads, bulk[OUT_BIAS : DOWN_BIAS + 1]], axis=0)
        for ref, rows in ((r.vec_gain, gain_rows), (r.vec_bias, bias_rows)):
            for i in range(ref.shape[0]):
                ref[i, layer : layer + 1] = rows[i : i + 1]
        for z in range(LINE):
            at = slice(z * PLANE * 128, (z + 1) * PLANE * 128)
            r.mid_gain[layer : layer + 1, at] = bulk[MID + z : MID + z + 1]
            for i in range(2):
                row = MID + (i + 1) * LINE + z
                r.mid_bias[layer, i : i + 1, at] = bulk[row : row + 1]
        row = rest[4:5] if layer == 0 else bulk[SCALES : SCALES + 1]
        heads_here = r.head_scale.shape[1]
        r.head_scale[layer : layer + 1] = row[:, layer * heads_here : (layer + 1) * heads_here]


def assemble(results, dx, back, shapes):
    vmem, anywhere = pl.BlockSpec(memory_space=pltpu.VMEM), pl.BlockSpec(memory_space=pl.ANY)
    arrays = [results, dx]
    for got in back:
        arrays += [got.head_got, got.unit_near, got.unit_far, got.down_near, got.down_far, got.out_near, got.out_far]

    arrays += [back[0].bulk_out, back[0].rest_out]
    n = len(arrays)

    def body(*refs):
        ins, outs, held, sem = refs[:n], refs[n : n + 11], refs[n + 11 : -1], refs[-1]
        loads = [pltpu.make_async_copy(ins[i], held[i], sem.at[i]) for i in range(n)]
        passes = [pltpu.make_async_copy(held[i], outs[i], sem.at[i]) for i in range(2)]
        for load in loads:
            load.start()
        for load in loads:
            load.wait()
        for copy in passes:
            copy.start()
        qkv, out, up, down, vec_gain, vec_bias, mid_gain, mid_bias, head_scale = outs[2:]
        refs = held[2:]
        assemble_kernel(
            Refs(
                layer0=refs[0:7], layer1=refs[7:14], bulk=refs[14], rest=refs[15], qkv=qkv, out=out, up=up, down=down,
                vec_gain=vec_gain, vec_bias=vec_bias, mid_gain=mid_gain, mid_bias=mid_bias, head_scale=head_scale,
            )
        )
        for copy in passes:
            copy.wait()

    return pl.pallas_call(
        body,
        out_shape=[jax.ShapeDtypeStruct(array.shape, array.dtype) for array in (results, dx)]
        + [jax.ShapeDtypeStruct(shape, jnp.float32) for shape in shapes],
        in_specs=[anywhere] * n,
        out_specs=[anywhere] * 2 + [vmem] * len(shapes),
        scratch_shapes=[pltpu.VMEM(array.shape, array.dtype) for array in arrays] + [pltpu.SemaphoreType.DMA((n,))],
        cost_estimate=lasting(5),
        compiler_params=pltpu.CompilerParams(vmem_limit_bytes=62 << 20),
        name="assemble",
    )(*arrays)


def chunk_table(first_rows, span_of, rows_here):
    blocks = span_of.shape[0]
    first = first_rows[0]
    second = rows_here - first
    row = jnp.arange(blocks * rows_here // CHUNK, dtype=jnp.int32) * CHUNK
    later = row >= first * blocks
    inside = jnp.where(later, row - first * blocks, row)
    length = jnp.where(later, jnp.maximum(second, 1), first)
    span = inside // length
    of_span = (span_of[None, :] == span[:, None]).astype(jnp.int32)
    device_of = jnp.sum(of_span * jnp.arange(blocks, dtype=jnp.int32)[None, :], axis=1)
    source = device_of * rows_here + jnp.where(later, first, 0) + inside - span * length
    within = row % rows_here
    behind = within >= first
    place = jnp.repeat(span_of, rows_here // CHUNK) * jnp.where(behind, second, first) + within
    place = place + jnp.where(behind, first * (blocks - 1), 0)
    return jnp.concatenate([source // CHUNK, place // CHUNK, (first * blocks // TILE)[None]]).astype(jnp.int32)


def travel(
    tokens, grad_out, first_rows, span_of, w_qkv, w_out, w_up, w_down, vec_gain, vec_bias, mid_gain, mid_bias, head_scale
):
    rows_here, row_width = tokens.shape
    table = chunk_table(first_rows, span_of, rows_here)
    params = Refs(
        w_qkv=w_qkv, w_up=w_up, w_out=w_out.reshape(2, 2, -1, row_width), w_down=w_down.reshape(2, 2, -1, row_width),
        vec_gain=vec_gain.transpose(1, 0, 2), vec_bias=vec_bias.transpose(1, 0, 2), mid_gain=mid_gain, mid_bias=mid_bias,
        head_scale=head_scale,
    )
    first = layer_forward_kernel(0, table, tokens, params, None, None, jnp.float32, 0)
    first.x_in = tokens
    blocks = Refs(head=first.next_head, unit=first.next_unit)
    second = layer_forward_kernel(1, table, first.y_out, params, blocks, grad_out, jnp.bfloat16, 1)
    second.x_in, second.head_blocks = first.y_out, first.next_head
    back_second = layer_backward_kernel(1, table, grad_out, params, second, None, 2)
    back_first = layer_backward_kernel(0, table, back_second.dx, params, first, back_second.small, 3)
    kinds = (w_qkv, w_out, w_up, w_down, params.vec_gain, params.vec_bias, mid_gain, mid_bias, head_scale)
    results = assemble(second.y_out, back_first.dx, [back_first, back_second], [array.shape for array in kinds])
    return (*results[:6], results[6].transpose(1, 0, 2), results[7].transpose(1, 0, 2), *results[8:])


def local(*args):
    tokens, w_qkv = args[0], args[4]
    blocks = lax.axis_size("blk")
    heads = w_qkv.shape[2] // (3 * HEAD_DIM)
    if blocks == heads == 4 * LINE and lax.axis_size("batch") == 2 and tokens.shape[0] * blocks % TILE == 0:
        return travel(*args)
    return general(*args)


def solution(mesh):
    placed = (
        P(("batch", "blk"), None),
        P(("batch", "blk"), None),
        P("batch"),
        P(),
        P(None, "blk", None),
        P(None, "blk", None),
        P(None, "blk", None),
        P(None, "blk", None),
        P(),
        P(),
        P(),
        P(),
        P(),
    )
    return jax.shard_map(
        local,
        mesh=mesh,
        in_specs=placed,
        out_specs=(
            P(("batch", "blk"), None),
            P(("batch", "blk"), None),
            P(None, "blk", None),
            P(None, "blk", None),
            P(None, "blk", None),
            P(None, "blk", None),
            P(),
            P(),
            P(),
            P(),
            P(),
        ),
        check_vma=False,
    )
```

```python
import functools

import jax
import jax.numpy as jnp
from jax import lax
from jax.experimental import pallas as pl
from jax.experimental.pallas import tpu as pltpu
from jax.sharding import PartitionSpec as P

HEAD_DIM = 64


EPSILON = 1e-05
NEGATIVE = -1e30


def shifted(x, axis, by):
    devices = lax.axis_size(axis)
    return lax.ppermute(x, axis, [(i, (i + by) % devices) for i in range(devices)])


def norm_rows(values, gains, shifts):
    average = jnp.mean(values, axis=-1, keepdims=True)
    centered = values - average
    spread = jnp.mean(centered * centered, axis=-1, keepdims=True)
    return centered * lax.rsqrt(spread + EPSILON) * gains + shifts


def mid_piece(upper, gains, shifts):
    return norm_rows(jax.nn.gelu(upper, approximate=False), gains, shifts)


def split_heads(matrix):
    return matrix.reshape(matrix.shape[0], -1, HEAD_DIM)


def block_rows(total_rows):
    chosen = total_rows
    while chosen > 1024 and chosen % 2 == 0:
        chosen = chosen // 2
    return chosen


def row_layout(first_rows, rows_here):
    within = jnp.arange(rows_here, dtype=jnp.int32)
    first_len = first_rows[0]
    second = (within >= first_len).astype(jnp.int32)
    return (second, within - second * first_len)


def visible_pairs(query_seq, query_off, query_span, key_seq, key_off, key_span):
    earlier = key_span[None, :] < query_span[:, None]
    same_span = (key_span[None, :] == query_span[:, None]) & (
        key_off[None, :] <= query_off[:, None]
    )
    return (query_seq[:, None] == key_seq[None, :]) & (earlier | same_span)


def merge_block(state_in, query_heads, keys_block, values_block, visible):
    run_peak, run_total, accumulated = state_in
    query_rows = query_heads.shape[0]
    scores = jnp.einsum(
        "qhd,khd->hqk", query_heads, split_heads(keys_block), preferred_element_type=jnp.float32
    ) * HEAD_DIM ** (-0.5)
    masked = jnp.where(visible[None], scores, NEGATIVE)
    new_peak = jnp.maximum(run_peak, jnp.max(masked, axis=-1))
    weights = jnp.where(visible[None], jnp.exp(masked - new_peak[:, :, None]), 0.0)
    factor = jnp.exp(run_peak - new_peak)
    new_total = run_total * factor + jnp.sum(weights, axis=-1)
    update = jnp.einsum(
        "hqk,khd->qhd",
        weights.astype(jnp.bfloat16),
        split_heads(values_block),
        preferred_element_type=jnp.float32,
    )
    rescaled = split_heads(accumulated) * jnp.transpose(factor)[:, :, None]
    return (new_peak, new_total, (rescaled + update).reshape(query_rows, -1))


def grad_block(query_heads, log_total, delta, dout_heads, keys_block, values_block, visible):
    key_heads = split_heads(keys_block)
    value_heads = split_heads(values_block)
    scores = jnp.einsum(
        "qhd,khd->hqk", query_heads, key_heads, preferred_element_type=jnp.float32
    ) * HEAD_DIM ** (-0.5)
    probs = jnp.where(visible[None], jnp.exp(scores - log_total[:, :, None]), 0.0)
    dprobs = jnp.einsum("qhd,khd->hqk", dout_heads, value_heads, preferred_element_type=jnp.float32)
    dscores = (probs * (dprobs - delta[:, :, None])).astype(jnp.bfloat16)
    add_query = jnp.einsum("hqk,khd->qhd", dscores, key_heads, preferred_element_type=jnp.float32)
    add_keys = jnp.einsum("hqk,qhd->khd", dscores, query_heads, preferred_element_type=jnp.float32)
    add_values = jnp.einsum(
        "hqk,qhd->khd", probs.astype(jnp.bfloat16), dout_heads, preferred_element_type=jnp.float32
    )
    return (
        add_query.reshape(query_heads.shape[0], -1),
        add_keys.reshape(key_heads.shape[0], -1),
        add_values.reshape(key_heads.shape[0], -1),
    )


def unchanged(state_in):
    return state_in


def attention_forward(query_low, keys_low, values_low, layout):
    seq_ids, offsets, span_of, my_span, my_index = layout
    rows_here, row_width = query_low.shape
    heads_here = row_width // HEAD_DIM
    query_heads = split_heads(query_low)
    query_span = jnp.full((rows_here,), my_span, jnp.int32)
    initial = (
        jnp.full((heads_here, rows_here), NEGATIVE, jnp.float32),
        jnp.zeros((heads_here, rows_here), jnp.float32),
        jnp.zeros((rows_here, row_width), jnp.float32),
    )
    running = initial
    key_part = lax.all_gather(keys_low, "blk", axis=0, tiled=True)
    value_part = lax.all_gather(values_low, "blk", axis=0, tiled=True)
    part_rows = key_part.shape[0]
    step_rows = block_rows(part_rows)

    def one_step(state_in, step_index):
        block_start = step_index * step_rows
        global_rows = block_start + jnp.arange(step_rows, dtype=jnp.int32)
        key_span = span_of[global_rows // rows_here]
        local_rows = global_rows % rows_here
        visible = visible_pairs(
            seq_ids, offsets, query_span, seq_ids[local_rows], offsets[local_rows], key_span
        )
        keys_block = lax.dynamic_slice_in_dim(key_part, block_start, step_rows, 0)
        values_block = lax.dynamic_slice_in_dim(value_part, block_start, step_rows, 0)

        def one_compute(inner_state):
            return merge_block(inner_state, query_heads, keys_block, values_block, visible)

        return (lax.cond(jnp.any(key_span <= my_span), one_compute, unchanged, state_in), None)

    running, _ = lax.scan(one_step, running, jnp.arange(part_rows // step_rows, dtype=jnp.int32))
    run_peak, run_total, accumulated = running
    mixed_heads = (split_heads(accumulated) / jnp.transpose(run_total)[:, :, None]).reshape(
        rows_here, row_width
    )
    return (mixed_heads, run_peak + jnp.log(run_total))


def cycle_backward(query_low, keys_low, values_low, log_total, delta, dout_low, layout):
    seq_ids, offsets, span_of, my_span, my_index = layout
    rows_here, row_width = query_low.shape
    blocks_total = lax.axis_size("blk")
    query_heads = split_heads(query_low)
    dout_heads = split_heads(dout_low)
    query_span = jnp.full((rows_here,), my_span, jnp.int32)

    def turn(turn_index, carried):
        keys_now, values_now, dkeys, dvalues, dquery = carried
        source = (my_index - turn_index) % blocks_total
        source_span = span_of[source]
        key_span = jnp.full((rows_here,), source_span, jnp.int32)
        visible = visible_pairs(seq_ids, offsets, query_span, seq_ids, offsets, key_span)

        def turn_compute(inner_state):
            add_query, add_keys, add_values = grad_block(
                query_heads, log_total, delta, dout_heads, keys_now, values_now, visible
            )
            return (
                inner_state[0] + add_query,
                inner_state[1] + add_keys,
                inner_state[2] + add_values,
            )

        dquery, dkeys, dvalues = lax.cond(
            source_span <= my_span, turn_compute, unchanged, (dquery, dkeys, dvalues)
        )
        keys_now, values_now = shifted((keys_now, values_now), "blk", 1)
        dkeys, dvalues = (
            shifted(dkeys.astype(jnp.bfloat16), "blk", 1).astype(dkeys.dtype),
            shifted(dvalues.astype(jnp.bfloat16), "blk", 1).astype(dvalues.dtype),
        )
        return (keys_now, values_now, dkeys, dvalues, dquery)

    zeros_rows = jnp.zeros((rows_here, row_width), jnp.float32)
    result = lax.fori_loop(
        0, blocks_total, turn, (keys_low, values_low, zeros_rows, zeros_rows, zeros_rows)
    )
    return (result[4], result[2], result[3])


def layer_forward(inputs, weights, gains, biases, middle_gain, middle_bias, heads_scale, layout):
    weight_qkv, weight_out, weight_up, weight_down = weights
    row_width = inputs.shape[1]
    normed, pre_pull = jax.vjp(norm_rows, inputs, gains[0], biases[0])
    normed_low = normed.astype(jnp.bfloat16)
    projected = jnp.dot(normed_low, weight_qkv, preferred_element_type=jnp.float32)
    query_low = (projected[:, :row_width] + biases[3]).astype(jnp.bfloat16)
    keys_low = projected[:, row_width : 2 * row_width].astype(jnp.bfloat16)
    values_low = (projected[:, 2 * row_width :] + biases[4]).astype(jnp.bfloat16)
    mixed_heads, log_total = attention_forward(query_low, keys_low, values_low, layout)
    scaled_low = (mixed_heads * jnp.repeat(heads_scale, HEAD_DIM)).astype(jnp.bfloat16)
    branch = jnp.dot(scaled_low, weight_out, preferred_element_type=jnp.float32) + biases[5]
    post_normed, post_pull = jax.vjp(norm_rows, branch, gains[1], biases[1])
    middle_res = inputs + post_normed
    ffn_normed, ffn_pull = jax.vjp(norm_rows, middle_res, gains[2], biases[2])
    ffn_low = ffn_normed.astype(jnp.bfloat16)
    upper = jnp.dot(ffn_low, weight_up, preferred_element_type=jnp.float32) + middle_bias[1]
    middle, mid_pull = jax.vjp(mid_piece, upper, middle_gain, middle_bias[0])
    middle_low = middle.astype(jnp.bfloat16)
    results = middle_res + (
        jnp.dot(middle_low, weight_down, preferred_element_type=jnp.float32) + biases[6]
    )
    record = {
        "pre_pull": pre_pull,
        "normed_low": normed_low,
        "query_low": query_low,
        "keys_low": keys_low,
        "values_low": values_low,
        "log_total": log_total,
        "mixed_heads": mixed_heads,
        "scaled_low": scaled_low,
        "post_pull": post_pull,
        "ffn_pull": ffn_pull,
        "ffn_low": ffn_low,
        "mid_pull": mid_pull,
        "middle_low": middle_low,
        "weights": weights,
    }
    return (results, record)


def layer_backward(d_results, record, weights, heads_scale, layout):
    weight_qkv, weight_out, weight_up, weight_down = weights
    rows_here, row_width = d_results.shape
    d_results_low = d_results.astype(jnp.bfloat16)
    grad_down = jnp.einsum(
        "tf,td->fd", record["middle_low"], d_results_low, preferred_element_type=jnp.float32
    )
    grad_down_bias = jnp.sum(d_results_low, axis=0, dtype=jnp.float32)
    d_middle = jnp.einsum(
        "td,fd->tf", d_results_low, weight_down, preferred_element_type=jnp.float32
    )
    d_upper, grad_mid_gain, grad_mid_shift = record["mid_pull"](d_middle)
    d_upper_low = d_upper.astype(jnp.bfloat16)
    grad_up = jnp.einsum(
        "td,tf->df", record["ffn_low"], d_upper_low, preferred_element_type=jnp.float32
    )
    grad_up_bias = jnp.sum(d_upper_low, axis=0, dtype=jnp.float32)
    d_ffn = jnp.einsum("tf,df->td", d_upper_low, weight_up, preferred_element_type=jnp.float32)
    d_res_part, grad_gain_ffn, grad_shift_ffn = record["ffn_pull"](d_ffn)
    d_middle_res = d_results + d_res_part
    d_branch, grad_gain_post, grad_shift_post = record["post_pull"](d_middle_res)
    d_branch_low = d_branch.astype(jnp.bfloat16)
    grad_out_w = jnp.einsum(
        "tc,td->cd", record["scaled_low"], d_branch_low, preferred_element_type=jnp.float32
    )
    grad_out_bias = jnp.sum(d_branch_low, axis=0, dtype=jnp.float32)
    d_scaled = jnp.einsum("td,cd->tc", d_branch_low, weight_out, preferred_element_type=jnp.float32)
    mixed_heads = record["mixed_heads"]
    grad_heads = jnp.sum((d_scaled * mixed_heads).reshape(rows_here, -1, HEAD_DIM), axis=(0, 2))
    d_mixed_low = (d_scaled * jnp.repeat(heads_scale, HEAD_DIM)).astype(jnp.bfloat16)
    delta = jnp.transpose(
        jnp.sum(
            (d_mixed_low.astype(jnp.float32) * mixed_heads).reshape(rows_here, -1, HEAD_DIM), axis=2
        )
    )
    dquery, dkeys, dvalues = cycle_backward(
        record["query_low"],
        record["keys_low"],
        record["values_low"],
        record["log_total"],
        delta,
        d_mixed_low,
        layout,
    )
    scale_factor = HEAD_DIM ** (-0.5)
    d_proj_low = jnp.concatenate(
        [dquery * scale_factor, dkeys * scale_factor, dvalues], axis=1
    ).astype(jnp.bfloat16)
    grad_qkv = jnp.einsum(
        "tc,te->ce", record["normed_low"], d_proj_low, preferred_element_type=jnp.float32
    )
    grad_q_bias = jnp.sum(d_proj_low[:, :row_width], axis=0, dtype=jnp.float32)
    grad_v_bias = jnp.sum(d_proj_low[:, 2 * row_width :], axis=0, dtype=jnp.float32)
    d_normed = jnp.einsum("te,ce->tc", d_proj_low, weight_qkv, preferred_element_type=jnp.float32)
    d_in_part, grad_gain_pre, grad_shift_pre = record["pre_pull"](d_normed)
    d_inputs = d_middle_res + d_in_part
    big_grads = (grad_qkv, grad_out_w, grad_up, grad_down)
    gain_grads = jnp.stack([grad_gain_pre, grad_gain_post, grad_gain_ffn])
    bias_grads = jnp.stack(
        [
            grad_shift_pre,
            grad_shift_post,
            grad_shift_ffn,
            grad_q_bias,
            grad_v_bias,
            grad_out_bias,
            grad_down_bias,
        ]
    )
    small_grads = (
        gain_grads,
        bias_grads,
        grad_mid_gain,
        jnp.stack([grad_mid_shift, grad_up_bias]),
        grad_heads,
    )
    return (d_inputs, big_grads, small_grads)


def general(
    tokens,
    grad_out,
    first_rows,
    span_of,
    w_qkv,
    w_out,
    w_up,
    w_down,
    vec_gain,
    vec_bias,
    mid_gain,
    mid_bias,
    head_scale,
):
    rows_here = tokens.shape[0]
    my_index = lax.axis_index("blk")
    my_span = span_of[my_index]
    seq_ids, offsets = row_layout(first_rows, rows_here)
    layout = (seq_ids, offsets, span_of, my_span, my_index)
    current = tokens.astype(jnp.float32)
    records = []
    for layer_index in range(2):
        weights = (
            lax.all_gather(w_qkv[layer_index], "blk", axis=0, tiled=True),
            lax.all_gather(w_out[layer_index], "blk", axis=0, tiled=True),
            lax.all_gather(w_up[layer_index], "blk", axis=0, tiled=True),
            lax.all_gather(w_down[layer_index], "blk", axis=0, tiled=True),
        )
        current, record = layer_forward(
            current,
            weights,
            vec_gain[layer_index],
            vec_bias[layer_index],
            mid_gain[layer_index],
            mid_bias[layer_index],
            head_scale[layer_index],
            layout,
        )
        records.append(record)
    results_low = current.astype(jnp.bfloat16)
    d_current = grad_out.astype(jnp.float32)
    shard_grads = [None, None]
    small_grads = [None, None]
    for layer_index in (1, 0):
        weights = (
            lax.all_gather(w_qkv[layer_index], "blk", axis=0, tiled=True),
            lax.all_gather(w_out[layer_index], "blk", axis=0, tiled=True),
            lax.all_gather(w_up[layer_index], "blk", axis=0, tiled=True),
            lax.all_gather(w_down[layer_index], "blk", axis=0, tiled=True),
        )
        d_current, big_grads, small_part = layer_backward(
            d_current, records[layer_index], weights, head_scale[layer_index], layout
        )
        shard_grads[layer_index] = (
            lax.psum_scatter(
                big_grads[0].astype(jnp.bfloat16), "blk", scatter_dimension=0, tiled=True
            ).astype(jnp.float32),
            lax.psum_scatter(
                big_grads[1].astype(jnp.bfloat16), "blk", scatter_dimension=0, tiled=True
            ).astype(jnp.float32),
            lax.psum_scatter(
                big_grads[2].astype(jnp.bfloat16), "blk", scatter_dimension=0, tiled=True
            ).astype(jnp.float32),
            lax.psum_scatter(
                big_grads[3].astype(jnp.bfloat16), "blk", scatter_dimension=0, tiled=True
            ).astype(jnp.float32),
        )
        small_grads[layer_index] = small_part
    stacked_small = [
        jnp.stack([small_grads[0][item_index], small_grads[1][item_index]])
        for item_index in range(5)
    ]
    summed_small = (
        lax.psum(stacked_small[0].astype(jnp.bfloat16), "blk").astype(jnp.float32),
        lax.psum(stacked_small[1].astype(jnp.bfloat16), "blk").astype(jnp.float32),
        lax.psum(stacked_small[2].astype(jnp.bfloat16), "blk").astype(jnp.float32),
        lax.psum(stacked_small[3].astype(jnp.bfloat16), "blk").astype(jnp.float32),
        lax.psum(stacked_small[4].astype(jnp.bfloat16), "blk").astype(jnp.float32),
    )
    stacked_big = [
        jnp.stack([shard_grads[0][item_index], shard_grads[1][item_index]])
        for item_index in range(4)
    ]
    totals = (
        lax.psum(stacked_big[0].astype(jnp.bfloat16), "batch").astype(jnp.float32),
        lax.psum(stacked_big[1].astype(jnp.bfloat16), "batch").astype(jnp.float32),
        lax.psum(stacked_big[2].astype(jnp.bfloat16), "batch").astype(jnp.float32),
        lax.psum(stacked_big[3].astype(jnp.bfloat16), "batch").astype(jnp.float32),
        lax.psum(summed_small[0].astype(jnp.bfloat16), "batch").astype(jnp.float32),
        lax.psum(summed_small[1].astype(jnp.bfloat16), "batch").astype(jnp.float32),
        lax.psum(summed_small[2].astype(jnp.bfloat16), "batch").astype(jnp.float32),
        lax.psum(summed_small[3].astype(jnp.bfloat16), "batch").astype(jnp.float32),
        lax.psum(summed_small[4].astype(jnp.bfloat16), "batch").astype(jnp.float32),
    )
    return (
        results_low,
        d_current,
        totals[0],
        totals[1],
        totals[2],
        totals[3],
        totals[4],
        totals[5],
        totals[6],
        totals[7],
        totals[8],
    )


MESH = pl.DeviceIdType.MESH
LINE = 4
HALVES = 2
CHUNK = 32
TILE = 512


def place():
    k = lax.axis_index("blk")
    return k // 4, lax.rem(k // 2, 2), lax.rem(k, 2)


def index_of(z, y, c):
    return (z * 2 + y) * 2 + c


def device(z, y, c):
    return {"blk": index_of(z, y, c)}


def hail(where):
    pl.semaphore_signal(pltpu.get_barrier_semaphore(), inc=1, device_id=where, device_id_type=MESH)


def other_group():
    return {"batch": 1 - lax.axis_index("batch")}


def lasting(microseconds):
    return pl.CostEstimate(flops=0, bytes_accessed=int(microseconds * 3.5e6), transcendentals=0)


def remote(src, dst, send, recv, where):
    return pltpu.make_async_remote_copy(
        src_ref=src, dst_ref=dst, send_sem=send, recv_sem=recv, device_id=where, device_id_type=MESH
    )


class Swap:
    def __init__(self, x_ref, o_ref, ss, rs, own_sem, per=1):
        self.x_ref, self.o_ref, self.ss, self.rs, self.own_sem = x_ref, o_ref, ss, rs, own_sem
        self.k, self.n, self.per = lax.axis_index("blk"), 4 * LINE, per

    @staticmethod
    def scratch():
        dma = pltpu.SemaphoreType.DMA
        return [dma((4 * LINE,)), dma((4 * LINE,)), dma]

    def source(self, to):
        return self.x_ref.at[pl.ds(lax.rem(to, self.x_ref.shape[0] // self.per) * self.per, self.per)]

    def place(self, at):
        return self.o_ref.at[pl.ds(at * self.per, self.per)]

    def send(self, i):
        to = lax.rem(self.k + i, self.n)
        return remote(self.source(to), self.place(self.k), self.ss.at[i], self.rs.at[i], {"blk": to})

    def receive(self, i):
        at = lax.rem(self.k - i + self.n, self.n)
        return remote(self.place(at), self.place(at), self.ss.at[i], self.rs.at[i], {"blk": at})

    def own(self):
        return pltpu.make_async_copy(self.source(self.k), self.place(self.k), self.own_sem)

    def start(self):
        def one(i, carry):
            self.send(i).start()
            return carry

        lax.fori_loop(1, self.n, one, 0)
        self.own().start()

    def finish(self):
        def one(i, carry):
            self.receive(i).wait_recv()
            self.send(i).wait_send()
            return carry

        self.own().wait()
        lax.fori_loop(1, self.n, one, 0)


class Trade:
    def __init__(self, x_ref, o_ref, ss, rs, own_sem):
        self.x_ref, self.o_ref, self.ss, self.rs, self.own_sem = x_ref, o_ref, ss, rs, own_sem
        self.z, self.y, self.c = place()

    @staticmethod
    def scratch():
        dma = pltpu.SemaphoreType.DMA
        return [dma((LINE,)), dma((LINE,)), dma]

    def source(self, to):
        return self.x_ref.at[lax.rem(to, self.x_ref.shape[0])]

    def send(self, s):
        to = lax.rem(self.z + s, LINE)
        return remote(self.source(to), self.o_ref.at[self.z], self.ss.at[s], self.rs.at[s], device(to, self.y, self.c))

    def own(self):
        return pltpu.make_async_copy(self.source(self.z), self.o_ref.at[self.z], self.own_sem)

    def start(self):
        for s in range(1, LINE):
            self.send(s).start()
        self.own().start()

    def finish(self):
        self.own().wait()
        for s in range(1, LINE):
            at = lax.rem(self.z - s + LINE, LINE)
            slot = self.o_ref.at[at]
            remote(slot, slot, self.ss.at[s], self.rs.at[s], device(at, self.y, self.c)).wait_recv()
            self.send(s).wait_send()


class Share:
    def __init__(self, x_ref, o_ref, sr, rr, sl, rl, own_sem):
        self.x_ref, self.o_ref, self.own_sem = x_ref, o_ref, own_sem
        self.sr, self.rr, self.sl, self.rl = sr, rr, sl, rl
        self.z, self.y, self.c = place()

    @staticmethod
    def scratch():
        dma = pltpu.SemaphoreType.DMA
        return [dma((LINE,))] * 4 + [dma]

    def right(self, s):
        slot = self.o_ref.at[self.z - s]
        source = self.x_ref.at[0] if s == 0 else slot
        return remote(source, slot, self.sr.at[s], self.rr.at[s + 1], device(self.z + 1, self.y, self.c))

    def left(self, s):
        slot = self.o_ref.at[self.z + s]
        source = self.x_ref.at[0] if s == 0 else slot
        return remote(source, slot, self.sl.at[s], self.rl.at[s + 1], device(self.z - 1, self.y, self.c))

    def own(self):
        return pltpu.make_async_copy(self.x_ref.at[0], self.o_ref.at[self.z], self.own_sem)

    def start(self):
        self.own().start()

        @pl.when(self.z < LINE - 1)
        def _():
            self.right(0).start()

        @pl.when(self.z > 0)
        def _():
            self.left(0).start()

    def step(self, s):
        @pl.when(self.z >= s)
        def _():
            slot = self.o_ref.at[self.z - s]
            remote(slot, slot, self.sr.at[s], self.rr.at[s], device(self.z, self.y, 1 - self.c)).wait_recv()
            if s < LINE - 1:

                @pl.when(self.z < LINE - 1)
                def _():
                    self.right(s).start()

        @pl.when(self.z + s <= LINE - 1)
        def _():
            slot = self.o_ref.at[self.z + s]
            remote(slot, slot, self.sl.at[s], self.rl.at[s], device(self.z, self.y, 1 - self.c)).wait_recv()
            if s < LINE - 1:

                @pl.when(self.z > 0)
                def _():
                    self.left(s).start()

    def finish(self):
        self.step(LINE - 1)
        self.own().wait()
        for s in range(LINE - 1):

            @pl.when((self.z < LINE - 1) & (self.z >= s))
            def _():
                self.right(s).wait_send()

            @pl.when((self.z > 0) & (self.z + s <= LINE - 1))
            def _():
                self.left(s).wait_send()


class Quad:
    def __init__(self, x_ref, o_ref, send, recv, own_sem):
        self.x_ref, self.o_ref, self.send, self.recv, self.own_sem = x_ref, o_ref, send, recv, own_sem
        self.z, self.y, self.c = place()

    @staticmethod
    def scratch():
        dma = pltpu.SemaphoreType.DMA
        return [dma((4,)), dma((4,)), dma]

    def to(self, d):
        y = 1 - self.y if d & 2 else self.y
        c = 1 - self.c if d & 1 else self.c
        dest = self.o_ref.at[self.y * 2 + self.c]
        return remote(self.x_ref.at[y * 2 + c], dest, self.send.at[d], self.recv.at[d], device(self.z, y, c))

    def own(self):
        q = self.y * 2 + self.c
        return pltpu.make_async_copy(self.x_ref.at[q], self.o_ref.at[q], self.own_sem)

    def start(self):
        for d in range(1, 4):
            self.to(d).start()
        self.own().start()

    def finish(self):
        self.own().wait()
        for d in range(1, 4):
            y = 1 - self.y if d & 2 else self.y
            c = 1 - self.c if d & 1 else self.c
            slot = self.o_ref.at[y * 2 + c]
            remote(slot, slot, self.send.at[d], self.recv.at[d], device(self.z, y, c)).wait_recv()
            self.to(d).wait_send()


class Cross:
    def __init__(self, x_ref, o_ref, ss, rs):
        self.copy = remote(x_ref, o_ref, ss, rs, other_group())

    @staticmethod
    def scratch():
        return [pltpu.SemaphoreType.DMA] * 2

    def start(self):
        self.copy.start()

    def finish(self):
        self.copy.wait()


def start_all(rides):
    for ride in rides:
        ride.start()


def finish_all(rides):
    for ride in rides:
        ride.finish()


def hail_all():
    k, n = lax.axis_index("blk"), 4 * LINE

    def one(i, carry):
        hail({"blk": lax.rem(k + i, n)})
        return carry

    lax.fori_loop(1, n, one, 0)
    x, z, y, c = plane_place()
    for d in range(4):
        hail(plane_device(1 - x, z, 1 - y if d & 2 else y, 1 - c if d & 1 else c))


def hailed_by_all():
    pl.semaphore_wait(pltpu.get_barrier_semaphore(), 4 * LINE - 1 + 4)


class GroupGather:
    def __init__(self, all_ref, sems):
        self.all_ref = all_ref
        self.sr, self.rr, self.sl, self.rl, self.sy, self.ry, self.sc, self.rc, self.se, self.re = sems
        self.z, self.y, self.c = place()
        self.half = all_ref.shape[0] // (4 * LINE * HALVES)

    @staticmethod
    def scratch():
        dma = pltpu.SemaphoreType.DMA
        return [dma((LINE, HALVES))] * 6 + [dma((2 * LINE, HALVES))] * 2 + [dma((2,))] * 2

    def block(self, z, y, h, c=None):
        c = self.c if c is None else c
        return self.all_ref.at[pl.ds((index_of(z, y, c) * HALVES + h) * self.half, self.half)]

    def right(self, s, h):
        block = self.block(self.z - s + 1, self.y, h)
        return remote(block, block, self.sr.at[s, h], self.rr.at[s, h], device(self.z + 1, self.y, self.c))

    def left(self, s, h):
        block = self.block(self.z + s - 1, self.y, h)
        return remote(block, block, self.sl.at[s, h], self.rl.at[s, h], device(self.z - 1, self.y, self.c))

    def across(self, zz, h):
        block = self.block(zz, self.y, h)
        return remote(block, block, self.sy.at[zz, h], self.ry.at[zz, h], device(self.z, 1 - self.y, self.c))

    def detour(self, to_right):
        block = self.block(self.z, 1 - self.y, HALVES - 1)
        where = device(self.z + 1, self.y, self.c) if to_right else device(self.z - 1, self.y, self.c)
        return remote(block, block, self.se.at[to_right], self.re.at[to_right], where)

    def twin(self, zz, yy, h):
        block = self.block(zz, yy, h)
        slot = zz * 2 + yy
        return remote(block, block, self.sc.at[slot, h], self.rc.at[slot, h], device(self.z, self.y, 1 - self.c))

    def arrival(self, block, send, recv):
        remote(block, block, send, recv, device(self.z, self.y, 1 - self.c)).wait_recv()

    def start(self):
        z, y = self.z, self.y
        for h in range(HALVES):

            @pl.when(z < LINE - 1)
            def _():
                self.right(1, h).start()

            @pl.when(z > 0)
            def _():
                self.left(1, h).start()

            self.across(z, h).start()
        for h in range(HALVES):
            self.twin(z, y, h).start()

    def from_across(self, zz, h, distance, to_right=0):
        if distance == 1 and h == HALVES - 1:
            self.arrival(self.block(zz, 1 - self.y, h), self.se.at[to_right], self.re.at[to_right])
        else:
            self.arrival(self.block(zz, 1 - self.y, h), self.sy.at[zz, h], self.ry.at[zz, h])
        if distance == 0 and h == HALVES - 1:

            @pl.when(self.z < LINE - 1)
            def _():
                self.detour(1).start()

            @pl.when(self.z > 0)
            def _():
                self.detour(0).start()

        self.twin(zz, 1 - self.y, h).start()

    def pass_on(self, zz, h, distance):
        if distance > 1 or h < HALVES - 1:
            self.across(zz, h).start()
        self.twin(zz, self.y, h).start()

    def run(self):
        z, y = self.z, self.y
        for s in range(1, LINE):
            for h in range(HALVES):

                @pl.when(z >= s)
                def _():
                    self.arrival(self.block(z - s, y, h), self.sr.at[s, h], self.rr.at[s, h])
                    if s < LINE - 1:

                        @pl.when(z < LINE - 1)
                        def _():
                            self.right(s + 1, h).start()

                    self.pass_on(z - s, h, s)

                @pl.when(z + s <= LINE - 1)
                def _():
                    self.arrival(self.block(z + s, y, h), self.sl.at[s, h], self.rl.at[s, h])
                    if s < LINE - 1:

                        @pl.when(z > 0)
                        def _():
                            self.left(s + 1, h).start()

                    self.pass_on(z + s, h, s)

                if s == 1:
                    self.from_across(z, h, 0)
                else:

                    @pl.when(z >= s - 1)
                    def _():
                        self.from_across(z - s + 1, h, s - 1, 1)

                    @pl.when(z + s - 1 <= LINE - 1)
                    def _():
                        self.from_across(z + s - 1, h, s - 1, 0)

        for h in range(HALVES):

            @pl.when(z >= LINE - 1)
            def _():
                self.from_across(z - LINE + 1, h, LINE - 1)

            @pl.when(z <= 0)
            def _():
                self.from_across(z + LINE - 1, h, LINE - 1)

        for h in range(HALVES):
            for zz in range(LINE):
                for yy in range(2):
                    slot = zz * 2 + yy
                    self.arrival(self.block(zz, yy, h, 1 - self.c), self.sc.at[slot, h], self.rc.at[slot, h])

    def finish(self):
        z = self.z

        @pl.when(z < LINE - 1)
        def _():
            self.detour(1).wait_send()

        @pl.when(z > 0)
        def _():
            self.detour(0).wait_send()

        for h in range(HALVES):
            for zz in range(LINE):
                if h < HALVES - 1:
                    self.across(zz, h).wait_send()
                else:

                    @pl.when((zz != z - 1) & (zz != z + 1))
                    def _():
                        self.across(zz, h).wait_send()

                for yy in range(2):
                    self.twin(zz, yy, h).wait_send()
            for s in range(1, LINE):

                @pl.when((z < LINE - 1) & (z >= s - 1))
                def _():
                    self.right(s, h).wait_send()

                @pl.when((z > 0) & (z + s - 1 <= LINE - 1))
                def _():
                    self.left(s, h).wait_send()


def order_at(z, t):
    table = ((3, 2, 1, 0), (3, 0, 2, 1), (0, 3, 1, 2), (0, 1, 2, 3))
    low = jnp.where(z == 0, table[0][t], table[1][t])
    high = jnp.where(z == 2, table[2][t], table[3][t])
    return jnp.where(z < 2, low, high)


class GroupScatter:
    def __init__(self, part_ref, bufs, sems):
        self.part_ref = part_ref
        self.twins, self.ysend, self.yrecv, self.zsend, self.zrecv, self.esend, self.erecv = bufs
        self.sc, self.rc, self.sy, self.ry, self.sz, self.rzr, self.rzl, self.se, self.re = sems
        self.z, self.y, self.c = place()
        self.half = part_ref.shape[0] // (4 * LINE * HALVES)

    @staticmethod
    def scratch(rows, columns):
        dma = pltpu.SemaphoreType.DMA
        bufs = [pltpu.VMEM((n, rows, columns), jnp.bfloat16) for n in (2 * LINE, LINE, LINE, LINE - 1, LINE + 1)]
        bufs += [pltpu.VMEM((2, rows // HALVES, columns), jnp.bfloat16)] * 2
        return bufs, [dma((2 * LINE, HALVES))] * 2 + [dma((LINE, HALVES))] * 5 + [dma((2,))] * 2

    def part(self, h):
        return pl.ds(h * self.half, self.half)

    def rows(self, t, own_y, c, h):
        y = self.y if own_y else 1 - self.y
        return pl.ds((index_of(order_at(self.z, t), y, c) * HALVES + h) * self.half, self.half)

    def twin(self, t, own_y, h):
        slot = t * 2 + own_y
        source = self.part_ref.at[self.rows(t, own_y, 1 - self.c, h)]
        dest = self.twins.at[slot, self.part(h)]
        return remote(source, dest, self.sc.at[slot, h], self.rc.at[slot, h], device(self.z, self.y, 1 - self.c))

    def across(self, t, h):
        source, dest = self.ysend.at[t, self.part(h)], self.yrecv.at[t, self.part(h)]
        return remote(source, dest, self.sy.at[t, h], self.ry.at[t, h], device(self.z, 1 - self.y, self.c))

    def along(self, d, t, h, to_right):
        sem = self.rzr if to_right else self.rzl
        where = device(self.z + 1, self.y, self.c) if to_right else device(self.z - 1, self.y, self.c)
        slot = d if to_right else self.from_right(d, self.z - 1)
        return remote(self.zsend.at[t, self.part(h)], self.zrecv.at[slot, self.part(h)], self.sz.at[t, h], sem.at[d, h], where)

    @staticmethod
    def from_right(d, z):
        return jnp.where(d == z, LINE, d)

    def arrived(self, d, h, to_right):
        sem = self.rzr if to_right else self.rzl
        slot = self.zrecv.at[d if to_right else self.from_right(d, self.z), self.part(h)]
        remote(slot, slot, self.sz.at[0, h], sem.at[d, h], device(self.z, self.y, 1 - self.c)).wait_recv()

    def wide(self, ref, slot, h):
        return ref[slot, self.part(h)].astype(jnp.float32)

    def chip(self, t, own_y, h):
        return self.part_ref[self.rows(t, own_y, self.c, h)].astype(jnp.float32) + self.wide(self.twins, t * 2 + own_y, h)

    def owner(self, t, own_y, c):
        return index_of(order_at(self.z, t), self.y if own_y else 1 - self.y, c)

    def start(self, t, own_y):
        for h in range(HALVES):
            self.twin(t, own_y, h).start()

    def detour(self, to_right):
        where = device(self.z + 1, self.y, self.c) if to_right else device(self.z - 1, self.y, self.c)
        source, dest = self.esend.at[to_right], self.erecv.at[to_right]
        return remote(source, dest, self.se.at[to_right], self.re.at[to_right], where)

    def detoured(self, t, h):
        d = order_at(self.z, t)
        return (d == self.z + 1, d == self.z - 1) if h == HALVES - 1 and t < LINE - 1 else (False, False)

    def first(self):
        z = self.z
        for t in range(LINE):
            for h in range(HALVES):
                self.twin(t, 0, h).wait_recv()
                if h < HALVES - 1:
                    self.ysend[t, self.part(h)] = self.chip(t, 0, h).astype(jnp.bfloat16)
                    self.across(t, h).start()
                elif t < LINE - 1:
                    right, left = self.detoured(t, h)
                    for to_right, here in ((1, right), (0, left)):

                        @pl.when(here)
                        def _():
                            self.esend[to_right] = self.chip(t, 0, h).astype(jnp.bfloat16)
                            self.detour(to_right).start()

                    @pl.when(jnp.logical_not(right | left))
                    def _():
                        self.ysend[t, self.part(h)] = self.chip(t, 0, h).astype(jnp.bfloat16)
                        self.across(t, h).start()
                else:

                    def added(to_right):
                        slot = self.erecv.at[to_right]
                        where = device(z, self.y, 1 - self.c)
                        remote(slot, slot, self.se.at[to_right], self.re.at[to_right], where).wait_recv()
                        return self.erecv[to_right].astype(jnp.float32)

                    @pl.when(z == 0)
                    def _():
                        self.ysend[t, self.part(h)] = (self.chip(t, 0, h) + added(0)).astype(jnp.bfloat16)

                    @pl.when(z == LINE - 1)
                    def _():
                        self.ysend[t, self.part(h)] = (self.chip(t, 0, h) + added(1)).astype(jnp.bfloat16)

                    @pl.when((z > 0) & (z < LINE - 1))
                    def _():
                        self.ysend[t, self.part(h)] = (self.chip(t, 0, h) + added(0) + added(1)).astype(jnp.bfloat16)

                    self.across(t, h).start()

    def second(self, o_ref, between=()):
        z = self.z
        for t in range(LINE):
            if 0 < t <= len(between):
                between[t - 1]()
            d = order_at(z, t)
            for h in range(HALVES):
                self.twin(t, 1, h).wait_recv()
                if h == HALVES - 1 and t < LINE - 1:
                    right, left = self.detoured(t, h)

                    @pl.when(right | left)
                    def _():
                        self.yrecv[t, self.part(h)] = jnp.zeros((self.half, self.yrecv.shape[2]), jnp.bfloat16)

                    @pl.when(jnp.logical_not(right | left))
                    def _():
                        self.across(t, h).wait_recv()
                else:
                    self.across(t, h).wait_recv()

                def summed(t=t, h=h):
                    return self.chip(t, 1, h) + self.wide(self.yrecv, t, h)

                if t < LINE - 1:
                    for to_right in (True, False):

                        @pl.when((d > z) if to_right else (d < z))
                        def _():
                            first = (z == 0) if to_right else (z == LINE - 1)

                            @pl.when(first)
                            def _():
                                self.zsend[t, self.part(h)] = summed().astype(jnp.bfloat16)

                            @pl.when(jnp.logical_not(first))
                            def _():
                                self.arrived(d, h, to_right)
                                self.zsend[t, self.part(h)] = (summed() + self.wide(self.zrecv, d, h)).astype(jnp.bfloat16)

                            self.along(d, t, h, to_right).start()
                else:

                    @pl.when(z > 0)
                    def _():
                        self.arrived(z, h, True)

                    @pl.when(z < LINE - 1)
                    def _():
                        self.arrived(z, h, False)

                    @pl.when(z == 0)
                    def _():
                        o_ref[self.part(h)] = summed() + self.wide(self.zrecv, LINE, h)

                    @pl.when(z == LINE - 1)
                    def _():
                        o_ref[self.part(h)] = summed() + self.wide(self.zrecv, z, h)

                    @pl.when((z > 0) & (z < LINE - 1))
                    def _():
                        o_ref[self.part(h)] = summed() + self.wide(self.zrecv, z, h) + self.wide(self.zrecv, LINE, h)

    def finish(self):
        for to_right, here in ((1, self.z < LINE - 1), (0, self.z > 0)):

            @pl.when(here)
            def _():
                self.detour(to_right).wait_send()

        for h in range(HALVES):
            for t in range(LINE):
                if h == HALVES - 1 and t < LINE - 1:
                    right, left = self.detoured(t, h)

                    @pl.when(jnp.logical_not(right | left))
                    def _():
                        self.across(t, h).wait_send()
                else:
                    self.across(t, h).wait_send()
                self.twin(t, 0, h).wait_send()
                self.twin(t, 1, h).wait_send()
            for t in range(LINE - 1):
                self.along(0, t, h, True).wait_send()


NN = (((1,), (0,)), ((), ()))
NT = (((1,), (1,)), ((), ()))
TN = (((0,), (0,)), ((), ()))


def mul(a, b, dims=NN):
    return lax.dot_general(a, b, dims, preferred_element_type=jnp.float32)


def tile_at(t):
    return pl.ds(pl.multiple_of(t * TILE, TILE), TILE)


def chunk_at(index, rows=CHUNK):
    return pl.ds(pl.multiple_of(index * rows, rows), rows)


def diagonal(p):
    key = lax.broadcasted_iota(jnp.int32, p.shape, 0)
    query = lax.broadcasted_iota(jnp.int32, p.shape, 1)
    return key <= query


PLANE = 8


def plane_place():
    x = lax.axis_index("batch")
    z, y, c = place()
    return x, z, y, c


def plane_device(x, z, y, c):
    return {"batch": x, "blk": index_of(z, y, c)}


def plane_index(x, y, c):
    return (x * 2 + y) * 2 + c


class PlaneGather:
    def __init__(self, all_ref, sems):
        self.all_ref = all_ref
        self.sx, self.rx, self.sy, self.ry, self.sc, self.rc = sems
        self.x, self.z, self.y, self.c = plane_place()
        self.half = all_ref.shape[0] // (2 * PLANE)

    @staticmethod
    def scratch():
        dma = pltpu.SemaphoreType.DMA
        return [dma((3,))] * 4 + [dma((PLANE,))] * 2

    def piece(self, x, y, c, h):
        return self.all_ref.at[pl.ds(plane_index(x, y, c) * 2 * self.half + h * self.half, self.half)]

    def over_x(self, i):
        x, y, c = self.x, self.y, self.c
        piece = self.piece(x, y if i < 2 else 1 - y, c, (0, 1, 1)[i])
        return remote(piece, piece, self.sx.at[i], self.rx.at[i], plane_device(1 - x, self.z, y, c))

    def over_y(self, i):
        x, y, c = self.x, self.y, self.c
        piece = self.piece(x if i < 2 else 1 - x, y, c, (1, 0, 0)[i])
        return remote(piece, piece, self.sy.at[i], self.ry.at[i], plane_device(x, self.z, 1 - y, c))

    def from_x(self, i):
        x, y, c = self.x, self.y, self.c
        piece = self.piece(1 - x, y if i < 2 else 1 - y, c, (0, 1, 1)[i])
        remote(piece, piece, self.sx.at[i], self.rx.at[i], plane_device(1 - x, self.z, y, c)).wait_recv()

    def from_y(self, i):
        x, y, c = self.x, self.y, self.c
        piece = self.piece(x if i < 2 else 1 - x, 1 - y, c, (1, 0, 0)[i])
        remote(piece, piece, self.sy.at[i], self.ry.at[i], plane_device(x, self.z, 1 - y, c)).wait_recv()

    def twin(self, other_x, other_y, h):
        x = 1 - self.x if other_x else self.x
        y = 1 - self.y if other_y else self.y
        slot = (other_x * 2 + other_y) * 2 + h
        piece = self.piece(x, y, self.c, h)
        return remote(piece, piece, self.sc.at[slot], self.rc.at[slot], plane_device(self.x, self.z, self.y, 1 - self.c))

    def from_twin(self, other_x, other_y, h):
        x = 1 - self.x if other_x else self.x
        y = 1 - self.y if other_y else self.y
        slot = (other_x * 2 + other_y) * 2 + h
        piece = self.piece(x, y, 1 - self.c, h)
        where = plane_device(self.x, self.z, self.y, 1 - self.c)
        remote(piece, piece, self.sc.at[slot], self.rc.at[slot], where).wait_recv()

    def start(self):
        self.over_x(0).start()
        self.over_y(0).start()
        self.over_x(1).start()
        self.over_y(1).start()
        self.twin(0, 0, 0).start()
        self.twin(0, 0, 1).start()

    def near(self):
        self.from_x(0)
        self.over_y(2).start()
        self.twin(1, 0, 0).start()
        self.from_y(0)
        self.over_x(2).start()
        self.twin(0, 1, 1).start()
        self.from_y(1)
        self.twin(0, 1, 0).start()
        for other_y in range(2):
            for h in range(2):
                self.from_twin(0, other_y, h)

    def far(self):
        self.from_x(1)
        self.twin(1, 0, 1).start()
        self.from_x(2)
        self.twin(1, 1, 1).start()
        self.from_y(2)
        self.twin(1, 1, 0).start()
        for other_y in range(2):
            for h in range(2):
                self.from_twin(1, other_y, h)

    def finish(self):
        for i in range(3):
            self.over_x(i).wait_send()
            self.over_y(i).wait_send()
        for other_x in range(2):
            for other_y in range(2):
                for h in range(2):
                    self.twin(other_x, other_y, h).wait_send()


class PlaneScatter:
    def __init__(self, part_ref, bufs, sems):
        self.part_ref = part_ref
        self.twins, self.xs, self.xr, self.ys, self.yr = bufs
        self.sx, self.rx, self.sy, self.ry, self.sc, self.rc = sems
        self.x, self.z, self.y, self.c = plane_place()
        self.half = part_ref.shape[0] // (2 * PLANE)

    @staticmethod
    def scratch(rows, columns):
        dma = pltpu.SemaphoreType.DMA
        half = pltpu.VMEM((3, rows // 2, columns), jnp.bfloat16)
        return [pltpu.VMEM((4, rows, columns), jnp.bfloat16)] + [half] * 4, [dma((3,))] * 4 + [dma((4,))] * 2

    def rows(self, which, c, h=None):
        x = self.x if which >= 2 else 1 - self.x
        y = self.y if which % 2 else 1 - self.y
        at = plane_index(x, y, c) * 2 * self.half
        return pl.ds(at, 2 * self.half) if h is None else pl.ds(at + h * self.half, self.half)

    def twin(self, which):
        where = plane_device(self.x, self.z, self.y, 1 - self.c)
        source = self.part_ref.at[self.rows(which, 1 - self.c)]
        return remote(source, self.twins.at[which], self.sc.at[which], self.rc.at[which], where)

    def over_x(self, i):
        return remote(
            self.xs.at[i], self.xr.at[i], self.sx.at[i], self.rx.at[i], plane_device(1 - self.x, self.z, self.y, self.c)
        )

    def over_y(self, i):
        return remote(
            self.ys.at[i], self.yr.at[i], self.sy.at[i], self.ry.at[i], plane_device(self.x, self.z, 1 - self.y, self.c)
        )

    def chip(self, which, h):
        own = self.part_ref[self.rows(which, self.c, h)].astype(jnp.float32)
        return own + self.twins[which, h * self.half : (h + 1) * self.half].astype(jnp.float32)

    def over_first(self):
        self.twin(0).wait_recv()
        self.xs[0] = self.chip(0, 0).astype(jnp.bfloat16)
        self.over_x(0).start()
        self.ys[0] = self.chip(0, 1).astype(jnp.bfloat16)
        self.over_y(0).start()
        self.twin(1).wait_recv()
        self.xs[1] = self.chip(1, 0).astype(jnp.bfloat16)
        self.over_x(1).start()

    def first(self):
        self.twin(2).wait_recv()
        self.ys[1] = self.chip(2, 1).astype(jnp.bfloat16)
        self.over_y(1).start()

    def second(self):
        self.over_x(0).wait_recv()
        self.ys[2] = (self.chip(2, 0) + self.xr[0].astype(jnp.float32)).astype(jnp.bfloat16)
        self.over_y(2).start()
        self.over_y(0).wait_recv()
        self.xs[2] = (self.chip(1, 1) + self.yr[0].astype(jnp.float32)).astype(jnp.bfloat16)
        self.over_x(2).start()

    def finish(self, o_ref):
        half = self.half
        self.twin(3).wait_recv()
        self.over_x(1).wait_recv()
        self.over_y(1).wait_recv()
        self.over_y(2).wait_recv()
        o_ref[0:half] = self.chip(3, 0) + self.xr[1].astype(jnp.float32) + self.yr[2].astype(jnp.float32)
        self.over_x(2).wait_recv()
        o_ref[half : 2 * half] = self.chip(3, 1) + self.yr[1].astype(jnp.float32) + self.xr[2].astype(jnp.float32)
        for which in range(4):
            self.twin(which).wait_send()
        for i in range(3):
            self.over_x(i).wait_send()
            self.over_y(i).wait_send()


class PlanePool:
    def __init__(self, own_ref, got_ref, send, recv):
        self.own_ref, self.got_ref, self.send, self.recv = own_ref, got_ref, send, recv
        self.x, self.z, self.y, self.c = plane_place()

    def others(self):
        for d in range(1, PLANE):
            x = 1 - self.x if d & 4 else self.x
            y = 1 - self.y if d & 2 else self.y
            c = 1 - self.c if d & 1 else self.c
            yield d, x, y, c

    def copies(self):
        slot = self.got_ref.at[plane_index(self.x, self.y, self.c)]
        own = self.own_ref.at[0] if len(self.own_ref.shape) == len(self.got_ref.shape) else self.own_ref
        for d, x, y, c in self.others():
            yield remote(own, slot, self.send.at[d], self.recv.at[d], plane_device(x, self.z, y, c))

    def start(self):
        for copy in self.copies():
            copy.start()
        self.got_ref[plane_index(self.x, self.y, self.c)] = self.own_ref[...].reshape(self.got_ref.shape[1:])

    def finish(self):
        for d, x, y, c in self.others():
            slot = self.got_ref.at[plane_index(x, y, c)]
            remote(slot, slot, self.send.at[d], self.recv.at[d], plane_device(x, self.z, y, c)).wait_recv()
        for copy in self.copies():
            copy.wait_send()


def span_at(th, width):
    return pl.ds(pl.multiple_of(th * width, 128), width)


def units_at(ut):
    return pl.ds(pl.multiple_of(ut * 256, 256), 256)


def mean_and_rate(stat, hidden_all):
    return stat[0:1], lax.rsqrt(stat[1:2] * (1.0 / hidden_all) + EPSILON)


class Refs:
    def __init__(self, **named):
        self.__dict__.update(named)


def launch(call, kernel, inputs, outputs, scratch, collective_id, microseconds, vmem_mib):
    def body(*refs):
        refs = list(refs)
        named = Refs()
        for key in [*inputs, *outputs]:
            setattr(named, key, refs.pop(0))
        for key, what in scratch.items():
            if isinstance(what, list):
                setattr(named, key, [refs.pop(0) for _ in what])
            else:
                setattr(named, key, refs.pop(0))
        kernel(named)

    results = call(
        body,
        out_shape=[shape for shape, _ in outputs.values()],
        in_specs=[pl.BlockSpec(memory_space=space) for _, space in inputs.values()],
        out_specs=[pl.BlockSpec(memory_space=space) for _, space in outputs.values()],
        scratch_shapes=[entry for what in scratch.values() for entry in (what if isinstance(what, list) else [what])],
        cost_estimate=lasting(microseconds),
        compiler_params=pltpu.CompilerParams(
            collective_id=collective_id, has_side_effects=True, vmem_limit_bytes=vmem_mib << 20
        ),
    )(*[array for array, _ in inputs.values()])
    return Refs(**dict(zip(outputs, results)))


def normed(values, gain, shift):
    centred = values - jnp.mean(values, axis=-1, keepdims=True)
    spread = jnp.mean(centred * centred, axis=-1, keepdims=True)
    return centred * lax.rsqrt(spread + EPSILON) * gain + shift


def normed_back(values, gain, grads):
    centred = values - jnp.mean(values, axis=-1, keepdims=True)
    rate = lax.rsqrt(jnp.mean(centred * centred, axis=-1, keepdims=True) + EPSILON)
    unit = centred * rate
    scaled = grads * gain
    back = rate * (
        scaled - jnp.mean(scaled, axis=-1, keepdims=True) - unit * jnp.mean(scaled * unit, axis=-1, keepdims=True)
    )
    return back, jnp.sum(grads * unit, axis=0, keepdims=True), jnp.sum(grads, axis=0, keepdims=True)


def unfold_head(blocks_ref, w_ref):
    for j in range(blocks_ref.shape[0]):
        for part in range(2):
            at = slice(64 * j + 32 * part, 64 * j + 32 * part + 32)
            w_ref[at, 0:128] = blocks_ref[j, :, 128 * part : 128 * part + 128]
            w_ref[at, 128:192] = blocks_ref[j, :, 256 + 64 * part : 320 + 64 * part]


def fold_head(w, head):
    width = w.shape[1] // 3
    at = [slice(part * width + 64 * head, part * width + 64 * head + 64) for part in range(3)]
    halves = [w[0:32], w[32:64]]
    pieces = [half[:, at[part]] for half in halves for part in (0, 2)] + [half[:, at[1]] for half in halves]
    return jnp.concatenate(pieces, axis=1)


def unit_lanes(z, slot):
    return pl.ds(pl.multiple_of(z * PLANE * 128 + slot * 128, 128), 128)


def unit_columns(vectors, slot, column_refs):
    pieces = [vector[:, unit_lanes(z, slot)] for vector in vectors for z in range(LINE)]
    pieces.append(jnp.zeros((16 - len(pieces), 128), jnp.float32))
    turned = jnp.transpose(jnp.concatenate(pieces, axis=0))
    for i, ref in enumerate(column_refs):
        for z in range(LINE):
            ref[128 * z : 128 * z + 128] = turned[:, i * LINE + z : i * LINE + z + 1]


def of_layer(ref, layer):
    return [ref.at[kind, pl.ds(layer, 1)] for kind in range(ref.shape[0])]


def own_head(row, index):
    pair = row[:, pl.ds(pl.multiple_of(index // 2 * 128, 128), 128)]
    return jnp.where(lax.rem(index, 2) == 0, pair[:, 0:64], pair[:, 64:128])


def chunks_of(ref, t):
    per_tile = TILE // CHUNK
    part = ref[pl.ds(t * per_tile, per_tile)]
    return part.reshape(per_tile * part.shape[1], part.shape[2])


def alive(cut, i, j):
    return jnp.where((i >= cut) & (j < cut), NEGATIVE, 0.0)


def natural_rows(slot, zz):
    x, y, c = slot // 4, slot // 2 % 2, slot % 2
    return 64 * index_of(zz, y, c) + 32 * x


def forward_kernel(layer, hidden_all, r):
    first = layer == 0
    x, z, y, c = plane_place()
    index, slot = index_of(z, y, c), plane_index(x, y, c)
    unit_slot = (y * 2 + c) * 2 + x
    rows, columns = r.x_in.shape
    total = r.hb_all.shape[0]
    tiles, chunks, per_tile = total // TILE, total // CHUNK, TILE // CHUNK
    gather = GroupGather(r.hb_all, r.gather_sems)
    hail_all()
    gains, biases = of_layer(r.gains, layer), of_layer(r.biases, layer)
    if first:
        load_qkv = pltpu.make_async_copy(r.w_qkv, r.qkv_in, r.prep_sem.at[0])
        load_qkv.start()
        for l in range(2):
            for q in range(4):
                for zz in range(LINE):
                    source = r.w_up.at[l, :, unit_lanes(zz, q * 2 + x)]
                    dest = r.unit_src.at[l, q, :, pl.ds(zz * 128, 128)]
                    pltpu.make_async_copy(source, dest, r.prep_sem.at[1 + l]).start()
    value = r.x_in[...].astype(jnp.float32)
    r.hb_all[pl.ds(index * rows, rows)] = normed(value, gains[0][...], biases[0][...]).astype(jnp.bfloat16)
    head_ride = Swap(r.head_src.at[0], r.head_blocks, *r.head_sems) if first else None
    down_ride = Share(r.w_down.at[layer, pl.ds(x, 1)], r.down_blocks, *r.down_sems)
    out_ride = Trade(r.w_out.at[layer, pl.ds(x, 1)], r.out_got, *r.out_sems)
    if first:
        quads = [Quad(r.unit_src.at[l], r.unit_quad.at[l], *r.quad_sems[3 * l : 3 * l + 3]) for l in range(2)]
        unit_ride = Share(r.unit_quad.at[pl.ds(0, 1)], r.unit_blocks, *r.unit_sems)
        next_unit_ride = Share(r.unit_quad.at[pl.ds(1, 1)], r.next_unit, *r.next_unit_sems)
        next_head_ride = Swap(r.head_src.at[1], r.next_head, *r.next_head_sems)
    if first:
        load_qkv.wait()
        for head in range(4 * LINE):
            r.head_src[0, head] = fold_head(r.qkv_in[0], head)
    load_head = pltpu.make_async_copy(r.head_blocks, r.head_in, r.load_sem.at[0])
    load_unit = pltpu.make_async_copy(r.unit_blocks, r.unit_in, r.load_sem.at[1])
    load_down = pltpu.make_async_copy(r.down_blocks, r.down_w, r.load_sem.at[2])
    hailed_by_all()
    if first:
        head_ride.start()
    gather.start()
    out_ride.start()
    mids = [r.mid_gain_all.at[pl.ds(layer, 1)], r.mid_bias_all.at[layer, pl.ds(0, 1)], r.mid_bias_all.at[layer, pl.ds(1, 1)]]
    unit_columns(mids, unit_slot, (r.mid_gain, r.mid_shift, r.mid_bias))
    head_bias = [own_head(biases[row], index) for row in (3, 4)] + [jnp.zeros((1, 64), jnp.float32)]
    head_bias = jnp.concatenate(head_bias, axis=1)
    if not first:
        load_head.start()
        r.dy_all[pl.ds(slot * rows, rows)] = r.dy[...]
        load_unit.start()
    if first:
        for l in range(2):
            pltpu.make_async_copy(r.unit_src.at[l], r.unit_src.at[l], r.prep_sem.at[1 + l]).wait()
        quads[0].start()
    gather.run()
    if first:
        quads[0].finish()
        unit_ride.start()
    out_ride.finish()
    out_rows = r.out_all.shape[0] // PLANE
    for zz in range(LINE):
        r.out_all[pl.ds(slot * out_rows + zz * 32, 32)] = r.out_got[zz]
    out_gather = PlaneGather(r.out_all, r.out_gather_sems)
    out_gather.start()
    dy_gather = None if first else PlaneGather(r.dy_all, r.dy_gather_sems)
    if first:
        head_ride.finish()
        load_head.start()
    else:
        dy_gather.start()
    load_head.wait()
    unfold_head(r.head_in, r.head_w)

    def project(t, carry):
        rows_t = (mul(r.hb_all[tile_at(t)], r.head_w[...]) + head_bias).astype(jnp.bfloat16)
        r.flat[pl.ds(t * per_tile, per_tile)] = rows_t.reshape(per_tile, CHUNK, 192)
        return carry

    lax.fori_loop(0, tiles, project, 0)
    def arrange(p, carry):
        r.qvk[p] = r.flat[r.table[p]]
        return carry

    lax.fori_loop(0, chunks, arrange, 0)

    def prepare(t, carry):
        rows_t = chunks_of(r.qvk, t)
        r.queries[tile_at(t)] = rows_t[:, 0:64] * 0.125
        r.keys[tile_at(t)] = rows_t[:, 128:192]
        turned = jnp.transpose(rows_t[:, 0:128].astype(jnp.float32))
        r.values_t[:, tile_at(t)] = turned[64:128].astype(jnp.bfloat16)
        return carry

    lax.fori_loop(0, tiles, prepare, 0)
    cut = r.table[2 * chunks]
    for i in range(tiles):
        at = slice(i * TILE, (i + 1) * TILE)
        query = r.queries[at]

        def block(j, state, masked):
            peak, part, mixed = state
            scores = mul(r.keys[tile_at(j)], query, NT)
            bias = 0.0 if masked else alive(cut, i, j)
            if masked:
                keep = diagonal(scores)
                scores = jnp.where(keep, scores, NEGATIVE)
            new_peak = jnp.maximum(peak, jnp.max(scores, axis=0, keepdims=True) + bias)
            weights = jnp.exp(scores - (new_peak - bias))
            if masked:
                weights = jnp.where(keep, weights, 0.0)
            factor = jnp.exp(peak - new_peak)
            part = part * factor + jnp.sum(weights, axis=0, keepdims=True)
            mixed = mixed * factor + mul(r.values_t[:, tile_at(j)], weights.astype(jnp.bfloat16))
            return (new_peak, part, mixed)

        state = (
            jnp.full((1, TILE), NEGATIVE, jnp.float32),
            jnp.zeros((1, TILE), jnp.float32),
            jnp.zeros((64, TILE), jnp.float32),
        )
        state = block(i, state, True)
        if i > 0:
            state = lax.fori_loop(0, i, functools.partial(block, masked=False), state)
        peak, part, mixed = state
        mixed = mixed / part
        r.lse[:, at] = peak + jnp.log(part)
        r.head_out[:, at] = mixed
        pairs = (jnp.transpose(mixed) * r.scales[layer, index]).reshape(per_tile, 2, CHUNK // 2, 64)
        pairs = jnp.concatenate([pairs[:, 0], pairs[:, 1]], axis=-1).astype(jnp.bfloat16)
        r.pairs[i * per_tile : (i + 1) * per_tile] = pairs
        if i == 2 and first:
            unit_ride.step(1)
        if i == 3:
            out_gather.near()
    if first:
        unit_ride.step(2)
    else:
        dy_gather.near()
    per_block = rows // CHUNK

    def pack(p, carry):
        r.packed[p] = r.pairs[r.table[chunks + p]]
        return carry

    lax.fori_loop(0, chunks, pack, 0)
    mix = Swap(r.packed, r.mixed, *r.mix_sems, per=per_block)
    mix.start()
    out_gather.far()
    if not first:
        dy_gather.far()
    for s in range(PLANE):
        for zz in range(LINE):
            at = natural_rows(s, zz)
            r.out_w[at : at + 32] = r.out_all[s * out_rows + zz * 32 : s * out_rows + zz * 32 + 32]
    out_gather.finish()

    def turn_units():
        for j in range(2 * LINE):
            pair = r.unit_in[j // 2, j % 2 * 2 : j % 2 * 2 + 2].reshape(128, r.unit_in.shape[3])
            r.unit_t[:, 128 * j : 128 * j + 128] = jnp.transpose(pair)

    if first:
        for head in range(4 * LINE):
            r.head_src[1, head] = fold_head(r.qkv_in[1], head)
    else:
        load_unit.wait()
        turn_units()
    saves = [
        pltpu.make_async_copy(source, dest, r.save_sem.at[i])
        for i, (source, dest) in enumerate(
            (
                (r.hb_all, r.hb_all_out), (r.qvk, r.qvk_out), (r.out_w, r.out_w_out), (r.rows_all, r.rows_all_out),
                (r.unit_t, r.unit_t_out), (r.act, r.act_out), (r.slope, r.slope_out), (r.mid, r.mid_out),
            )
        )
    ]
    start_all(saves[:3])
    mix.finish()
    down_ride.start()
    for g in range(columns // 128):
        left, right = (
            r.mixed[h * per_block : (h + 1) * per_block].reshape(rows // 2, 128) for h in (2 * g, 2 * g + 1)
        )
        low = jnp.concatenate([left[:, 0:64], right[:, 0:64]], axis=1)
        high = jnp.concatenate([left[:, 64:128], right[:, 64:128]], axis=1)
        for p in range(per_block):
            at = slice(p * (CHUNK // 2), (p + 1) * (CHUNK // 2))
            r.ab[p * CHUNK : p * CHUNK + CHUNK // 2, 128 * g : 128 * g + 128] = low[at]
            r.ab[p * CHUNK + CHUNK // 2 : (p + 1) * CHUNK, 128 * g : 128 * g + 128] = high[at]
    branch = mul(r.ab[...], r.out_w[...]) + biases[5][...]
    r.branch[...] = branch
    middle = value + normed(branch, gains[1][...], biases[1][...])
    r.middle[...] = middle

    own = pl.ds(slot * rows, rows)
    r.rows_all[own] = normed(middle, gains[2][...], biases[2][...]).astype(jnp.bfloat16)
    plane_gather = PlaneGather(r.rows_all, r.plane_gather_sems)
    plane_scatter = PlaneScatter(r.part, r.plane_bufs, r.plane_sems)
    pool = PlanePool(r.own_stat, r.got_stat, *r.pool_sems)
    plane_gather.start()
    hidden = r.act.shape[0]
    width = r.act.shape[1] // 2
    if first:
        unit_ride.finish()
        load_unit.start()
        quads[1].start()
    down_ride.step(1)
    if first:
        load_unit.wait()
        turn_units()

    def climb(th):
        at = span_at(th, width)

        def units(ut, carry):
            here = units_at(ut)
            upper = mul(r.unit_t[here], r.rows_all[pl.ds(th * width, width)], NT) + r.mid_bias[here]
            chance = 0.5 * (1.0 + lax.erf(upper * (0.5**0.5)))
            r.act[here, at] = upper * chance
            slope = chance + upper * (jnp.exp(-0.5 * upper * upper) * 0.3989422804014327)
            r.slope[here, at] = slope.astype(jnp.bfloat16)
            return carry

        lax.fori_loop(0, hidden // 256, units, 0)
        values = r.act[:, at]
        mean = jnp.mean(values, axis=0, keepdims=True)
        apart = values - mean
        r.own_stat[0:1, at] = mean
        r.own_stat[1:2, at] = jnp.sum(apart * apart, axis=0, keepdims=True)

    plane_gather.near()
    down_ride.step(2)
    climb(x)
    plane_gather.far()
    if first:
        down_ride.finish()
        load_down.start()
        quads[1].finish()
        next_unit_ride.start()
        next_head_ride.start()
    climb(1 - x)
    pool.start()
    if not first:
        down_ride.finish()
        load_down.start()
    start_all(saves[3:7])
    pool.finish()
    if first:
        next_unit_ride.step(1)
    load_down.wait()
    means = [r.got_stat[i, 0:1] for i in range(PLANE)]
    mean = functools.reduce(jnp.add, means) * (1.0 / PLANE)
    apart = functools.reduce(jnp.add, [(m - mean) * (m - mean) for m in means])
    r.stat[0:1] = mean
    r.stat[1:2] = functools.reduce(jnp.add, [r.got_stat[i, 1:2] for i in range(PLANE)]) + apart * float(hidden)

    def descend(th):
        at = span_at(th, width)
        mean, rate = mean_and_rate(r.stat[:, at], hidden_all)

        def units(ut, carry):
            here = units_at(ut)
            low = (r.act[here, at] - mean) * rate * r.mid_gain[here] + r.mid_shift[here]
            r.mid[here, at] = low.astype(jnp.bfloat16)
            return carry

        lax.fori_loop(0, hidden // 256, units, 0)
        down_w = r.down_w[...].reshape(hidden, columns)
        r.part[pl.ds(th * width, width)] = mul(r.mid[:, at], down_w, TN).astype(jnp.bfloat16)

    descend(1 - x)
    plane_scatter.twin(0).start()
    plane_scatter.twin(1).start()
    plane_scatter.over_first()
    descend(x)
    plane_scatter.twin(2).start()
    plane_scatter.twin(3).start()
    if not first:
        dy_gather.finish()
        saves.append(pltpu.make_async_copy(r.dy_all, r.dy_all_out, r.save_sem.at[8]))
    start_all(saves[7:])
    plane_scatter.first()
    if first:
        next_unit_ride.step(2)
    plane_scatter.second()
    plane_scatter.finish(r.result)
    r.y_out[...] = (r.middle[...] + (r.result[...] + biases[6][...])).astype(r.y_out.dtype)
    gather.finish()
    plane_gather.finish()
    for save in saves:
        save.wait()
    if first:
        next_unit_ride.finish()
        next_head_ride.finish()


def layer_forward_kernel(layer, table, x_in, params, blocks, dy, y_type, collective_id):
    rows, columns = x_in.shape
    hidden_all = params.mid_gain.shape[1]
    total, plane_rows, hidden = rows * 4 * LINE, rows * PLANE, hidden_all // PLANE
    vmem, anywhere, smem = pltpu.VMEM, pl.ANY, pltpu.SMEM
    dma = pltpu.SemaphoreType.DMA
    low = lambda *shape: pltpu.VMEM(shape, jnp.bfloat16)
    full = lambda *shape: pltpu.VMEM(shape, jnp.float32)
    low_out = lambda *shape: jax.ShapeDtypeStruct(shape, jnp.bfloat16)
    full_out = lambda *shape: jax.ShapeDtypeStruct(shape, jnp.float32)
    swap_sems, trade_sems, share_sems = Swap.scratch(), Trade.scratch(), Share.scratch()
    inputs = dict(
        table=(table, smem), scales=(params.head_scale, smem), x_in=(x_in, vmem), gains=(params.vec_gain, vmem),
        biases=(params.vec_bias, vmem), mid_gain_all=(params.mid_gain, vmem), mid_bias_all=(params.mid_bias, vmem),
        w_down=(params.w_down, anywhere), w_out=(params.w_out, anywhere),
    )
    head_shape, unit_shape = (4 * LINE, 32, 384), (LINE, 4, columns // (4 * LINE), hidden)
    outputs = dict(
        y_out=(jax.ShapeDtypeStruct((rows, columns), y_type), vmem), branch=(full_out(rows, columns), vmem),
        middle=(full_out(rows, columns), vmem), ab=(low_out(rows, columns), vmem),
        lse=(full_out(1, total), vmem), head_out=(full_out(64, total), vmem),
        stat=(full_out(2, plane_rows), vmem), hb_all_out=(low_out(total, columns), anywhere),
        qvk_out=(low_out(total // CHUNK, CHUNK, 192), anywhere), out_w_out=(low_out(columns, columns), anywhere),
        rows_all_out=(low_out(plane_rows, columns), anywhere), unit_t_out=(low_out(hidden, columns), anywhere),
        act_out=(full_out(hidden, plane_rows), anywhere), slope_out=(low_out(hidden, plane_rows), anywhere),
        mid_out=(low_out(hidden, plane_rows), anywhere), down_blocks=(low_out(LINE, hidden // LINE, columns), anywhere),
    )
    first = layer == 0
    if first:
        inputs.update(w_qkv=(params.w_qkv, anywhere), w_up=(params.w_up, anywhere))
        head_got, unit_got = (low_out(*head_shape), anywhere), (low_out(*unit_shape), anywhere)
        outputs.update(head_blocks=head_got, unit_blocks=unit_got, next_head=head_got, next_unit=unit_got)
    else:
        inputs.update(head_blocks=(blocks.head, anywhere), unit_blocks=(blocks.unit, anywhere), dy=(dy, vmem))
        outputs.update(dy_all_out=(low_out(plane_rows, columns), anywhere))
    plane_bufs, plane_sems = PlaneScatter.scratch(rows, columns)
    scratch = dict(
        hb_all=low(total, columns), flat=low(total // CHUNK, CHUNK, 192),
        qvk=low(total // CHUNK, CHUNK, 192), queries=low(total, 64), keys=low(total, 64),
        values_t=low(64, total), pairs=low(total // CHUNK, CHUNK // 2, 128),
        packed=low(total // CHUNK, CHUNK // 2, 128), mixed=low(total // CHUNK, CHUNK // 2, 128), head_in=low(4 * LINE, 32, 384), head_w=low(columns, 192),
        unit_in=low(*unit_shape), unit_t=low(hidden, columns),
        down_w=low(LINE, hidden // LINE, columns), out_got=low(LINE, 32, columns),
        out_all=low(columns, columns), out_w=low(columns, columns), rows_all=low(plane_rows, columns),
        act=full(hidden, plane_rows), slope=low(hidden, plane_rows), mid=low(hidden, plane_rows),
        part=low(plane_rows, columns), own_stat=full(2, plane_rows), got_stat=full(PLANE, 2, plane_rows),
        result=full(rows, columns), plane_bufs=plane_bufs, plane_sems=plane_sems,
        gather_sems=GroupGather.scratch(), plane_gather_sems=PlaneGather.scratch(),
        out_gather_sems=PlaneGather.scratch(), pool_sems=([dma((PLANE,)), dma((PLANE,))]),
        head_sems=swap_sems, unit_sems=share_sems, next_head_sems=swap_sems, next_unit_sems=share_sems,
        mix_sems=swap_sems, down_sems=share_sems, out_sems=trade_sems, load_sem=dma((3,)),
        save_sem=dma((9,)),
    )
    scratch.update(mid_gain=full(hidden, 1), mid_shift=full(hidden, 1), mid_bias=full(hidden, 1))
    if first:
        scratch.update(qkv_in=low(*params.w_qkv.shape), head_src=low(2, *head_shape), prep_sem=dma((3,)))
        scratch.update(unit_src=low(2, *unit_shape[1:]), unit_quad=low(2, *unit_shape[1:]), quad_sems=Quad.scratch() * 2)
    else:
        scratch.update(dy_all=low(plane_rows, columns), dy_gather_sems=PlaneGather.scratch())
    kernel = functools.partial(forward_kernel, layer, hidden_all)
    call = lambda body, **how: pl.pallas_call(body, name="layer_forward", **how)
    return launch(call, kernel, inputs, outputs, scratch, collective_id, 95, 56)


class TreeSum:
    def __init__(self, own_ref, total_ref, got, part, line, sems):
        self.own_ref, self.total_ref, self.got, self.part, self.line = own_ref, total_ref, got, part, line
        self.to_send, self.to_recv, self.back_send, self.back_recv = sems[0:4]
        self.trade = Trade(part, line, *sems[4:7])
        self.pool = PlanePool(None, got, None, None)
        self.me = plane_index(self.pool.x, self.pool.y, self.pool.c)

    @staticmethod
    def scratch(rows, columns):
        dma = pltpu.SemaphoreType.DMA
        bufs = [pltpu.VMEM((n, rows // PLANE, columns), jnp.float32) for n in (PLANE, 1, LINE)]
        return bufs, [dma((PLANE,))] * 4 + Trade.scratch()

    def slice(self, m):
        rows = self.part.shape[1]
        return pl.ds(pl.multiple_of(m * rows, 8), rows)

    def to(self, d, x, y, c):
        source = self.own_ref.at[self.slice(plane_index(x, y, c))]
        where = plane_device(x, self.pool.z, y, c)
        return remote(source, self.got.at[self.me], self.to_send.at[d], self.to_recv.at[d], where)

    def back(self, d, x, y, c):
        mine = self.total_ref.at[self.me]
        return remote(mine, mine, self.back_send.at[d], self.back_recv.at[d], plane_device(x, self.pool.z, y, c))

    def arrived(self, ref, recv):
        for d, x, y, c in self.pool.others():
            slot = ref.at[plane_index(x, y, c)]
            remote(slot, slot, recv.at[d], recv.at[d], plane_device(x, self.pool.z, y, c)).wait_recv()

    def start(self):
        for other in self.pool.others():
            self.to(*other).start()

    def along_line(self):
        self.arrived(self.got, self.to_recv)
        self.got[self.me] = self.own_ref[self.slice(self.me)]
        self.part[0] = functools.reduce(jnp.add, [self.got[m] for m in range(PLANE)])
        self.trade.start()

    def give_back(self):
        self.trade.finish()
        self.total_ref[self.me] = functools.reduce(jnp.add, [self.line[zz] for zz in range(LINE)])
        for other in self.pool.others():
            self.back(*other).start()

    def finish(self):
        self.arrived(self.total_ref, self.back_recv)
        for other in self.pool.others():
            self.to(*other).wait_send()
            self.back(*other).wait_send()


class QuickSum:
    def __init__(self, own_ref, plane_got, line_got, sems):
        self.own_ref, self.line_got = own_ref, line_got
        self.pool = PlanePool(own_ref, plane_got, *sems[0:2])
        self.trade = Trade(own_ref, line_got, *sems[2:5])
        self.plane_got = plane_got

    @staticmethod
    def scratch(shape):
        dma = pltpu.SemaphoreType.DMA
        got = [pltpu.VMEM((n, *shape), jnp.float32) for n in (PLANE, LINE)]
        return got, [dma((PLANE,))] * 2 + Trade.scratch()

    def run(self, o_ref):
        self.pool.start()
        self.pool.finish()
        self.own_ref[0] = functools.reduce(jnp.add, [self.plane_got[i] for i in range(PLANE)])
        self.trade.start()
        self.trade.finish()
        o_ref[...] = functools.reduce(jnp.add, [self.line_got[zz] for zz in range(LINE)])


OUT_BIAS, DOWN_BIAS, QUERY_BIAS, VALUE_BIAS, SCALES, MID, SMALL = 6, 7, 8, 9, 10, 12, 24


def spread_head(piece, index, width):
    nothing = jnp.zeros_like(piece)
    even = lax.rem(index, 2) == 0
    pair = jnp.concatenate([jnp.where(even, piece, nothing), jnp.where(even, nothing, piece)], axis=1)
    lanes = lax.broadcasted_iota(jnp.int32, (1, width), 1) // 128
    return jnp.where(lanes == index // 2, jnp.concatenate([pair] * (width // 128), axis=1), 0.0)


def backward_kernel(layer, hidden_all, r):
    first = layer == 1
    x, z, y, c = plane_place()
    index, unit_slot = index_of(z, y, c), (y * 2 + c) * 2 + x
    rows, columns = r.dy.shape
    total = r.hb_all_in.shape[0]
    tiles, chunks, per_tile = total // TILE, total // CHUNK, TILE // CHUNK
    hidden, plane_rows = r.act.shape
    width = plane_rows // 2
    dy_all, x_all = r.wide.at[pl.ds(0, plane_rows)], r.wide.at[pl.ds(plane_rows, plane_rows)]
    plane_gather = PlaneGather(dy_all, r.plane_gather_sems)
    plane_scatter = PlaneScatter(r.part, r.plane_bufs, r.plane_sems)
    out_part = r.part.at[pl.ds(0, LINE * PLANE * 32)]
    out_scatter = PlaneScatter(out_part, r.out_bufs, r.out_sems)
    scatter = GroupScatter(r.wide, r.group_bufs, r.group_sems)
    pool = PlanePool(r.own_sums, r.got_sums, *r.pool_sems)
    unit_ride = Swap(r.gup, r.unit_got, *r.unit_sems)
    out_ride = Trade(r.out_own, r.out_got, *r.out_ride_sems)
    head_cross = Cross(r.head_fold, r.head_other, *r.head_cross_sems)
    down_ride = Trade(r.gdown, r.gdown_got, *r.gdown_sems)
    near_rides = [
        Cross(r.unit_near, r.unit_far, *r.unit_cross_sems), Cross(r.down_near, r.down_far, *r.down_cross_sems),
        Cross(r.out_near, r.out_far, *r.out_cross_sems),
    ]
    if not first:
        late_head_ride = Swap(r.late_head, r.late_head_got, *r.late_head_sems)
        head_ride = Swap(r.head_fold, r.head_got, *r.head_sems)
        bulk = TreeSum(r.bulk, r.bulk_out, *r.bulk_bufs, r.bulk_sems)
        rest = QuickSum(r.rest, *r.rest_got, r.rest_sems)
    hail_all()
    gains = of_layer(r.gains, layer)
    r.small[...] = jnp.zeros_like(r.small)
    dy = r.dy[...].astype(jnp.float32)
    dy_low = dy.astype(jnp.bfloat16)
    r.small[DOWN_BIAS : DOWN_BIAS + 1] = jnp.sum(dy_low.astype(jnp.float32), axis=0, keepdims=True)
    if not first:
        dy_all[pl.ds(plane_index(x, y, c) * rows, rows)] = dy_low
    loads = [
        pltpu.make_async_copy(source, dest, r.load_sem.at[i])
        for i, (source, dest) in enumerate(
            (
                (r.down_blocks, r.down_w), (r.act_in, r.act), (r.slope_in, r.slope), (r.unit_t_in, r.unit_t),
                (r.mid_in, r.mid), (r.rows_all_in, x_all), (r.out_w_in, r.out_w), (r.qvk_in, r.qvk),
            )
        )
    ]
    load_dy = pltpu.make_async_copy(r.dy_all_in, dy_all, r.load_sem.at[8]) if first else None
    if first:
        load_dy.start()
    for load in loads[:6]:
        load.start()
    hailed_by_all()
    if not first:
        plane_gather.start()
    for load in loads[6:]:
        load.start()

    def tile_load(t):
        return pltpu.make_async_copy(r.hb_all_in.at[pl.ds(t * TILE, TILE)], r.hb_tiles.at[t % 2], r.tile_sem.at[t % 2])

    tile_load(0).start()
    tile_load(1).start()
    unit_columns([r.mid_gain_all.at[pl.ds(layer, 1)]], unit_slot, [r.mid_gain])
    r.gg[...] = jnp.zeros_like(r.gg)
    r.gs[...] = jnp.zeros_like(r.gs)
    r.gb[...] = jnp.zeros_like(r.gb)
    r.own_sums[...] = jnp.zeros_like(r.own_sums)

    def climb(th):
        at = span_at(th, width)
        mean, rate = mean_and_rate(r.stat[:, at], hidden_all)

        def units(ut, carry):
            here = units_at(ut)
            down_w = r.down_w[pl.ds(ut * 2, 2)].reshape(256, columns)
            dm = mul(down_w, dy_all[pl.ds(th * width, width)], NT)
            r.dmid[here, at] = dm
            vh = (r.act[here, at] - mean) * rate
            r.act[here, at] = vh
            r.gg[here] += jnp.sum(dm * vh, axis=1, keepdims=True)
            r.gs[here] += jnp.sum(dm, axis=1, keepdims=True)
            scaled = dm * r.mid_gain[here]
            r.own_sums[0:1, at] += jnp.sum(scaled, axis=0, keepdims=True)
            r.own_sums[1:2, at] += jnp.sum(scaled * vh, axis=0, keepdims=True)
            return carry

        lax.fori_loop(0, hidden // 256, units, 0)

    if first:
        load_dy.wait()
    else:
        plane_gather.near()
    loads[0].wait()
    loads[1].wait()
    climb(x)
    if not first:
        plane_gather.far()
        late_head_ride.start()
    climb(1 - x)
    pool.start()
    loads[4].wait()
    for ut in range(hidden // 256):
        grad = mul(r.mid[ut * 256 : (ut + 1) * 256], dy_all[...]).astype(jnp.bfloat16)
        r.gdown[2 * ut : 2 * ut + 2] = grad.reshape(2, 128, columns)
    down_ride.start()
    pool.finish()
    r.sums[...] = functools.reduce(jnp.add, [r.got_sums[i] for i in range(PLANE)]) * (1.0 / hidden_all)
    loads[2].wait()
    loads[3].wait()

    def descend(th):
        at = span_at(th, width)
        _, rate = mean_and_rate(r.stat[:, at], hidden_all)
        sum0, sum1 = r.sums[0:1, at], r.sums[1:2, at]

        def units(ut, carry):
            here = units_at(ut)
            dact = rate * (r.dmid[here, at] * r.mid_gain[here] - sum0 - r.act[here, at] * sum1)
            du = (dact * r.slope[here, at].astype(jnp.float32)).astype(jnp.bfloat16)
            r.du[here, at] = du
            r.gb[here] += jnp.sum(du.astype(jnp.float32), axis=1, keepdims=True)
            return carry

        lax.fori_loop(0, hidden // 256, units, 0)
        r.part[pl.ds(th * width, width)] = mul(r.du[:, at], r.unit_t[...], TN).astype(jnp.bfloat16)

    descend(1 - x)
    plane_scatter.twin(0).start()
    plane_scatter.twin(1).start()
    plane_scatter.over_first()
    descend(x)
    plane_scatter.twin(2).start()
    plane_scatter.twin(3).start()
    plane_scatter.first()
    loads[5].wait()
    plane_scatter.second()
    for ut in range(hidden // 256):
        grad = jnp.transpose(mul(r.du[ut * 256 : (ut + 1) * 256], x_all[...])).astype(jnp.bfloat16)
        r.gup[:, :, ut * 256 : (ut + 1) * 256] = grad.reshape(r.gup.shape[0], -1, 256)
    plane_scatter.finish(r.dffn)
    if not first:
        plane_gather.finish()

    back, r.small[2:3], r.small[5:6] = normed_back(r.middle[...], gains[2][...], r.dffn[...])
    r.dmiddle[...] = dy + back
    back, r.small[1:2], r.small[4:5] = normed_back(r.branch[...], gains[1][...], r.dmiddle[...])
    dz = back.astype(jnp.bfloat16)
    r.small[OUT_BIAS : OUT_BIAS + 1] = jnp.sum(dz.astype(jnp.float32), axis=0, keepdims=True)
    loads[6].wait()
    da = mul(dz, r.out_w[...], NT).astype(jnp.bfloat16)
    per_block = rows // CHUNK
    halves = da.reshape(per_block, 2, CHUNK // 2, columns)
    low, high = halves[:, 0].reshape(rows // 2, columns), halves[:, 1].reshape(rows // 2, columns)
    for h in range(columns // 64):
        at = slice(64 * h, 64 * h + 64)
        pairs = jnp.concatenate([low[:, at], high[:, at]], axis=1)
        r.packed[h * per_block : (h + 1) * per_block] = pairs.reshape(per_block, CHUNK // 2, 128)
    mix = Swap(r.packed, r.mixed, *r.mix_sems, per=per_block)
    mix.start()
    out_rows = LINE * 32
    for zz in range(LINE):
        grad = mul(r.ab[:, 256 * zz : 256 * zz + 256], dz, TN).astype(jnp.bfloat16)
        for s in range(PLANE):
            at = natural_rows(s, 0)
            out_part[s * out_rows + zz * 32 : s * out_rows + zz * 32 + 32] = grad[at : at + 32]
    for which in range(4):
        out_scatter.twin(which).start()
    turned = [ref[128 * zz : 128 * zz + 128] for ref in (r.gg, r.gs, r.gb) for zz in range(LINE)]
    turned = jnp.transpose(jnp.concatenate(turned + [jnp.zeros((128, 4), jnp.float32)], axis=1))
    for i in range(3 * LINE):
        r.small[MID + i : MID + i + 1, unit_lanes(0, unit_slot)] = turned[i : i + 1]
    loads[7].wait()
    load_head = pltpu.make_async_copy(r.head_blocks, r.head_fold, r.load_sem.at[6])
    load_head.start()
    scale = r.scales[layer, index]

    def prepare(t, carry):
        at = tile_at(t)
        rows_t = chunks_of(r.qvk, t)
        r.query[at] = rows_t[:, 0:64] * 0.125
        r.values[at] = rows_t[:, 64:128]
        key = rows_t[:, 128:192]
        r.keys[at] = key
        r.keys_t[:, at] = jnp.transpose(key.astype(jnp.float32)).astype(jnp.bfloat16)
        r.dkeys[at] = jnp.zeros((TILE, 64), jnp.float32)
        r.dvalues[at] = jnp.zeros((TILE, 64), jnp.float32)
        return carry

    lax.fori_loop(0, tiles, prepare, 0)
    load_head.wait()
    unfold_head(r.head_fold, r.head_w)
    out_scatter.over_first()
    out_scatter.first()
    mix.finish()
    unit_ride.start()

    def arrange(p, carry):
        r.packed[p] = r.mixed[r.table[p]]
        return carry

    lax.fori_loop(0, chunks, arrange, 0)

    def unpack(t, carry):
        at = tile_at(t)
        pairs = r.packed[pl.ds(t * per_tile, per_tile)].astype(jnp.float32)
        pairs = jnp.concatenate([pairs[:, :, 0:64], pairs[:, :, 64:128]], axis=1).reshape(TILE, 64)
        low = (pairs * scale).astype(jnp.bfloat16)
        r.dout[at] = low
        r.delta[:, at] = jnp.sum(jnp.transpose(low.astype(jnp.float32)) * r.head_out[:, at], axis=0, keepdims=True)
        return carry

    lax.fori_loop(0, tiles, unpack, 0)
    lanes = lax.broadcasted_iota(jnp.int32, (1, columns), 1)
    scale_grad = jnp.sum(r.delta[...], axis=1, keepdims=True) / scale
    r.small[SCALES : SCALES + 1] = jnp.where(lanes == layer * 4 * LINE + index, scale_grad, 0.0)
    cut = r.table[2 * chunks]
    for i in range(tiles):
        at = slice(i * TILE, (i + 1) * TILE)
        query, dout, lse, delta = r.query[at], r.dout[at], r.lse[:, at], r.delta[:, at]

        def block(j, total_dq, masked):
            there = tile_at(j)
            scores = mul(r.keys[there], query, NT)
            weights = jnp.exp(scores - (lse if masked else lse - alive(cut, i, j)))
            if masked:
                weights = jnp.where(diagonal(scores), weights, 0.0)
            dweights = mul(r.values[there], dout, NT)
            dscores = (weights * (dweights - delta)).astype(jnp.bfloat16)
            r.dvalues[there] += mul(weights.astype(jnp.bfloat16), dout)
            r.dkeys[there] += mul(dscores, query)
            return total_dq + mul(r.keys_t[:, there], dscores)

        total_dq = block(i, jnp.zeros((64, TILE), jnp.float32), True)
        if i > 0:
            total_dq = lax.fori_loop(0, i, functools.partial(block, masked=False), total_dq)
        r.dquery_t[:, at] = total_dq * 0.125
        if i == 2:
            out_scatter.second()
    out_sum = r.dffn.at[pl.ds(0, out_rows)]
    out_scatter.finish(out_sum)
    r.out_own[...] = out_sum[...].reshape(r.out_own.shape).astype(jnp.bfloat16)
    out_ride.start()

    head_bias = jnp.zeros((1, 192), jnp.float32)
    for i in range(tiles):
        at = slice(i * TILE, (i + 1) * TILE)
        joined = jnp.concatenate([jnp.transpose(r.dquery_t[:, at]), r.dvalues[at], r.dkeys[at]], axis=1).astype(jnp.bfloat16)
        head_bias += jnp.sum(joined.astype(jnp.float32), axis=0, keepdims=True)
        r.qvk[i * per_tile : (i + 1) * per_tile] = joined.reshape(per_tile, CHUNK, 192)

    r.small[QUERY_BIAS : QUERY_BIAS + 1] = spread_head(head_bias[:, 0:64], index, columns)
    r.small[VALUE_BIAS : VALUE_BIAS + 1] = spread_head(head_bias[:, 64:128], index, columns)

    if not first:
        r.bulk[0:SMALL] = r.small_in[...]
        r.bulk[SMALL : 2 * SMALL] = r.small[...]
        r.bulk[2 * SMALL :] = jnp.zeros((r.bulk.shape[0] - 2 * SMALL, columns), jnp.float32)
        bulk.start()

    def restore(p, carry):
        r.flat[p] = r.qvk[r.table[chunks + p]]
        return carry

    lax.fori_loop(0, chunks, restore, 0)

    def project(owner):
        rows_of = r.flat[pl.ds(owner * per_block, per_block)].reshape(rows, 192)
        r.wide[pl.ds(owner * rows, rows)] = mul(rows_of, r.head_w[...], NT).astype(jnp.bfloat16)

    for own_y in (0, 1):
        for t in range(LINE):
            for other_core in (1, 0):
                project(scatter.owner(t, own_y, 1 - c if other_core else c))
                if other_core:
                    scatter.start(t, own_y)
    for t in range(tiles):
        tile_load(t).wait()
        grad = mul(chunks_of(r.flat, t), r.hb_tiles[t % 2], TN)
        r.gw[...] = grad if t == 0 else r.gw[...] + grad
        if t + 2 < tiles:
            tile_load(t + 2).start()
    turned = jnp.transpose(r.gw[...]).astype(jnp.bfloat16)
    for j in range(r.head_fold.shape[0]):
        for part in range(2):
            piece = turned[64 * j + 32 * part : 64 * j + 32 * part + 32]
            r.head_fold[j, :, 128 * part : 128 * part + 128] = piece[:, 0:128]
            r.head_fold[j, :, 256 + 64 * part : 320 + 64 * part] = piece[:, 128:192]
    head_cross.start()
    scatter.first()
    if not first:
        bulk.along_line()
    down_ride.finish()
    out_ride.finish()
    unit_ride.finish()
    reloads = [
        pltpu.make_async_copy(source, dest, r.load_sem.at[i])
        for i, (source, dest) in enumerate(((r.unit_got, r.gup), (r.gdown_got, r.gdown), (r.out_got, r.out_own)))
    ]
    for load in reloads:
        load.start()
    head_cross.finish()
    both = (r.head_fold[...].astype(jnp.float32) + r.head_other[...].astype(jnp.float32)).astype(jnp.bfloat16)
    if first:
        r.head_sum[...] = both
    else:
        r.head_fold[...] = both
        head_ride.start()
    for load in reloads:
        load.wait()
    for q in range(4):
        parts = [r.gup[zz * 4 + q].astype(jnp.float32) for zz in range(LINE)]
        r.unit_near[q] = functools.reduce(jnp.add, parts).astype(jnp.bfloat16)
    for near, own in ((r.down_near, r.gdown), (r.out_near, r.out_own)):
        near[...] = functools.reduce(jnp.add, [own[zz].astype(jnp.float32) for zz in range(LINE)]).astype(jnp.bfloat16)
    start_all(near_rides)
    scatter.second(r.dffn)
    back, gain_grad, shift_grad = normed_back(r.x_in[...].astype(jnp.float32), gains[0][...], r.dffn[...])
    r.dx[...] = r.dmiddle[...] + back
    r.small[0:1] = gain_grad
    r.small[3:4] = shift_grad
    if not first:
        r.rest[0, 0:1] = gain_grad
        r.rest[0, 1:2] = shift_grad
        bulk.give_back()
        rest.run(r.rest_out)
        bulk.finish()
    scatter.finish()
    if not first:
        head_ride.finish()
        late_head_ride.finish()
    finish_all(near_rides)


def layer_backward_kernel(layer, table, dy, params, record, later, collective_id):
    rows, columns = dy.shape
    hidden_all = params.mid_gain.shape[1]
    total, plane_rows, hidden = rows * 4 * LINE, rows * PLANE, hidden_all // PLANE
    vmem, anywhere, smem = pltpu.VMEM, pl.ANY, pltpu.SMEM
    dma = pltpu.SemaphoreType.DMA
    low = lambda *shape: pltpu.VMEM(shape, jnp.bfloat16)
    full = lambda *shape: pltpu.VMEM(shape, jnp.float32)
    low_out = lambda *shape: jax.ShapeDtypeStruct(shape, jnp.bfloat16)
    full_out = lambda *shape: jax.ShapeDtypeStruct(shape, jnp.float32)
    swap_sems, trade_sems, cross_sems = Swap.scratch(), Trade.scratch(), Cross.scratch()
    unit_shape = (4 * LINE, columns // (4 * LINE), hidden)
    unit_near, down_near, out_near = (4, *unit_shape[1:]), (hidden // LINE, columns), (32, columns)
    down_shape = (LINE, hidden // LINE, columns)
    inputs = dict(
        table=(table, smem), scales=(params.head_scale, smem), dy=(dy, vmem), gains=(params.vec_gain, vmem),
        mid_gain_all=(params.mid_gain, vmem), x_in=(record.x_in, vmem), branch=(record.branch, vmem),
        middle=(record.middle, vmem), ab=(record.ab, vmem), lse=(record.lse, vmem),
        head_out=(record.head_out, vmem), stat=(record.stat, vmem), hb_all_in=(record.hb_all_out, anywhere),
        qvk_in=(record.qvk_out, anywhere), out_w_in=(record.out_w_out, anywhere),
        rows_all_in=(record.rows_all_out, anywhere), unit_t_in=(record.unit_t_out, anywhere),
        act_in=(record.act_out, anywhere), slope_in=(record.slope_out, anywhere),
        mid_in=(record.mid_out, anywhere), down_blocks=(record.down_blocks, anywhere),
        head_blocks=(record.head_blocks, anywhere),
    )
    outputs = dict(
        dx=(full_out(rows, columns), vmem), unit_got=(low_out(*unit_shape), anywhere),
        gdown_got=(low_out(*down_shape), anywhere), out_got=(low_out(LINE, *out_near), anywhere),
        unit_near=(low_out(*unit_near), vmem),
        down_near=(low_out(*down_near), vmem), out_near=(low_out(*out_near), vmem),
        unit_far=(low_out(*unit_near), anywhere), down_far=(low_out(*down_near), anywhere),
        out_far=(low_out(*out_near), anywhere),
    )
    first = layer == 1
    if first:
        inputs.update(dy_all_in=(record.dy_all_out, anywhere))
        outputs.update(small=(full_out(SMALL, columns), vmem), head_sum=(low_out(4 * LINE, 32, 384), vmem))
    else:
        inputs.update(small_in=(later.small, vmem), late_head=(later.head_sum, anywhere))
        outputs.update(head_got=(low_out(4 * LINE, 32, 384), anywhere), late_head_got=(low_out(4 * LINE, 32, 384), anywhere))
        outputs.update(bulk_out=(full_out(PLANE, 8, columns), vmem), rest_out=(full_out(2, columns), vmem))
    plane_bufs, plane_sems = PlaneScatter.scratch(rows, columns)
    out_bufs, out_sems = PlaneScatter.scratch(LINE * 32, columns)
    group_bufs, group_sems = GroupScatter.scratch(rows, columns)
    scratch = dict(
        wide=low(total, columns), down_w=low(*down_shape), act=full(hidden, plane_rows),
        slope=low(hidden, plane_rows), unit_t=low(hidden, columns), mid=low(hidden, plane_rows),
        out_w=low(columns, columns), qvk=low(total // CHUNK, CHUNK, 192), hb_tiles=low(2, TILE, columns),
        dmid=full(hidden, plane_rows), du=low(hidden, plane_rows), part=low(plane_rows, columns),
        own_sums=full(2, plane_rows), got_sums=full(PLANE, 2, plane_rows), sums=full(2, plane_rows),
        gup=low(*unit_shape), gdown=low(*down_shape), dffn=full(rows, columns),
        dmiddle=full(rows, columns), packed=low(total // CHUNK, CHUNK // 2, 128),
        mixed=low(total // CHUNK, CHUNK // 2, 128),
        out_own=low(LINE, 32, columns),
        dout=low(total, 64), delta=full(1, total), query=low(total, 64),
        keys=low(total, 64), values=low(total, 64), keys_t=low(64, total), dkeys=full(total, 64),
        dvalues=full(total, 64), dquery_t=full(64, total), flat=low(total // CHUNK, CHUNK, 192),
        head_w=low(columns, 192), gw=full(192, columns),
        head_other=low(4 * LINE, 32, 384), head_fold=low(4 * LINE, 32, 384),
        plane_bufs=plane_bufs, plane_sems=plane_sems, out_bufs=out_bufs, out_sems=out_sems,
        group_bufs=group_bufs, group_sems=group_sems, plane_gather_sems=PlaneGather.scratch(),
        pool_sems=([dma((PLANE,)), dma((PLANE,))]), unit_sems=swap_sems, gdown_sems=trade_sems, head_sems=swap_sems,
        mix_sems=swap_sems, out_ride_sems=trade_sems, head_cross_sems=cross_sems, load_sem=dma((10,)),
        tile_sem=dma((2,)),
    )
    scratch.update(unit_cross_sems=cross_sems, down_cross_sems=cross_sems, out_cross_sems=cross_sems)
    scratch.update(mid_gain=full(hidden, 1), gg=full(hidden, 1), gs=full(hidden, 1), gb=full(hidden, 1))
    if not first:
        scratch.update(late_head_sems=swap_sems, small=full(SMALL, columns), bulk=full(8 * PLANE, columns), rest=full(1, 2, columns))
        bulk_bufs, bulk_sems = TreeSum.scratch(8 * PLANE, columns)
        scratch.update(bulk_bufs=bulk_bufs, bulk_sems=bulk_sems)
        rest_got, rest_sems = QuickSum.scratch((2, columns))
        scratch.update(rest_got=rest_got, rest_sems=rest_sems)
    kernel = functools.partial(backward_kernel, layer, hidden_all)
    call = lambda body, **how: pl.pallas_call(body, name="layer_backward", **how)
    return launch(call, kernel, inputs, outputs, scratch, collective_id, 105, 63)


def assemble_kernel(r):
    x = lax.axis_index("batch")
    for layer, got in enumerate((r.layer0, r.layer1)):
        head_ref, unit_near, unit_far, down_near, down_far, out_near, out_far = got
        width = 64 * head_ref.shape[0]
        for j in range(0, head_ref.shape[0], 2):
            left, right = head_ref[j].astype(jnp.float32), head_ref[j + 1].astype(jnp.float32)
            for part in range(2):
                for at, source in ((0, 128 * part), (width, 256 + 64 * part), (2 * width, 64 + 128 * part)):
                    pair = jnp.concatenate([left[:, source : source + 64], right[:, source : source + 64]], axis=1)
                    r.qkv[layer, 32 * part : 32 * part + 32, at + j * 64 : at + (j + 2) * 64] = pair
        for half, unit_ref, down_ref, out_ref in ((x, unit_near, down_near, out_near), (1 - x, unit_far, down_far, out_far)):
            for q in range(unit_ref.shape[0]):
                for z in range(LINE):
                    piece = unit_ref[q, :, z * 128 : (z + 1) * 128].astype(jnp.float32)
                    r.up[layer, :, unit_lanes(z, q * 2 + half)] = piece
            for ref, dest in ((down_ref, r.down), (out_ref, r.out)):
                rows = ref.shape[0]
                dest[layer, pl.ds(pl.multiple_of(half * rows, rows), rows)] = ref[...].astype(jnp.float32)
        per = r.bulk.shape[1]
        bulk = r.bulk[SMALL // per * (1 - layer) : SMALL // per * (2 - layer)].reshape(SMALL, -1)
        gain, shift = (r.rest[0:1], r.rest[1:2]) if layer == 0 else (bulk[0:1], bulk[3:4])
        heads = bulk[QUERY_BIAS : VALUE_BIAS + 1]
        gain_rows = jnp.concatenate([gain, bulk[1:3]], axis=0)
        bias_rows = jnp.concatenate([shift, bulk[4:6], heads, bulk[OUT_BIAS : DOWN_BIAS + 1]], axis=0)
        for ref, rows in ((r.vec_gain, gain_rows), (r.vec_bias, bias_rows)):
            for i in range(ref.shape[0]):
                ref[i, layer : layer + 1] = rows[i : i + 1]
        for z in range(LINE):
            at = slice(z * PLANE * 128, (z + 1) * PLANE * 128)
            r.mid_gain[layer : layer + 1, at] = bulk[MID + z : MID + z + 1]
            for i in range(2):
                row = MID + (i + 1) * LINE + z
                r.mid_bias[layer, i : i + 1, at] = bulk[row : row + 1]
        row = bulk[SCALES : SCALES + 1]
        heads_here = r.head_scale.shape[1]
        r.head_scale[layer : layer + 1] = row[:, layer * heads_here : (layer + 1) * heads_here]


def assemble(results, dx, back, shapes):
    vmem, anywhere = pl.BlockSpec(memory_space=pltpu.VMEM), pl.BlockSpec(memory_space=pl.ANY)
    arrays = [results, dx]
    for got, head in zip(back, (back[0].head_got, back[0].late_head_got)):
        arrays += [head, got.unit_near, got.unit_far, got.down_near, got.down_far, got.out_near, got.out_far]

    arrays += [back[0].bulk_out, back[0].rest_out]
    n = len(arrays)

    def body(*refs):
        ins, outs, held, sem = refs[:n], refs[n : n + 11], refs[n + 11 : -1], refs[-1]
        loads = [pltpu.make_async_copy(ins[i], held[i], sem.at[i]) for i in range(n)]
        passes = [pltpu.make_async_copy(held[i], outs[i], sem.at[i]) for i in range(2)]
        for load in loads:
            load.start()
        for load in loads:
            load.wait()
        for copy in passes:
            copy.start()
        qkv, out, up, down, vec_gain, vec_bias, mid_gain, mid_bias, head_scale = outs[2:]
        refs = held[2:]
        assemble_kernel(
            Refs(
                layer0=refs[0:7], layer1=refs[7:14], bulk=refs[14], rest=refs[15], qkv=qkv, out=out, up=up, down=down,
                vec_gain=vec_gain, vec_bias=vec_bias, mid_gain=mid_gain, mid_bias=mid_bias, head_scale=head_scale,
            )
        )
        for copy in passes:
            copy.wait()

    return pl.pallas_call(
        body,
        out_shape=[jax.ShapeDtypeStruct(array.shape, array.dtype) for array in (results, dx)]
        + [jax.ShapeDtypeStruct(shape, jnp.float32) for shape in shapes],
        in_specs=[anywhere] * n,
        out_specs=[anywhere] * 2 + [vmem] * len(shapes),
        scratch_shapes=[pltpu.VMEM(array.shape, array.dtype) for array in arrays] + [pltpu.SemaphoreType.DMA((n,))],
        cost_estimate=lasting(5),
        compiler_params=pltpu.CompilerParams(vmem_limit_bytes=62 << 20),
        name="assemble",
    )(*arrays)


def chunk_table(first_rows, span_of, rows_here):
    blocks = span_of.shape[0]
    first = first_rows[0]
    second = rows_here - first
    row = jnp.arange(blocks * rows_here // CHUNK, dtype=jnp.int32) * CHUNK
    later = row >= first * blocks
    inside = jnp.where(later, row - first * blocks, row)
    length = jnp.where(later, jnp.maximum(second, 1), first)
    span = inside // length
    of_span = (span_of[None, :] == span[:, None]).astype(jnp.int32)
    device_of = jnp.sum(of_span * jnp.arange(blocks, dtype=jnp.int32)[None, :], axis=1)
    source = device_of * rows_here + jnp.where(later, first, 0) + inside - span * length
    within = row % rows_here
    behind = within >= first
    place = jnp.repeat(span_of, rows_here // CHUNK) * jnp.where(behind, second, first) + within
    place = place + jnp.where(behind, first * (blocks - 1), 0)
    return jnp.concatenate([source // CHUNK, place // CHUNK, (first * blocks // TILE)[None]]).astype(jnp.int32)


def travel(
    tokens, grad_out, first_rows, span_of, w_qkv, w_out, w_up, w_down, vec_gain, vec_bias, mid_gain, mid_bias, head_scale
):
    rows_here, row_width = tokens.shape
    table = chunk_table(first_rows, span_of, rows_here)
    params = Refs(
        w_qkv=w_qkv, w_up=w_up, w_out=w_out.reshape(2, 2, -1, row_width), w_down=w_down.reshape(2, 2, -1, row_width),
        vec_gain=vec_gain.transpose(1, 0, 2), vec_bias=vec_bias.transpose(1, 0, 2), mid_gain=mid_gain, mid_bias=mid_bias,
        head_scale=head_scale,
    )
    first = layer_forward_kernel(0, table, tokens, params, None, None, jnp.float32, 0)
    first.x_in = tokens
    blocks = Refs(head=first.next_head, unit=first.next_unit)
    second = layer_forward_kernel(1, table, first.y_out, params, blocks, grad_out, jnp.bfloat16, 1)
    second.x_in, second.head_blocks = first.y_out, first.next_head
    back_second = layer_backward_kernel(1, table, grad_out, params, second, None, 2)
    back_first = layer_backward_kernel(0, table, back_second.dx, params, first, back_second, 3)
    kinds = (w_qkv, w_out, w_up, w_down, params.vec_gain, params.vec_bias, mid_gain, mid_bias, head_scale)
    results = assemble(second.y_out, back_first.dx, [back_first, back_second], [array.shape for array in kinds])
    return (*results[:6], results[6].transpose(1, 0, 2), results[7].transpose(1, 0, 2), *results[8:])


def local(*args):
    tokens, w_qkv = args[0], args[4]
    blocks = lax.axis_size("blk")
    heads = w_qkv.shape[2] // (3 * HEAD_DIM)
    if blocks == heads == 4 * LINE and lax.axis_size("batch") == 2 and tokens.shape[0] * blocks % TILE == 0:
        return travel(*args)
    return general(*args)


def solution(mesh):
    placed = (
        P(("batch", "blk"), None),
        P(("batch", "blk"), None),
        P("batch"),
        P(),
        P(None, "blk", None),
        P(None, "blk", None),
        P(None, "blk", None),
        P(None, "blk", None),
        P(),
        P(),
        P(),
        P(),
        P(),
    )
    return jax.shard_map(
        local,
        mesh=mesh,
        in_specs=placed,
        out_specs=(
            P(("batch", "blk"), None),
            P(("batch", "blk"), None),
            P(None, "blk", None),
            P(None, "blk", None),
            P(None, "blk", None),
            P(None, "blk", None),
            P(),
            P(),
            P(),
            P(),
            P(),
        ),
        check_vma=False,
    )
```

```python
import functools

import jax
import jax.numpy as jnp
from jax import lax
from jax.experimental import pallas as pl
from jax.experimental.pallas import tpu as pltpu
from jax.sharding import PartitionSpec as P

HEAD_DIM = 64


EPSILON = 1e-05
NEGATIVE = -1e30


def shifted(x, axis, by):
    devices = lax.axis_size(axis)
    return lax.ppermute(x, axis, [(i, (i + by) % devices) for i in range(devices)])


def norm_rows(values, gains, shifts):
    average = jnp.mean(values, axis=-1, keepdims=True)
    centered = values - average
    spread = jnp.mean(centered * centered, axis=-1, keepdims=True)
    return centered * lax.rsqrt(spread + EPSILON) * gains + shifts


def mid_piece(upper, gains, shifts):
    return norm_rows(jax.nn.gelu(upper, approximate=False), gains, shifts)


def split_heads(matrix):
    return matrix.reshape(matrix.shape[0], -1, HEAD_DIM)


def block_rows(total_rows):
    chosen = total_rows
    while chosen > 1024 and chosen % 2 == 0:
        chosen = chosen // 2
    return chosen


def row_layout(first_rows, rows_here):
    within = jnp.arange(rows_here, dtype=jnp.int32)
    first_len = first_rows[0]
    second = (within >= first_len).astype(jnp.int32)
    return (second, within - second * first_len)


def visible_pairs(query_seq, query_off, query_span, key_seq, key_off, key_span):
    earlier = key_span[None, :] < query_span[:, None]
    same_span = (key_span[None, :] == query_span[:, None]) & (
        key_off[None, :] <= query_off[:, None]
    )
    return (query_seq[:, None] == key_seq[None, :]) & (earlier | same_span)


def merge_block(state_in, query_heads, keys_block, values_block, visible):
    run_peak, run_total, accumulated = state_in
    query_rows = query_heads.shape[0]
    scores = jnp.einsum(
        "qhd,khd->hqk", query_heads, split_heads(keys_block), preferred_element_type=jnp.float32
    ) * HEAD_DIM ** (-0.5)
    masked = jnp.where(visible[None], scores, NEGATIVE)
    new_peak = jnp.maximum(run_peak, jnp.max(masked, axis=-1))
    weights = jnp.where(visible[None], jnp.exp(masked - new_peak[:, :, None]), 0.0)
    factor = jnp.exp(run_peak - new_peak)
    new_total = run_total * factor + jnp.sum(weights, axis=-1)
    update = jnp.einsum(
        "hqk,khd->qhd",
        weights.astype(jnp.bfloat16),
        split_heads(values_block),
        preferred_element_type=jnp.float32,
    )
    rescaled = split_heads(accumulated) * jnp.transpose(factor)[:, :, None]
    return (new_peak, new_total, (rescaled + update).reshape(query_rows, -1))


def grad_block(query_heads, log_total, delta, dout_heads, keys_block, values_block, visible):
    key_heads = split_heads(keys_block)
    value_heads = split_heads(values_block)
    scores = jnp.einsum(
        "qhd,khd->hqk", query_heads, key_heads, preferred_element_type=jnp.float32
    ) * HEAD_DIM ** (-0.5)
    probs = jnp.where(visible[None], jnp.exp(scores - log_total[:, :, None]), 0.0)
    dprobs = jnp.einsum("qhd,khd->hqk", dout_heads, value_heads, preferred_element_type=jnp.float32)
    dscores = (probs * (dprobs - delta[:, :, None])).astype(jnp.bfloat16)
    add_query = jnp.einsum("hqk,khd->qhd", dscores, key_heads, preferred_element_type=jnp.float32)
    add_keys = jnp.einsum("hqk,qhd->khd", dscores, query_heads, preferred_element_type=jnp.float32)
    add_values = jnp.einsum(
        "hqk,qhd->khd", probs.astype(jnp.bfloat16), dout_heads, preferred_element_type=jnp.float32
    )
    return (
        add_query.reshape(query_heads.shape[0], -1),
        add_keys.reshape(key_heads.shape[0], -1),
        add_values.reshape(key_heads.shape[0], -1),
    )


def unchanged(state_in):
    return state_in


def attention_forward(query_low, keys_low, values_low, layout):
    seq_ids, offsets, span_of, my_span, my_index = layout
    rows_here, row_width = query_low.shape
    heads_here = row_width // HEAD_DIM
    query_heads = split_heads(query_low)
    query_span = jnp.full((rows_here,), my_span, jnp.int32)
    initial = (
        jnp.full((heads_here, rows_here), NEGATIVE, jnp.float32),
        jnp.zeros((heads_here, rows_here), jnp.float32),
        jnp.zeros((rows_here, row_width), jnp.float32),
    )
    running = initial
    key_part = lax.all_gather(keys_low, "blk", axis=0, tiled=True)
    value_part = lax.all_gather(values_low, "blk", axis=0, tiled=True)
    part_rows = key_part.shape[0]
    step_rows = block_rows(part_rows)

    def one_step(state_in, step_index):
        block_start = step_index * step_rows
        global_rows = block_start + jnp.arange(step_rows, dtype=jnp.int32)
        key_span = span_of[global_rows // rows_here]
        local_rows = global_rows % rows_here
        visible = visible_pairs(
            seq_ids, offsets, query_span, seq_ids[local_rows], offsets[local_rows], key_span
        )
        keys_block = lax.dynamic_slice_in_dim(key_part, block_start, step_rows, 0)
        values_block = lax.dynamic_slice_in_dim(value_part, block_start, step_rows, 0)

        def one_compute(inner_state):
            return merge_block(inner_state, query_heads, keys_block, values_block, visible)

        return (lax.cond(jnp.any(key_span <= my_span), one_compute, unchanged, state_in), None)

    running, _ = lax.scan(one_step, running, jnp.arange(part_rows // step_rows, dtype=jnp.int32))
    run_peak, run_total, accumulated = running
    mixed_heads = (split_heads(accumulated) / jnp.transpose(run_total)[:, :, None]).reshape(
        rows_here, row_width
    )
    return (mixed_heads, run_peak + jnp.log(run_total))


def cycle_backward(query_low, keys_low, values_low, log_total, delta, dout_low, layout):
    seq_ids, offsets, span_of, my_span, my_index = layout
    rows_here, row_width = query_low.shape
    blocks_total = lax.axis_size("blk")
    query_heads = split_heads(query_low)
    dout_heads = split_heads(dout_low)
    query_span = jnp.full((rows_here,), my_span, jnp.int32)

    def turn(turn_index, carried):
        keys_now, values_now, dkeys, dvalues, dquery = carried
        source = (my_index - turn_index) % blocks_total
        source_span = span_of[source]
        key_span = jnp.full((rows_here,), source_span, jnp.int32)
        visible = visible_pairs(seq_ids, offsets, query_span, seq_ids, offsets, key_span)

        def turn_compute(inner_state):
            add_query, add_keys, add_values = grad_block(
                query_heads, log_total, delta, dout_heads, keys_now, values_now, visible
            )
            return (
                inner_state[0] + add_query,
                inner_state[1] + add_keys,
                inner_state[2] + add_values,
            )

        dquery, dkeys, dvalues = lax.cond(
            source_span <= my_span, turn_compute, unchanged, (dquery, dkeys, dvalues)
        )
        keys_now, values_now = shifted((keys_now, values_now), "blk", 1)
        dkeys, dvalues = (
            shifted(dkeys.astype(jnp.bfloat16), "blk", 1).astype(dkeys.dtype),
            shifted(dvalues.astype(jnp.bfloat16), "blk", 1).astype(dvalues.dtype),
        )
        return (keys_now, values_now, dkeys, dvalues, dquery)

    zeros_rows = jnp.zeros((rows_here, row_width), jnp.float32)
    result = lax.fori_loop(
        0, blocks_total, turn, (keys_low, values_low, zeros_rows, zeros_rows, zeros_rows)
    )
    return (result[4], result[2], result[3])


def layer_forward(inputs, weights, gains, biases, middle_gain, middle_bias, heads_scale, layout):
    weight_qkv, weight_out, weight_up, weight_down = weights
    row_width = inputs.shape[1]
    normed, pre_pull = jax.vjp(norm_rows, inputs, gains[0], biases[0])
    normed_low = normed.astype(jnp.bfloat16)
    projected = jnp.dot(normed_low, weight_qkv, preferred_element_type=jnp.float32)
    query_low = (projected[:, :row_width] + biases[3]).astype(jnp.bfloat16)
    keys_low = projected[:, row_width : 2 * row_width].astype(jnp.bfloat16)
    values_low = (projected[:, 2 * row_width :] + biases[4]).astype(jnp.bfloat16)
    mixed_heads, log_total = attention_forward(query_low, keys_low, values_low, layout)
    scaled_low = (mixed_heads * jnp.repeat(heads_scale, HEAD_DIM)).astype(jnp.bfloat16)
    branch = jnp.dot(scaled_low, weight_out, preferred_element_type=jnp.float32) + biases[5]
    post_normed, post_pull = jax.vjp(norm_rows, branch, gains[1], biases[1])
    middle_res = inputs + post_normed
    ffn_normed, ffn_pull = jax.vjp(norm_rows, middle_res, gains[2], biases[2])
    ffn_low = ffn_normed.astype(jnp.bfloat16)
    upper = jnp.dot(ffn_low, weight_up, preferred_element_type=jnp.float32) + middle_bias[1]
    middle, mid_pull = jax.vjp(mid_piece, upper, middle_gain, middle_bias[0])
    middle_low = middle.astype(jnp.bfloat16)
    results = middle_res + (
        jnp.dot(middle_low, weight_down, preferred_element_type=jnp.float32) + biases[6]
    )
    record = {
        "pre_pull": pre_pull,
        "normed_low": normed_low,
        "query_low": query_low,
        "keys_low": keys_low,
        "values_low": values_low,
        "log_total": log_total,
        "mixed_heads": mixed_heads,
        "scaled_low": scaled_low,
        "post_pull": post_pull,
        "ffn_pull": ffn_pull,
        "ffn_low": ffn_low,
        "mid_pull": mid_pull,
        "middle_low": middle_low,
        "weights": weights,
    }
    return (results, record)


def layer_backward(d_results, record, weights, heads_scale, layout):
    weight_qkv, weight_out, weight_up, weight_down = weights
    rows_here, row_width = d_results.shape
    d_results_low = d_results.astype(jnp.bfloat16)
    grad_down = jnp.einsum(
        "tf,td->fd", record["middle_low"], d_results_low, preferred_element_type=jnp.float32
    )
    grad_down_bias = jnp.sum(d_results_low, axis=0, dtype=jnp.float32)
    d_middle = jnp.einsum(
        "td,fd->tf", d_results_low, weight_down, preferred_element_type=jnp.float32
    )
    d_upper, grad_mid_gain, grad_mid_shift = record["mid_pull"](d_middle)
    d_upper_low = d_upper.astype(jnp.bfloat16)
    grad_up = jnp.einsum(
        "td,tf->df", record["ffn_low"], d_upper_low, preferred_element_type=jnp.float32
    )
    grad_up_bias = jnp.sum(d_upper_low, axis=0, dtype=jnp.float32)
    d_ffn = jnp.einsum("tf,df->td", d_upper_low, weight_up, preferred_element_type=jnp.float32)
    d_res_part, grad_gain_ffn, grad_shift_ffn = record["ffn_pull"](d_ffn)
    d_middle_res = d_results + d_res_part
    d_branch, grad_gain_post, grad_shift_post = record["post_pull"](d_middle_res)
    d_branch_low = d_branch.astype(jnp.bfloat16)
    grad_out_w = jnp.einsum(
        "tc,td->cd", record["scaled_low"], d_branch_low, preferred_element_type=jnp.float32
    )
    grad_out_bias = jnp.sum(d_branch_low, axis=0, dtype=jnp.float32)
    d_scaled = jnp.einsum("td,cd->tc", d_branch_low, weight_out, preferred_element_type=jnp.float32)
    mixed_heads = record["mixed_heads"]
    grad_heads = jnp.sum((d_scaled * mixed_heads).reshape(rows_here, -1, HEAD_DIM), axis=(0, 2))
    d_mixed_low = (d_scaled * jnp.repeat(heads_scale, HEAD_DIM)).astype(jnp.bfloat16)
    delta = jnp.transpose(
        jnp.sum(
            (d_mixed_low.astype(jnp.float32) * mixed_heads).reshape(rows_here, -1, HEAD_DIM), axis=2
        )
    )
    dquery, dkeys, dvalues = cycle_backward(
        record["query_low"],
        record["keys_low"],
        record["values_low"],
        record["log_total"],
        delta,
        d_mixed_low,
        layout,
    )
    scale_factor = HEAD_DIM ** (-0.5)
    d_proj_low = jnp.concatenate(
        [dquery * scale_factor, dkeys * scale_factor, dvalues], axis=1
    ).astype(jnp.bfloat16)
    grad_qkv = jnp.einsum(
        "tc,te->ce", record["normed_low"], d_proj_low, preferred_element_type=jnp.float32
    )
    grad_q_bias = jnp.sum(d_proj_low[:, :row_width], axis=0, dtype=jnp.float32)
    grad_v_bias = jnp.sum(d_proj_low[:, 2 * row_width :], axis=0, dtype=jnp.float32)
    d_normed = jnp.einsum("te,ce->tc", d_proj_low, weight_qkv, preferred_element_type=jnp.float32)
    d_in_part, grad_gain_pre, grad_shift_pre = record["pre_pull"](d_normed)
    d_inputs = d_middle_res + d_in_part
    big_grads = (grad_qkv, grad_out_w, grad_up, grad_down)
    gain_grads = jnp.stack([grad_gain_pre, grad_gain_post, grad_gain_ffn])
    bias_grads = jnp.stack(
        [
            grad_shift_pre,
            grad_shift_post,
            grad_shift_ffn,
            grad_q_bias,
            grad_v_bias,
            grad_out_bias,
            grad_down_bias,
        ]
    )
    small_grads = (
        gain_grads,
        bias_grads,
        grad_mid_gain,
        jnp.stack([grad_mid_shift, grad_up_bias]),
        grad_heads,
    )
    return (d_inputs, big_grads, small_grads)


def general(
    tokens,
    grad_out,
    first_rows,
    span_of,
    w_qkv,
    w_out,
    w_up,
    w_down,
    vec_gain,
    vec_bias,
    mid_gain,
    mid_bias,
    head_scale,
):
    rows_here = tokens.shape[0]
    my_index = lax.axis_index("blk")
    my_span = span_of[my_index]
    seq_ids, offsets = row_layout(first_rows, rows_here)
    layout = (seq_ids, offsets, span_of, my_span, my_index)
    current = tokens.astype(jnp.float32)
    records = []
    for layer_index in range(2):
        weights = (
            lax.all_gather(w_qkv[layer_index], "blk", axis=0, tiled=True),
            lax.all_gather(w_out[layer_index], "blk", axis=0, tiled=True),
            lax.all_gather(w_up[layer_index], "blk", axis=0, tiled=True),
            lax.all_gather(w_down[layer_index], "blk", axis=0, tiled=True),
        )
        current, record = layer_forward(
            current,
            weights,
            vec_gain[layer_index],
            vec_bias[layer_index],
            mid_gain[layer_index],
            mid_bias[layer_index],
            head_scale[layer_index],
            layout,
        )
        records.append(record)
    results_low = current.astype(jnp.bfloat16)
    d_current = grad_out.astype(jnp.float32)
    shard_grads = [None, None]
    small_grads = [None, None]
    for layer_index in (1, 0):
        weights = (
            lax.all_gather(w_qkv[layer_index], "blk", axis=0, tiled=True),
            lax.all_gather(w_out[layer_index], "blk", axis=0, tiled=True),
            lax.all_gather(w_up[layer_index], "blk", axis=0, tiled=True),
            lax.all_gather(w_down[layer_index], "blk", axis=0, tiled=True),
        )
        d_current, big_grads, small_part = layer_backward(
            d_current, records[layer_index], weights, head_scale[layer_index], layout
        )
        shard_grads[layer_index] = (
            lax.psum_scatter(
                big_grads[0].astype(jnp.bfloat16), "blk", scatter_dimension=0, tiled=True
            ).astype(jnp.float32),
            lax.psum_scatter(
                big_grads[1].astype(jnp.bfloat16), "blk", scatter_dimension=0, tiled=True
            ).astype(jnp.float32),
            lax.psum_scatter(
                big_grads[2].astype(jnp.bfloat16), "blk", scatter_dimension=0, tiled=True
            ).astype(jnp.float32),
            lax.psum_scatter(
                big_grads[3].astype(jnp.bfloat16), "blk", scatter_dimension=0, tiled=True
            ).astype(jnp.float32),
        )
        small_grads[layer_index] = small_part
    stacked_small = [
        jnp.stack([small_grads[0][item_index], small_grads[1][item_index]])
        for item_index in range(5)
    ]
    summed_small = (
        lax.psum(stacked_small[0].astype(jnp.bfloat16), "blk").astype(jnp.float32),
        lax.psum(stacked_small[1].astype(jnp.bfloat16), "blk").astype(jnp.float32),
        lax.psum(stacked_small[2].astype(jnp.bfloat16), "blk").astype(jnp.float32),
        lax.psum(stacked_small[3].astype(jnp.bfloat16), "blk").astype(jnp.float32),
        lax.psum(stacked_small[4].astype(jnp.bfloat16), "blk").astype(jnp.float32),
    )
    stacked_big = [
        jnp.stack([shard_grads[0][item_index], shard_grads[1][item_index]])
        for item_index in range(4)
    ]
    totals = (
        lax.psum(stacked_big[0].astype(jnp.bfloat16), "batch").astype(jnp.float32),
        lax.psum(stacked_big[1].astype(jnp.bfloat16), "batch").astype(jnp.float32),
        lax.psum(stacked_big[2].astype(jnp.bfloat16), "batch").astype(jnp.float32),
        lax.psum(stacked_big[3].astype(jnp.bfloat16), "batch").astype(jnp.float32),
        lax.psum(summed_small[0].astype(jnp.bfloat16), "batch").astype(jnp.float32),
        lax.psum(summed_small[1].astype(jnp.bfloat16), "batch").astype(jnp.float32),
        lax.psum(summed_small[2].astype(jnp.bfloat16), "batch").astype(jnp.float32),
        lax.psum(summed_small[3].astype(jnp.bfloat16), "batch").astype(jnp.float32),
        lax.psum(summed_small[4].astype(jnp.bfloat16), "batch").astype(jnp.float32),
    )
    return (
        results_low,
        d_current,
        totals[0],
        totals[1],
        totals[2],
        totals[3],
        totals[4],
        totals[5],
        totals[6],
        totals[7],
        totals[8],
    )


MESH = pl.DeviceIdType.MESH
LINE = 4
HALVES = 2
CHUNK = 32
TILE = 512


def place():
    k = lax.axis_index("blk")
    return k // 4, lax.rem(k // 2, 2), lax.rem(k, 2)


def index_of(z, y, c):
    return (z * 2 + y) * 2 + c


def device(z, y, c):
    return {"blk": index_of(z, y, c)}


def hail(where):
    pl.semaphore_signal(pltpu.get_barrier_semaphore(), inc=1, device_id=where, device_id_type=MESH)


def other_group():
    return {"batch": 1 - lax.axis_index("batch")}


def lasting(microseconds):
    return pl.CostEstimate(flops=0, bytes_accessed=int(microseconds * 3.5e6), transcendentals=0)


def remote(src, dst, send, recv, where):
    return pltpu.make_async_remote_copy(
        src_ref=src, dst_ref=dst, send_sem=send, recv_sem=recv, device_id=where, device_id_type=MESH
    )


class Swap:
    def __init__(self, x_ref, o_ref, ss, rs, own_sem, per=1):
        self.x_ref, self.o_ref, self.ss, self.rs, self.own_sem = x_ref, o_ref, ss, rs, own_sem
        self.k, self.n, self.per = lax.axis_index("blk"), 4 * LINE, per

    @staticmethod
    def scratch():
        dma = pltpu.SemaphoreType.DMA
        return [dma((4 * LINE,)), dma((4 * LINE,)), dma]

    def source(self, to):
        return self.x_ref.at[pl.ds(lax.rem(to, self.x_ref.shape[0] // self.per) * self.per, self.per)]

    def place(self, at):
        return self.o_ref.at[pl.ds(at * self.per, self.per)]

    def send(self, i):
        to = lax.rem(self.k + i, self.n)
        return remote(self.source(to), self.place(self.k), self.ss.at[i], self.rs.at[i], {"blk": to})

    def receive(self, i):
        at = lax.rem(self.k - i + self.n, self.n)
        return remote(self.place(at), self.place(at), self.ss.at[i], self.rs.at[i], {"blk": at})

    def own(self):
        return pltpu.make_async_copy(self.source(self.k), self.place(self.k), self.own_sem)

    def start(self):
        def one(i, carry):
            self.send(i).start()
            return carry

        lax.fori_loop(1, self.n, one, 0)
        self.own().start()

    def finish(self):
        def one(i, carry):
            self.receive(i).wait_recv()
            self.send(i).wait_send()
            return carry

        self.own().wait()
        lax.fori_loop(1, self.n, one, 0)


class Trade:
    def __init__(self, x_ref, o_ref, ss, rs, own_sem):
        self.x_ref, self.o_ref, self.ss, self.rs, self.own_sem = x_ref, o_ref, ss, rs, own_sem
        self.z, self.y, self.c = place()

    @staticmethod
    def scratch():
        dma = pltpu.SemaphoreType.DMA
        return [dma((LINE,)), dma((LINE,)), dma]

    def source(self, to):
        return self.x_ref.at[lax.rem(to, self.x_ref.shape[0])]

    def send(self, s):
        to = lax.rem(self.z + s, LINE)
        return remote(self.source(to), self.o_ref.at[self.z], self.ss.at[s], self.rs.at[s], device(to, self.y, self.c))

    def own(self):
        return pltpu.make_async_copy(self.source(self.z), self.o_ref.at[self.z], self.own_sem)

    def start(self):
        for s in range(1, LINE):
            self.send(s).start()
        self.own().start()

    def finish(self):
        self.own().wait()
        for s in range(1, LINE):
            at = lax.rem(self.z - s + LINE, LINE)
            slot = self.o_ref.at[at]
            remote(slot, slot, self.ss.at[s], self.rs.at[s], device(at, self.y, self.c)).wait_recv()
            self.send(s).wait_send()


class Share:
    def __init__(self, x_ref, o_ref, sr, rr, sl, rl, own_sem):
        self.x_ref, self.o_ref, self.own_sem = x_ref, o_ref, own_sem
        self.sr, self.rr, self.sl, self.rl = sr, rr, sl, rl
        self.z, self.y, self.c = place()

    @staticmethod
    def scratch():
        dma = pltpu.SemaphoreType.DMA
        return [dma((LINE,))] * 4 + [dma]

    def right(self, s):
        slot = self.o_ref.at[self.z - s]
        source = self.x_ref.at[0] if s == 0 else slot
        return remote(source, slot, self.sr.at[s], self.rr.at[s + 1], device(self.z + 1, self.y, self.c))

    def left(self, s):
        slot = self.o_ref.at[self.z + s]
        source = self.x_ref.at[0] if s == 0 else slot
        return remote(source, slot, self.sl.at[s], self.rl.at[s + 1], device(self.z - 1, self.y, self.c))

    def own(self):
        return pltpu.make_async_copy(self.x_ref.at[0], self.o_ref.at[self.z], self.own_sem)

    def start(self):
        self.own().start()

        @pl.when(self.z < LINE - 1)
        def _():
            self.right(0).start()

        @pl.when(self.z > 0)
        def _():
            self.left(0).start()

    def step(self, s):
        @pl.when(self.z >= s)
        def _():
            slot = self.o_ref.at[self.z - s]
            remote(slot, slot, self.sr.at[s], self.rr.at[s], device(self.z, self.y, 1 - self.c)).wait_recv()
            if s < LINE - 1:

                @pl.when(self.z < LINE - 1)
                def _():
                    self.right(s).start()

        @pl.when(self.z + s <= LINE - 1)
        def _():
            slot = self.o_ref.at[self.z + s]
            remote(slot, slot, self.sl.at[s], self.rl.at[s], device(self.z, self.y, 1 - self.c)).wait_recv()
            if s < LINE - 1:

                @pl.when(self.z > 0)
                def _():
                    self.left(s).start()

    def finish(self):
        self.step(LINE - 1)
        self.own().wait()
        for s in range(LINE - 1):

            @pl.when((self.z < LINE - 1) & (self.z >= s))
            def _():
                self.right(s).wait_send()

            @pl.when((self.z > 0) & (self.z + s <= LINE - 1))
            def _():
                self.left(s).wait_send()


class Quad:
    def __init__(self, x_ref, o_ref, send, recv, own_sem):
        self.x_ref, self.o_ref, self.send, self.recv, self.own_sem = x_ref, o_ref, send, recv, own_sem
        self.z, self.y, self.c = place()

    @staticmethod
    def scratch():
        dma = pltpu.SemaphoreType.DMA
        return [dma((4,)), dma((4,)), dma]

    def to(self, d):
        y = 1 - self.y if d & 2 else self.y
        c = 1 - self.c if d & 1 else self.c
        dest = self.o_ref.at[self.y * 2 + self.c]
        return remote(self.x_ref.at[y * 2 + c], dest, self.send.at[d], self.recv.at[d], device(self.z, y, c))

    def own(self):
        q = self.y * 2 + self.c
        return pltpu.make_async_copy(self.x_ref.at[q], self.o_ref.at[q], self.own_sem)

    def start(self):
        for d in range(1, 4):
            self.to(d).start()
        self.own().start()

    def finish(self):
        self.own().wait()
        for d in range(1, 4):
            y = 1 - self.y if d & 2 else self.y
            c = 1 - self.c if d & 1 else self.c
            slot = self.o_ref.at[y * 2 + c]
            remote(slot, slot, self.send.at[d], self.recv.at[d], device(self.z, y, c)).wait_recv()
            self.to(d).wait_send()


class Cross:
    def __init__(self, x_ref, o_ref, ss, rs):
        self.copy = remote(x_ref, o_ref, ss, rs, other_group())

    @staticmethod
    def scratch():
        return [pltpu.SemaphoreType.DMA] * 2

    def start(self):
        self.copy.start()

    def finish(self):
        self.copy.wait()


def start_all(rides):
    for ride in rides:
        ride.start()


def finish_all(rides):
    for ride in rides:
        ride.finish()


def hail_all():
    k, n = lax.axis_index("blk"), 4 * LINE

    def one(i, carry):
        hail({"blk": lax.rem(k + i, n)})
        return carry

    lax.fori_loop(1, n, one, 0)
    x, z, y, c = plane_place()
    for d in range(4):
        hail(plane_device(1 - x, z, 1 - y if d & 2 else y, 1 - c if d & 1 else c))


def hailed_by_all():
    pl.semaphore_wait(pltpu.get_barrier_semaphore(), 4 * LINE - 1 + 4)


class GroupGather:
    def __init__(self, all_ref, sems):
        self.all_ref = all_ref
        self.sr, self.rr, self.sl, self.rl, self.sy, self.ry, self.sc, self.rc, self.se, self.re = sems
        self.z, self.y, self.c = place()
        self.half = all_ref.shape[0] // (4 * LINE * HALVES)

    @staticmethod
    def scratch():
        dma = pltpu.SemaphoreType.DMA
        return [dma((LINE, HALVES))] * 6 + [dma((2 * LINE, HALVES))] * 2 + [dma((2,))] * 2

    def block(self, z, y, h, c=None):
        c = self.c if c is None else c
        return self.all_ref.at[pl.ds((index_of(z, y, c) * HALVES + h) * self.half, self.half)]

    def right(self, s, h):
        block = self.block(self.z - s + 1, self.y, h)
        return remote(block, block, self.sr.at[s, h], self.rr.at[s, h], device(self.z + 1, self.y, self.c))

    def left(self, s, h):
        block = self.block(self.z + s - 1, self.y, h)
        return remote(block, block, self.sl.at[s, h], self.rl.at[s, h], device(self.z - 1, self.y, self.c))

    def across(self, zz, h):
        block = self.block(zz, self.y, h)
        return remote(block, block, self.sy.at[zz, h], self.ry.at[zz, h], device(self.z, 1 - self.y, self.c))

    def detour(self, to_right):
        block = self.block(self.z, 1 - self.y, HALVES - 1)
        where = device(self.z + 1, self.y, self.c) if to_right else device(self.z - 1, self.y, self.c)
        return remote(block, block, self.se.at[to_right], self.re.at[to_right], where)

    def twin(self, zz, yy, h):
        block = self.block(zz, yy, h)
        slot = zz * 2 + yy
        return remote(block, block, self.sc.at[slot, h], self.rc.at[slot, h], device(self.z, self.y, 1 - self.c))

    def arrival(self, block, send, recv):
        remote(block, block, send, recv, device(self.z, self.y, 1 - self.c)).wait_recv()

    def start(self):
        z, y = self.z, self.y
        for h in range(HALVES):

            @pl.when(z < LINE - 1)
            def _():
                self.right(1, h).start()

            @pl.when(z > 0)
            def _():
                self.left(1, h).start()

            self.across(z, h).start()
        for h in range(HALVES):
            self.twin(z, y, h).start()

    def from_across(self, zz, h, distance, to_right=0):
        if distance == 1 and h == HALVES - 1:
            self.arrival(self.block(zz, 1 - self.y, h), self.se.at[to_right], self.re.at[to_right])
        else:
            self.arrival(self.block(zz, 1 - self.y, h), self.sy.at[zz, h], self.ry.at[zz, h])
        if distance == 0 and h == HALVES - 1:

            @pl.when(self.z < LINE - 1)
            def _():
                self.detour(1).start()

            @pl.when(self.z > 0)
            def _():
                self.detour(0).start()

        self.twin(zz, 1 - self.y, h).start()

    def pass_on(self, zz, h, distance):
        if distance > 1 or h < HALVES - 1:
            self.across(zz, h).start()
        self.twin(zz, self.y, h).start()

    def run(self):
        z, y = self.z, self.y
        for s in range(1, LINE):
            for h in range(HALVES):

                @pl.when(z >= s)
                def _():
                    self.arrival(self.block(z - s, y, h), self.sr.at[s, h], self.rr.at[s, h])
                    if s < LINE - 1:

                        @pl.when(z < LINE - 1)
                        def _():
                            self.right(s + 1, h).start()

                    self.pass_on(z - s, h, s)

                @pl.when(z + s <= LINE - 1)
                def _():
                    self.arrival(self.block(z + s, y, h), self.sl.at[s, h], self.rl.at[s, h])
                    if s < LINE - 1:

                        @pl.when(z > 0)
                        def _():
                            self.left(s + 1, h).start()

                    self.pass_on(z + s, h, s)

                if s == 1:
                    self.from_across(z, h, 0)
                else:

                    @pl.when(z >= s - 1)
                    def _():
                        self.from_across(z - s + 1, h, s - 1, 1)

                    @pl.when(z + s - 1 <= LINE - 1)
                    def _():
                        self.from_across(z + s - 1, h, s - 1, 0)

        for h in range(HALVES):

            @pl.when(z >= LINE - 1)
            def _():
                self.from_across(z - LINE + 1, h, LINE - 1)

            @pl.when(z <= 0)
            def _():
                self.from_across(z + LINE - 1, h, LINE - 1)

        for h in range(HALVES):
            for zz in range(LINE):
                for yy in range(2):
                    slot = zz * 2 + yy
                    self.arrival(self.block(zz, yy, h, 1 - self.c), self.sc.at[slot, h], self.rc.at[slot, h])

    def finish(self):
        z = self.z

        @pl.when(z < LINE - 1)
        def _():
            self.detour(1).wait_send()

        @pl.when(z > 0)
        def _():
            self.detour(0).wait_send()

        for h in range(HALVES):
            for zz in range(LINE):
                if h < HALVES - 1:
                    self.across(zz, h).wait_send()
                else:

                    @pl.when((zz != z - 1) & (zz != z + 1))
                    def _():
                        self.across(zz, h).wait_send()

                for yy in range(2):
                    self.twin(zz, yy, h).wait_send()
            for s in range(1, LINE):

                @pl.when((z < LINE - 1) & (z >= s - 1))
                def _():
                    self.right(s, h).wait_send()

                @pl.when((z > 0) & (z + s - 1 <= LINE - 1))
                def _():
                    self.left(s, h).wait_send()


def order_at(z, t):
    table = ((3, 2, 1, 0), (3, 0, 2, 1), (0, 3, 1, 2), (0, 1, 2, 3))
    low = jnp.where(z == 0, table[0][t], table[1][t])
    high = jnp.where(z == 2, table[2][t], table[3][t])
    return jnp.where(z < 2, low, high)


class GroupScatter:
    def __init__(self, part_ref, bufs, sems):
        self.part_ref = part_ref
        self.twins, self.ysend, self.yrecv, self.zsend, self.zrecv, self.esend, self.erecv = bufs
        self.sc, self.rc, self.sy, self.ry, self.sz, self.rzr, self.rzl, self.se, self.re = sems
        self.z, self.y, self.c = place()
        self.half = part_ref.shape[0] // (4 * LINE * HALVES)

    @staticmethod
    def scratch(rows, columns):
        dma = pltpu.SemaphoreType.DMA
        bufs = [pltpu.VMEM((n, rows, columns), jnp.bfloat16) for n in (2 * LINE, LINE, LINE, LINE - 1, LINE + 1)]
        bufs += [pltpu.VMEM((2, rows // HALVES, columns), jnp.bfloat16)] * 2
        return bufs, [dma((2 * LINE, HALVES))] * 2 + [dma((LINE, HALVES))] * 5 + [dma((2,))] * 2

    def part(self, h):
        return pl.ds(h * self.half, self.half)

    def rows(self, t, own_y, c, h):
        y = self.y if own_y else 1 - self.y
        return pl.ds((index_of(order_at(self.z, t), y, c) * HALVES + h) * self.half, self.half)

    def twin(self, t, own_y, h):
        slot = t * 2 + own_y
        source = self.part_ref.at[self.rows(t, own_y, 1 - self.c, h)]
        dest = self.twins.at[slot, self.part(h)]
        return remote(source, dest, self.sc.at[slot, h], self.rc.at[slot, h], device(self.z, self.y, 1 - self.c))

    def across(self, t, h):
        source, dest = self.ysend.at[t, self.part(h)], self.yrecv.at[t, self.part(h)]
        return remote(source, dest, self.sy.at[t, h], self.ry.at[t, h], device(self.z, 1 - self.y, self.c))

    def along(self, d, t, h, to_right):
        sem = self.rzr if to_right else self.rzl
        where = device(self.z + 1, self.y, self.c) if to_right else device(self.z - 1, self.y, self.c)
        slot = d if to_right else self.from_right(d, self.z - 1)
        return remote(self.zsend.at[t, self.part(h)], self.zrecv.at[slot, self.part(h)], self.sz.at[t, h], sem.at[d, h], where)

    @staticmethod
    def from_right(d, z):
        return jnp.where(d == z, LINE, d)

    def arrived(self, d, h, to_right):
        sem = self.rzr if to_right else self.rzl
        slot = self.zrecv.at[d if to_right else self.from_right(d, self.z), self.part(h)]
        remote(slot, slot, self.sz.at[0, h], sem.at[d, h], device(self.z, self.y, 1 - self.c)).wait_recv()

    def wide(self, ref, slot, h):
        return ref[slot, self.part(h)].astype(jnp.float32)

    def chip(self, t, own_y, h):
        return self.part_ref[self.rows(t, own_y, self.c, h)].astype(jnp.float32) + self.wide(self.twins, t * 2 + own_y, h)

    def owner(self, t, own_y, c):
        return index_of(order_at(self.z, t), self.y if own_y else 1 - self.y, c)

    def start(self, t, own_y):
        for h in range(HALVES):
            self.twin(t, own_y, h).start()

    def detour(self, to_right):
        where = device(self.z + 1, self.y, self.c) if to_right else device(self.z - 1, self.y, self.c)
        source, dest = self.esend.at[to_right], self.erecv.at[to_right]
        return remote(source, dest, self.se.at[to_right], self.re.at[to_right], where)

    def detoured(self, t, h):
        d = order_at(self.z, t)
        return (d == self.z + 1, d == self.z - 1) if h == HALVES - 1 and t < LINE - 1 else (False, False)

    def first(self):
        z = self.z
        for t in range(LINE):
            for h in range(HALVES):
                self.twin(t, 0, h).wait_recv()
                if h < HALVES - 1:
                    self.ysend[t, self.part(h)] = self.chip(t, 0, h).astype(jnp.bfloat16)
                    self.across(t, h).start()
                elif t < LINE - 1:
                    right, left = self.detoured(t, h)
                    for to_right, here in ((1, right), (0, left)):

                        @pl.when(here)
                        def _():
                            self.esend[to_right] = self.chip(t, 0, h).astype(jnp.bfloat16)
                            self.detour(to_right).start()

                    @pl.when(jnp.logical_not(right | left))
                    def _():
                        self.ysend[t, self.part(h)] = self.chip(t, 0, h).astype(jnp.bfloat16)
                        self.across(t, h).start()
                else:

                    def added(to_right):
                        slot = self.erecv.at[to_right]
                        where = device(z, self.y, 1 - self.c)
                        remote(slot, slot, self.se.at[to_right], self.re.at[to_right], where).wait_recv()
                        return self.erecv[to_right].astype(jnp.float32)

                    @pl.when(z == 0)
                    def _():
                        self.ysend[t, self.part(h)] = (self.chip(t, 0, h) + added(0)).astype(jnp.bfloat16)

                    @pl.when(z == LINE - 1)
                    def _():
                        self.ysend[t, self.part(h)] = (self.chip(t, 0, h) + added(1)).astype(jnp.bfloat16)

                    @pl.when((z > 0) & (z < LINE - 1))
                    def _():
                        self.ysend[t, self.part(h)] = (self.chip(t, 0, h) + added(0) + added(1)).astype(jnp.bfloat16)

                    self.across(t, h).start()

    def second(self, o_ref, between=()):
        z = self.z
        for t in range(LINE):
            if 0 < t <= len(between):
                between[t - 1]()
            d = order_at(z, t)
            for h in range(HALVES):
                self.twin(t, 1, h).wait_recv()
                if h == HALVES - 1 and t < LINE - 1:
                    right, left = self.detoured(t, h)

                    @pl.when(right | left)
                    def _():
                        self.yrecv[t, self.part(h)] = jnp.zeros((self.half, self.yrecv.shape[2]), jnp.bfloat16)

                    @pl.when(jnp.logical_not(right | left))
                    def _():
                        self.across(t, h).wait_recv()
                else:
                    self.across(t, h).wait_recv()

                def summed(t=t, h=h):
                    return self.chip(t, 1, h) + self.wide(self.yrecv, t, h)

                if t < LINE - 1:
                    for to_right in (True, False):

                        @pl.when((d > z) if to_right else (d < z))
                        def _():
                            first = (z == 0) if to_right else (z == LINE - 1)

                            @pl.when(first)
                            def _():
                                self.zsend[t, self.part(h)] = summed().astype(jnp.bfloat16)

                            @pl.when(jnp.logical_not(first))
                            def _():
                                self.arrived(d, h, to_right)
                                self.zsend[t, self.part(h)] = (summed() + self.wide(self.zrecv, d, h)).astype(jnp.bfloat16)

                            self.along(d, t, h, to_right).start()
                else:

                    @pl.when(z > 0)
                    def _():
                        self.arrived(z, h, True)

                    @pl.when(z < LINE - 1)
                    def _():
                        self.arrived(z, h, False)

                    @pl.when(z == 0)
                    def _():
                        o_ref[self.part(h)] = summed() + self.wide(self.zrecv, LINE, h)

                    @pl.when(z == LINE - 1)
                    def _():
                        o_ref[self.part(h)] = summed() + self.wide(self.zrecv, z, h)

                    @pl.when((z > 0) & (z < LINE - 1))
                    def _():
                        o_ref[self.part(h)] = summed() + self.wide(self.zrecv, z, h) + self.wide(self.zrecv, LINE, h)

    def finish(self):
        for to_right, here in ((1, self.z < LINE - 1), (0, self.z > 0)):

            @pl.when(here)
            def _():
                self.detour(to_right).wait_send()

        for h in range(HALVES):
            for t in range(LINE):
                if h == HALVES - 1 and t < LINE - 1:
                    right, left = self.detoured(t, h)

                    @pl.when(jnp.logical_not(right | left))
                    def _():
                        self.across(t, h).wait_send()
                else:
                    self.across(t, h).wait_send()
                self.twin(t, 0, h).wait_send()
                self.twin(t, 1, h).wait_send()
            for t in range(LINE - 1):
                self.along(0, t, h, True).wait_send()


NN = (((1,), (0,)), ((), ()))
NT = (((1,), (1,)), ((), ()))
TN = (((0,), (0,)), ((), ()))


def mul(a, b, dims=NN):
    return lax.dot_general(a, b, dims, preferred_element_type=jnp.float32)


def tile_at(t):
    return pl.ds(pl.multiple_of(t * TILE, TILE), TILE)


def chunk_at(index, rows=CHUNK):
    return pl.ds(pl.multiple_of(index * rows, rows), rows)


def diagonal(p):
    key = lax.broadcasted_iota(jnp.int32, p.shape, 0)
    query = lax.broadcasted_iota(jnp.int32, p.shape, 1)
    return key <= query


PLANE = 8


def plane_place():
    x = lax.axis_index("batch")
    z, y, c = place()
    return x, z, y, c


def plane_device(x, z, y, c):
    return {"batch": x, "blk": index_of(z, y, c)}


def plane_index(x, y, c):
    return (x * 2 + y) * 2 + c


class PlaneGather:
    def __init__(self, all_ref, sems):
        self.all_ref = all_ref
        self.sx, self.rx, self.sy, self.ry, self.sc, self.rc = sems
        self.x, self.z, self.y, self.c = plane_place()
        self.half = all_ref.shape[0] // (2 * PLANE)

    @staticmethod
    def scratch():
        dma = pltpu.SemaphoreType.DMA
        return [dma((3,))] * 4 + [dma((PLANE,))] * 2

    def piece(self, x, y, c, h):
        return self.all_ref.at[pl.ds(plane_index(x, y, c) * 2 * self.half + h * self.half, self.half)]

    def over_x(self, i):
        x, y, c = self.x, self.y, self.c
        piece = self.piece(x, y if i < 2 else 1 - y, c, (0, 1, 1)[i])
        return remote(piece, piece, self.sx.at[i], self.rx.at[i], plane_device(1 - x, self.z, y, c))

    def over_y(self, i):
        x, y, c = self.x, self.y, self.c
        piece = self.piece(x if i < 2 else 1 - x, y, c, (1, 0, 0)[i])
        return remote(piece, piece, self.sy.at[i], self.ry.at[i], plane_device(x, self.z, 1 - y, c))

    def from_x(self, i):
        x, y, c = self.x, self.y, self.c
        piece = self.piece(1 - x, y if i < 2 else 1 - y, c, (0, 1, 1)[i])
        remote(piece, piece, self.sx.at[i], self.rx.at[i], plane_device(1 - x, self.z, y, c)).wait_recv()

    def from_y(self, i):
        x, y, c = self.x, self.y, self.c
        piece = self.piece(x if i < 2 else 1 - x, 1 - y, c, (1, 0, 0)[i])
        remote(piece, piece, self.sy.at[i], self.ry.at[i], plane_device(x, self.z, 1 - y, c)).wait_recv()

    def twin(self, other_x, other_y, h):
        x = 1 - self.x if other_x else self.x
        y = 1 - self.y if other_y else self.y
        slot = (other_x * 2 + other_y) * 2 + h
        piece = self.piece(x, y, self.c, h)
        return remote(piece, piece, self.sc.at[slot], self.rc.at[slot], plane_device(self.x, self.z, self.y, 1 - self.c))

    def from_twin(self, other_x, other_y, h):
        x = 1 - self.x if other_x else self.x
        y = 1 - self.y if other_y else self.y
        slot = (other_x * 2 + other_y) * 2 + h
        piece = self.piece(x, y, 1 - self.c, h)
        where = plane_device(self.x, self.z, self.y, 1 - self.c)
        remote(piece, piece, self.sc.at[slot], self.rc.at[slot], where).wait_recv()

    def start(self):
        self.over_x(0).start()
        self.over_y(0).start()
        self.over_x(1).start()
        self.over_y(1).start()
        self.twin(0, 0, 0).start()
        self.twin(0, 0, 1).start()

    def near(self):
        self.from_x(0)
        self.over_y(2).start()
        self.twin(1, 0, 0).start()
        self.from_y(0)
        self.over_x(2).start()
        self.twin(0, 1, 1).start()
        self.from_y(1)
        self.twin(0, 1, 0).start()
        for other_y in range(2):
            for h in range(2):
                self.from_twin(0, other_y, h)

    def far(self):
        self.from_x(1)
        self.twin(1, 0, 1).start()
        self.from_x(2)
        self.twin(1, 1, 1).start()
        self.from_y(2)
        self.twin(1, 1, 0).start()
        for other_y in range(2):
            for h in range(2):
                self.from_twin(1, other_y, h)

    def finish(self):
        for i in range(3):
            self.over_x(i).wait_send()
            self.over_y(i).wait_send()
        for other_x in range(2):
            for other_y in range(2):
                for h in range(2):
                    self.twin(other_x, other_y, h).wait_send()


class PlaneScatter:
    def __init__(self, part_ref, bufs, sems):
        self.part_ref = part_ref
        self.twins, self.xs, self.xr, self.ys, self.yr = bufs
        self.sx, self.rx, self.sy, self.ry, self.sc, self.rc = sems
        self.x, self.z, self.y, self.c = plane_place()
        self.half = part_ref.shape[0] // (2 * PLANE)

    @staticmethod
    def scratch(rows, columns):
        dma = pltpu.SemaphoreType.DMA
        half = pltpu.VMEM((3, rows // 2, columns), jnp.bfloat16)
        return [pltpu.VMEM((4, rows, columns), jnp.bfloat16)] + [half] * 4, [dma((3,))] * 4 + [dma((4,))] * 2

    def rows(self, which, c, h=None):
        x = self.x if which >= 2 else 1 - self.x
        y = self.y if which % 2 else 1 - self.y
        at = plane_index(x, y, c) * 2 * self.half
        return pl.ds(at, 2 * self.half) if h is None else pl.ds(at + h * self.half, self.half)

    def twin(self, which):
        where = plane_device(self.x, self.z, self.y, 1 - self.c)
        source = self.part_ref.at[self.rows(which, 1 - self.c)]
        return remote(source, self.twins.at[which], self.sc.at[which], self.rc.at[which], where)

    def over_x(self, i):
        return remote(
            self.xs.at[i], self.xr.at[i], self.sx.at[i], self.rx.at[i], plane_device(1 - self.x, self.z, self.y, self.c)
        )

    def over_y(self, i):
        return remote(
            self.ys.at[i], self.yr.at[i], self.sy.at[i], self.ry.at[i], plane_device(self.x, self.z, 1 - self.y, self.c)
        )

    def chip(self, which, h):
        own = self.part_ref[self.rows(which, self.c, h)].astype(jnp.float32)
        return own + self.twins[which, h * self.half : (h + 1) * self.half].astype(jnp.float32)

    def over_first(self):
        self.twin(0).wait_recv()
        self.xs[0] = self.chip(0, 0).astype(jnp.bfloat16)
        self.over_x(0).start()
        self.ys[0] = self.chip(0, 1).astype(jnp.bfloat16)
        self.over_y(0).start()
        self.twin(1).wait_recv()
        self.xs[1] = self.chip(1, 0).astype(jnp.bfloat16)
        self.over_x(1).start()

    def first(self):
        self.twin(2).wait_recv()
        self.ys[1] = self.chip(2, 1).astype(jnp.bfloat16)
        self.over_y(1).start()

    def second(self):
        self.over_x(0).wait_recv()
        self.ys[2] = (self.chip(2, 0) + self.xr[0].astype(jnp.float32)).astype(jnp.bfloat16)
        self.over_y(2).start()
        self.over_y(0).wait_recv()
        self.xs[2] = (self.chip(1, 1) + self.yr[0].astype(jnp.float32)).astype(jnp.bfloat16)
        self.over_x(2).start()

    def finish(self, o_ref):
        half = self.half
        self.twin(3).wait_recv()
        self.over_x(1).wait_recv()
        self.over_y(1).wait_recv()
        self.over_y(2).wait_recv()
        o_ref[0:half] = self.chip(3, 0) + self.xr[1].astype(jnp.float32) + self.yr[2].astype(jnp.float32)
        self.over_x(2).wait_recv()
        o_ref[half : 2 * half] = self.chip(3, 1) + self.yr[1].astype(jnp.float32) + self.xr[2].astype(jnp.float32)
        for which in range(4):
            self.twin(which).wait_send()
        for i in range(3):
            self.over_x(i).wait_send()
            self.over_y(i).wait_send()


class PlanePool:
    def __init__(self, own_ref, got_ref, send, recv):
        self.own_ref, self.got_ref, self.send, self.recv = own_ref, got_ref, send, recv
        self.x, self.z, self.y, self.c = plane_place()

    def others(self):
        for d in range(1, PLANE):
            x = 1 - self.x if d & 4 else self.x
            y = 1 - self.y if d & 2 else self.y
            c = 1 - self.c if d & 1 else self.c
            yield d, x, y, c

    def copies(self):
        slot = self.got_ref.at[plane_index(self.x, self.y, self.c)]
        own = self.own_ref.at[0] if len(self.own_ref.shape) == len(self.got_ref.shape) else self.own_ref
        for d, x, y, c in self.others():
            yield remote(own, slot, self.send.at[d], self.recv.at[d], plane_device(x, self.z, y, c))

    def start(self):
        for copy in self.copies():
            copy.start()
        self.got_ref[plane_index(self.x, self.y, self.c)] = self.own_ref[...].reshape(self.got_ref.shape[1:])

    def finish(self):
        for d, x, y, c in self.others():
            slot = self.got_ref.at[plane_index(x, y, c)]
            remote(slot, slot, self.send.at[d], self.recv.at[d], plane_device(x, self.z, y, c)).wait_recv()
        for copy in self.copies():
            copy.wait_send()


def span_at(th, width):
    return pl.ds(pl.multiple_of(th * width, 128), width)


def units_at(ut):
    return pl.ds(pl.multiple_of(ut * 256, 256), 256)


def mean_and_rate(stat, hidden_all):
    return stat[0:1], lax.rsqrt(stat[1:2] * (1.0 / hidden_all) + EPSILON)


class Refs:
    def __init__(self, **named):
        self.__dict__.update(named)


def launch(call, kernel, inputs, outputs, scratch, collective_id, microseconds, vmem_mib):
    def body(*refs):
        refs = list(refs)
        named = Refs()
        for key in [*inputs, *outputs]:
            setattr(named, key, refs.pop(0))
        for key, what in scratch.items():
            if isinstance(what, list):
                setattr(named, key, [refs.pop(0) for _ in what])
            else:
                setattr(named, key, refs.pop(0))
        kernel(named)

    results = call(
        body,
        out_shape=[shape for shape, _ in outputs.values()],
        in_specs=[pl.BlockSpec(memory_space=space) for _, space in inputs.values()],
        out_specs=[pl.BlockSpec(memory_space=space) for _, space in outputs.values()],
        scratch_shapes=[entry for what in scratch.values() for entry in (what if isinstance(what, list) else [what])],
        cost_estimate=lasting(microseconds),
        compiler_params=pltpu.CompilerParams(
            collective_id=collective_id, has_side_effects=True, vmem_limit_bytes=vmem_mib << 20
        ),
    )(*[array for array, _ in inputs.values()])
    return Refs(**dict(zip(outputs, results)))


def normed(values, gain, shift):
    centred = values - jnp.mean(values, axis=-1, keepdims=True)
    spread = jnp.mean(centred * centred, axis=-1, keepdims=True)
    return centred * lax.rsqrt(spread + EPSILON) * gain + shift


def normed_back(values, gain, grads):
    centred = values - jnp.mean(values, axis=-1, keepdims=True)
    rate = lax.rsqrt(jnp.mean(centred * centred, axis=-1, keepdims=True) + EPSILON)
    unit = centred * rate
    scaled = grads * gain
    back = rate * (
        scaled - jnp.mean(scaled, axis=-1, keepdims=True) - unit * jnp.mean(scaled * unit, axis=-1, keepdims=True)
    )
    return back, jnp.sum(grads * unit, axis=0, keepdims=True), jnp.sum(grads, axis=0, keepdims=True)


def unfold_head(blocks_ref, w_ref):
    for j in range(blocks_ref.shape[0]):
        for part in range(2):
            at = slice(64 * j + 32 * part, 64 * j + 32 * part + 32)
            w_ref[at, 0:128] = blocks_ref[j, :, 128 * part : 128 * part + 128]
            w_ref[at, 128:192] = blocks_ref[j, :, 256 + 64 * part : 320 + 64 * part]


def fold_head(w, head):
    width = w.shape[1] // 3
    at = [slice(part * width + 64 * head, part * width + 64 * head + 64) for part in range(3)]
    halves = [w[0:32], w[32:64]]
    pieces = [half[:, at[part]] for half in halves for part in (0, 2)] + [half[:, at[1]] for half in halves]
    return jnp.concatenate(pieces, axis=1)


def unit_lanes(z, slot):
    return pl.ds(pl.multiple_of(z * PLANE * 128 + slot * 128, 128), 128)


def unit_columns(vectors, slot, column_refs):
    pieces = [vector[:, unit_lanes(z, slot)] for vector in vectors for z in range(LINE)]
    pieces.append(jnp.zeros((16 - len(pieces), 128), jnp.float32))
    turned = jnp.transpose(jnp.concatenate(pieces, axis=0))
    for i, ref in enumerate(column_refs):
        for z in range(LINE):
            ref[128 * z : 128 * z + 128] = turned[:, i * LINE + z : i * LINE + z + 1]


def of_layer(ref, layer):
    return [ref.at[kind, pl.ds(layer, 1)] for kind in range(ref.shape[0])]


def own_head(row, index):
    pair = row[:, pl.ds(pl.multiple_of(index // 2 * 128, 128), 128)]
    return jnp.where(lax.rem(index, 2) == 0, pair[:, 0:64], pair[:, 64:128])


def chunks_of(ref, t):
    per_tile = TILE // CHUNK
    part = ref[pl.ds(t * per_tile, per_tile)]
    return part.reshape(per_tile * part.shape[1], part.shape[2])


def alive(cut, i, j):
    return jnp.where((i >= cut) & (j < cut), NEGATIVE, 0.0)


def natural_rows(slot, zz):
    x, y, c = slot // 4, slot // 2 % 2, slot % 2
    return 64 * index_of(zz, y, c) + 32 * x


def forward_kernel(layer, hidden_all, r):
    first = layer == 0
    x, z, y, c = plane_place()
    index, slot = index_of(z, y, c), plane_index(x, y, c)
    unit_slot = (y * 2 + c) * 2 + x
    rows, columns = r.x_in.shape
    total = r.hb_all.shape[0]
    tiles, chunks, per_tile = total // TILE, total // CHUNK, TILE // CHUNK
    gather = GroupGather(r.hb_all, r.gather_sems)
    hail_all()
    gains, biases = of_layer(r.gains, layer), of_layer(r.biases, layer)
    if first:
        load_qkv = pltpu.make_async_copy(r.w_qkv, r.qkv_in, r.prep_sem.at[0])
        load_qkv.start()
        for l in range(2):
            for q in range(4):
                for zz in range(LINE):
                    source = r.w_up.at[l, :, unit_lanes(zz, q * 2 + x)]
                    dest = r.unit_src.at[l, q, :, pl.ds(zz * 128, 128)]
                    pltpu.make_async_copy(source, dest, r.prep_sem.at[1 + l]).start()
    value = r.x_in[...].astype(jnp.float32)
    r.hb_all[pl.ds(index * rows, rows)] = normed(value, gains[0][...], biases[0][...]).astype(jnp.bfloat16)
    head_ride = Swap(r.head_src.at[0], r.head_blocks, *r.head_sems) if first else None
    down_ride = Share(r.w_down.at[layer, pl.ds(x, 1)], r.down_blocks, *r.down_sems)
    out_ride = Trade(r.w_out.at[layer, pl.ds(x, 1)], r.out_got, *r.out_sems)
    if first:
        quads = [Quad(r.unit_src.at[l], r.unit_quad.at[l], *r.quad_sems[3 * l : 3 * l + 3]) for l in range(2)]
        unit_ride = Share(r.unit_quad.at[pl.ds(0, 1)], r.unit_blocks, *r.unit_sems)
        next_unit_ride = Share(r.unit_quad.at[pl.ds(1, 1)], r.next_unit, *r.next_unit_sems)
        next_head_ride = Swap(r.head_src.at[1], r.next_head, *r.next_head_sems)
    if first:
        load_qkv.wait()
        for head in range(4 * LINE):
            r.head_src[0, head] = fold_head(r.qkv_in[0], head)
    load_head = pltpu.make_async_copy(r.head_blocks, r.head_in, r.load_sem.at[0])
    load_unit = pltpu.make_async_copy(r.unit_blocks, r.unit_in, r.load_sem.at[1])
    load_down = pltpu.make_async_copy(r.down_blocks, r.down_w, r.load_sem.at[2])
    hailed_by_all()
    if first:
        head_ride.start()
    gather.start()
    out_ride.start()
    mids = [r.mid_gain_all.at[pl.ds(layer, 1)], r.mid_bias_all.at[layer, pl.ds(0, 1)], r.mid_bias_all.at[layer, pl.ds(1, 1)]]
    unit_columns(mids, unit_slot, (r.mid_gain, r.mid_shift, r.mid_bias))
    head_bias = [own_head(biases[row], index) for row in (3, 4)] + [jnp.zeros((1, 64), jnp.float32)]
    head_bias = jnp.concatenate(head_bias, axis=1)
    if not first:
        load_head.start()
        r.dy_all[pl.ds(slot * rows, rows)] = r.dy[...]
        load_unit.start()
    if first:
        for l in range(2):
            pltpu.make_async_copy(r.unit_src.at[l], r.unit_src.at[l], r.prep_sem.at[1 + l]).wait()
        quads[0].start()
    gather.run()
    if first:
        quads[0].finish()
        unit_ride.start()
    out_ride.finish()
    out_rows = r.out_all.shape[0] // PLANE
    for zz in range(LINE):
        r.out_all[pl.ds(slot * out_rows + zz * 32, 32)] = r.out_got[zz]
    out_gather = PlaneGather(r.out_all, r.out_gather_sems)
    out_gather.start()
    dy_gather = None if first else PlaneGather(r.dy_all, r.dy_gather_sems)
    if first:
        head_ride.finish()
        load_head.start()
    else:
        dy_gather.start()
    load_head.wait()
    unfold_head(r.head_in, r.head_w)

    def project(t, carry):
        rows_t = (mul(r.hb_all[tile_at(t)], r.head_w[...]) + head_bias).astype(jnp.bfloat16)
        r.flat[pl.ds(t * per_tile, per_tile)] = rows_t.reshape(per_tile, CHUNK, 192)
        return carry

    lax.fori_loop(0, tiles, project, 0)
    def arrange(p, carry):
        r.qvk[p] = r.flat[r.table[p]]
        return carry

    lax.fori_loop(0, chunks, arrange, 0)

    def prepare(t, carry):
        rows_t = chunks_of(r.qvk, t)
        r.queries[tile_at(t)] = rows_t[:, 0:64] * 0.125
        r.keys[tile_at(t)] = rows_t[:, 128:192]
        turned = jnp.transpose(rows_t[:, 0:128].astype(jnp.float32))
        r.values_t[:, tile_at(t)] = turned[64:128].astype(jnp.bfloat16)
        return carry

    lax.fori_loop(0, tiles, prepare, 0)
    cut = r.table[2 * chunks]
    for i in range(tiles):
        at = slice(i * TILE, (i + 1) * TILE)
        query = r.queries[at]

        def block(j, state, masked):
            peak, part, mixed = state
            scores = mul(r.keys[tile_at(j)], query, NT)
            bias = 0.0 if masked else alive(cut, i, j)
            if masked:
                keep = diagonal(scores)
                scores = jnp.where(keep, scores, NEGATIVE)
            new_peak = jnp.maximum(peak, jnp.max(scores, axis=0, keepdims=True) + bias)
            weights = jnp.exp(scores - (new_peak - bias))
            if masked:
                weights = jnp.where(keep, weights, 0.0)
            factor = jnp.exp(peak - new_peak)
            part = part * factor + jnp.sum(weights, axis=0, keepdims=True)
            mixed = mixed * factor + mul(r.values_t[:, tile_at(j)], weights.astype(jnp.bfloat16))
            return (new_peak, part, mixed)

        state = (
            jnp.full((1, TILE), NEGATIVE, jnp.float32),
            jnp.zeros((1, TILE), jnp.float32),
            jnp.zeros((64, TILE), jnp.float32),
        )
        state = block(i, state, True)
        if i > 0:
            state = lax.fori_loop(0, i, functools.partial(block, masked=False), state)
        peak, part, mixed = state
        mixed = mixed / part
        r.lse[:, at] = peak + jnp.log(part)
        r.head_out[:, at] = mixed
        pairs = (jnp.transpose(mixed) * r.scales[layer, index]).reshape(per_tile, 2, CHUNK // 2, 64)
        pairs = jnp.concatenate([pairs[:, 0], pairs[:, 1]], axis=-1).astype(jnp.bfloat16)
        r.pairs[i * per_tile : (i + 1) * per_tile] = pairs
        if i == 2 and first:
            unit_ride.step(1)
        if i == 3:
            out_gather.near()
    if first:
        unit_ride.step(2)
    else:
        dy_gather.near()
    per_block = rows // CHUNK

    def pack(p, carry):
        r.packed[p] = r.pairs[r.table[chunks + p]]
        return carry

    lax.fori_loop(0, chunks, pack, 0)
    mix = Swap(r.packed, r.mixed, *r.mix_sems, per=per_block)
    mix.start()
    out_gather.far()
    if not first:
        dy_gather.far()
    for s in range(PLANE):
        for zz in range(LINE):
            at = natural_rows(s, zz)
            r.out_w[at : at + 32] = r.out_all[s * out_rows + zz * 32 : s * out_rows + zz * 32 + 32]
    out_gather.finish()

    def turn_units():
        for j in range(2 * LINE):
            pair = r.unit_in[j // 2, j % 2 * 2 : j % 2 * 2 + 2].reshape(128, r.unit_in.shape[3])
            r.unit_t[:, 128 * j : 128 * j + 128] = jnp.transpose(pair)

    if first:
        for head in range(4 * LINE):
            r.head_src[1, head] = fold_head(r.qkv_in[1], head)
    else:
        load_unit.wait()
        turn_units()
    saves = [
        pltpu.make_async_copy(source, dest, r.save_sem.at[i])
        for i, (source, dest) in enumerate(
            (
                (r.hb_all, r.hb_all_out), (r.qvk, r.qvk_out), (r.out_w, r.out_w_out), (r.rows_all, r.rows_all_out),
                (r.unit_t, r.unit_t_out), (r.act, r.act_out), (r.slope, r.slope_out), (r.mid, r.mid_out),
            )
        )
    ]
    start_all(saves[:3])
    mix.finish()
    down_ride.start()
    for g in range(columns // 128):
        left, right = (
            r.mixed[h * per_block : (h + 1) * per_block].reshape(rows // 2, 128) for h in (2 * g, 2 * g + 1)
        )
        low = jnp.concatenate([left[:, 0:64], right[:, 0:64]], axis=1)
        high = jnp.concatenate([left[:, 64:128], right[:, 64:128]], axis=1)
        for p in range(per_block):
            at = slice(p * (CHUNK // 2), (p + 1) * (CHUNK // 2))
            r.ab[p * CHUNK : p * CHUNK + CHUNK // 2, 128 * g : 128 * g + 128] = low[at]
            r.ab[p * CHUNK + CHUNK // 2 : (p + 1) * CHUNK, 128 * g : 128 * g + 128] = high[at]
    branch = mul(r.ab[...], r.out_w[...]) + biases[5][...]
    r.branch[...] = branch
    middle = value + normed(branch, gains[1][...], biases[1][...])
    r.middle[...] = middle

    own = pl.ds(slot * rows, rows)
    r.rows_all[own] = normed(middle, gains[2][...], biases[2][...]).astype(jnp.bfloat16)
    plane_gather = PlaneGather(r.rows_all, r.plane_gather_sems)
    plane_scatter = PlaneScatter(r.part, r.plane_bufs, r.plane_sems)
    pool = PlanePool(r.own_stat, r.got_stat, *r.pool_sems)
    plane_gather.start()
    hidden = r.act.shape[0]
    width = r.act.shape[1] // 2
    if first:
        unit_ride.finish()
        load_unit.start()
        quads[1].start()
    down_ride.step(1)
    if first:
        load_unit.wait()
        turn_units()

    def climb(th):
        at = span_at(th, width)

        def units(ut, carry):
            here = units_at(ut)
            upper = mul(r.unit_t[here], r.rows_all[pl.ds(th * width, width)], NT) + r.mid_bias[here]
            chance = 0.5 * (1.0 + lax.erf(upper * (0.5**0.5)))
            r.act[here, at] = upper * chance
            slope = chance + upper * (jnp.exp(-0.5 * upper * upper) * 0.3989422804014327)
            r.slope[here, at] = slope.astype(jnp.bfloat16)
            return carry

        lax.fori_loop(0, hidden // 256, units, 0)
        values = r.act[:, at]
        mean = jnp.mean(values, axis=0, keepdims=True)
        apart = values - mean
        r.own_stat[0:1, at] = mean
        r.own_stat[1:2, at] = jnp.sum(apart * apart, axis=0, keepdims=True)

    plane_gather.near()
    down_ride.step(2)
    climb(x)
    plane_gather.far()
    if first:
        down_ride.finish()
        load_down.start()
        quads[1].finish()
        next_unit_ride.start()
        next_head_ride.start()
    climb(1 - x)
    pool.start()
    if not first:
        down_ride.finish()
        load_down.start()
    start_all(saves[3:7])
    pool.finish()
    if first:
        next_unit_ride.step(1)
    load_down.wait()
    means = [r.got_stat[i, 0:1] for i in range(PLANE)]
    mean = functools.reduce(jnp.add, means) * (1.0 / PLANE)
    apart = functools.reduce(jnp.add, [(m - mean) * (m - mean) for m in means])
    r.stat[0:1] = mean
    r.stat[1:2] = functools.reduce(jnp.add, [r.got_stat[i, 1:2] for i in range(PLANE)]) + apart * float(hidden)

    def descend(th):
        at = span_at(th, width)
        mean, rate = mean_and_rate(r.stat[:, at], hidden_all)

        def units(ut, carry):
            here = units_at(ut)
            low = (r.act[here, at] - mean) * rate * r.mid_gain[here] + r.mid_shift[here]
            r.mid[here, at] = low.astype(jnp.bfloat16)
            return carry

        lax.fori_loop(0, hidden // 256, units, 0)
        down_w = r.down_w[...].reshape(hidden, columns)
        r.part[pl.ds(th * width, width)] = mul(r.mid[:, at], down_w, TN).astype(jnp.bfloat16)

    descend(1 - x)
    plane_scatter.twin(0).start()
    plane_scatter.twin(1).start()
    plane_scatter.over_first()
    descend(x)
    plane_scatter.twin(2).start()
    plane_scatter.twin(3).start()
    if not first:
        dy_gather.finish()
        saves.append(pltpu.make_async_copy(r.dy_all, r.dy_all_out, r.save_sem.at[8]))
    start_all(saves[7:])
    plane_scatter.first()
    if first:
        next_unit_ride.step(2)
    plane_scatter.second()
    plane_scatter.finish(r.result)
    r.y_out[...] = (r.middle[...] + (r.result[...] + biases[6][...])).astype(r.y_out.dtype)
    gather.finish()
    plane_gather.finish()
    for save in saves:
        save.wait()
    if first:
        next_unit_ride.finish()
        next_head_ride.finish()


def layer_forward_kernel(layer, table, x_in, params, blocks, dy, y_type, collective_id):
    rows, columns = x_in.shape
    hidden_all = params.mid_gain.shape[1]
    total, plane_rows, hidden = rows * 4 * LINE, rows * PLANE, hidden_all // PLANE
    vmem, anywhere, smem = pltpu.VMEM, pl.ANY, pltpu.SMEM
    dma = pltpu.SemaphoreType.DMA
    low = lambda *shape: pltpu.VMEM(shape, jnp.bfloat16)
    full = lambda *shape: pltpu.VMEM(shape, jnp.float32)
    low_out = lambda *shape: jax.ShapeDtypeStruct(shape, jnp.bfloat16)
    full_out = lambda *shape: jax.ShapeDtypeStruct(shape, jnp.float32)
    swap_sems, trade_sems, share_sems = Swap.scratch(), Trade.scratch(), Share.scratch()
    inputs = dict(
        table=(table, smem), scales=(params.head_scale, smem), x_in=(x_in, vmem), gains=(params.vec_gain, vmem),
        biases=(params.vec_bias, vmem), mid_gain_all=(params.mid_gain, vmem), mid_bias_all=(params.mid_bias, vmem),
        w_down=(params.w_down, anywhere), w_out=(params.w_out, anywhere),
    )
    head_shape, unit_shape = (4 * LINE, 32, 384), (LINE, 4, columns // (4 * LINE), hidden)
    outputs = dict(
        y_out=(jax.ShapeDtypeStruct((rows, columns), y_type), vmem), branch=(full_out(rows, columns), vmem),
        middle=(full_out(rows, columns), vmem), ab=(low_out(rows, columns), vmem),
        lse=(full_out(1, total), vmem), head_out=(full_out(64, total), vmem),
        stat=(full_out(2, plane_rows), vmem), hb_all_out=(low_out(total, columns), anywhere),
        qvk_out=(low_out(total // CHUNK, CHUNK, 192), anywhere), out_w_out=(low_out(columns, columns), anywhere),
        rows_all_out=(low_out(plane_rows, columns), anywhere), unit_t_out=(low_out(hidden, columns), anywhere),
        act_out=(full_out(hidden, plane_rows), anywhere), slope_out=(low_out(hidden, plane_rows), anywhere),
        mid_out=(low_out(hidden, plane_rows), anywhere), down_blocks=(low_out(LINE, hidden // LINE, columns), anywhere),
    )
    first = layer == 0
    if first:
        inputs.update(w_qkv=(params.w_qkv, anywhere), w_up=(params.w_up, anywhere))
        head_got, unit_got = (low_out(*head_shape), anywhere), (low_out(*unit_shape), anywhere)
        outputs.update(head_blocks=head_got, unit_blocks=unit_got, next_head=head_got, next_unit=unit_got)
    else:
        inputs.update(head_blocks=(blocks.head, anywhere), unit_blocks=(blocks.unit, anywhere), dy=(dy, vmem))
        outputs.update(dy_all_out=(low_out(plane_rows, columns), anywhere))
    plane_bufs, plane_sems = PlaneScatter.scratch(rows, columns)
    scratch = dict(
        hb_all=low(total, columns), flat=low(total // CHUNK, CHUNK, 192),
        qvk=low(total // CHUNK, CHUNK, 192), queries=low(total, 64), keys=low(total, 64),
        values_t=low(64, total), pairs=low(total // CHUNK, CHUNK // 2, 128),
        packed=low(total // CHUNK, CHUNK // 2, 128), mixed=low(total // CHUNK, CHUNK // 2, 128), head_in=low(4 * LINE, 32, 384), head_w=low(columns, 192),
        unit_in=low(*unit_shape), unit_t=low(hidden, columns),
        down_w=low(LINE, hidden // LINE, columns), out_got=low(LINE, 32, columns),
        out_all=low(columns, columns), out_w=low(columns, columns), rows_all=low(plane_rows, columns),
        act=full(hidden, plane_rows), slope=low(hidden, plane_rows), mid=low(hidden, plane_rows),
        part=low(plane_rows, columns), own_stat=full(2, plane_rows), got_stat=full(PLANE, 2, plane_rows),
        result=full(rows, columns), plane_bufs=plane_bufs, plane_sems=plane_sems,
        gather_sems=GroupGather.scratch(), plane_gather_sems=PlaneGather.scratch(),
        out_gather_sems=PlaneGather.scratch(), pool_sems=([dma((PLANE,)), dma((PLANE,))]),
        head_sems=swap_sems, unit_sems=share_sems, next_head_sems=swap_sems, next_unit_sems=share_sems,
        mix_sems=swap_sems, down_sems=share_sems, out_sems=trade_sems, load_sem=dma((3,)),
        save_sem=dma((9,)),
    )
    scratch.update(mid_gain=full(hidden, 1), mid_shift=full(hidden, 1), mid_bias=full(hidden, 1))
    if first:
        scratch.update(qkv_in=low(*params.w_qkv.shape), head_src=low(2, *head_shape), prep_sem=dma((3,)))
        scratch.update(unit_src=low(2, *unit_shape[1:]), unit_quad=low(2, *unit_shape[1:]), quad_sems=Quad.scratch() * 2)
    else:
        scratch.update(dy_all=low(plane_rows, columns), dy_gather_sems=PlaneGather.scratch())
    kernel = functools.partial(forward_kernel, layer, hidden_all)
    call = lambda body, **how: pl.pallas_call(body, name="layer_forward", **how)
    return launch(call, kernel, inputs, outputs, scratch, collective_id, 95, 56)


class TreeSum:
    def __init__(self, own_ref, total_ref, got, part, line, sems):
        self.own_ref, self.total_ref, self.got, self.part, self.line = own_ref, total_ref, got, part, line
        self.to_send, self.to_recv, self.back_send, self.back_recv = sems[0:4]
        self.trade = Trade(part, line, *sems[4:7])
        self.pool = PlanePool(None, got, None, None)
        self.me = plane_index(self.pool.x, self.pool.y, self.pool.c)

    @staticmethod
    def scratch(rows, columns):
        dma = pltpu.SemaphoreType.DMA
        bufs = [pltpu.VMEM((n, rows // PLANE, columns), jnp.float32) for n in (PLANE, 1, LINE)]
        return bufs, [dma((PLANE,))] * 4 + Trade.scratch()

    def slice(self, m):
        rows = self.part.shape[1]
        return pl.ds(pl.multiple_of(m * rows, 8), rows)

    def to(self, d, x, y, c):
        source = self.own_ref.at[self.slice(plane_index(x, y, c))]
        where = plane_device(x, self.pool.z, y, c)
        return remote(source, self.got.at[self.me], self.to_send.at[d], self.to_recv.at[d], where)

    def back(self, d, x, y, c):
        mine = self.total_ref.at[self.me]
        return remote(mine, mine, self.back_send.at[d], self.back_recv.at[d], plane_device(x, self.pool.z, y, c))

    def arrived(self, ref, recv):
        for d, x, y, c in self.pool.others():
            slot = ref.at[plane_index(x, y, c)]
            remote(slot, slot, recv.at[d], recv.at[d], plane_device(x, self.pool.z, y, c)).wait_recv()

    def start(self):
        for other in self.pool.others():
            self.to(*other).start()

    def along_line(self):
        self.arrived(self.got, self.to_recv)
        self.got[self.me] = self.own_ref[self.slice(self.me)]
        self.part[0] = functools.reduce(jnp.add, [self.got[m] for m in range(PLANE)])
        self.trade.start()

    def give_back(self):
        self.trade.finish()
        self.total_ref[self.me] = functools.reduce(jnp.add, [self.line[zz] for zz in range(LINE)])
        for other in self.pool.others():
            self.back(*other).start()

    def finish(self):
        self.arrived(self.total_ref, self.back_recv)
        for other in self.pool.others():
            self.to(*other).wait_send()
            self.back(*other).wait_send()


class QuickSum:
    def __init__(self, own_ref, plane_got, line_got, sems):
        self.own_ref, self.line_got = own_ref, line_got
        self.pool = PlanePool(own_ref, plane_got, *sems[0:2])
        self.trade = Trade(own_ref, line_got, *sems[2:5])
        self.plane_got = plane_got

    @staticmethod
    def scratch(shape):
        dma = pltpu.SemaphoreType.DMA
        got = [pltpu.VMEM((n, *shape), jnp.float32) for n in (PLANE, LINE)]
        return got, [dma((PLANE,))] * 2 + Trade.scratch()

    def run(self, o_ref):
        self.pool.start()
        self.pool.finish()
        self.own_ref[0] = functools.reduce(jnp.add, [self.plane_got[i] for i in range(PLANE)])
        self.trade.start()
        self.trade.finish()
        o_ref[...] = functools.reduce(jnp.add, [self.line_got[zz] for zz in range(LINE)])


OUT_BIAS, DOWN_BIAS, QUERY_BIAS, VALUE_BIAS, SCALES, MID, SMALL = 6, 7, 8, 9, 10, 12, 24


def spread_head(piece, index, width):
    nothing = jnp.zeros_like(piece)
    even = lax.rem(index, 2) == 0
    pair = jnp.concatenate([jnp.where(even, piece, nothing), jnp.where(even, nothing, piece)], axis=1)
    lanes = lax.broadcasted_iota(jnp.int32, (1, width), 1) // 128
    return jnp.where(lanes == index // 2, jnp.concatenate([pair] * (width // 128), axis=1), 0.0)


def backward_kernel(layer, hidden_all, r):
    first = layer == 1
    x, z, y, c = plane_place()
    index, unit_slot = index_of(z, y, c), (y * 2 + c) * 2 + x
    rows, columns = r.dy.shape
    total = r.hb_all_in.shape[0]
    tiles, chunks, per_tile = total // TILE, total // CHUNK, TILE // CHUNK
    hidden, plane_rows = r.act.shape
    width = plane_rows // 2
    dy_all, x_all = r.wide.at[pl.ds(0, plane_rows)], r.wide.at[pl.ds(plane_rows, plane_rows)]
    plane_gather = PlaneGather(dy_all, r.plane_gather_sems)
    plane_scatter = PlaneScatter(r.part, r.plane_bufs, r.plane_sems)
    out_part = r.part.at[pl.ds(0, LINE * PLANE * 32)]
    out_scatter = PlaneScatter(out_part, r.out_bufs, r.out_sems)
    scatter = GroupScatter(r.wide, r.group_bufs, r.group_sems)
    pool = PlanePool(r.own_sums, r.got_sums, *r.pool_sems)
    unit_ride = Swap(r.gup, r.unit_got, *r.unit_sems)
    out_ride = Trade(r.out_own, r.out_got, *r.out_ride_sems)
    head_cross = Cross(r.head_fold, r.head_other, *r.head_cross_sems)
    down_ride = Trade(r.gdown, r.gdown_got, *r.gdown_sems)
    near_rides = [
        Cross(r.unit_near, r.unit_far, *r.unit_cross_sems), Cross(r.down_near, r.down_far, *r.down_cross_sems),
        Cross(r.out_near, r.out_far, *r.out_cross_sems),
    ]
    if not first:
        late_head_ride = Swap(r.late_head, r.late_head_got, *r.late_head_sems)
        head_ride = Swap(r.head_fold, r.head_got, *r.head_sems)
        bulk = TreeSum(r.bulk, r.bulk_out, *r.bulk_bufs, r.bulk_sems)
        rest = QuickSum(r.rest, *r.rest_got, r.rest_sems)
    hail_all()
    gains = of_layer(r.gains, layer)
    r.small[...] = jnp.zeros_like(r.small)
    dy = r.dy[...].astype(jnp.float32)
    dy_low = dy.astype(jnp.bfloat16)
    r.small[DOWN_BIAS : DOWN_BIAS + 1] = jnp.sum(dy_low.astype(jnp.float32), axis=0, keepdims=True)
    if not first:
        dy_all[pl.ds(plane_index(x, y, c) * rows, rows)] = dy_low
    loads = [
        pltpu.make_async_copy(source, dest, r.load_sem.at[i])
        for i, (source, dest) in enumerate(
            (
                (r.down_blocks, r.down_w), (r.act_in, r.act), (r.slope_in, r.slope), (r.unit_t_in, r.unit_t),
                (r.mid_in, r.mid), (r.rows_all_in, x_all), (r.out_w_in, r.out_w), (r.qvk_in, r.qvk),
            )
        )
    ]
    load_dy = pltpu.make_async_copy(r.dy_all_in, dy_all, r.load_sem.at[8]) if first else None
    if first:
        load_dy.start()
    for load in loads[:6]:
        load.start()
    hailed_by_all()
    if not first:
        plane_gather.start()
        late_head_ride.start()
    for load in loads[6:]:
        load.start()

    def tile_load(t):
        return pltpu.make_async_copy(r.hb_all_in.at[pl.ds(t * TILE, TILE)], r.hb_tiles.at[t % 2], r.tile_sem.at[t % 2])

    tile_load(0).start()
    tile_load(1).start()
    unit_columns([r.mid_gain_all.at[pl.ds(layer, 1)]], unit_slot, [r.mid_gain])
    r.gg[...] = jnp.zeros_like(r.gg)
    r.gs[...] = jnp.zeros_like(r.gs)
    r.gb[...] = jnp.zeros_like(r.gb)
    r.own_sums[...] = jnp.zeros_like(r.own_sums)

    def climb(th):
        at = span_at(th, width)
        mean, rate = mean_and_rate(r.stat[:, at], hidden_all)

        def units(ut, carry):
            here = units_at(ut)
            down_w = r.down_w[pl.ds(ut * 2, 2)].reshape(256, columns)
            dm = mul(down_w, dy_all[pl.ds(th * width, width)], NT)
            r.dmid[here, at] = dm
            vh = (r.act[here, at] - mean) * rate
            r.act[here, at] = vh
            r.gg[here] += jnp.sum(dm * vh, axis=1, keepdims=True)
            r.gs[here] += jnp.sum(dm, axis=1, keepdims=True)
            scaled = dm * r.mid_gain[here]
            r.own_sums[0:1, at] += jnp.sum(scaled, axis=0, keepdims=True)
            r.own_sums[1:2, at] += jnp.sum(scaled * vh, axis=0, keepdims=True)
            return carry

        lax.fori_loop(0, hidden // 256, units, 0)

    if first:
        load_dy.wait()
    else:
        plane_gather.near()
    loads[0].wait()
    loads[1].wait()
    climb(x)
    if not first:
        plane_gather.far()
    climb(1 - x)
    pool.start()
    loads[4].wait()
    for ut in range(hidden // 256):
        grad = mul(r.mid[ut * 256 : (ut + 1) * 256], dy_all[...]).astype(jnp.bfloat16)
        r.gdown[2 * ut : 2 * ut + 2] = grad.reshape(2, 128, columns)
    down_ride.start()
    pool.finish()
    r.sums[...] = functools.reduce(jnp.add, [r.got_sums[i] for i in range(PLANE)]) * (1.0 / hidden_all)
    loads[2].wait()
    loads[3].wait()

    def descend(th):
        at = span_at(th, width)
        _, rate = mean_and_rate(r.stat[:, at], hidden_all)
        sum0, sum1 = r.sums[0:1, at], r.sums[1:2, at]

        def units(ut, carry):
            here = units_at(ut)
            dact = rate * (r.dmid[here, at] * r.mid_gain[here] - sum0 - r.act[here, at] * sum1)
            du = (dact * r.slope[here, at].astype(jnp.float32)).astype(jnp.bfloat16)
            r.du[here, at] = du
            r.gb[here] += jnp.sum(du.astype(jnp.float32), axis=1, keepdims=True)
            return carry

        lax.fori_loop(0, hidden // 256, units, 0)
        r.part[pl.ds(th * width, width)] = mul(r.du[:, at], r.unit_t[...], TN).astype(jnp.bfloat16)

    descend(1 - x)
    plane_scatter.twin(0).start()
    plane_scatter.twin(1).start()
    plane_scatter.over_first()
    descend(x)
    plane_scatter.twin(2).start()
    plane_scatter.twin(3).start()
    plane_scatter.first()
    loads[5].wait()
    plane_scatter.second()
    for ut in range(hidden // 256):
        grad = jnp.transpose(mul(r.du[ut * 256 : (ut + 1) * 256], x_all[...])).astype(jnp.bfloat16)
        r.gup[:, :, ut * 256 : (ut + 1) * 256] = grad.reshape(r.gup.shape[0], -1, 256)
    plane_scatter.finish(r.dffn)
    if not first:
        plane_gather.finish()

    back, r.small[2:3], r.small[5:6] = normed_back(r.middle[...], gains[2][...], r.dffn[...])
    r.dmiddle[...] = dy + back
    back, r.small[1:2], r.small[4:5] = normed_back(r.branch[...], gains[1][...], r.dmiddle[...])
    dz = back.astype(jnp.bfloat16)
    r.small[OUT_BIAS : OUT_BIAS + 1] = jnp.sum(dz.astype(jnp.float32), axis=0, keepdims=True)
    loads[6].wait()
    da = mul(dz, r.out_w[...], NT).astype(jnp.bfloat16)
    per_block = rows // CHUNK
    halves = da.reshape(per_block, 2, CHUNK // 2, columns)
    low, high = halves[:, 0].reshape(rows // 2, columns), halves[:, 1].reshape(rows // 2, columns)
    for h in range(columns // 64):
        at = slice(64 * h, 64 * h + 64)
        pairs = jnp.concatenate([low[:, at], high[:, at]], axis=1)
        r.packed[h * per_block : (h + 1) * per_block] = pairs.reshape(per_block, CHUNK // 2, 128)
    mix = Swap(r.packed, r.mixed, *r.mix_sems, per=per_block)
    mix.start()
    out_rows = LINE * 32
    for zz in range(LINE):
        grad = mul(r.ab[:, 256 * zz : 256 * zz + 256], dz, TN).astype(jnp.bfloat16)
        for s in range(PLANE):
            at = natural_rows(s, 0)
            out_part[s * out_rows + zz * 32 : s * out_rows + zz * 32 + 32] = grad[at : at + 32]
    for which in range(4):
        out_scatter.twin(which).start()
    turned = [ref[128 * zz : 128 * zz + 128] for ref in (r.gg, r.gs, r.gb) for zz in range(LINE)]
    turned = jnp.transpose(jnp.concatenate(turned + [jnp.zeros((128, 4), jnp.float32)], axis=1))
    for i in range(3 * LINE):
        r.small[MID + i : MID + i + 1, unit_lanes(0, unit_slot)] = turned[i : i + 1]
    loads[7].wait()
    load_head = pltpu.make_async_copy(r.head_blocks, r.head_fold, r.load_sem.at[6])
    load_head.start()
    scale = r.scales[layer, index]

    def prepare(t, carry):
        at = tile_at(t)
        rows_t = chunks_of(r.qvk, t)
        r.query[at] = rows_t[:, 0:64] * 0.125
        r.values[at] = rows_t[:, 64:128]
        key = rows_t[:, 128:192]
        r.keys[at] = key
        r.keys_t[:, at] = jnp.transpose(key.astype(jnp.float32)).astype(jnp.bfloat16)
        r.dkeys[at] = jnp.zeros((TILE, 64), jnp.float32)
        r.dvalues[at] = jnp.zeros((TILE, 64), jnp.float32)
        return carry

    lax.fori_loop(0, tiles, prepare, 0)
    load_head.wait()
    unfold_head(r.head_fold, r.head_w)
    out_scatter.over_first()
    out_scatter.first()
    mix.finish()
    unit_ride.start()

    def arrange(p, carry):
        r.packed[p] = r.mixed[r.table[p]]
        return carry

    lax.fori_loop(0, chunks, arrange, 0)

    def unpack(t, carry):
        at = tile_at(t)
        pairs = r.packed[pl.ds(t * per_tile, per_tile)].astype(jnp.float32)
        pairs = jnp.concatenate([pairs[:, :, 0:64], pairs[:, :, 64:128]], axis=1).reshape(TILE, 64)
        low = (pairs * scale).astype(jnp.bfloat16)
        r.dout[at] = low
        r.delta[:, at] = jnp.sum(jnp.transpose(low.astype(jnp.float32)) * r.head_out[:, at], axis=0, keepdims=True)
        return carry

    lax.fori_loop(0, tiles, unpack, 0)
    lanes = lax.broadcasted_iota(jnp.int32, (1, columns), 1)
    scale_grad = jnp.sum(r.delta[...], axis=1, keepdims=True) / scale
    r.small[SCALES : SCALES + 1] = jnp.where(lanes == layer * 4 * LINE + index, scale_grad, 0.0)
    cut = r.table[2 * chunks]
    for i in range(tiles):
        at = slice(i * TILE, (i + 1) * TILE)
        query, dout, lse, delta = r.query[at], r.dout[at], r.lse[:, at], r.delta[:, at]

        def block(j, total_dq, masked):
            there = tile_at(j)
            scores = mul(r.keys[there], query, NT)
            weights = jnp.exp(scores - (lse if masked else lse - alive(cut, i, j)))
            if masked:
                weights = jnp.where(diagonal(scores), weights, 0.0)
            dweights = mul(r.values[there], dout, NT)
            dscores = (weights * (dweights - delta)).astype(jnp.bfloat16)
            r.dvalues[there] += mul(weights.astype(jnp.bfloat16), dout)
            r.dkeys[there] += mul(dscores, query)
            return total_dq + mul(r.keys_t[:, there], dscores)

        total_dq = block(i, jnp.zeros((64, TILE), jnp.float32), True)
        if i > 0:
            total_dq = lax.fori_loop(0, i, functools.partial(block, masked=False), total_dq)
        r.dquery_t[:, at] = total_dq * 0.125
        if i == 2:
            out_scatter.second()
    out_sum = r.dffn.at[pl.ds(0, out_rows)]
    out_scatter.finish(out_sum)
    r.out_own[...] = out_sum[...].reshape(r.out_own.shape).astype(jnp.bfloat16)
    out_ride.start()

    head_bias = jnp.zeros((1, 192), jnp.float32)
    for i in range(tiles):
        at = slice(i * TILE, (i + 1) * TILE)
        joined = jnp.concatenate([jnp.transpose(r.dquery_t[:, at]), r.dvalues[at], r.dkeys[at]], axis=1).astype(jnp.bfloat16)
        head_bias += jnp.sum(joined.astype(jnp.float32), axis=0, keepdims=True)
        r.qvk[i * per_tile : (i + 1) * per_tile] = joined.reshape(per_tile, CHUNK, 192)

    r.small[QUERY_BIAS : QUERY_BIAS + 1] = spread_head(head_bias[:, 0:64], index, columns)
    r.small[VALUE_BIAS : VALUE_BIAS + 1] = spread_head(head_bias[:, 64:128], index, columns)

    if not first:
        r.bulk[0:SMALL] = r.small_in[...]
        r.bulk[SMALL : 2 * SMALL] = r.small[...]
        r.bulk[2 * SMALL :] = jnp.zeros((r.bulk.shape[0] - 2 * SMALL, columns), jnp.float32)
        bulk.start()

    def restore(p, carry):
        r.flat[p] = r.qvk[r.table[chunks + p]]
        return carry

    lax.fori_loop(0, chunks, restore, 0)

    def project(owner):
        rows_of = r.flat[pl.ds(owner * per_block, per_block)].reshape(rows, 192)
        r.wide[pl.ds(owner * rows, rows)] = mul(rows_of, r.head_w[...], NT).astype(jnp.bfloat16)

    for own_y in (0, 1):
        for t in range(LINE):
            for other_core in (1, 0):
                project(scatter.owner(t, own_y, 1 - c if other_core else c))
                if other_core:
                    scatter.start(t, own_y)
    for t in range(tiles):
        tile_load(t).wait()
        grad = mul(chunks_of(r.flat, t), r.hb_tiles[t % 2], TN)
        r.gw[...] = grad if t == 0 else r.gw[...] + grad
        if t + 2 < tiles:
            tile_load(t + 2).start()
    turned = jnp.transpose(r.gw[...]).astype(jnp.bfloat16)
    for j in range(r.head_fold.shape[0]):
        for part in range(2):
            piece = turned[64 * j + 32 * part : 64 * j + 32 * part + 32]
            r.head_fold[j, :, 128 * part : 128 * part + 128] = piece[:, 0:128]
            r.head_fold[j, :, 256 + 64 * part : 320 + 64 * part] = piece[:, 128:192]
    head_cross.start()
    scatter.first()
    if not first:
        bulk.along_line()
    down_ride.finish()
    out_ride.finish()
    unit_ride.finish()
    reloads = [
        pltpu.make_async_copy(source, dest, r.load_sem.at[i])
        for i, (source, dest) in enumerate(((r.unit_got, r.gup), (r.gdown_got, r.gdown), (r.out_got, r.out_own)))
    ]
    for load in reloads:
        load.start()
    head_cross.finish()
    both = (r.head_fold[...].astype(jnp.float32) + r.head_other[...].astype(jnp.float32)).astype(jnp.bfloat16)
    if first:
        r.head_sum[...] = both
    else:
        r.head_fold[...] = both
        head_ride.start()
    for load in reloads:
        load.wait()
    for q in range(4):
        parts = [r.gup[zz * 4 + q].astype(jnp.float32) for zz in range(LINE)]
        r.unit_near[q] = functools.reduce(jnp.add, parts).astype(jnp.bfloat16)
    for near, own in ((r.down_near, r.gdown), (r.out_near, r.out_own)):
        near[...] = functools.reduce(jnp.add, [own[zz].astype(jnp.float32) for zz in range(LINE)]).astype(jnp.bfloat16)
    start_all(near_rides)
    scatter.second(r.dffn)
    back, gain_grad, shift_grad = normed_back(r.x_in[...].astype(jnp.float32), gains[0][...], r.dffn[...])
    r.dx[...] = r.dmiddle[...] + back
    r.small[0:1] = gain_grad
    r.small[3:4] = shift_grad
    if not first:
        r.rest[0, 0:1] = gain_grad
        r.rest[0, 1:2] = shift_grad
        bulk.give_back()
        rest.run(r.rest_out)
        bulk.finish()
    scatter.finish()
    if not first:
        head_ride.finish()
        late_head_ride.finish()
    finish_all(near_rides)


def layer_backward_kernel(layer, table, dy, params, record, later, collective_id):
    rows, columns = dy.shape
    hidden_all = params.mid_gain.shape[1]
    total, plane_rows, hidden = rows * 4 * LINE, rows * PLANE, hidden_all // PLANE
    vmem, anywhere, smem = pltpu.VMEM, pl.ANY, pltpu.SMEM
    dma = pltpu.SemaphoreType.DMA
    low = lambda *shape: pltpu.VMEM(shape, jnp.bfloat16)
    full = lambda *shape: pltpu.VMEM(shape, jnp.float32)
    low_out = lambda *shape: jax.ShapeDtypeStruct(shape, jnp.bfloat16)
    full_out = lambda *shape: jax.ShapeDtypeStruct(shape, jnp.float32)
    swap_sems, trade_sems, cross_sems = Swap.scratch(), Trade.scratch(), Cross.scratch()
    unit_shape = (4 * LINE, columns // (4 * LINE), hidden)
    unit_near, down_near, out_near = (4, *unit_shape[1:]), (hidden // LINE, columns), (32, columns)
    down_shape = (LINE, hidden // LINE, columns)
    inputs = dict(
        table=(table, smem), scales=(params.head_scale, smem), dy=(dy, vmem), gains=(params.vec_gain, vmem),
        mid_gain_all=(params.mid_gain, vmem), x_in=(record.x_in, vmem), branch=(record.branch, vmem),
        middle=(record.middle, vmem), ab=(record.ab, vmem), lse=(record.lse, vmem),
        head_out=(record.head_out, vmem), stat=(record.stat, vmem), hb_all_in=(record.hb_all_out, anywhere),
        qvk_in=(record.qvk_out, anywhere), out_w_in=(record.out_w_out, anywhere),
        rows_all_in=(record.rows_all_out, anywhere), unit_t_in=(record.unit_t_out, anywhere),
        act_in=(record.act_out, anywhere), slope_in=(record.slope_out, anywhere),
        mid_in=(record.mid_out, anywhere), down_blocks=(record.down_blocks, anywhere),
        head_blocks=(record.head_blocks, anywhere),
    )
    outputs = dict(
        dx=(full_out(rows, columns), vmem), unit_got=(low_out(*unit_shape), anywhere),
        gdown_got=(low_out(*down_shape), anywhere), out_got=(low_out(LINE, *out_near), anywhere),
        unit_near=(low_out(*unit_near), vmem),
        down_near=(low_out(*down_near), vmem), out_near=(low_out(*out_near), vmem),
        unit_far=(low_out(*unit_near), anywhere), down_far=(low_out(*down_near), anywhere),
        out_far=(low_out(*out_near), anywhere),
    )
    first = layer == 1
    if first:
        inputs.update(dy_all_in=(record.dy_all_out, anywhere))
        outputs.update(small=(full_out(SMALL, columns), vmem), head_sum=(low_out(4 * LINE, 32, 384), vmem))
    else:
        inputs.update(small_in=(later.small, vmem), late_head=(later.head_sum, anywhere))
        outputs.update(head_got=(low_out(4 * LINE, 32, 384), anywhere), late_head_got=(low_out(4 * LINE, 32, 384), anywhere))
        outputs.update(bulk_out=(full_out(PLANE, 8, columns), vmem), rest_out=(full_out(2, columns), vmem))
    plane_bufs, plane_sems = PlaneScatter.scratch(rows, columns)
    out_bufs, out_sems = PlaneScatter.scratch(LINE * 32, columns)
    group_bufs, group_sems = GroupScatter.scratch(rows, columns)
    scratch = dict(
        wide=low(total, columns), down_w=low(*down_shape), act=full(hidden, plane_rows),
        slope=low(hidden, plane_rows), unit_t=low(hidden, columns), mid=low(hidden, plane_rows),
        out_w=low(columns, columns), qvk=low(total // CHUNK, CHUNK, 192), hb_tiles=low(2, TILE, columns),
        dmid=full(hidden, plane_rows), du=low(hidden, plane_rows), part=low(plane_rows, columns),
        own_sums=full(2, plane_rows), got_sums=full(PLANE, 2, plane_rows), sums=full(2, plane_rows),
        gup=low(*unit_shape), gdown=low(*down_shape), dffn=full(rows, columns),
        dmiddle=full(rows, columns), packed=low(total // CHUNK, CHUNK // 2, 128),
        mixed=low(total // CHUNK, CHUNK // 2, 128),
        out_own=low(LINE, 32, columns),
        dout=low(total, 64), delta=full(1, total), query=low(total, 64),
        keys=low(total, 64), values=low(total, 64), keys_t=low(64, total), dkeys=full(total, 64),
        dvalues=full(total, 64), dquery_t=full(64, total), flat=low(total // CHUNK, CHUNK, 192),
        head_w=low(columns, 192), gw=full(192, columns),
        head_other=low(4 * LINE, 32, 384), head_fold=low(4 * LINE, 32, 384),
        plane_bufs=plane_bufs, plane_sems=plane_sems, out_bufs=out_bufs, out_sems=out_sems,
        group_bufs=group_bufs, group_sems=group_sems, plane_gather_sems=PlaneGather.scratch(),
        pool_sems=([dma((PLANE,)), dma((PLANE,))]), unit_sems=swap_sems, gdown_sems=trade_sems, head_sems=swap_sems,
        mix_sems=swap_sems, out_ride_sems=trade_sems, head_cross_sems=cross_sems, load_sem=dma((10,)),
        tile_sem=dma((2,)),
    )
    scratch.update(unit_cross_sems=cross_sems, down_cross_sems=cross_sems, out_cross_sems=cross_sems)
    scratch.update(mid_gain=full(hidden, 1), gg=full(hidden, 1), gs=full(hidden, 1), gb=full(hidden, 1))
    if not first:
        scratch.update(late_head_sems=swap_sems, small=full(SMALL, columns), bulk=full(8 * PLANE, columns), rest=full(1, 2, columns))
        bulk_bufs, bulk_sems = TreeSum.scratch(8 * PLANE, columns)
        scratch.update(bulk_bufs=bulk_bufs, bulk_sems=bulk_sems)
        rest_got, rest_sems = QuickSum.scratch((2, columns))
        scratch.update(rest_got=rest_got, rest_sems=rest_sems)
    kernel = functools.partial(backward_kernel, layer, hidden_all)
    call = lambda body, **how: pl.pallas_call(body, name="layer_backward", **how)
    return launch(call, kernel, inputs, outputs, scratch, collective_id, 105, 63)


def assemble_kernel(r):
    x = lax.axis_index("batch")
    for layer, got in enumerate((r.layer0, r.layer1)):
        head_ref, unit_near, unit_far, down_near, down_far, out_near, out_far = got
        width = 64 * head_ref.shape[0]
        for j in range(0, head_ref.shape[0], 2):
            left, right = head_ref[j].astype(jnp.float32), head_ref[j + 1].astype(jnp.float32)
            for part in range(2):
                for at, source in ((0, 128 * part), (width, 256 + 64 * part), (2 * width, 64 + 128 * part)):
                    pair = jnp.concatenate([left[:, source : source + 64], right[:, source : source + 64]], axis=1)
                    r.qkv[layer, 32 * part : 32 * part + 32, at + j * 64 : at + (j + 2) * 64] = pair
        for half, unit_ref, down_ref, out_ref in ((x, unit_near, down_near, out_near), (1 - x, unit_far, down_far, out_far)):
            for q in range(unit_ref.shape[0]):
                for z in range(LINE):
                    piece = unit_ref[q, :, z * 128 : (z + 1) * 128].astype(jnp.float32)
                    r.up[layer, :, unit_lanes(z, q * 2 + half)] = piece
            for ref, dest in ((down_ref, r.down), (out_ref, r.out)):
                rows = ref.shape[0]
                dest[layer, pl.ds(pl.multiple_of(half * rows, rows), rows)] = ref[...].astype(jnp.float32)
        per = r.bulk.shape[1]
        bulk = r.bulk[SMALL // per * (1 - layer) : SMALL // per * (2 - layer)].reshape(SMALL, -1)
        gain, shift = (r.rest[0:1], r.rest[1:2]) if layer == 0 else (bulk[0:1], bulk[3:4])
        heads = bulk[QUERY_BIAS : VALUE_BIAS + 1]
        gain_rows = jnp.concatenate([gain, bulk[1:3]], axis=0)
        bias_rows = jnp.concatenate([shift, bulk[4:6], heads, bulk[OUT_BIAS : DOWN_BIAS + 1]], axis=0)
        for ref, rows in ((r.vec_gain, gain_rows), (r.vec_bias, bias_rows)):
            for i in range(ref.shape[0]):
                ref[i, layer : layer + 1] = rows[i : i + 1]
        for z in range(LINE):
            at = slice(z * PLANE * 128, (z + 1) * PLANE * 128)
            r.mid_gain[layer : layer + 1, at] = bulk[MID + z : MID + z + 1]
            for i in range(2):
                row = MID + (i + 1) * LINE + z
                r.mid_bias[layer, i : i + 1, at] = bulk[row : row + 1]
        row = bulk[SCALES : SCALES + 1]
        heads_here = r.head_scale.shape[1]
        r.head_scale[layer : layer + 1] = row[:, layer * heads_here : (layer + 1) * heads_here]


def assemble(results, dx, back, shapes):
    vmem, anywhere = pl.BlockSpec(memory_space=pltpu.VMEM), pl.BlockSpec(memory_space=pl.ANY)
    arrays = [results, dx]
    for got, head in zip(back, (back[0].head_got, back[0].late_head_got)):
        arrays += [head, got.unit_near, got.unit_far, got.down_near, got.down_far, got.out_near, got.out_far]

    arrays += [back[0].bulk_out, back[0].rest_out]
    n = len(arrays)

    def body(*refs):
        ins, outs, held, sem = refs[:n], refs[n : n + 11], refs[n + 11 : -1], refs[-1]
        loads = [pltpu.make_async_copy(ins[i], held[i], sem.at[i]) for i in range(n)]
        passes = [pltpu.make_async_copy(held[i], outs[i], sem.at[i]) for i in range(2)]
        for load in loads:
            load.start()
        for load in loads:
            load.wait()
        for copy in passes:
            copy.start()
        qkv, out, up, down, vec_gain, vec_bias, mid_gain, mid_bias, head_scale = outs[2:]
        refs = held[2:]
        assemble_kernel(
            Refs(
                layer0=refs[0:7], layer1=refs[7:14], bulk=refs[14], rest=refs[15], qkv=qkv, out=out, up=up, down=down,
                vec_gain=vec_gain, vec_bias=vec_bias, mid_gain=mid_gain, mid_bias=mid_bias, head_scale=head_scale,
            )
        )
        for copy in passes:
            copy.wait()

    return pl.pallas_call(
        body,
        out_shape=[jax.ShapeDtypeStruct(array.shape, array.dtype) for array in (results, dx)]
        + [jax.ShapeDtypeStruct(shape, jnp.float32) for shape in shapes],
        in_specs=[anywhere] * n,
        out_specs=[anywhere] * 2 + [vmem] * len(shapes),
        scratch_shapes=[pltpu.VMEM(array.shape, array.dtype) for array in arrays] + [pltpu.SemaphoreType.DMA((n,))],
        cost_estimate=lasting(5),
        compiler_params=pltpu.CompilerParams(vmem_limit_bytes=62 << 20),
        name="assemble",
    )(*arrays)


def chunk_table(first_rows, span_of, rows_here):
    blocks = span_of.shape[0]
    first = first_rows[0]
    second = rows_here - first
    row = jnp.arange(blocks * rows_here // CHUNK, dtype=jnp.int32) * CHUNK
    later = row >= first * blocks
    inside = jnp.where(later, row - first * blocks, row)
    length = jnp.where(later, jnp.maximum(second, 1), first)
    span = inside // length
    of_span = (span_of[None, :] == span[:, None]).astype(jnp.int32)
    device_of = jnp.sum(of_span * jnp.arange(blocks, dtype=jnp.int32)[None, :], axis=1)
    source = device_of * rows_here + jnp.where(later, first, 0) + inside - span * length
    within = row % rows_here
    behind = within >= first
    place = jnp.repeat(span_of, rows_here // CHUNK) * jnp.where(behind, second, first) + within
    place = place + jnp.where(behind, first * (blocks - 1), 0)
    return jnp.concatenate([source // CHUNK, place // CHUNK, (first * blocks // TILE)[None]]).astype(jnp.int32)


def travel(
    tokens, grad_out, first_rows, span_of, w_qkv, w_out, w_up, w_down, vec_gain, vec_bias, mid_gain, mid_bias, head_scale
):
    rows_here, row_width = tokens.shape
    table = chunk_table(first_rows, span_of, rows_here)
    params = Refs(
        w_qkv=w_qkv, w_up=w_up, w_out=w_out.reshape(2, 2, -1, row_width), w_down=w_down.reshape(2, 2, -1, row_width),
        vec_gain=vec_gain.transpose(1, 0, 2), vec_bias=vec_bias.transpose(1, 0, 2), mid_gain=mid_gain, mid_bias=mid_bias,
        head_scale=head_scale,
    )
    first = layer_forward_kernel(0, table, tokens, params, None, None, jnp.float32, 0)
    first.x_in = tokens
    blocks = Refs(head=first.next_head, unit=first.next_unit)
    second = layer_forward_kernel(1, table, first.y_out, params, blocks, grad_out, jnp.bfloat16, 1)
    second.x_in, second.head_blocks = first.y_out, first.next_head
    back_second = layer_backward_kernel(1, table, grad_out, params, second, None, 2)
    back_first = layer_backward_kernel(0, table, back_second.dx, params, first, back_second, 3)
    kinds = (w_qkv, w_out, w_up, w_down, params.vec_gain, params.vec_bias, mid_gain, mid_bias, head_scale)
    results = assemble(second.y_out, back_first.dx, [back_first, back_second], [array.shape for array in kinds])
    return (*results[:6], results[6].transpose(1, 0, 2), results[7].transpose(1, 0, 2), *results[8:])


def local(*args):
    tokens, w_qkv = args[0], args[4]
    blocks = lax.axis_size("blk")
    heads = w_qkv.shape[2] // (3 * HEAD_DIM)
    if blocks == heads == 4 * LINE and lax.axis_size("batch") == 2 and tokens.shape[0] * blocks % TILE == 0:
        return travel(*args)
    return general(*args)


def solution(mesh):
    placed = (
        P(("batch", "blk"), None),
        P(("batch", "blk"), None),
        P("batch"),
        P(),
        P(None, "blk", None),
        P(None, "blk", None),
        P(None, "blk", None),
        P(None, "blk", None),
        P(),
        P(),
        P(),
        P(),
        P(),
    )
    return jax.shard_map(
        local,
        mesh=mesh,
        in_specs=placed,
        out_specs=(
            P(("batch", "blk"), None),
            P(("batch", "blk"), None),
            P(None, "blk", None),
            P(None, "blk", None),
            P(None, "blk", None),
            P(None, "blk", None),
            P(),
            P(),
            P(),
            P(),
            P(),
        ),
        check_vma=False,
    )
```

```python
import functools

import jax
import jax.numpy as jnp
from jax import lax
from jax.experimental import pallas as pl
from jax.experimental.pallas import tpu as pltpu
from jax.sharding import PartitionSpec as P

HEAD_DIM = 64


EPSILON = 1e-05
NEGATIVE = -1e30


def shifted(x, axis, by):
    devices = lax.axis_size(axis)
    return lax.ppermute(x, axis, [(i, (i + by) % devices) for i in range(devices)])


def norm_rows(values, gains, shifts):
    average = jnp.mean(values, axis=-1, keepdims=True)
    centered = values - average
    spread = jnp.mean(centered * centered, axis=-1, keepdims=True)
    return centered * lax.rsqrt(spread + EPSILON) * gains + shifts


def mid_piece(upper, gains, shifts):
    return norm_rows(jax.nn.gelu(upper, approximate=False), gains, shifts)


def split_heads(matrix):
    return matrix.reshape(matrix.shape[0], -1, HEAD_DIM)


def block_rows(total_rows):
    chosen = total_rows
    while chosen > 1024 and chosen % 2 == 0:
        chosen = chosen // 2
    return chosen


def row_layout(first_rows, rows_here):
    within = jnp.arange(rows_here, dtype=jnp.int32)
    first_len = first_rows[0]
    second = (within >= first_len).astype(jnp.int32)
    return (second, within - second * first_len)


def visible_pairs(query_seq, query_off, query_span, key_seq, key_off, key_span):
    earlier = key_span[None, :] < query_span[:, None]
    same_span = (key_span[None, :] == query_span[:, None]) & (
        key_off[None, :] <= query_off[:, None]
    )
    return (query_seq[:, None] == key_seq[None, :]) & (earlier | same_span)


def merge_block(state_in, query_heads, keys_block, values_block, visible):
    run_peak, run_total, accumulated = state_in
    query_rows = query_heads.shape[0]
    scores = jnp.einsum(
        "qhd,khd->hqk", query_heads, split_heads(keys_block), preferred_element_type=jnp.float32
    ) * HEAD_DIM ** (-0.5)
    masked = jnp.where(visible[None], scores, NEGATIVE)
    new_peak = jnp.maximum(run_peak, jnp.max(masked, axis=-1))
    weights = jnp.where(visible[None], jnp.exp(masked - new_peak[:, :, None]), 0.0)
    factor = jnp.exp(run_peak - new_peak)
    new_total = run_total * factor + jnp.sum(weights, axis=-1)
    update = jnp.einsum(
        "hqk,khd->qhd",
        weights.astype(jnp.bfloat16),
        split_heads(values_block),
        preferred_element_type=jnp.float32,
    )
    rescaled = split_heads(accumulated) * jnp.transpose(factor)[:, :, None]
    return (new_peak, new_total, (rescaled + update).reshape(query_rows, -1))


def grad_block(query_heads, log_total, delta, dout_heads, keys_block, values_block, visible):
    key_heads = split_heads(keys_block)
    value_heads = split_heads(values_block)
    scores = jnp.einsum(
        "qhd,khd->hqk", query_heads, key_heads, preferred_element_type=jnp.float32
    ) * HEAD_DIM ** (-0.5)
    probs = jnp.where(visible[None], jnp.exp(scores - log_total[:, :, None]), 0.0)
    dprobs = jnp.einsum("qhd,khd->hqk", dout_heads, value_heads, preferred_element_type=jnp.float32)
    dscores = (probs * (dprobs - delta[:, :, None])).astype(jnp.bfloat16)
    add_query = jnp.einsum("hqk,khd->qhd", dscores, key_heads, preferred_element_type=jnp.float32)
    add_keys = jnp.einsum("hqk,qhd->khd", dscores, query_heads, preferred_element_type=jnp.float32)
    add_values = jnp.einsum(
        "hqk,qhd->khd", probs.astype(jnp.bfloat16), dout_heads, preferred_element_type=jnp.float32
    )
    return (
        add_query.reshape(query_heads.shape[0], -1),
        add_keys.reshape(key_heads.shape[0], -1),
        add_values.reshape(key_heads.shape[0], -1),
    )


def unchanged(state_in):
    return state_in


def attention_forward(query_low, keys_low, values_low, layout):
    seq_ids, offsets, span_of, my_span, my_index = layout
    rows_here, row_width = query_low.shape
    heads_here = row_width // HEAD_DIM
    query_heads = split_heads(query_low)
    query_span = jnp.full((rows_here,), my_span, jnp.int32)
    initial = (
        jnp.full((heads_here, rows_here), NEGATIVE, jnp.float32),
        jnp.zeros((heads_here, rows_here), jnp.float32),
        jnp.zeros((rows_here, row_width), jnp.float32),
    )
    running = initial
    key_part = lax.all_gather(keys_low, "blk", axis=0, tiled=True)
    value_part = lax.all_gather(values_low, "blk", axis=0, tiled=True)
    part_rows = key_part.shape[0]
    step_rows = block_rows(part_rows)

    def one_step(state_in, step_index):
        block_start = step_index * step_rows
        global_rows = block_start + jnp.arange(step_rows, dtype=jnp.int32)
        key_span = span_of[global_rows // rows_here]
        local_rows = global_rows % rows_here
        visible = visible_pairs(
            seq_ids, offsets, query_span, seq_ids[local_rows], offsets[local_rows], key_span
        )
        keys_block = lax.dynamic_slice_in_dim(key_part, block_start, step_rows, 0)
        values_block = lax.dynamic_slice_in_dim(value_part, block_start, step_rows, 0)

        def one_compute(inner_state):
            return merge_block(inner_state, query_heads, keys_block, values_block, visible)

        return (lax.cond(jnp.any(key_span <= my_span), one_compute, unchanged, state_in), None)

    running, _ = lax.scan(one_step, running, jnp.arange(part_rows // step_rows, dtype=jnp.int32))
    run_peak, run_total, accumulated = running
    mixed_heads = (split_heads(accumulated) / jnp.transpose(run_total)[:, :, None]).reshape(
        rows_here, row_width
    )
    return (mixed_heads, run_peak + jnp.log(run_total))


def cycle_backward(query_low, keys_low, values_low, log_total, delta, dout_low, layout):
    seq_ids, offsets, span_of, my_span, my_index = layout
    rows_here, row_width = query_low.shape
    blocks_total = lax.axis_size("blk")
    query_heads = split_heads(query_low)
    dout_heads = split_heads(dout_low)
    query_span = jnp.full((rows_here,), my_span, jnp.int32)

    def turn(turn_index, carried):
        keys_now, values_now, dkeys, dvalues, dquery = carried
        source = (my_index - turn_index) % blocks_total
        source_span = span_of[source]
        key_span = jnp.full((rows_here,), source_span, jnp.int32)
        visible = visible_pairs(seq_ids, offsets, query_span, seq_ids, offsets, key_span)

        def turn_compute(inner_state):
            add_query, add_keys, add_values = grad_block(
                query_heads, log_total, delta, dout_heads, keys_now, values_now, visible
            )
            return (
                inner_state[0] + add_query,
                inner_state[1] + add_keys,
                inner_state[2] + add_values,
            )

        dquery, dkeys, dvalues = lax.cond(
            source_span <= my_span, turn_compute, unchanged, (dquery, dkeys, dvalues)
        )
        keys_now, values_now = shifted((keys_now, values_now), "blk", 1)
        dkeys, dvalues = (
            shifted(dkeys.astype(jnp.bfloat16), "blk", 1).astype(dkeys.dtype),
            shifted(dvalues.astype(jnp.bfloat16), "blk", 1).astype(dvalues.dtype),
        )
        return (keys_now, values_now, dkeys, dvalues, dquery)

    zeros_rows = jnp.zeros((rows_here, row_width), jnp.float32)
    result = lax.fori_loop(
        0, blocks_total, turn, (keys_low, values_low, zeros_rows, zeros_rows, zeros_rows)
    )
    return (result[4], result[2], result[3])


def layer_forward(inputs, weights, gains, biases, middle_gain, middle_bias, heads_scale, layout):
    weight_qkv, weight_out, weight_up, weight_down = weights
    row_width = inputs.shape[1]
    normed, pre_pull = jax.vjp(norm_rows, inputs, gains[0], biases[0])
    normed_low = normed.astype(jnp.bfloat16)
    projected = jnp.dot(normed_low, weight_qkv, preferred_element_type=jnp.float32)
    query_low = (projected[:, :row_width] + biases[3]).astype(jnp.bfloat16)
    keys_low = projected[:, row_width : 2 * row_width].astype(jnp.bfloat16)
    values_low = (projected[:, 2 * row_width :] + biases[4]).astype(jnp.bfloat16)
    mixed_heads, log_total = attention_forward(query_low, keys_low, values_low, layout)
    scaled_low = (mixed_heads * jnp.repeat(heads_scale, HEAD_DIM)).astype(jnp.bfloat16)
    branch = jnp.dot(scaled_low, weight_out, preferred_element_type=jnp.float32) + biases[5]
    post_normed, post_pull = jax.vjp(norm_rows, branch, gains[1], biases[1])
    middle_res = inputs + post_normed
    ffn_normed, ffn_pull = jax.vjp(norm_rows, middle_res, gains[2], biases[2])
    ffn_low = ffn_normed.astype(jnp.bfloat16)
    upper = jnp.dot(ffn_low, weight_up, preferred_element_type=jnp.float32) + middle_bias[1]
    middle, mid_pull = jax.vjp(mid_piece, upper, middle_gain, middle_bias[0])
    middle_low = middle.astype(jnp.bfloat16)
    results = middle_res + (
        jnp.dot(middle_low, weight_down, preferred_element_type=jnp.float32) + biases[6]
    )
    record = {
        "pre_pull": pre_pull,
        "normed_low": normed_low,
        "query_low": query_low,
        "keys_low": keys_low,
        "values_low": values_low,
        "log_total": log_total,
        "mixed_heads": mixed_heads,
        "scaled_low": scaled_low,
        "post_pull": post_pull,
        "ffn_pull": ffn_pull,
        "ffn_low": ffn_low,
        "mid_pull": mid_pull,
        "middle_low": middle_low,
        "weights": weights,
    }
    return (results, record)


def layer_backward(d_results, record, weights, heads_scale, layout):
    weight_qkv, weight_out, weight_up, weight_down = weights
    rows_here, row_width = d_results.shape
    d_results_low = d_results.astype(jnp.bfloat16)
    grad_down = jnp.einsum(
        "tf,td->fd", record["middle_low"], d_results_low, preferred_element_type=jnp.float32
    )
    grad_down_bias = jnp.sum(d_results_low, axis=0, dtype=jnp.float32)
    d_middle = jnp.einsum(
        "td,fd->tf", d_results_low, weight_down, preferred_element_type=jnp.float32
    )
    d_upper, grad_mid_gain, grad_mid_shift = record["mid_pull"](d_middle)
    d_upper_low = d_upper.astype(jnp.bfloat16)
    grad_up = jnp.einsum(
        "td,tf->df", record["ffn_low"], d_upper_low, preferred_element_type=jnp.float32
    )
    grad_up_bias = jnp.sum(d_upper_low, axis=0, dtype=jnp.float32)
    d_ffn = jnp.einsum("tf,df->td", d_upper_low, weight_up, preferred_element_type=jnp.float32)
    d_res_part, grad_gain_ffn, grad_shift_ffn = record["ffn_pull"](d_ffn)
    d_middle_res = d_results + d_res_part
    d_branch, grad_gain_post, grad_shift_post = record["post_pull"](d_middle_res)
    d_branch_low = d_branch.astype(jnp.bfloat16)
    grad_out_w = jnp.einsum(
        "tc,td->cd", record["scaled_low"], d_branch_low, preferred_element_type=jnp.float32
    )
    grad_out_bias = jnp.sum(d_branch_low, axis=0, dtype=jnp.float32)
    d_scaled = jnp.einsum("td,cd->tc", d_branch_low, weight_out, preferred_element_type=jnp.float32)
    mixed_heads = record["mixed_heads"]
    grad_heads = jnp.sum((d_scaled * mixed_heads).reshape(rows_here, -1, HEAD_DIM), axis=(0, 2))
    d_mixed_low = (d_scaled * jnp.repeat(heads_scale, HEAD_DIM)).astype(jnp.bfloat16)
    delta = jnp.transpose(
        jnp.sum(
            (d_mixed_low.astype(jnp.float32) * mixed_heads).reshape(rows_here, -1, HEAD_DIM), axis=2
        )
    )
    dquery, dkeys, dvalues = cycle_backward(
        record["query_low"],
        record["keys_low"],
        record["values_low"],
        record["log_total"],
        delta,
        d_mixed_low,
        layout,
    )
    scale_factor = HEAD_DIM ** (-0.5)
    d_proj_low = jnp.concatenate(
        [dquery * scale_factor, dkeys * scale_factor, dvalues], axis=1
    ).astype(jnp.bfloat16)
    grad_qkv = jnp.einsum(
        "tc,te->ce", record["normed_low"], d_proj_low, preferred_element_type=jnp.float32
    )
    grad_q_bias = jnp.sum(d_proj_low[:, :row_width], axis=0, dtype=jnp.float32)
    grad_v_bias = jnp.sum(d_proj_low[:, 2 * row_width :], axis=0, dtype=jnp.float32)
    d_normed = jnp.einsum("te,ce->tc", d_proj_low, weight_qkv, preferred_element_type=jnp.float32)
    d_in_part, grad_gain_pre, grad_shift_pre = record["pre_pull"](d_normed)
    d_inputs = d_middle_res + d_in_part
    big_grads = (grad_qkv, grad_out_w, grad_up, grad_down)
    gain_grads = jnp.stack([grad_gain_pre, grad_gain_post, grad_gain_ffn])
    bias_grads = jnp.stack(
        [
            grad_shift_pre,
            grad_shift_post,
            grad_shift_ffn,
            grad_q_bias,
            grad_v_bias,
            grad_out_bias,
            grad_down_bias,
        ]
    )
    small_grads = (
        gain_grads,
        bias_grads,
        grad_mid_gain,
        jnp.stack([grad_mid_shift, grad_up_bias]),
        grad_heads,
    )
    return (d_inputs, big_grads, small_grads)


def general(
    tokens,
    grad_out,
    first_rows,
    span_of,
    w_qkv,
    w_out,
    w_up,
    w_down,
    vec_gain,
    vec_bias,
    mid_gain,
    mid_bias,
    head_scale,
):
    rows_here = tokens.shape[0]
    my_index = lax.axis_index("blk")
    my_span = span_of[my_index]
    seq_ids, offsets = row_layout(first_rows, rows_here)
    layout = (seq_ids, offsets, span_of, my_span, my_index)
    current = tokens.astype(jnp.float32)
    records = []
    for layer_index in range(2):
        weights = (
            lax.all_gather(w_qkv[layer_index], "blk", axis=0, tiled=True),
            lax.all_gather(w_out[layer_index], "blk", axis=0, tiled=True),
            lax.all_gather(w_up[layer_index], "blk", axis=0, tiled=True),
            lax.all_gather(w_down[layer_index], "blk", axis=0, tiled=True),
        )
        current, record = layer_forward(
            current,
            weights,
            vec_gain[layer_index],
            vec_bias[layer_index],
            mid_gain[layer_index],
            mid_bias[layer_index],
            head_scale[layer_index],
            layout,
        )
        records.append(record)
    results_low = current.astype(jnp.bfloat16)
    d_current = grad_out.astype(jnp.float32)
    shard_grads = [None, None]
    small_grads = [None, None]
    for layer_index in (1, 0):
        weights = (
            lax.all_gather(w_qkv[layer_index], "blk", axis=0, tiled=True),
            lax.all_gather(w_out[layer_index], "blk", axis=0, tiled=True),
            lax.all_gather(w_up[layer_index], "blk", axis=0, tiled=True),
            lax.all_gather(w_down[layer_index], "blk", axis=0, tiled=True),
        )
        d_current, big_grads, small_part = layer_backward(
            d_current, records[layer_index], weights, head_scale[layer_index], layout
        )
        shard_grads[layer_index] = (
            lax.psum_scatter(
                big_grads[0].astype(jnp.bfloat16), "blk", scatter_dimension=0, tiled=True
            ).astype(jnp.float32),
            lax.psum_scatter(
                big_grads[1].astype(jnp.bfloat16), "blk", scatter_dimension=0, tiled=True
            ).astype(jnp.float32),
            lax.psum_scatter(
                big_grads[2].astype(jnp.bfloat16), "blk", scatter_dimension=0, tiled=True
            ).astype(jnp.float32),
            lax.psum_scatter(
                big_grads[3].astype(jnp.bfloat16), "blk", scatter_dimension=0, tiled=True
            ).astype(jnp.float32),
        )
        small_grads[layer_index] = small_part
    stacked_small = [
        jnp.stack([small_grads[0][item_index], small_grads[1][item_index]])
        for item_index in range(5)
    ]
    summed_small = (
        lax.psum(stacked_small[0].astype(jnp.bfloat16), "blk").astype(jnp.float32),
        lax.psum(stacked_small[1].astype(jnp.bfloat16), "blk").astype(jnp.float32),
        lax.psum(stacked_small[2].astype(jnp.bfloat16), "blk").astype(jnp.float32),
        lax.psum(stacked_small[3].astype(jnp.bfloat16), "blk").astype(jnp.float32),
        lax.psum(stacked_small[4].astype(jnp.bfloat16), "blk").astype(jnp.float32),
    )
    stacked_big = [
        jnp.stack([shard_grads[0][item_index], shard_grads[1][item_index]])
        for item_index in range(4)
    ]
    totals = (
        lax.psum(stacked_big[0].astype(jnp.bfloat16), "batch").astype(jnp.float32),
        lax.psum(stacked_big[1].astype(jnp.bfloat16), "batch").astype(jnp.float32),
        lax.psum(stacked_big[2].astype(jnp.bfloat16), "batch").astype(jnp.float32),
        lax.psum(stacked_big[3].astype(jnp.bfloat16), "batch").astype(jnp.float32),
        lax.psum(summed_small[0].astype(jnp.bfloat16), "batch").astype(jnp.float32),
        lax.psum(summed_small[1].astype(jnp.bfloat16), "batch").astype(jnp.float32),
        lax.psum(summed_small[2].astype(jnp.bfloat16), "batch").astype(jnp.float32),
        lax.psum(summed_small[3].astype(jnp.bfloat16), "batch").astype(jnp.float32),
        lax.psum(summed_small[4].astype(jnp.bfloat16), "batch").astype(jnp.float32),
    )
    return (
        results_low,
        d_current,
        totals[0],
        totals[1],
        totals[2],
        totals[3],
        totals[4],
        totals[5],
        totals[6],
        totals[7],
        totals[8],
    )


MESH = pl.DeviceIdType.MESH
LINE = 4
HALVES = 2
CHUNK = 32
TILE = 512


def place():
    k = lax.axis_index("blk")
    return k // 4, lax.rem(k // 2, 2), lax.rem(k, 2)


def index_of(z, y, c):
    return (z * 2 + y) * 2 + c


def device(z, y, c):
    return {"blk": index_of(z, y, c)}


def hail(where):
    pl.semaphore_signal(pltpu.get_barrier_semaphore(), inc=1, device_id=where, device_id_type=MESH)


def other_group():
    return {"batch": 1 - lax.axis_index("batch")}


def lasting(microseconds):
    return pl.CostEstimate(flops=0, bytes_accessed=int(microseconds * 3.5e6), transcendentals=0)


def remote(src, dst, send, recv, where):
    return pltpu.make_async_remote_copy(
        src_ref=src, dst_ref=dst, send_sem=send, recv_sem=recv, device_id=where, device_id_type=MESH
    )


class Swap:
    def __init__(self, x_ref, o_ref, ss, rs, own_sem, per=1):
        self.x_ref, self.o_ref, self.ss, self.rs, self.own_sem = x_ref, o_ref, ss, rs, own_sem
        self.k, self.n, self.per = lax.axis_index("blk"), 4 * LINE, per

    @staticmethod
    def scratch():
        dma = pltpu.SemaphoreType.DMA
        return [dma((4 * LINE,)), dma((4 * LINE,)), dma]

    def source(self, to):
        return self.x_ref.at[pl.ds(lax.rem(to, self.x_ref.shape[0] // self.per) * self.per, self.per)]

    def place(self, at):
        return self.o_ref.at[pl.ds(at * self.per, self.per)]

    def send(self, i):
        to = lax.rem(self.k + i, self.n)
        return remote(self.source(to), self.place(self.k), self.ss.at[i], self.rs.at[i], {"blk": to})

    def receive(self, i):
        at = lax.rem(self.k - i + self.n, self.n)
        return remote(self.place(at), self.place(at), self.ss.at[i], self.rs.at[i], {"blk": at})

    def own(self):
        return pltpu.make_async_copy(self.source(self.k), self.place(self.k), self.own_sem)

    def start(self):
        def one(i, carry):
            self.send(i).start()
            return carry

        lax.fori_loop(1, self.n, one, 0)
        self.own().start()

    def finish(self):
        def one(i, carry):
            self.receive(i).wait_recv()
            self.send(i).wait_send()
            return carry

        self.own().wait()
        lax.fori_loop(1, self.n, one, 0)


class Trade:
    def __init__(self, x_ref, o_ref, ss, rs, own_sem):
        self.x_ref, self.o_ref, self.ss, self.rs, self.own_sem = x_ref, o_ref, ss, rs, own_sem
        self.z, self.y, self.c = place()

    @staticmethod
    def scratch():
        dma = pltpu.SemaphoreType.DMA
        return [dma((LINE,)), dma((LINE,)), dma]

    def source(self, to):
        return self.x_ref.at[lax.rem(to, self.x_ref.shape[0])]

    def send(self, s):
        to = lax.rem(self.z + s, LINE)
        return remote(self.source(to), self.o_ref.at[self.z], self.ss.at[s], self.rs.at[s], device(to, self.y, self.c))

    def own(self):
        return pltpu.make_async_copy(self.source(self.z), self.o_ref.at[self.z], self.own_sem)

    def start(self):
        for s in range(1, LINE):
            self.send(s).start()
        self.own().start()

    def finish(self):
        self.own().wait()
        for s in range(1, LINE):
            at = lax.rem(self.z - s + LINE, LINE)
            slot = self.o_ref.at[at]
            remote(slot, slot, self.ss.at[s], self.rs.at[s], device(at, self.y, self.c)).wait_recv()
            self.send(s).wait_send()


class Share:
    def __init__(self, x_ref, o_ref, sr, rr, sl, rl, own_sem):
        self.x_ref, self.o_ref, self.own_sem = x_ref, o_ref, own_sem
        self.sr, self.rr, self.sl, self.rl = sr, rr, sl, rl
        self.z, self.y, self.c = place()

    @staticmethod
    def scratch():
        dma = pltpu.SemaphoreType.DMA
        return [dma((LINE,))] * 4 + [dma]

    def right(self, s):
        slot = self.o_ref.at[self.z - s]
        source = self.x_ref.at[0] if s == 0 else slot
        return remote(source, slot, self.sr.at[s], self.rr.at[s + 1], device(self.z + 1, self.y, self.c))

    def left(self, s):
        slot = self.o_ref.at[self.z + s]
        source = self.x_ref.at[0] if s == 0 else slot
        return remote(source, slot, self.sl.at[s], self.rl.at[s + 1], device(self.z - 1, self.y, self.c))

    def own(self):
        return pltpu.make_async_copy(self.x_ref.at[0], self.o_ref.at[self.z], self.own_sem)

    def start(self):
        self.own().start()

        @pl.when(self.z < LINE - 1)
        def _():
            self.right(0).start()

        @pl.when(self.z > 0)
        def _():
            self.left(0).start()

    def step(self, s):
        @pl.when(self.z >= s)
        def _():
            slot = self.o_ref.at[self.z - s]
            remote(slot, slot, self.sr.at[s], self.rr.at[s], device(self.z, self.y, 1 - self.c)).wait_recv()
            if s < LINE - 1:

                @pl.when(self.z < LINE - 1)
                def _():
                    self.right(s).start()

        @pl.when(self.z + s <= LINE - 1)
        def _():
            slot = self.o_ref.at[self.z + s]
            remote(slot, slot, self.sl.at[s], self.rl.at[s], device(self.z, self.y, 1 - self.c)).wait_recv()
            if s < LINE - 1:

                @pl.when(self.z > 0)
                def _():
                    self.left(s).start()

    def finish(self):
        self.step(LINE - 1)
        self.own().wait()
        for s in range(LINE - 1):

            @pl.when((self.z < LINE - 1) & (self.z >= s))
            def _():
                self.right(s).wait_send()

            @pl.when((self.z > 0) & (self.z + s <= LINE - 1))
            def _():
                self.left(s).wait_send()


class Quad:
    def __init__(self, x_ref, o_ref, send, recv, own_sem):
        self.x_ref, self.o_ref, self.send, self.recv, self.own_sem = x_ref, o_ref, send, recv, own_sem
        self.z, self.y, self.c = place()

    @staticmethod
    def scratch():
        dma = pltpu.SemaphoreType.DMA
        return [dma((4,)), dma((4,)), dma]

    def to(self, d):
        y = 1 - self.y if d & 2 else self.y
        c = 1 - self.c if d & 1 else self.c
        dest = self.o_ref.at[self.y * 2 + self.c]
        return remote(self.x_ref.at[y * 2 + c], dest, self.send.at[d], self.recv.at[d], device(self.z, y, c))

    def own(self):
        q = self.y * 2 + self.c
        return pltpu.make_async_copy(self.x_ref.at[q], self.o_ref.at[q], self.own_sem)

    def start(self):
        for d in range(1, 4):
            self.to(d).start()
        self.own().start()

    def finish(self):
        self.own().wait()
        for d in range(1, 4):
            y = 1 - self.y if d & 2 else self.y
            c = 1 - self.c if d & 1 else self.c
            slot = self.o_ref.at[y * 2 + c]
            remote(slot, slot, self.send.at[d], self.recv.at[d], device(self.z, y, c)).wait_recv()
            self.to(d).wait_send()


class Cross:
    def __init__(self, x_ref, o_ref, ss, rs):
        self.copy = remote(x_ref, o_ref, ss, rs, other_group())

    @staticmethod
    def scratch():
        return [pltpu.SemaphoreType.DMA] * 2

    def start(self):
        self.copy.start()

    def finish(self):
        self.copy.wait()


def start_all(rides):
    for ride in rides:
        ride.start()


def finish_all(rides):
    for ride in rides:
        ride.finish()


def hail_all():
    k, n = lax.axis_index("blk"), 4 * LINE

    def one(i, carry):
        hail({"blk": lax.rem(k + i, n)})
        return carry

    lax.fori_loop(1, n, one, 0)
    x, z, y, c = plane_place()
    for d in range(4):
        hail(plane_device(1 - x, z, 1 - y if d & 2 else y, 1 - c if d & 1 else c))


def hailed_by_all():
    pl.semaphore_wait(pltpu.get_barrier_semaphore(), 4 * LINE - 1 + 4)


class GroupGather:
    def __init__(self, all_ref, sems):
        self.all_ref = all_ref
        self.sr, self.rr, self.sl, self.rl, self.sy, self.ry, self.sc, self.rc, self.se, self.re = sems
        self.z, self.y, self.c = place()
        self.half = all_ref.shape[0] // (4 * LINE * HALVES)

    @staticmethod
    def scratch():
        dma = pltpu.SemaphoreType.DMA
        return [dma((LINE, HALVES))] * 6 + [dma((2 * LINE, HALVES))] * 2 + [dma((2,))] * 2

    def block(self, z, y, h, c=None):
        c = self.c if c is None else c
        return self.all_ref.at[pl.ds((index_of(z, y, c) * HALVES + h) * self.half, self.half)]

    def right(self, s, h):
        block = self.block(self.z - s + 1, self.y, h)
        return remote(block, block, self.sr.at[s, h], self.rr.at[s, h], device(self.z + 1, self.y, self.c))

    def left(self, s, h):
        block = self.block(self.z + s - 1, self.y, h)
        return remote(block, block, self.sl.at[s, h], self.rl.at[s, h], device(self.z - 1, self.y, self.c))

    def across(self, zz, h):
        block = self.block(zz, self.y, h)
        return remote(block, block, self.sy.at[zz, h], self.ry.at[zz, h], device(self.z, 1 - self.y, self.c))

    def detour(self, to_right):
        block = self.block(self.z, 1 - self.y, HALVES - 1)
        where = device(self.z + 1, self.y, self.c) if to_right else device(self.z - 1, self.y, self.c)
        return remote(block, block, self.se.at[to_right], self.re.at[to_right], where)

    def twin(self, zz, yy, h):
        block = self.block(zz, yy, h)
        slot = zz * 2 + yy
        return remote(block, block, self.sc.at[slot, h], self.rc.at[slot, h], device(self.z, self.y, 1 - self.c))

    def arrival(self, block, send, recv):
        remote(block, block, send, recv, device(self.z, self.y, 1 - self.c)).wait_recv()

    def start(self):
        z, y = self.z, self.y
        for h in range(HALVES):

            @pl.when(z < LINE - 1)
            def _():
                self.right(1, h).start()

            @pl.when(z > 0)
            def _():
                self.left(1, h).start()

            self.across(z, h).start()
        for h in range(HALVES):
            self.twin(z, y, h).start()

    def from_across(self, zz, h, distance, to_right=0):
        if distance == 1 and h == HALVES - 1:
            self.arrival(self.block(zz, 1 - self.y, h), self.se.at[to_right], self.re.at[to_right])
        else:
            self.arrival(self.block(zz, 1 - self.y, h), self.sy.at[zz, h], self.ry.at[zz, h])
        if distance == 0 and h == HALVES - 1:

            @pl.when(self.z < LINE - 1)
            def _():
                self.detour(1).start()

            @pl.when(self.z > 0)
            def _():
                self.detour(0).start()

        self.twin(zz, 1 - self.y, h).start()

    def pass_on(self, zz, h, distance):
        if distance > 1 or h < HALVES - 1:
            self.across(zz, h).start()
        self.twin(zz, self.y, h).start()

    def run(self):
        z, y = self.z, self.y
        for s in range(1, LINE):
            for h in range(HALVES):

                @pl.when(z >= s)
                def _():
                    self.arrival(self.block(z - s, y, h), self.sr.at[s, h], self.rr.at[s, h])
                    if s < LINE - 1:

                        @pl.when(z < LINE - 1)
                        def _():
                            self.right(s + 1, h).start()

                    self.pass_on(z - s, h, s)

                @pl.when(z + s <= LINE - 1)
                def _():
                    self.arrival(self.block(z + s, y, h), self.sl.at[s, h], self.rl.at[s, h])
                    if s < LINE - 1:

                        @pl.when(z > 0)
                        def _():
                            self.left(s + 1, h).start()

                    self.pass_on(z + s, h, s)

                if s == 1:
                    self.from_across(z, h, 0)
                else:

                    @pl.when(z >= s - 1)
                    def _():
                        self.from_across(z - s + 1, h, s - 1, 1)

                    @pl.when(z + s - 1 <= LINE - 1)
                    def _():
                        self.from_across(z + s - 1, h, s - 1, 0)

        for h in range(HALVES):

            @pl.when(z >= LINE - 1)
            def _():
                self.from_across(z - LINE + 1, h, LINE - 1)

            @pl.when(z <= 0)
            def _():
                self.from_across(z + LINE - 1, h, LINE - 1)

        for h in range(HALVES):
            for zz in range(LINE):
                for yy in range(2):
                    slot = zz * 2 + yy
                    self.arrival(self.block(zz, yy, h, 1 - self.c), self.sc.at[slot, h], self.rc.at[slot, h])

    def finish(self):
        z = self.z

        @pl.when(z < LINE - 1)
        def _():
            self.detour(1).wait_send()

        @pl.when(z > 0)
        def _():
            self.detour(0).wait_send()

        for h in range(HALVES):
            for zz in range(LINE):
                if h < HALVES - 1:
                    self.across(zz, h).wait_send()
                else:

                    @pl.when((zz != z - 1) & (zz != z + 1))
                    def _():
                        self.across(zz, h).wait_send()

                for yy in range(2):
                    self.twin(zz, yy, h).wait_send()
            for s in range(1, LINE):

                @pl.when((z < LINE - 1) & (z >= s - 1))
                def _():
                    self.right(s, h).wait_send()

                @pl.when((z > 0) & (z + s - 1 <= LINE - 1))
                def _():
                    self.left(s, h).wait_send()


def order_at(z, t):
    table = ((3, 2, 1, 0), (3, 0, 2, 1), (0, 3, 1, 2), (0, 1, 2, 3))
    low = jnp.where(z == 0, table[0][t], table[1][t])
    high = jnp.where(z == 2, table[2][t], table[3][t])
    return jnp.where(z < 2, low, high)


class GroupScatter:
    def __init__(self, part_ref, bufs, sems):
        self.part_ref = part_ref
        self.twins, self.ysend, self.yrecv, self.zsend, self.zrecv, self.esend, self.erecv = bufs
        self.sc, self.rc, self.sy, self.ry, self.sz, self.rzr, self.rzl, self.se, self.re = sems
        self.z, self.y, self.c = place()
        self.half = part_ref.shape[0] // (4 * LINE * HALVES)

    @staticmethod
    def scratch(rows, columns):
        dma = pltpu.SemaphoreType.DMA
        bufs = [pltpu.VMEM((n, rows, columns), jnp.bfloat16) for n in (2 * LINE, LINE, LINE, LINE - 1, LINE + 1)]
        bufs += [pltpu.VMEM((2, rows // HALVES, columns), jnp.bfloat16)] * 2
        return bufs, [dma((2 * LINE, HALVES))] * 2 + [dma((LINE, HALVES))] * 5 + [dma((2,))] * 2

    def part(self, h):
        return pl.ds(h * self.half, self.half)

    def rows(self, t, own_y, c, h):
        y = self.y if own_y else 1 - self.y
        return pl.ds((index_of(order_at(self.z, t), y, c) * HALVES + h) * self.half, self.half)

    def twin(self, t, own_y, h):
        slot = t * 2 + own_y
        source = self.part_ref.at[self.rows(t, own_y, 1 - self.c, h)]
        dest = self.twins.at[slot, self.part(h)]
        return remote(source, dest, self.sc.at[slot, h], self.rc.at[slot, h], device(self.z, self.y, 1 - self.c))

    def across(self, t, h):
        source, dest = self.ysend.at[t, self.part(h)], self.yrecv.at[t, self.part(h)]
        return remote(source, dest, self.sy.at[t, h], self.ry.at[t, h], device(self.z, 1 - self.y, self.c))

    def along(self, d, t, h, to_right):
        sem = self.rzr if to_right else self.rzl
        where = device(self.z + 1, self.y, self.c) if to_right else device(self.z - 1, self.y, self.c)
        slot = d if to_right else self.from_right(d, self.z - 1)
        return remote(self.zsend.at[t, self.part(h)], self.zrecv.at[slot, self.part(h)], self.sz.at[t, h], sem.at[d, h], where)

    @staticmethod
    def from_right(d, z):
        return jnp.where(d == z, LINE, d)

    def arrived(self, d, h, to_right):
        sem = self.rzr if to_right else self.rzl
        slot = self.zrecv.at[d if to_right else self.from_right(d, self.z), self.part(h)]
        remote(slot, slot, self.sz.at[0, h], sem.at[d, h], device(self.z, self.y, 1 - self.c)).wait_recv()

    def wide(self, ref, slot, h):
        return ref[slot, self.part(h)].astype(jnp.float32)

    def chip(self, t, own_y, h):
        return self.part_ref[self.rows(t, own_y, self.c, h)].astype(jnp.float32) + self.wide(self.twins, t * 2 + own_y, h)

    def owner(self, t, own_y, c):
        return index_of(order_at(self.z, t), self.y if own_y else 1 - self.y, c)

    def start(self, t, own_y):
        for h in range(HALVES):
            self.twin(t, own_y, h).start()

    def detour(self, to_right):
        where = device(self.z + 1, self.y, self.c) if to_right else device(self.z - 1, self.y, self.c)
        source, dest = self.esend.at[to_right], self.erecv.at[to_right]
        return remote(source, dest, self.se.at[to_right], self.re.at[to_right], where)

    def detoured(self, t, h):
        d = order_at(self.z, t)
        return (d == self.z + 1, d == self.z - 1) if h == HALVES - 1 and t < LINE - 1 else (False, False)

    def first(self):
        z = self.z
        for t in range(LINE):
            for h in range(HALVES):
                self.twin(t, 0, h).wait_recv()
                if h < HALVES - 1:
                    self.ysend[t, self.part(h)] = self.chip(t, 0, h).astype(jnp.bfloat16)
                    self.across(t, h).start()
                elif t < LINE - 1:
                    right, left = self.detoured(t, h)
                    for to_right, here in ((1, right), (0, left)):

                        @pl.when(here)
                        def _():
                            self.esend[to_right] = self.chip(t, 0, h).astype(jnp.bfloat16)
                            self.detour(to_right).start()

                    @pl.when(jnp.logical_not(right | left))
                    def _():
                        self.ysend[t, self.part(h)] = self.chip(t, 0, h).astype(jnp.bfloat16)
                        self.across(t, h).start()
                else:

                    def added(to_right):
                        slot = self.erecv.at[to_right]
                        where = device(z, self.y, 1 - self.c)
                        remote(slot, slot, self.se.at[to_right], self.re.at[to_right], where).wait_recv()
                        return self.erecv[to_right].astype(jnp.float32)

                    @pl.when(z == 0)
                    def _():
                        self.ysend[t, self.part(h)] = (self.chip(t, 0, h) + added(0)).astype(jnp.bfloat16)

                    @pl.when(z == LINE - 1)
                    def _():
                        self.ysend[t, self.part(h)] = (self.chip(t, 0, h) + added(1)).astype(jnp.bfloat16)

                    @pl.when((z > 0) & (z < LINE - 1))
                    def _():
                        self.ysend[t, self.part(h)] = (self.chip(t, 0, h) + added(0) + added(1)).astype(jnp.bfloat16)

                    self.across(t, h).start()

    def second(self, o_ref, between=()):
        z = self.z
        for t in range(LINE):
            if 0 < t <= len(between):
                between[t - 1]()
            d = order_at(z, t)
            for h in range(HALVES):
                self.twin(t, 1, h).wait_recv()
                if h == HALVES - 1 and t < LINE - 1:
                    right, left = self.detoured(t, h)

                    @pl.when(right | left)
                    def _():
                        self.yrecv[t, self.part(h)] = jnp.zeros((self.half, self.yrecv.shape[2]), jnp.bfloat16)

                    @pl.when(jnp.logical_not(right | left))
                    def _():
                        self.across(t, h).wait_recv()
                else:
                    self.across(t, h).wait_recv()

                def summed(t=t, h=h):
                    return self.chip(t, 1, h) + self.wide(self.yrecv, t, h)

                if t < LINE - 1:
                    for to_right in (True, False):

                        @pl.when((d > z) if to_right else (d < z))
                        def _():
                            first = (z == 0) if to_right else (z == LINE - 1)

                            @pl.when(first)
                            def _():
                                self.zsend[t, self.part(h)] = summed().astype(jnp.bfloat16)

                            @pl.when(jnp.logical_not(first))
                            def _():
                                self.arrived(d, h, to_right)
                                self.zsend[t, self.part(h)] = (summed() + self.wide(self.zrecv, d, h)).astype(jnp.bfloat16)

                            self.along(d, t, h, to_right).start()
                else:

                    @pl.when(z > 0)
                    def _():
                        self.arrived(z, h, True)

                    @pl.when(z < LINE - 1)
                    def _():
                        self.arrived(z, h, False)

                    @pl.when(z == 0)
                    def _():
                        o_ref[self.part(h)] = summed() + self.wide(self.zrecv, LINE, h)

                    @pl.when(z == LINE - 1)
                    def _():
                        o_ref[self.part(h)] = summed() + self.wide(self.zrecv, z, h)

                    @pl.when((z > 0) & (z < LINE - 1))
                    def _():
                        o_ref[self.part(h)] = summed() + self.wide(self.zrecv, z, h) + self.wide(self.zrecv, LINE, h)

    def finish(self):
        for to_right, here in ((1, self.z < LINE - 1), (0, self.z > 0)):

            @pl.when(here)
            def _():
                self.detour(to_right).wait_send()

        for h in range(HALVES):
            for t in range(LINE):
                if h == HALVES - 1 and t < LINE - 1:
                    right, left = self.detoured(t, h)

                    @pl.when(jnp.logical_not(right | left))
                    def _():
                        self.across(t, h).wait_send()
                else:
                    self.across(t, h).wait_send()
                self.twin(t, 0, h).wait_send()
                self.twin(t, 1, h).wait_send()
            for t in range(LINE - 1):
                self.along(0, t, h, True).wait_send()


NN = (((1,), (0,)), ((), ()))
NT = (((1,), (1,)), ((), ()))
TN = (((0,), (0,)), ((), ()))


def mul(a, b, dims=NN):
    return lax.dot_general(a, b, dims, preferred_element_type=jnp.float32)


def tile_at(t):
    return pl.ds(pl.multiple_of(t * TILE, TILE), TILE)


def chunk_at(index, rows=CHUNK):
    return pl.ds(pl.multiple_of(index * rows, rows), rows)


def diagonal(p):
    key = lax.broadcasted_iota(jnp.int32, p.shape, 0)
    query = lax.broadcasted_iota(jnp.int32, p.shape, 1)
    return key <= query


PLANE = 8


def plane_place():
    x = lax.axis_index("batch")
    z, y, c = place()
    return x, z, y, c


def plane_device(x, z, y, c):
    return {"batch": x, "blk": index_of(z, y, c)}


def plane_index(x, y, c):
    return (x * 2 + y) * 2 + c


class PlaneGather:
    def __init__(self, all_ref, sems):
        self.all_ref = all_ref
        self.sx, self.rx, self.sy, self.ry, self.sc, self.rc = sems
        self.x, self.z, self.y, self.c = plane_place()
        self.half = all_ref.shape[0] // (2 * PLANE)

    @staticmethod
    def scratch():
        dma = pltpu.SemaphoreType.DMA
        return [dma((3,))] * 4 + [dma((PLANE,))] * 2

    def piece(self, x, y, c, h):
        return self.all_ref.at[pl.ds(plane_index(x, y, c) * 2 * self.half + h * self.half, self.half)]

    def over_x(self, i):
        x, y, c = self.x, self.y, self.c
        piece = self.piece(x, y if i < 2 else 1 - y, c, (0, 1, 1)[i])
        return remote(piece, piece, self.sx.at[i], self.rx.at[i], plane_device(1 - x, self.z, y, c))

    def over_y(self, i):
        x, y, c = self.x, self.y, self.c
        piece = self.piece(x if i < 2 else 1 - x, y, c, (1, 0, 0)[i])
        return remote(piece, piece, self.sy.at[i], self.ry.at[i], plane_device(x, self.z, 1 - y, c))

    def from_x(self, i):
        x, y, c = self.x, self.y, self.c
        piece = self.piece(1 - x, y if i < 2 else 1 - y, c, (0, 1, 1)[i])
        remote(piece, piece, self.sx.at[i], self.rx.at[i], plane_device(1 - x, self.z, y, c)).wait_recv()

    def from_y(self, i):
        x, y, c = self.x, self.y, self.c
        piece = self.piece(x if i < 2 else 1 - x, 1 - y, c, (1, 0, 0)[i])
        remote(piece, piece, self.sy.at[i], self.ry.at[i], plane_device(x, self.z, 1 - y, c)).wait_recv()

    def twin(self, other_x, other_y, h):
        x = 1 - self.x if other_x else self.x
        y = 1 - self.y if other_y else self.y
        slot = (other_x * 2 + other_y) * 2 + h
        piece = self.piece(x, y, self.c, h)
        return remote(piece, piece, self.sc.at[slot], self.rc.at[slot], plane_device(self.x, self.z, self.y, 1 - self.c))

    def from_twin(self, other_x, other_y, h):
        x = 1 - self.x if other_x else self.x
        y = 1 - self.y if other_y else self.y
        slot = (other_x * 2 + other_y) * 2 + h
        piece = self.piece(x, y, 1 - self.c, h)
        where = plane_device(self.x, self.z, self.y, 1 - self.c)
        remote(piece, piece, self.sc.at[slot], self.rc.at[slot], where).wait_recv()

    def start(self):
        self.over_x(0).start()
        self.over_y(0).start()
        self.over_x(1).start()
        self.over_y(1).start()
        self.twin(0, 0, 0).start()
        self.twin(0, 0, 1).start()

    def near(self):
        self.from_x(0)
        self.over_y(2).start()
        self.twin(1, 0, 0).start()
        self.from_y(0)
        self.over_x(2).start()
        self.twin(0, 1, 1).start()
        self.from_y(1)
        self.twin(0, 1, 0).start()
        for other_y in range(2):
            for h in range(2):
                self.from_twin(0, other_y, h)

    def far(self):
        self.from_x(1)
        self.twin(1, 0, 1).start()
        self.from_x(2)
        self.twin(1, 1, 1).start()
        self.from_y(2)
        self.twin(1, 1, 0).start()
        for other_y in range(2):
            for h in range(2):
                self.from_twin(1, other_y, h)

    def finish(self):
        for i in range(3):
            self.over_x(i).wait_send()
            self.over_y(i).wait_send()
        for other_x in range(2):
            for other_y in range(2):
                for h in range(2):
                    self.twin(other_x, other_y, h).wait_send()


class PlaneScatter:
    def __init__(self, part_ref, bufs, sems):
        self.part_ref = part_ref
        self.twins, self.xs, self.xr, self.ys, self.yr = bufs
        self.sx, self.rx, self.sy, self.ry, self.sc, self.rc = sems
        self.x, self.z, self.y, self.c = plane_place()
        self.half = part_ref.shape[0] // (2 * PLANE)

    @staticmethod
    def scratch(rows, columns):
        dma = pltpu.SemaphoreType.DMA
        half = pltpu.VMEM((3, rows // 2, columns), jnp.bfloat16)
        return [pltpu.VMEM((4, rows, columns), jnp.bfloat16)] + [half] * 4, [dma((3,))] * 4 + [dma((4,))] * 2

    def rows(self, which, c, h=None):
        x = self.x if which >= 2 else 1 - self.x
        y = self.y if which % 2 else 1 - self.y
        at = plane_index(x, y, c) * 2 * self.half
        return pl.ds(at, 2 * self.half) if h is None else pl.ds(at + h * self.half, self.half)

    def twin(self, which):
        where = plane_device(self.x, self.z, self.y, 1 - self.c)
        source = self.part_ref.at[self.rows(which, 1 - self.c)]
        return remote(source, self.twins.at[which], self.sc.at[which], self.rc.at[which], where)

    def over_x(self, i):
        return remote(
            self.xs.at[i], self.xr.at[i], self.sx.at[i], self.rx.at[i], plane_device(1 - self.x, self.z, self.y, self.c)
        )

    def over_y(self, i):
        return remote(
            self.ys.at[i], self.yr.at[i], self.sy.at[i], self.ry.at[i], plane_device(self.x, self.z, 1 - self.y, self.c)
        )

    def chip(self, which, h):
        own = self.part_ref[self.rows(which, self.c, h)].astype(jnp.float32)
        return own + self.twins[which, h * self.half : (h + 1) * self.half].astype(jnp.float32)

    def over_first(self):
        self.twin(0).wait_recv()
        self.xs[0] = self.chip(0, 0).astype(jnp.bfloat16)
        self.over_x(0).start()
        self.ys[0] = self.chip(0, 1).astype(jnp.bfloat16)
        self.over_y(0).start()
        self.twin(1).wait_recv()
        self.xs[1] = self.chip(1, 0).astype(jnp.bfloat16)
        self.over_x(1).start()

    def first(self):
        self.twin(2).wait_recv()
        self.ys[1] = self.chip(2, 1).astype(jnp.bfloat16)
        self.over_y(1).start()

    def second(self):
        self.over_x(0).wait_recv()
        self.ys[2] = (self.chip(2, 0) + self.xr[0].astype(jnp.float32)).astype(jnp.bfloat16)
        self.over_y(2).start()
        self.over_y(0).wait_recv()
        self.xs[2] = (self.chip(1, 1) + self.yr[0].astype(jnp.float32)).astype(jnp.bfloat16)
        self.over_x(2).start()

    def finish(self, o_ref):
        half = self.half
        self.twin(3).wait_recv()
        self.over_x(1).wait_recv()
        self.over_y(1).wait_recv()
        self.over_y(2).wait_recv()
        o_ref[0:half] = self.chip(3, 0) + self.xr[1].astype(jnp.float32) + self.yr[2].astype(jnp.float32)
        self.over_x(2).wait_recv()
        o_ref[half : 2 * half] = self.chip(3, 1) + self.yr[1].astype(jnp.float32) + self.xr[2].astype(jnp.float32)
        for which in range(4):
            self.twin(which).wait_send()
        for i in range(3):
            self.over_x(i).wait_send()
            self.over_y(i).wait_send()


class PlanePool:
    def __init__(self, own_ref, got_ref, send, recv):
        self.own_ref, self.got_ref, self.send, self.recv = own_ref, got_ref, send, recv
        self.x, self.z, self.y, self.c = plane_place()

    def others(self):
        for d in range(1, PLANE):
            x = 1 - self.x if d & 4 else self.x
            y = 1 - self.y if d & 2 else self.y
            c = 1 - self.c if d & 1 else self.c
            yield d, x, y, c

    def copies(self):
        slot = self.got_ref.at[plane_index(self.x, self.y, self.c)]
        own = self.own_ref.at[0] if len(self.own_ref.shape) == len(self.got_ref.shape) else self.own_ref
        for d, x, y, c in self.others():
            yield remote(own, slot, self.send.at[d], self.recv.at[d], plane_device(x, self.z, y, c))

    def start(self):
        for copy in self.copies():
            copy.start()
        self.got_ref[plane_index(self.x, self.y, self.c)] = self.own_ref[...].reshape(self.got_ref.shape[1:])

    def finish(self):
        for d, x, y, c in self.others():
            slot = self.got_ref.at[plane_index(x, y, c)]
            remote(slot, slot, self.send.at[d], self.recv.at[d], plane_device(x, self.z, y, c)).wait_recv()
        for copy in self.copies():
            copy.wait_send()


def span_at(th, width):
    return pl.ds(pl.multiple_of(th * width, 128), width)


def units_at(ut):
    return pl.ds(pl.multiple_of(ut * 256, 256), 256)


def mean_and_rate(stat, hidden_all):
    return stat[0:1], lax.rsqrt(stat[1:2] * (1.0 / hidden_all) + EPSILON)


class Refs:
    def __init__(self, **named):
        self.__dict__.update(named)


def launch(call, kernel, inputs, outputs, scratch, collective_id, microseconds, vmem_mib):
    def body(*refs):
        refs = list(refs)
        named = Refs()
        for key in [*inputs, *outputs]:
            setattr(named, key, refs.pop(0))
        for key, what in scratch.items():
            if isinstance(what, list):
                setattr(named, key, [refs.pop(0) for _ in what])
            else:
                setattr(named, key, refs.pop(0))
        kernel(named)

    results = call(
        body,
        out_shape=[shape for shape, _ in outputs.values()],
        in_specs=[pl.BlockSpec(memory_space=space) for _, space in inputs.values()],
        out_specs=[pl.BlockSpec(memory_space=space) for _, space in outputs.values()],
        scratch_shapes=[entry for what in scratch.values() for entry in (what if isinstance(what, list) else [what])],
        cost_estimate=lasting(microseconds),
        compiler_params=pltpu.CompilerParams(
            collective_id=collective_id, has_side_effects=True, vmem_limit_bytes=vmem_mib << 20
        ),
    )(*[array for array, _ in inputs.values()])
    return Refs(**dict(zip(outputs, results)))


def normed(values, gain, shift):
    centred = values - jnp.mean(values, axis=-1, keepdims=True)
    spread = jnp.mean(centred * centred, axis=-1, keepdims=True)
    return centred * lax.rsqrt(spread + EPSILON) * gain + shift


def normed_back(values, gain, grads):
    centred = values - jnp.mean(values, axis=-1, keepdims=True)
    rate = lax.rsqrt(jnp.mean(centred * centred, axis=-1, keepdims=True) + EPSILON)
    unit = centred * rate
    scaled = grads * gain
    back = rate * (
        scaled - jnp.mean(scaled, axis=-1, keepdims=True) - unit * jnp.mean(scaled * unit, axis=-1, keepdims=True)
    )
    return back, jnp.sum(grads * unit, axis=0, keepdims=True), jnp.sum(grads, axis=0, keepdims=True)


def unfold_head(blocks_ref, w_ref):
    for j in range(blocks_ref.shape[0]):
        for part in range(2):
            at = slice(64 * j + 32 * part, 64 * j + 32 * part + 32)
            w_ref[at, 0:128] = blocks_ref[j, :, 128 * part : 128 * part + 128]
            w_ref[at, 128:192] = blocks_ref[j, :, 256 + 64 * part : 320 + 64 * part]


def fold_head(w, head):
    width = w.shape[1] // 3
    at = [slice(part * width + 64 * head, part * width + 64 * head + 64) for part in range(3)]
    halves = [w[0:32], w[32:64]]
    pieces = [half[:, at[part]] for half in halves for part in (0, 2)] + [half[:, at[1]] for half in halves]
    return jnp.concatenate(pieces, axis=1)


def unit_lanes(z, slot):
    return pl.ds(pl.multiple_of(z * PLANE * 128 + slot * 128, 128), 128)


def unit_columns(vectors, slot, column_refs):
    pieces = [vector[:, unit_lanes(z, slot)] for vector in vectors for z in range(LINE)]
    pieces.append(jnp.zeros((16 - len(pieces), 128), jnp.float32))
    turned = jnp.transpose(jnp.concatenate(pieces, axis=0))
    for i, ref in enumerate(column_refs):
        for z in range(LINE):
            ref[128 * z : 128 * z + 128] = turned[:, i * LINE + z : i * LINE + z + 1]


def of_layer(ref, layer):
    return [ref.at[kind, pl.ds(layer, 1)] for kind in range(ref.shape[0])]


def own_head(row, index):
    pair = row[:, pl.ds(pl.multiple_of(index // 2 * 128, 128), 128)]
    return jnp.where(lax.rem(index, 2) == 0, pair[:, 0:64], pair[:, 64:128])


def chunks_of(ref, t):
    per_tile = TILE // CHUNK
    part = ref[pl.ds(t * per_tile, per_tile)]
    return part.reshape(per_tile * part.shape[1], part.shape[2])


def alive(cut, i, j):
    return jnp.where((i >= cut) & (j < cut), NEGATIVE, 0.0)


def natural_rows(slot, zz):
    x, y, c = slot // 4, slot // 2 % 2, slot % 2
    return 64 * index_of(zz, y, c) + 32 * x


def forward_kernel(layer, hidden_all, r):
    first = layer == 0
    x, z, y, c = plane_place()
    index, slot = index_of(z, y, c), plane_index(x, y, c)
    unit_slot = (y * 2 + c) * 2 + x
    rows, columns = r.x_in.shape
    total = r.hb_all.shape[0]
    tiles, chunks, per_tile = total // TILE, total // CHUNK, TILE // CHUNK
    gather = GroupGather(r.hb_all, r.gather_sems)
    hail_all()
    gains, biases = of_layer(r.gains, layer), of_layer(r.biases, layer)
    if first:
        load_qkv = pltpu.make_async_copy(r.w_qkv, r.qkv_in, r.prep_sem.at[0])
        load_qkv.start()
        for l in range(2):
            for q in range(4):
                for zz in range(LINE):
                    source = r.w_up.at[l, :, unit_lanes(zz, q * 2 + x)]
                    dest = r.unit_src.at[l, q, :, pl.ds(zz * 128, 128)]
                    pltpu.make_async_copy(source, dest, r.prep_sem.at[1 + l]).start()
    value = r.x_in[...].astype(jnp.float32)
    r.hb_all[pl.ds(index * rows, rows)] = normed(value, gains[0][...], biases[0][...]).astype(jnp.bfloat16)
    head_ride = Swap(r.head_src.at[0], r.head_blocks, *r.head_sems) if first else None
    down_ride = Share(r.w_down.at[layer, pl.ds(x, 1)], r.down_blocks, *r.down_sems)
    out_ride = Trade(r.w_out.at[layer, pl.ds(x, 1)], r.out_got, *r.out_sems)
    if first:
        quads = [Quad(r.unit_src.at[l], r.unit_quad.at[l], *r.quad_sems[3 * l : 3 * l + 3]) for l in range(2)]
        unit_ride = Share(r.unit_quad.at[pl.ds(0, 1)], r.unit_blocks, *r.unit_sems)
        next_unit_ride = Share(r.unit_quad.at[pl.ds(1, 1)], r.next_unit, *r.next_unit_sems)
        next_head_ride = Swap(r.head_src.at[1], r.next_head, *r.next_head_sems)
    if first:
        load_qkv.wait()
        for head in range(4 * LINE):
            r.head_src[0, head] = fold_head(r.qkv_in[0], head)
    load_head = pltpu.make_async_copy(r.head_blocks, r.head_in, r.load_sem.at[0])
    load_unit = pltpu.make_async_copy(r.unit_blocks, r.unit_in, r.load_sem.at[1])
    load_down = pltpu.make_async_copy(r.down_blocks, r.down_w, r.load_sem.at[2])
    hailed_by_all()
    if first:
        head_ride.start()
    gather.start()
    if first:
        out_ride.start()
    mids = [r.mid_gain_all.at[pl.ds(layer, 1)], r.mid_bias_all.at[layer, pl.ds(0, 1)], r.mid_bias_all.at[layer, pl.ds(1, 1)]]
    unit_columns(mids, unit_slot, (r.mid_gain, r.mid_shift, r.mid_bias))
    head_bias = [own_head(biases[row], index) for row in (3, 4)] + [jnp.zeros((1, 64), jnp.float32)]
    head_bias = jnp.concatenate(head_bias, axis=1)
    if not first:
        load_head.start()
        r.dy_all[pl.ds(slot * rows, rows)] = r.dy[...]
        load_unit.start()
    if first:
        for l in range(2):
            pltpu.make_async_copy(r.unit_src.at[l], r.unit_src.at[l], r.prep_sem.at[1 + l]).wait()
        quads[0].start()
    gather.run()
    if first:
        quads[0].finish()
        unit_ride.start()
    out_rows = r.out_all.shape[0] // PLANE
    out_gather = PlaneGather(r.out_all, r.out_gather_sems)

    def gather_out():
        out_ride.finish()
        for zz in range(LINE):
            r.out_all[pl.ds(slot * out_rows + zz * 32, 32)] = r.out_got[zz]
        out_gather.start()

    if first:
        gather_out()
    else:
        out_ride.start()
    dy_gather = None if first else PlaneGather(r.dy_all, r.dy_gather_sems)
    if first:
        head_ride.finish()
        load_head.start()
    else:
        dy_gather.start()
    load_head.wait()
    unfold_head(r.head_in, r.head_w)

    def project(t, carry):
        rows_t = (mul(r.hb_all[tile_at(t)], r.head_w[...]) + head_bias).astype(jnp.bfloat16)
        r.flat[pl.ds(t * per_tile, per_tile)] = rows_t.reshape(per_tile, CHUNK, 192)
        return carry

    lax.fori_loop(0, tiles, project, 0)
    def arrange(p, carry):
        r.qvk[p] = r.flat[r.table[p]]
        return carry

    lax.fori_loop(0, chunks, arrange, 0)

    def prepare(t, carry):
        rows_t = chunks_of(r.qvk, t)
        r.queries[tile_at(t)] = rows_t[:, 0:64] * 0.125
        r.keys[tile_at(t)] = rows_t[:, 128:192]
        turned = jnp.transpose(rows_t[:, 0:128].astype(jnp.float32))
        r.values_t[:, tile_at(t)] = turned[64:128].astype(jnp.bfloat16)
        return carry

    lax.fori_loop(0, tiles, prepare, 0)
    cut = r.table[2 * chunks]
    for i in range(tiles):
        at = slice(i * TILE, (i + 1) * TILE)
        query = r.queries[at]

        def block(j, state, masked):
            peak, part, mixed = state
            scores = mul(r.keys[tile_at(j)], query, NT)
            bias = 0.0 if masked else alive(cut, i, j)
            if masked:
                keep = diagonal(scores)
                scores = jnp.where(keep, scores, NEGATIVE)
            new_peak = jnp.maximum(peak, jnp.max(scores, axis=0, keepdims=True) + bias)
            weights = jnp.exp(scores - (new_peak - bias))
            if masked:
                weights = jnp.where(keep, weights, 0.0)
            factor = jnp.exp(peak - new_peak)
            part = part * factor + jnp.sum(weights, axis=0, keepdims=True)
            mixed = mixed * factor + mul(r.values_t[:, tile_at(j)], weights.astype(jnp.bfloat16))
            return (new_peak, part, mixed)

        state = (
            jnp.full((1, TILE), NEGATIVE, jnp.float32),
            jnp.zeros((1, TILE), jnp.float32),
            jnp.zeros((64, TILE), jnp.float32),
        )
        state = block(i, state, True)
        if i > 0:
            state = lax.fori_loop(0, i, functools.partial(block, masked=False), state)
        peak, part, mixed = state
        mixed = mixed / part
        r.lse[:, at] = peak + jnp.log(part)
        r.head_out[:, at] = mixed
        pairs = (jnp.transpose(mixed) * r.scales[layer, index]).reshape(per_tile, 2, CHUNK // 2, 64)
        pairs = jnp.concatenate([pairs[:, 0], pairs[:, 1]], axis=-1).astype(jnp.bfloat16)
        r.pairs[i * per_tile : (i + 1) * per_tile] = pairs
        if i == 2 and first:
            unit_ride.step(1)
        if i == 1 and not first:
            gather_out()
        if i == (3 if first else tiles - 1):
            out_gather.near()
    if first:
        unit_ride.step(2)
    else:
        dy_gather.near()
    per_block = rows // CHUNK

    def pack(p, carry):
        r.packed[p] = r.pairs[r.table[chunks + p]]
        return carry

    lax.fori_loop(0, chunks, pack, 0)
    mix = Swap(r.packed, r.mixed, *r.mix_sems, per=per_block)
    mix.start()
    out_gather.far()
    if not first:
        dy_gather.far()
    for s in range(PLANE):
        for zz in range(LINE):
            at = natural_rows(s, zz)
            r.out_w[at : at + 32] = r.out_all[s * out_rows + zz * 32 : s * out_rows + zz * 32 + 32]
    out_gather.finish()

    def turn_units():
        for j in range(2 * LINE):
            pair = r.unit_in[j // 2, j % 2 * 2 : j % 2 * 2 + 2].reshape(128, r.unit_in.shape[3])
            r.unit_t[:, 128 * j : 128 * j + 128] = jnp.transpose(pair)

    if first:
        for head in range(4 * LINE):
            r.head_src[1, head] = fold_head(r.qkv_in[1], head)
    else:
        load_unit.wait()
        turn_units()
    saves = [
        pltpu.make_async_copy(source, dest, r.save_sem.at[i])
        for i, (source, dest) in enumerate(
            (
                (r.hb_all, r.hb_all_out), (r.qvk, r.qvk_out), (r.out_w, r.out_w_out), (r.rows_all, r.rows_all_out),
                (r.unit_t, r.unit_t_out), (r.act, r.act_out), (r.slope, r.slope_out), (r.mid, r.mid_out),
            )
        )
    ]
    start_all(saves[:3])
    mix.finish()
    down_ride.start()
    for g in range(columns // 128):
        left, right = (
            r.mixed[h * per_block : (h + 1) * per_block].reshape(rows // 2, 128) for h in (2 * g, 2 * g + 1)
        )
        low = jnp.concatenate([left[:, 0:64], right[:, 0:64]], axis=1)
        high = jnp.concatenate([left[:, 64:128], right[:, 64:128]], axis=1)
        for p in range(per_block):
            at = slice(p * (CHUNK // 2), (p + 1) * (CHUNK // 2))
            r.ab[p * CHUNK : p * CHUNK + CHUNK // 2, 128 * g : 128 * g + 128] = low[at]
            r.ab[p * CHUNK + CHUNK // 2 : (p + 1) * CHUNK, 128 * g : 128 * g + 128] = high[at]
    branch = mul(r.ab[...], r.out_w[...]) + biases[5][...]
    r.branch[...] = branch
    middle = value + normed(branch, gains[1][...], biases[1][...])
    r.middle[...] = middle

    own = pl.ds(slot * rows, rows)
    r.rows_all[own] = normed(middle, gains[2][...], biases[2][...]).astype(jnp.bfloat16)
    plane_gather = PlaneGather(r.rows_all, r.plane_gather_sems)
    plane_scatter = PlaneScatter(r.part, r.plane_bufs, r.plane_sems)
    pool = PlanePool(r.own_stat, r.got_stat, *r.pool_sems)
    plane_gather.start()
    hidden = r.act.shape[0]
    width = r.act.shape[1] // 2
    if first:
        unit_ride.finish()
        load_unit.start()
        quads[1].start()
    down_ride.step(1)
    if first:
        load_unit.wait()
        turn_units()

    def climb(th):
        at = span_at(th, width)

        def units(ut, carry):
            here = units_at(ut)
            upper = mul(r.unit_t[here], r.rows_all[pl.ds(th * width, width)], NT) + r.mid_bias[here]
            chance = 0.5 * (1.0 + lax.erf(upper * (0.5**0.5)))
            r.act[here, at] = upper * chance
            slope = chance + upper * (jnp.exp(-0.5 * upper * upper) * 0.3989422804014327)
            r.slope[here, at] = slope.astype(jnp.bfloat16)
            return carry

        lax.fori_loop(0, hidden // 256, units, 0)
        values = r.act[:, at]
        mean = jnp.mean(values, axis=0, keepdims=True)
        apart = values - mean
        r.own_stat[0:1, at] = mean
        r.own_stat[1:2, at] = jnp.sum(apart * apart, axis=0, keepdims=True)

    plane_gather.near()
    down_ride.step(2)
    climb(x)
    plane_gather.far()
    if first:
        down_ride.finish()
        load_down.start()
        quads[1].finish()
        next_unit_ride.start()
        next_head_ride.start()
    climb(1 - x)
    pool.start()
    if not first:
        down_ride.finish()
        load_down.start()
    start_all(saves[3:7])
    pool.finish()
    if first:
        next_unit_ride.step(1)
    load_down.wait()
    means = [r.got_stat[i, 0:1] for i in range(PLANE)]
    mean = functools.reduce(jnp.add, means) * (1.0 / PLANE)
    apart = functools.reduce(jnp.add, [(m - mean) * (m - mean) for m in means])
    r.stat[0:1] = mean
    r.stat[1:2] = functools.reduce(jnp.add, [r.got_stat[i, 1:2] for i in range(PLANE)]) + apart * float(hidden)

    def descend(th):
        at = span_at(th, width)
        mean, rate = mean_and_rate(r.stat[:, at], hidden_all)

        def units(ut, carry):
            here = units_at(ut)
            low = (r.act[here, at] - mean) * rate * r.mid_gain[here] + r.mid_shift[here]
            r.mid[here, at] = low.astype(jnp.bfloat16)
            return carry

        lax.fori_loop(0, hidden // 256, units, 0)
        down_w = r.down_w[...].reshape(hidden, columns)
        r.part[pl.ds(th * width, width)] = mul(r.mid[:, at], down_w, TN).astype(jnp.bfloat16)

    descend(1 - x)
    plane_scatter.twin(0).start()
    plane_scatter.twin(1).start()
    plane_scatter.over_first()
    descend(x)
    plane_scatter.twin(2).start()
    plane_scatter.twin(3).start()
    if not first:
        dy_gather.finish()
        saves.append(pltpu.make_async_copy(r.dy_all, r.dy_all_out, r.save_sem.at[8]))
    start_all(saves[7:])
    plane_scatter.first()
    if first:
        next_unit_ride.step(2)
    plane_scatter.second()
    plane_scatter.finish(r.result)
    r.y_out[...] = (r.middle[...] + (r.result[...] + biases[6][...])).astype(r.y_out.dtype)
    gather.finish()
    plane_gather.finish()
    for save in saves:
        save.wait()
    if first:
        next_unit_ride.finish()
        next_head_ride.finish()


def layer_forward_kernel(layer, table, x_in, params, blocks, dy, y_type, collective_id):
    rows, columns = x_in.shape
    hidden_all = params.mid_gain.shape[1]
    total, plane_rows, hidden = rows * 4 * LINE, rows * PLANE, hidden_all // PLANE
    vmem, anywhere, smem = pltpu.VMEM, pl.ANY, pltpu.SMEM
    dma = pltpu.SemaphoreType.DMA
    low = lambda *shape: pltpu.VMEM(shape, jnp.bfloat16)
    full = lambda *shape: pltpu.VMEM(shape, jnp.float32)
    low_out = lambda *shape: jax.ShapeDtypeStruct(shape, jnp.bfloat16)
    full_out = lambda *shape: jax.ShapeDtypeStruct(shape, jnp.float32)
    swap_sems, trade_sems, share_sems = Swap.scratch(), Trade.scratch(), Share.scratch()
    inputs = dict(
        table=(table, smem), scales=(params.head_scale, smem), x_in=(x_in, vmem), gains=(params.vec_gain, vmem),
        biases=(params.vec_bias, vmem), mid_gain_all=(params.mid_gain, vmem), mid_bias_all=(params.mid_bias, vmem),
        w_down=(params.w_down, anywhere), w_out=(params.w_out, anywhere),
    )
    head_shape, unit_shape = (4 * LINE, 32, 384), (LINE, 4, columns // (4 * LINE), hidden)
    outputs = dict(
        y_out=(jax.ShapeDtypeStruct((rows, columns), y_type), vmem), branch=(full_out(rows, columns), vmem),
        middle=(full_out(rows, columns), vmem), ab=(low_out(rows, columns), vmem),
        lse=(full_out(1, total), vmem), head_out=(full_out(64, total), vmem),
        stat=(full_out(2, plane_rows), vmem), hb_all_out=(low_out(total, columns), anywhere),
        qvk_out=(low_out(total // CHUNK, CHUNK, 192), anywhere), out_w_out=(low_out(columns, columns), anywhere),
        rows_all_out=(low_out(plane_rows, columns), anywhere), unit_t_out=(low_out(hidden, columns), anywhere),
        act_out=(full_out(hidden, plane_rows), anywhere), slope_out=(low_out(hidden, plane_rows), anywhere),
        mid_out=(low_out(hidden, plane_rows), anywhere), down_blocks=(low_out(LINE, hidden // LINE, columns), anywhere),
    )
    first = layer == 0
    if first:
        inputs.update(w_qkv=(params.w_qkv, anywhere), w_up=(params.w_up, anywhere))
        head_got, unit_got = (low_out(*head_shape), anywhere), (low_out(*unit_shape), anywhere)
        outputs.update(head_blocks=head_got, unit_blocks=unit_got, next_head=head_got, next_unit=unit_got)
    else:
        inputs.update(head_blocks=(blocks.head, anywhere), unit_blocks=(blocks.unit, anywhere), dy=(dy, vmem))
        outputs.update(dy_all_out=(low_out(plane_rows, columns), anywhere))
    plane_bufs, plane_sems = PlaneScatter.scratch(rows, columns)
    scratch = dict(
        hb_all=low(total, columns), flat=low(total // CHUNK, CHUNK, 192),
        qvk=low(total // CHUNK, CHUNK, 192), queries=low(total, 64), keys=low(total, 64),
        values_t=low(64, total), pairs=low(total // CHUNK, CHUNK // 2, 128),
        packed=low(total // CHUNK, CHUNK // 2, 128), mixed=low(total // CHUNK, CHUNK // 2, 128), head_in=low(4 * LINE, 32, 384), head_w=low(columns, 192),
        unit_in=low(*unit_shape), unit_t=low(hidden, columns),
        down_w=low(LINE, hidden // LINE, columns), out_got=low(LINE, 32, columns),
        out_all=low(columns, columns), out_w=low(columns, columns), rows_all=low(plane_rows, columns),
        act=full(hidden, plane_rows), slope=low(hidden, plane_rows), mid=low(hidden, plane_rows),
        part=low(plane_rows, columns), own_stat=full(2, plane_rows), got_stat=full(PLANE, 2, plane_rows),
        result=full(rows, columns), plane_bufs=plane_bufs, plane_sems=plane_sems,
        gather_sems=GroupGather.scratch(), plane_gather_sems=PlaneGather.scratch(),
        out_gather_sems=PlaneGather.scratch(), pool_sems=([dma((PLANE,)), dma((PLANE,))]),
        head_sems=swap_sems, unit_sems=share_sems, next_head_sems=swap_sems, next_unit_sems=share_sems,
        mix_sems=swap_sems, down_sems=share_sems, out_sems=trade_sems, load_sem=dma((3,)),
        save_sem=dma((9,)),
    )
    scratch.update(mid_gain=full(hidden, 1), mid_shift=full(hidden, 1), mid_bias=full(hidden, 1))
    if first:
        scratch.update(qkv_in=low(*params.w_qkv.shape), head_src=low(2, *head_shape), prep_sem=dma((3,)))
        scratch.update(unit_src=low(2, *unit_shape[1:]), unit_quad=low(2, *unit_shape[1:]), quad_sems=Quad.scratch() * 2)
    else:
        scratch.update(dy_all=low(plane_rows, columns), dy_gather_sems=PlaneGather.scratch())
    kernel = functools.partial(forward_kernel, layer, hidden_all)
    call = lambda body, **how: pl.pallas_call(body, name="layer_forward", **how)
    return launch(call, kernel, inputs, outputs, scratch, collective_id, 95, 56)


class TreeSum:
    def __init__(self, own_ref, total_ref, got, part, line, sems):
        self.own_ref, self.total_ref, self.got, self.part, self.line = own_ref, total_ref, got, part, line
        self.to_send, self.to_recv, self.back_send, self.back_recv = sems[0:4]
        self.trade = Trade(part, line, *sems[4:7])
        self.pool = PlanePool(None, got, None, None)
        self.me = plane_index(self.pool.x, self.pool.y, self.pool.c)

    @staticmethod
    def scratch(rows, columns):
        dma = pltpu.SemaphoreType.DMA
        bufs = [pltpu.VMEM((n, rows // PLANE, columns), jnp.float32) for n in (PLANE, 1, LINE)]
        return bufs, [dma((PLANE,))] * 4 + Trade.scratch()

    def slice(self, m):
        rows = self.part.shape[1]
        return pl.ds(pl.multiple_of(m * rows, 8), rows)

    def to(self, d, x, y, c):
        source = self.own_ref.at[self.slice(plane_index(x, y, c))]
        where = plane_device(x, self.pool.z, y, c)
        return remote(source, self.got.at[self.me], self.to_send.at[d], self.to_recv.at[d], where)

    def back(self, d, x, y, c):
        mine = self.total_ref.at[self.me]
        return remote(mine, mine, self.back_send.at[d], self.back_recv.at[d], plane_device(x, self.pool.z, y, c))

    def arrived(self, ref, recv):
        for d, x, y, c in self.pool.others():
            slot = ref.at[plane_index(x, y, c)]
            remote(slot, slot, recv.at[d], recv.at[d], plane_device(x, self.pool.z, y, c)).wait_recv()

    def start(self):
        for other in self.pool.others():
            self.to(*other).start()

    def along_line(self):
        self.arrived(self.got, self.to_recv)
        self.got[self.me] = self.own_ref[self.slice(self.me)]
        self.part[0] = functools.reduce(jnp.add, [self.got[m] for m in range(PLANE)])
        self.trade.start()

    def give_back(self):
        self.trade.finish()
        self.total_ref[self.me] = functools.reduce(jnp.add, [self.line[zz] for zz in range(LINE)])
        for other in self.pool.others():
            self.back(*other).start()

    def finish(self):
        self.arrived(self.total_ref, self.back_recv)
        for other in self.pool.others():
            self.to(*other).wait_send()
            self.back(*other).wait_send()


class QuickSum:
    def __init__(self, own_ref, plane_got, line_got, sems):
        self.own_ref, self.line_got = own_ref, line_got
        self.pool = PlanePool(own_ref, plane_got, *sems[0:2])
        self.trade = Trade(own_ref, line_got, *sems[2:5])
        self.plane_got = plane_got

    @staticmethod
    def scratch(shape):
        dma = pltpu.SemaphoreType.DMA
        got = [pltpu.VMEM((n, *shape), jnp.float32) for n in (PLANE, LINE)]
        return got, [dma((PLANE,))] * 2 + Trade.scratch()

    def run(self, o_ref):
        self.pool.start()
        self.pool.finish()
        self.own_ref[0] = functools.reduce(jnp.add, [self.plane_got[i] for i in range(PLANE)])
        self.trade.start()
        self.trade.finish()
        o_ref[...] = functools.reduce(jnp.add, [self.line_got[zz] for zz in range(LINE)])


OUT_BIAS, DOWN_BIAS, QUERY_BIAS, VALUE_BIAS, SCALES, MID, SMALL = 6, 7, 8, 9, 10, 12, 24


def spread_head(piece, index, width):
    nothing = jnp.zeros_like(piece)
    even = lax.rem(index, 2) == 0
    pair = jnp.concatenate([jnp.where(even, piece, nothing), jnp.where(even, nothing, piece)], axis=1)
    lanes = lax.broadcasted_iota(jnp.int32, (1, width), 1) // 128
    return jnp.where(lanes == index // 2, jnp.concatenate([pair] * (width // 128), axis=1), 0.0)


def backward_kernel(layer, hidden_all, r):
    first = layer == 1
    x, z, y, c = plane_place()
    index, unit_slot = index_of(z, y, c), (y * 2 + c) * 2 + x
    rows, columns = r.dy.shape
    total = r.hb_all_in.shape[0]
    tiles, chunks, per_tile = total // TILE, total // CHUNK, TILE // CHUNK
    hidden, plane_rows = r.act.shape
    width = plane_rows // 2
    dy_all, x_all = r.wide.at[pl.ds(0, plane_rows)], r.wide.at[pl.ds(plane_rows, plane_rows)]
    plane_gather = PlaneGather(dy_all, r.plane_gather_sems)
    plane_scatter = PlaneScatter(r.part, r.plane_bufs, r.plane_sems)
    out_part = r.part.at[pl.ds(0, LINE * PLANE * 32)]
    out_scatter = PlaneScatter(out_part, r.out_bufs, r.out_sems)
    scatter = GroupScatter(r.wide, r.group_bufs, r.group_sems)
    pool = PlanePool(r.own_sums, r.got_sums, *r.pool_sems)
    unit_ride = Swap(r.gup, r.unit_got, *r.unit_sems)
    out_ride = Trade(r.out_own, r.out_got, *r.out_ride_sems)
    head_cross = Cross(r.head_fold, r.head_other, *r.head_cross_sems)
    down_ride = Trade(r.gdown, r.gdown_got, *r.gdown_sems)
    near_rides = [
        Cross(r.unit_near, r.unit_far, *r.unit_cross_sems), Cross(r.down_near, r.down_far, *r.down_cross_sems),
        Cross(r.out_near, r.out_far, *r.out_cross_sems),
    ]
    if not first:
        late_head_ride = Swap(r.late_head, r.late_head_got, *r.late_head_sems)
        head_ride = Swap(r.head_fold, r.head_got, *r.head_sems)
        bulk = TreeSum(r.bulk, r.bulk_out, *r.bulk_bufs, r.bulk_sems)
        rest = QuickSum(r.rest, *r.rest_got, r.rest_sems)
    hail_all()
    gains = of_layer(r.gains, layer)
    r.small[...] = jnp.zeros_like(r.small)
    dy = r.dy[...].astype(jnp.float32)
    dy_low = dy.astype(jnp.bfloat16)
    r.small[DOWN_BIAS : DOWN_BIAS + 1] = jnp.sum(dy_low.astype(jnp.float32), axis=0, keepdims=True)
    if not first:
        dy_all[pl.ds(plane_index(x, y, c) * rows, rows)] = dy_low
    loads = [
        pltpu.make_async_copy(source, dest, r.load_sem.at[i])
        for i, (source, dest) in enumerate(
            (
                (r.down_blocks, r.down_w), (r.act_in, r.act), (r.slope_in, r.slope), (r.unit_t_in, r.unit_t),
                (r.mid_in, r.mid), (r.rows_all_in, x_all), (r.out_w_in, r.out_w), (r.qvk_in, r.qvk),
            )
        )
    ]
    load_dy = pltpu.make_async_copy(r.dy_all_in, dy_all, r.load_sem.at[8]) if first else None
    if first:
        load_dy.start()
    for load in loads[:6]:
        load.start()
    hailed_by_all()
    if not first:
        plane_gather.start()
        late_head_ride.start()
    for load in loads[6:]:
        load.start()

    def tile_load(t):
        return pltpu.make_async_copy(r.hb_all_in.at[pl.ds(t * TILE, TILE)], r.hb_tiles.at[t % 2], r.tile_sem.at[t % 2])

    tile_load(0).start()
    tile_load(1).start()
    unit_columns([r.mid_gain_all.at[pl.ds(layer, 1)]], unit_slot, [r.mid_gain])
    r.gg[...] = jnp.zeros_like(r.gg)
    r.gs[...] = jnp.zeros_like(r.gs)
    r.gb[...] = jnp.zeros_like(r.gb)
    r.own_sums[...] = jnp.zeros_like(r.own_sums)

    def climb(th):
        at = span_at(th, width)
        mean, rate = mean_and_rate(r.stat[:, at], hidden_all)

        def units(ut, carry):
            here = units_at(ut)
            down_w = r.down_w[pl.ds(ut * 2, 2)].reshape(256, columns)
            dm = mul(down_w, dy_all[pl.ds(th * width, width)], NT)
            r.dmid[here, at] = dm
            vh = (r.act[here, at] - mean) * rate
            r.act[here, at] = vh
            r.gg[here] += jnp.sum(dm * vh, axis=1, keepdims=True)
            r.gs[here] += jnp.sum(dm, axis=1, keepdims=True)
            scaled = dm * r.mid_gain[here]
            r.own_sums[0:1, at] += jnp.sum(scaled, axis=0, keepdims=True)
            r.own_sums[1:2, at] += jnp.sum(scaled * vh, axis=0, keepdims=True)
            return carry

        lax.fori_loop(0, hidden // 256, units, 0)

    if first:
        load_dy.wait()
    else:
        plane_gather.near()
    loads[0].wait()
    loads[1].wait()
    climb(x)
    if not first:
        plane_gather.far()
    climb(1 - x)
    pool.start()
    loads[4].wait()
    for ut in range(hidden // 256):
        grad = mul(r.mid[ut * 256 : (ut + 1) * 256], dy_all[...]).astype(jnp.bfloat16)
        r.gdown[2 * ut : 2 * ut + 2] = grad.reshape(2, 128, columns)
    down_ride.start()
    pool.finish()
    r.sums[...] = functools.reduce(jnp.add, [r.got_sums[i] for i in range(PLANE)]) * (1.0 / hidden_all)
    loads[2].wait()
    loads[3].wait()

    def descend(th):
        at = span_at(th, width)
        _, rate = mean_and_rate(r.stat[:, at], hidden_all)
        sum0, sum1 = r.sums[0:1, at], r.sums[1:2, at]

        def units(ut, carry):
            here = units_at(ut)
            dact = rate * (r.dmid[here, at] * r.mid_gain[here] - sum0 - r.act[here, at] * sum1)
            du = (dact * r.slope[here, at].astype(jnp.float32)).astype(jnp.bfloat16)
            r.du[here, at] = du
            r.gb[here] += jnp.sum(du.astype(jnp.float32), axis=1, keepdims=True)
            return carry

        lax.fori_loop(0, hidden // 256, units, 0)
        r.part[pl.ds(th * width, width)] = mul(r.du[:, at], r.unit_t[...], TN).astype(jnp.bfloat16)

    descend(1 - x)
    plane_scatter.twin(0).start()
    plane_scatter.twin(1).start()
    plane_scatter.over_first()
    descend(x)
    plane_scatter.twin(2).start()
    plane_scatter.twin(3).start()
    plane_scatter.first()
    loads[5].wait()
    plane_scatter.second()
    for ut in range(hidden // 256):
        grad = jnp.transpose(mul(r.du[ut * 256 : (ut + 1) * 256], x_all[...])).astype(jnp.bfloat16)
        r.gup[:, :, ut * 256 : (ut + 1) * 256] = grad.reshape(r.gup.shape[0], -1, 256)
    plane_scatter.finish(r.dffn)
    if not first:
        plane_gather.finish()

    back, r.small[2:3], r.small[5:6] = normed_back(r.middle[...], gains[2][...], r.dffn[...])
    r.dmiddle[...] = dy + back
    back, r.small[1:2], r.small[4:5] = normed_back(r.branch[...], gains[1][...], r.dmiddle[...])
    dz = back.astype(jnp.bfloat16)
    r.small[OUT_BIAS : OUT_BIAS + 1] = jnp.sum(dz.astype(jnp.float32), axis=0, keepdims=True)
    loads[6].wait()
    da = mul(dz, r.out_w[...], NT).astype(jnp.bfloat16)
    per_block = rows // CHUNK
    halves = da.reshape(per_block, 2, CHUNK // 2, columns)
    low, high = halves[:, 0].reshape(rows // 2, columns), halves[:, 1].reshape(rows // 2, columns)
    for h in range(columns // 64):
        at = slice(64 * h, 64 * h + 64)
        pairs = jnp.concatenate([low[:, at], high[:, at]], axis=1)
        r.packed[h * per_block : (h + 1) * per_block] = pairs.reshape(per_block, CHUNK // 2, 128)
    mix = Swap(r.packed, r.mixed, *r.mix_sems, per=per_block)
    mix.start()
    out_rows = LINE * 32
    for zz in range(LINE):
        grad = mul(r.ab[:, 256 * zz : 256 * zz + 256], dz, TN).astype(jnp.bfloat16)
        for s in range(PLANE):
            at = natural_rows(s, 0)
            out_part[s * out_rows + zz * 32 : s * out_rows + zz * 32 + 32] = grad[at : at + 32]
    for which in range(4):
        out_scatter.twin(which).start()
    turned = [ref[128 * zz : 128 * zz + 128] for ref in (r.gg, r.gs, r.gb) for zz in range(LINE)]
    turned = jnp.transpose(jnp.concatenate(turned + [jnp.zeros((128, 4), jnp.float32)], axis=1))
    for i in range(3 * LINE):
        r.small[MID + i : MID + i + 1, unit_lanes(0, unit_slot)] = turned[i : i + 1]
    loads[7].wait()
    load_head = pltpu.make_async_copy(r.head_blocks, r.head_fold, r.load_sem.at[6])
    load_head.start()
    scale = r.scales[layer, index]

    def prepare(t, carry):
        at = tile_at(t)
        rows_t = chunks_of(r.qvk, t)
        r.query[at] = rows_t[:, 0:64] * 0.125
        r.values[at] = rows_t[:, 64:128]
        key = rows_t[:, 128:192]
        r.keys[at] = key
        r.keys_t[:, at] = jnp.transpose(key.astype(jnp.float32)).astype(jnp.bfloat16)
        r.dkeys[at] = jnp.zeros((TILE, 64), jnp.float32)
        r.dvalues[at] = jnp.zeros((TILE, 64), jnp.float32)
        return carry

    lax.fori_loop(0, tiles, prepare, 0)
    load_head.wait()
    unfold_head(r.head_fold, r.head_w)
    out_scatter.over_first()
    out_scatter.first()
    mix.finish()
    unit_ride.start()

    def arrange(p, carry):
        r.packed[p] = r.mixed[r.table[p]]
        return carry

    lax.fori_loop(0, chunks, arrange, 0)

    def unpack(t, carry):
        at = tile_at(t)
        pairs = r.packed[pl.ds(t * per_tile, per_tile)].astype(jnp.float32)
        pairs = jnp.concatenate([pairs[:, :, 0:64], pairs[:, :, 64:128]], axis=1).reshape(TILE, 64)
        low = (pairs * scale).astype(jnp.bfloat16)
        r.dout[at] = low
        r.delta[:, at] = jnp.sum(jnp.transpose(low.astype(jnp.float32)) * r.head_out[:, at], axis=0, keepdims=True)
        return carry

    lax.fori_loop(0, tiles, unpack, 0)
    lanes = lax.broadcasted_iota(jnp.int32, (1, columns), 1)
    scale_grad = jnp.sum(r.delta[...], axis=1, keepdims=True) / scale
    r.small[SCALES : SCALES + 1] = jnp.where(lanes == layer * 4 * LINE + index, scale_grad, 0.0)
    cut = r.table[2 * chunks]
    for i in range(tiles):
        at = slice(i * TILE, (i + 1) * TILE)
        query, dout, lse, delta = r.query[at], r.dout[at], r.lse[:, at], r.delta[:, at]

        def block(j, total_dq, masked):
            there = tile_at(j)
            scores = mul(r.keys[there], query, NT)
            weights = jnp.exp(scores - (lse if masked else lse - alive(cut, i, j)))
            if masked:
                weights = jnp.where(diagonal(scores), weights, 0.0)
            dweights = mul(r.values[there], dout, NT)
            dscores = (weights * (dweights - delta)).astype(jnp.bfloat16)
            r.dvalues[there] += mul(weights.astype(jnp.bfloat16), dout)
            r.dkeys[there] += mul(dscores, query)
            return total_dq + mul(r.keys_t[:, there], dscores)

        total_dq = block(i, jnp.zeros((64, TILE), jnp.float32), True)
        if i > 0:
            total_dq = lax.fori_loop(0, i, functools.partial(block, masked=False), total_dq)
        r.dquery_t[:, at] = total_dq * 0.125
        if i == 2:
            out_scatter.second()
    out_sum = r.dffn.at[pl.ds(0, out_rows)]
    out_scatter.finish(out_sum)
    r.out_own[...] = out_sum[...].reshape(r.out_own.shape).astype(jnp.bfloat16)
    out_ride.start()

    head_bias = jnp.zeros((1, 192), jnp.float32)
    for i in range(tiles):
        at = slice(i * TILE, (i + 1) * TILE)
        joined = jnp.concatenate([jnp.transpose(r.dquery_t[:, at]), r.dvalues[at], r.dkeys[at]], axis=1).astype(jnp.bfloat16)
        head_bias += jnp.sum(joined.astype(jnp.float32), axis=0, keepdims=True)
        r.qvk[i * per_tile : (i + 1) * per_tile] = joined.reshape(per_tile, CHUNK, 192)

    r.small[QUERY_BIAS : QUERY_BIAS + 1] = spread_head(head_bias[:, 0:64], index, columns)
    r.small[VALUE_BIAS : VALUE_BIAS + 1] = spread_head(head_bias[:, 64:128], index, columns)

    if not first:
        r.bulk[0:SMALL] = r.small_in[...]
        r.bulk[SMALL : 2 * SMALL] = r.small[...]
        r.bulk[2 * SMALL :] = jnp.zeros((r.bulk.shape[0] - 2 * SMALL, columns), jnp.float32)
        bulk.start()

    def restore(p, carry):
        r.flat[p] = r.qvk[r.table[chunks + p]]
        return carry

    lax.fori_loop(0, chunks, restore, 0)

    def project(owner):
        rows_of = r.flat[pl.ds(owner * per_block, per_block)].reshape(rows, 192)
        r.wide[pl.ds(owner * rows, rows)] = mul(rows_of, r.head_w[...], NT).astype(jnp.bfloat16)

    for own_y in (0, 1):
        for t in range(LINE):
            for other_core in (1, 0):
                project(scatter.owner(t, own_y, 1 - c if other_core else c))
                if other_core:
                    scatter.start(t, own_y)
    for t in range(tiles):
        tile_load(t).wait()
        grad = mul(chunks_of(r.flat, t), r.hb_tiles[t % 2], TN)
        r.gw[...] = grad if t == 0 else r.gw[...] + grad
        if t + 2 < tiles:
            tile_load(t + 2).start()
    turned = jnp.transpose(r.gw[...]).astype(jnp.bfloat16)
    for j in range(r.head_fold.shape[0]):
        for part in range(2):
            piece = turned[64 * j + 32 * part : 64 * j + 32 * part + 32]
            r.head_fold[j, :, 128 * part : 128 * part + 128] = piece[:, 0:128]
            r.head_fold[j, :, 256 + 64 * part : 320 + 64 * part] = piece[:, 128:192]
    head_cross.start()
    scatter.first()
    if not first:
        bulk.along_line()
    down_ride.finish()
    out_ride.finish()
    unit_ride.finish()
    reloads = [
        pltpu.make_async_copy(source, dest, r.load_sem.at[i])
        for i, (source, dest) in enumerate(((r.unit_got, r.gup), (r.gdown_got, r.gdown), (r.out_got, r.out_own)))
    ]
    for load in reloads:
        load.start()
    head_cross.finish()
    both = (r.head_fold[...].astype(jnp.float32) + r.head_other[...].astype(jnp.float32)).astype(jnp.bfloat16)
    if first:
        r.head_sum[...] = both
    else:
        r.head_fold[...] = both
        head_ride.start()
    for load in reloads:
        load.wait()
    for q in range(4):
        parts = [r.gup[zz * 4 + q].astype(jnp.float32) for zz in range(LINE)]
        r.unit_near[q] = functools.reduce(jnp.add, parts).astype(jnp.bfloat16)
    for near, own in ((r.down_near, r.gdown), (r.out_near, r.out_own)):
        near[...] = functools.reduce(jnp.add, [own[zz].astype(jnp.float32) for zz in range(LINE)]).astype(jnp.bfloat16)
    start_all(near_rides)
    scatter.second(r.dffn)
    back, gain_grad, shift_grad = normed_back(r.x_in[...].astype(jnp.float32), gains[0][...], r.dffn[...])
    r.dx[...] = r.dmiddle[...] + back
    r.small[0:1] = gain_grad
    r.small[3:4] = shift_grad
    if not first:
        r.rest[0, 0:1] = gain_grad
        r.rest[0, 1:2] = shift_grad
        bulk.give_back()
        rest.run(r.rest_out)
        bulk.finish()
    scatter.finish()
    if not first:
        head_ride.finish()
        late_head_ride.finish()
    finish_all(near_rides)


def layer_backward_kernel(layer, table, dy, params, record, later, collective_id):
    rows, columns = dy.shape
    hidden_all = params.mid_gain.shape[1]
    total, plane_rows, hidden = rows * 4 * LINE, rows * PLANE, hidden_all // PLANE
    vmem, anywhere, smem = pltpu.VMEM, pl.ANY, pltpu.SMEM
    dma = pltpu.SemaphoreType.DMA
    low = lambda *shape: pltpu.VMEM(shape, jnp.bfloat16)
    full = lambda *shape: pltpu.VMEM(shape, jnp.float32)
    low_out = lambda *shape: jax.ShapeDtypeStruct(shape, jnp.bfloat16)
    full_out = lambda *shape: jax.ShapeDtypeStruct(shape, jnp.float32)
    swap_sems, trade_sems, cross_sems = Swap.scratch(), Trade.scratch(), Cross.scratch()
    unit_shape = (4 * LINE, columns // (4 * LINE), hidden)
    unit_near, down_near, out_near = (4, *unit_shape[1:]), (hidden // LINE, columns), (32, columns)
    down_shape = (LINE, hidden // LINE, columns)
    inputs = dict(
        table=(table, smem), scales=(params.head_scale, smem), dy=(dy, vmem), gains=(params.vec_gain, vmem),
        mid_gain_all=(params.mid_gain, vmem), x_in=(record.x_in, vmem), branch=(record.branch, vmem),
        middle=(record.middle, vmem), ab=(record.ab, vmem), lse=(record.lse, vmem),
        head_out=(record.head_out, vmem), stat=(record.stat, vmem), hb_all_in=(record.hb_all_out, anywhere),
        qvk_in=(record.qvk_out, anywhere), out_w_in=(record.out_w_out, anywhere),
        rows_all_in=(record.rows_all_out, anywhere), unit_t_in=(record.unit_t_out, anywhere),
        act_in=(record.act_out, anywhere), slope_in=(record.slope_out, anywhere),
        mid_in=(record.mid_out, anywhere), down_blocks=(record.down_blocks, anywhere),
        head_blocks=(record.head_blocks, anywhere),
    )
    outputs = dict(
        dx=(full_out(rows, columns), vmem), unit_got=(low_out(*unit_shape), anywhere),
        gdown_got=(low_out(*down_shape), anywhere), out_got=(low_out(LINE, *out_near), anywhere),
        unit_near=(low_out(*unit_near), vmem),
        down_near=(low_out(*down_near), vmem), out_near=(low_out(*out_near), vmem),
        unit_far=(low_out(*unit_near), anywhere), down_far=(low_out(*down_near), anywhere),
        out_far=(low_out(*out_near), anywhere),
    )
    first = layer == 1
    if first:
        inputs.update(dy_all_in=(record.dy_all_out, anywhere))
        outputs.update(small=(full_out(SMALL, columns), vmem), head_sum=(low_out(4 * LINE, 32, 384), vmem))
    else:
        inputs.update(small_in=(later.small, vmem), late_head=(later.head_sum, anywhere))
        outputs.update(head_got=(low_out(4 * LINE, 32, 384), anywhere), late_head_got=(low_out(4 * LINE, 32, 384), anywhere))
        outputs.update(bulk_out=(full_out(PLANE, 8, columns), vmem), rest_out=(full_out(2, columns), vmem))
    plane_bufs, plane_sems = PlaneScatter.scratch(rows, columns)
    out_bufs, out_sems = PlaneScatter.scratch(LINE * 32, columns)
    group_bufs, group_sems = GroupScatter.scratch(rows, columns)
    scratch = dict(
        wide=low(total, columns), down_w=low(*down_shape), act=full(hidden, plane_rows),
        slope=low(hidden, plane_rows), unit_t=low(hidden, columns), mid=low(hidden, plane_rows),
        out_w=low(columns, columns), qvk=low(total // CHUNK, CHUNK, 192), hb_tiles=low(2, TILE, columns),
        dmid=full(hidden, plane_rows), du=low(hidden, plane_rows), part=low(plane_rows, columns),
        own_sums=full(2, plane_rows), got_sums=full(PLANE, 2, plane_rows), sums=full(2, plane_rows),
        gup=low(*unit_shape), gdown=low(*down_shape), dffn=full(rows, columns),
        dmiddle=full(rows, columns), packed=low(total // CHUNK, CHUNK // 2, 128),
        mixed=low(total // CHUNK, CHUNK // 2, 128),
        out_own=low(LINE, 32, columns),
        dout=low(total, 64), delta=full(1, total), query=low(total, 64),
        keys=low(total, 64), values=low(total, 64), keys_t=low(64, total), dkeys=full(total, 64),
        dvalues=full(total, 64), dquery_t=full(64, total), flat=low(total // CHUNK, CHUNK, 192),
        head_w=low(columns, 192), gw=full(192, columns),
        head_other=low(4 * LINE, 32, 384), head_fold=low(4 * LINE, 32, 384),
        plane_bufs=plane_bufs, plane_sems=plane_sems, out_bufs=out_bufs, out_sems=out_sems,
        group_bufs=group_bufs, group_sems=group_sems, plane_gather_sems=PlaneGather.scratch(),
        pool_sems=([dma((PLANE,)), dma((PLANE,))]), unit_sems=swap_sems, gdown_sems=trade_sems, head_sems=swap_sems,
        mix_sems=swap_sems, out_ride_sems=trade_sems, head_cross_sems=cross_sems, load_sem=dma((10,)),
        tile_sem=dma((2,)),
    )
    scratch.update(unit_cross_sems=cross_sems, down_cross_sems=cross_sems, out_cross_sems=cross_sems)
    scratch.update(mid_gain=full(hidden, 1), gg=full(hidden, 1), gs=full(hidden, 1), gb=full(hidden, 1))
    if not first:
        scratch.update(late_head_sems=swap_sems, small=full(SMALL, columns), bulk=full(8 * PLANE, columns), rest=full(1, 2, columns))
        bulk_bufs, bulk_sems = TreeSum.scratch(8 * PLANE, columns)
        scratch.update(bulk_bufs=bulk_bufs, bulk_sems=bulk_sems)
        rest_got, rest_sems = QuickSum.scratch((2, columns))
        scratch.update(rest_got=rest_got, rest_sems=rest_sems)
    kernel = functools.partial(backward_kernel, layer, hidden_all)
    call = lambda body, **how: pl.pallas_call(body, name="layer_backward", **how)
    return launch(call, kernel, inputs, outputs, scratch, collective_id, 105, 63)


def assemble_kernel(r):
    x = lax.axis_index("batch")
    for layer, got in enumerate((r.layer0, r.layer1)):
        head_ref, unit_near, unit_far, down_near, down_far, out_near, out_far = got
        width = 64 * head_ref.shape[0]
        for j in range(0, head_ref.shape[0], 2):
            left, right = head_ref[j].astype(jnp.float32), head_ref[j + 1].astype(jnp.float32)
            for part in range(2):
                for at, source in ((0, 128 * part), (width, 256 + 64 * part), (2 * width, 64 + 128 * part)):
                    pair = jnp.concatenate([left[:, source : source + 64], right[:, source : source + 64]], axis=1)
                    r.qkv[layer, 32 * part : 32 * part + 32, at + j * 64 : at + (j + 2) * 64] = pair
        for half, unit_ref, down_ref, out_ref in ((x, unit_near, down_near, out_near), (1 - x, unit_far, down_far, out_far)):
            for q in range(unit_ref.shape[0]):
                for z in range(LINE):
                    piece = unit_ref[q, :, z * 128 : (z + 1) * 128].astype(jnp.float32)
                    r.up[layer, :, unit_lanes(z, q * 2 + half)] = piece
            for ref, dest in ((down_ref, r.down), (out_ref, r.out)):
                rows = ref.shape[0]
                dest[layer, pl.ds(pl.multiple_of(half * rows, rows), rows)] = ref[...].astype(jnp.float32)
        per = r.bulk.shape[1]
        bulk = r.bulk[SMALL // per * (1 - layer) : SMALL // per * (2 - layer)].reshape(SMALL, -1)
        gain, shift = (r.rest[0:1], r.rest[1:2]) if layer == 0 else (bulk[0:1], bulk[3:4])
        heads = bulk[QUERY_BIAS : VALUE_BIAS + 1]
        gain_rows = jnp.concatenate([gain, bulk[1:3]], axis=0)
        bias_rows = jnp.concatenate([shift, bulk[4:6], heads, bulk[OUT_BIAS : DOWN_BIAS + 1]], axis=0)
        for ref, rows in ((r.vec_gain, gain_rows), (r.vec_bias, bias_rows)):
            for i in range(ref.shape[0]):
                ref[i, layer : layer + 1] = rows[i : i + 1]
        for z in range(LINE):
            at = slice(z * PLANE * 128, (z + 1) * PLANE * 128)
            r.mid_gain[layer : layer + 1, at] = bulk[MID + z : MID + z + 1]
            for i in range(2):
                row = MID + (i + 1) * LINE + z
                r.mid_bias[layer, i : i + 1, at] = bulk[row : row + 1]
        row = bulk[SCALES : SCALES + 1]
        heads_here = r.head_scale.shape[1]
        r.head_scale[layer : layer + 1] = row[:, layer * heads_here : (layer + 1) * heads_here]


def assemble(results, dx, back, shapes):
    vmem, anywhere = pl.BlockSpec(memory_space=pltpu.VMEM), pl.BlockSpec(memory_space=pl.ANY)
    arrays = [results, dx]
    for got, head in zip(back, (back[0].head_got, back[0].late_head_got)):
        arrays += [head, got.unit_near, got.unit_far, got.down_near, got.down_far, got.out_near, got.out_far]

    arrays += [back[0].bulk_out, back[0].rest_out]
    n = len(arrays)

    def body(*refs):
        ins, outs, held, sem = refs[:n], refs[n : n + 11], refs[n + 11 : -1], refs[-1]
        loads = [pltpu.make_async_copy(ins[i], held[i], sem.at[i]) for i in range(n)]
        passes = [pltpu.make_async_copy(held[i], outs[i], sem.at[i]) for i in range(2)]
        for load in loads:
            load.start()
        for load in loads:
            load.wait()
        for copy in passes:
            copy.start()
        qkv, out, up, down, vec_gain, vec_bias, mid_gain, mid_bias, head_scale = outs[2:]
        refs = held[2:]
        assemble_kernel(
            Refs(
                layer0=refs[0:7], layer1=refs[7:14], bulk=refs[14], rest=refs[15], qkv=qkv, out=out, up=up, down=down,
                vec_gain=vec_gain, vec_bias=vec_bias, mid_gain=mid_gain, mid_bias=mid_bias, head_scale=head_scale,
            )
        )
        for copy in passes:
            copy.wait()

    return pl.pallas_call(
        body,
        out_shape=[jax.ShapeDtypeStruct(array.shape, array.dtype) for array in (results, dx)]
        + [jax.ShapeDtypeStruct(shape, jnp.float32) for shape in shapes],
        in_specs=[anywhere] * n,
        out_specs=[anywhere] * 2 + [vmem] * len(shapes),
        scratch_shapes=[pltpu.VMEM(array.shape, array.dtype) for array in arrays] + [pltpu.SemaphoreType.DMA((n,))],
        cost_estimate=lasting(5),
        compiler_params=pltpu.CompilerParams(vmem_limit_bytes=62 << 20),
        name="assemble",
    )(*arrays)


def chunk_table(first_rows, span_of, rows_here):
    blocks = span_of.shape[0]
    first = first_rows[0]
    second = rows_here - first
    row = jnp.arange(blocks * rows_here // CHUNK, dtype=jnp.int32) * CHUNK
    later = row >= first * blocks
    inside = jnp.where(later, row - first * blocks, row)
    length = jnp.where(later, jnp.maximum(second, 1), first)
    span = inside // length
    of_span = (span_of[None, :] == span[:, None]).astype(jnp.int32)
    device_of = jnp.sum(of_span * jnp.arange(blocks, dtype=jnp.int32)[None, :], axis=1)
    source = device_of * rows_here + jnp.where(later, first, 0) + inside - span * length
    within = row % rows_here
    behind = within >= first
    place = jnp.repeat(span_of, rows_here // CHUNK) * jnp.where(behind, second, first) + within
    place = place + jnp.where(behind, first * (blocks - 1), 0)
    return jnp.concatenate([source // CHUNK, place // CHUNK, (first * blocks // TILE)[None]]).astype(jnp.int32)


def travel(
    tokens, grad_out, first_rows, span_of, w_qkv, w_out, w_up, w_down, vec_gain, vec_bias, mid_gain, mid_bias, head_scale
):
    rows_here, row_width = tokens.shape
    table = chunk_table(first_rows, span_of, rows_here)
    params = Refs(
        w_qkv=w_qkv, w_up=w_up, w_out=w_out.reshape(2, 2, -1, row_width), w_down=w_down.reshape(2, 2, -1, row_width),
        vec_gain=vec_gain.transpose(1, 0, 2), vec_bias=vec_bias.transpose(1, 0, 2), mid_gain=mid_gain, mid_bias=mid_bias,
        head_scale=head_scale,
    )
    first = layer_forward_kernel(0, table, tokens, params, None, None, jnp.float32, 0)
    first.x_in = tokens
    blocks = Refs(head=first.next_head, unit=first.next_unit)
    second = layer_forward_kernel(1, table, first.y_out, params, blocks, grad_out, jnp.bfloat16, 1)
    second.x_in, second.head_blocks = first.y_out, first.next_head
    back_second = layer_backward_kernel(1, table, grad_out, params, second, None, 2)
    back_first = layer_backward_kernel(0, table, back_second.dx, params, first, back_second, 3)
    kinds = (w_qkv, w_out, w_up, w_down, params.vec_gain, params.vec_bias, mid_gain, mid_bias, head_scale)
    results = assemble(second.y_out, back_first.dx, [back_first, back_second], [array.shape for array in kinds])
    return (*results[:6], results[6].transpose(1, 0, 2), results[7].transpose(1, 0, 2), *results[8:])


def local(*args):
    tokens, w_qkv = args[0], args[4]
    blocks = lax.axis_size("blk")
    heads = w_qkv.shape[2] // (3 * HEAD_DIM)
    if blocks == heads == 4 * LINE and lax.axis_size("batch") == 2 and tokens.shape[0] * blocks % TILE == 0:
        return travel(*args)
    return general(*args)


def solution(mesh):
    placed = (
        P(("batch", "blk"), None),
        P(("batch", "blk"), None),
        P("batch"),
        P(),
        P(None, "blk", None),
        P(None, "blk", None),
        P(None, "blk", None),
        P(None, "blk", None),
        P(),
        P(),
        P(),
        P(),
        P(),
    )
    return jax.shard_map(
        local,
        mesh=mesh,
        in_specs=placed,
        out_specs=(
            P(("batch", "blk"), None),
            P(("batch", "blk"), None),
            P(None, "blk", None),
            P(None, "blk", None),
            P(None, "blk", None),
            P(None, "blk", None),
            P(),
            P(),
            P(),
            P(),
            P(),
        ),
        check_vma=False,
    )
```
